32 devices in a mesh: dp: 16 (over z, x, core), tensor: 2 (over y).
Axes of the slice: x: 2, y: 2, z: 4, core: 2. Of those that a mesh axis runs over, the one named last changes fastest.
Arguments:
- inputs: bfloat16 [16384, 512], P('dp'), may hold values from -6 to 6
- memory: bfloat16 [16384, 512], P('dp'), may hold values from -6 to 6
- cotangent: bfloat16 [16384, 512], P('dp'), may hold values from -6 to 6
- dec_lengths: int32 [16, 16], P('dp'), may hold values from 1 to 384, 1024 in all within a row
- mem_lengths: int32 [16, 16], P('dp'), may hold values from 1 to 384, 1024 in all within a row
- counts: int32 [16], P('dp'), may hold values from 8 to 16
- self_gain: float32 [512], replicated, may hold values from 0.5 to 1.5
- self_query: bfloat16 [512, 512], P(None, 'tensor'), may hold values from -0.0625 to 0.0625
- self_key: bfloat16 [512, 512], P(None, 'tensor'), may hold values from -0.25 to 0.25
- self_value: bfloat16 [512, 512], P(None, 'tensor'), may hold values from -0.25 to 0.25
- self_out: bfloat16 [512, 512], P('tensor'), may hold values from -0.75 to 0.75
- rel_table: float32 [32, 8], P(None, 'tensor'), may hold values from -4 to 4
- cross_gain: float32 [512], replicated, may hold values from 0.5 to 1.5
- cross_query: bfloat16 [512, 512], P(None, 'tensor'), may hold values from -0.0625 to 0.0625
- cross_key: bfloat16 [512, 512], P(None, 'tensor'), may hold values from -0.25 to 0.25
- cross_value: bfloat16 [512, 512], P(None, 'tensor'), may hold values from -0.25 to 0.25
- cross_out: bfloat16 [512, 512], P('tensor'), may hold values from -0.75 to 0.75
- feed_gain: float32 [512], replicated, may hold values from 0.5 to 1.5
- feed_in: bfloat16 [512, 2048], P(None, 'tensor'), may hold values from -0.25 to 0.25
- feed_out: bfloat16 [2048, 512], P('tensor'), may hold values from -0.125 to 0.125
Outputs:
- output: bfloat16 [16384, 512], P('dp')
- grad_inputs: bfloat16 [16384, 512], P('dp')
- grad_memory: bfloat16 [16384, 512], P('dp', 'tensor')
- grad_self_gain: float32 [512], replicated
- grad_self_query: float32 [512, 512], P(None, 'tensor')
- grad_self_key: float32 [512, 512], P(None, 'tensor')
- grad_self_value: float32 [512, 512], P(None, 'tensor')
- grad_self_out: float32 [512, 512], P('tensor')
- grad_rel_table: float32 [32, 8], P(None, 'tensor')
- grad_cross_gain: float32 [512], replicated
- grad_cross_query: float32 [512, 512], P(None, 'tensor')
- grad_cross_key: float32 [512, 512], P(None, 'tensor')
- grad_cross_value: float32 [512, 512], P(None, 'tensor')
- grad_cross_out: float32 [512, 512], P('tensor')
- grad_feed_gain: float32 [512], replicated
- grad_feed_in: float32 [512, 2048], P(None, 'tensor')
- grad_feed_out: float32 [2048, 512], P('tensor')
The draws below stay inside these ranges and needn't reach their ends.
Inputs may be any that keep to these rules, and one draw needn't show every extreme that they name: `dec_lengths`: A row's 16 decoder example lengths in order, summing to 1024; slots from the row's count on are padding. `mem_lengths`: A row's 16 memory example lengths in order, summing to 1024; decoder example k reads memory example k.
All inputs are finite; a program needn't handle non-finite values.
Results may differ from the reference program's by a relative error of at most 0.039.
Values may be sent and summed in bfloat16 or wider, within the bound.
No kernel may reach another device: no remote copies, remote signals or barrier semaphores. Data moves between devices by JAX's collectives and lax.ppermute only.
A program may use at most 192 MiB of HBM per device.

```python
import math
import jax
import jax.numpy as jnp
import numpy as np
from jax import lax

D = 512
HEADS = 8
DK = 64
FF = 2048
NB = 32
MAXDIST = 128
LEN = 1024
SEGS = 16
MOST = 384
HD = 512
ROWS = 16
TOKENS = 16384
N_TENSOR = 2


def with_ends(entries, rng, least, top_value):
    place = [jax.random.randint(jax.random.fold_in(rng, axis), (), 0, length) for axis, length in enumerate(entries.shape)]
    longest = entries.shape.index(max(entries.shape))
    next_to = place[:longest] + [(place[longest] + 1) % entries.shape[longest]] + place[longest + 1:]
    return entries.at[tuple(place)].set(least).at[tuple(next_to)].set(top_value)


def shard_levels(own_key, dims, pieces, least, top_value):
    loudness, own = 1.0, jax.random.fold_in(own_key, 6)
    for position, blocks in pieces:
        draws = jnp.exp(jax.random.uniform(jax.random.fold_in(own, position), (blocks,), jnp.float32, least / len(pieces), top_value / len(pieces)))
        loudness = loudness * jnp.repeat(draws, dims[position] // blocks).reshape([-1 if axis == position else 1 for axis in range(len(dims))])
    return loudness


def length_profile(count, total, bound, slope):
    loads = [(1 << 20) // math.isqrt(rank ** slope) + 1 for rank in range(2, count + 1)]
    rest, holding = total - bound - (count - 1), [1] * (count - 1)
    while rest > 0:
        free = [i for i in range(count - 1) if holding[i] < bound]
        whole, remaining = sum([loads[i] for i in free]), rest
        for i in free:
            extra = min(bound - holding[i], max(1, remaining * loads[i] // whole), rest)
            holding[i] = holding[i] + extra
            rest = rest - extra
    return np.array([bound] + holding)


def ragged_sizes(own_key, amount, total, limit, lean):
    if amount == 2:
        one = jax.random.randint(own_key, (), max(1, total - limit), min(limit, total - 1) + 1)
        return jnp.stack([one, total - one])
    sizes = jnp.asarray(length_profile(amount, total, limit, lean), jnp.int32)
    pairs = (amount - 1) // 2
    giver, sink = sizes[1:1 + 2 * pairs:2], sizes[2:2 + 2 * pairs:2]
    margin = jnp.minimum(giver - 1, limit - sink)
    moved = jax.random.randint(jax.random.fold_in(own_key, 1), (pairs,), 0, 1 << 20) % (margin + 1)
    sizes = sizes.at[1:1 + 2 * pairs:2].set(giver - moved).at[2:2 + 2 * pairs:2].set(sink + moved)
    return sizes[jax.random.permutation(jax.random.fold_in(own_key, 2), amount)]


def centred(own_key, shape, deviation, reach, split=(), held_as=jnp.bfloat16):
    array = jax.random.normal(own_key, shape, jnp.float32) * deviation
    if len(split) > 0:
        array = shard_levels(own_key, shape, split, -0.22, 0.18) * array
    return jnp.clip(array, min=-reach, max=reach).astype(held_as)


def setup_inputs(seed: int = 0) -> dict:
    arg_keys = jax.random.split(jax.random.key(seed), 21)
    return {
        "inputs": centred(arg_keys[0], (TOKENS, D), 1.0, 6.0, ((0, 16),)),
        "memory": centred(arg_keys[1], (TOKENS, D), 1.0, 6.0, ((0, 16),)),
        "cotangent": centred(arg_keys[2], (TOKENS, D), 1.0, 6.0, ((0, 16),)),
        "dec_lengths": jax.vmap(lambda own: ragged_sizes(own, SEGS, LEN, MOST, 1))(jax.random.split(arg_keys[3], ROWS)).reshape((ROWS, SEGS)).astype(jnp.int32),
        "mem_lengths": jax.vmap(lambda own: ragged_sizes(own, SEGS, LEN, MOST, 1))(jax.random.split(arg_keys[4], ROWS)).reshape((ROWS, SEGS)).astype(jnp.int32),
        "counts": with_ends(jax.random.randint(arg_keys[5], (ROWS,), SEGS // 2, SEGS + 1), jax.random.fold_in(arg_keys[5], 1), SEGS // 2, SEGS).astype(jnp.int32),
        "self_gain": jnp.clip(1.0 + 0.1 * jax.random.normal(arg_keys[6], (D,), jnp.float32), 0.5, 1.5),
        "self_query": centred(arg_keys[7], (D, HD), (16 * D) ** -0.5, 0.0625, ((1, 2),)),
        "self_key": centred(arg_keys[8], (D, HD), D ** -0.5, 0.25, ((1, 2),)),
        "self_value": centred(arg_keys[9], (D, HD), D ** -0.5, 0.25, ((1, 2),)),
        "self_out": centred(arg_keys[10], (HD, D), (HD // 8) ** -0.5, 0.75, ((0, 2),)),
        "rel_table": centred(arg_keys[11], (NB, HEADS), 1.0, 4.0, ((1, 2),), jnp.float32),
        "cross_gain": jnp.clip(1.0 + 0.1 * jax.random.normal(arg_keys[12], (D,), jnp.float32), 0.5, 1.5),
        "cross_query": centred(arg_keys[13], (D, HD), (16 * D) ** -0.5, 0.0625, ((1, 2),)),
        "cross_key": centred(arg_keys[14], (D, HD), D ** -0.5, 0.25, ((1, 2),)),
        "cross_value": centred(arg_keys[15], (D, HD), D ** -0.5, 0.25, ((1, 2),)),
        "cross_out": centred(arg_keys[16], (HD, D), (HD // 8) ** -0.5, 0.75, ((0, 2),)),
        "feed_gain": jnp.clip(1.0 + 0.1 * jax.random.normal(arg_keys[17], (D,), jnp.float32), 0.5, 1.5),
        "feed_in": centred(arg_keys[18], (D, FF), D ** -0.5, 0.25, ((1, 2),)),
        "feed_out": centred(arg_keys[19], (FF, D), FF ** -0.5, 0.125, ((0, 2),)),
    }


masked_score = -1e+30
epsilon = 1e-06
highest = lax.Precision.HIGHEST

@jax.custom_vjp
def low(v):
    return lax.optimization_barrier(v.astype(jnp.bfloat16)).astype(jnp.float32)

@jax.custom_vjp
def low_back(v):
    return v

def low_keep(v):
    return (low(v), None)

def low_pass(kept, grad):
    return (grad,)

def back_keep(v):
    return (v, None)

def back_low(kept, grad):
    return (low(grad),)
low.defvjp(low_keep, low_pass)
low_back.defvjp(back_keep, back_low)

def rounded_both(value):
    return low_back(low(value))

def high_dot(left, right):
    return jnp.dot(left, right, precision=highest)

def bucket_of(gap):
    exact = NB // 2
    larger = jnp.full(gap.shape, exact, jnp.int32)
    for level in range(1, NB - exact):
        edge = math.ceil(exact * (MAXDIST / exact) ** (level / (NB - exact)))
        larger = larger + (gap >= edge).astype(jnp.int32)
    return jnp.where(gap < exact, gap, larger)

def row_segments(lengths, count):
    ends = jnp.cumsum(lengths).astype(jnp.int32)
    places = jnp.arange(LEN, dtype=jnp.int32)
    segment = lax.optimization_barrier(jnp.sum((places[:, None] >= ends[None, :]).astype(jnp.int32), axis=1))
    return (segment, segment < count)

def rms(value, gain):
    return value * lax.rsqrt(lax.optimization_barrier(jnp.mean(value * value, axis=-1, keepdims=True)) + epsilon) * gain

def attention(queries, keys, values, allowed, bias, live):
    shape = (queries.shape[0], HEADS, DK)
    product = jnp.einsum('qhd,khd->hqk', queries.reshape(shape), keys.reshape(shape), precision=highest)
    scores = low_back(product)
    if bias is not None:
        scores = scores + bias
    scores = jnp.where(allowed[None], scores, masked_score)
    peak = lax.optimization_barrier(jnp.max(scores, axis=-1, keepdims=True))
    raised = jnp.exp(scores - peak)
    probs = low(raised / lax.optimization_barrier(jnp.sum(raised, axis=-1, keepdims=True)))
    mixed = jnp.einsum('hqk,khd->qhd', probs, values.reshape(shape), precision=highest)
    mixed = mixed * live[:, None, None].astype(mixed.dtype)
    return rounded_both(mixed.reshape(queries.shape[0], HD))

def branch(mixed, weight):
    width = weight.shape[0] // N_TENSOR
    total = jnp.zeros((mixed.shape[0], weight.shape[1]), mixed.dtype)
    for group in range(N_TENSOR):
        part = high_dot(mixed[:, group * width:(group + 1) * width], weight[group * width:(group + 1) * width])
        total = total + rounded_both(part)
    return total

def layer(params, row_in, row_mem, seg_dec, live_dec, seg_mem):
    self_gain, self_query, self_key, self_value, self_out, rel_table, cross_gain, cross_query, cross_key, cross_value, cross_out, feed_gain, feed_in, feed_out = params
    places = jnp.arange(LEN, dtype=jnp.int32)
    normed1 = low(rms(row_in, self_gain))
    queries = rounded_both(high_dot(normed1, self_query))
    keys = rounded_both(high_dot(normed1, self_key))
    values = rounded_both(high_dot(normed1, self_value))
    bucket = bucket_of(jnp.maximum(places[:, None] - places[None, :], 0))
    bias = jnp.transpose(rel_table[bucket], (2, 0, 1))
    allowed = (seg_dec[:, None] == seg_dec[None, :]) & live_dec[:, None] & (places[None, :] <= places[:, None])
    hidden1 = row_in + branch(attention(queries, keys, values, allowed, bias, live_dec), self_out)
    normed2 = low(rms(hidden1, cross_gain))
    cross_queries = rounded_both(high_dot(normed2, cross_query))
    mem_keys = rounded_both(high_dot(row_mem, cross_key))
    mem_values = rounded_both(high_dot(row_mem, cross_value))
    cross_allowed = (seg_dec[:, None] == seg_mem[None, :]) & live_dec[:, None]
    hidden2 = hidden1 + branch(attention(cross_queries, mem_keys, mem_values, cross_allowed, None, live_dec), cross_out)
    normed3 = low(rms(hidden2, feed_gain))
    preact = low_back(high_dot(normed3, feed_in))
    activated = low(jax.nn.gelu(preact))
    return hidden2 + branch(activated, feed_out)

def reference(inputs, memory, cotangent, dec_lengths, mem_lengths, counts, self_gain, self_query, self_key, self_value, self_out, rel_table, cross_gain, cross_query, cross_key, cross_value, cross_out, feed_gain, feed_in, feed_out):
    params = tuple((weight.astype(jnp.float32) for weight in (self_gain, self_query, self_key, self_value, self_out, rel_table, cross_gain, cross_query, cross_key, cross_value, cross_out, feed_gain, feed_in, feed_out)))
    rows_in = inputs.astype(jnp.float32).reshape(ROWS, LEN, D)
    rows_mem = memory.astype(jnp.float32).reshape(ROWS, LEN, D)
    rows_grad = cotangent.astype(jnp.float32).reshape(ROWS, LEN, D)

    def one_row(total, parts):
        row_in, row_mem, row_grad, dec_len, mem_len, count = parts
        seg_dec, live_dec = row_segments(dec_len, count)
        seg_mem, unused = row_segments(mem_len, count)

        def apply(weights, first, second):
            return layer(weights, first, second, seg_dec, live_dec, seg_mem)
        result, pullback = jax.vjp(apply, params, row_in, row_mem)
        grad_params, grad_in, grad_mem = pullback(row_grad)
        total = jax.tree.map(lambda left, right: left + right, total, grad_params)
        return (total, (result.astype(jnp.bfloat16), grad_in.astype(jnp.bfloat16), grad_mem.astype(jnp.bfloat16)))
    start = jax.tree.map(jnp.zeros_like, params)
    total, (output, grad_in, grad_mem) = lax.scan(one_row, start, (rows_in, rows_mem, rows_grad, dec_lengths, mem_lengths, counts))
    return (output.reshape(TOKENS, D), grad_in.reshape(TOKENS, D), grad_mem.reshape(TOKENS, D), total[0], total[1], total[2], total[3], total[4], total[5], total[6], total[7], total[8], total[9], total[10], total[11], total[12], total[13])
```

```python
import functools
import math

import jax
import jax.numpy as jnp
from jax import lax
from jax.experimental import pallas as pl
from jax.experimental.pallas import tpu as pltpu
from jax.sharding import PartitionSpec as P

NB = 32
MAXDIST = 128
SEGS = 16
LEN = 1024
HALF = 512
WIDTH = 512
OWN = 256
BLK = 128
BIG = 1 << 30
MASKED = -1e30
EPS = 1e-06
f32 = jnp.float32
bf16 = jnp.bfloat16
VMEM_BYTES = 56 * 1024 * 1024


def thresholds():
    exact = NB // 2
    edges = [
        math.ceil(exact * (MAXDIST / exact) ** (level / (NB - exact)))
        for level in range(1, NB - exact)
    ]
    return list(range(exact + 1)) + edges


THRESHOLDS = thresholds()


def nn(a, b):
    return jnp.dot(a, b, preferred_element_type=f32)


def nt(a, b):
    return lax.dot_general(a, b, (((1,), (1,)), ((), ())), preferred_element_type=f32)


def tn(a, b):
    return lax.dot_general(a, b, (((0,), (0,)), ((), ())), preferred_element_type=f32)


def call(body, out_shapes, scratch, args, smem=0):
    specs = [pl.BlockSpec(memory_space=pltpu.SMEM)] * smem
    specs += [pl.BlockSpec(memory_space=pltpu.VMEM)] * (len(args) - smem)
    return pl.pallas_call(
        body,
        out_shape=tuple(jax.ShapeDtypeStruct(s, d) for s, d in out_shapes),
        in_specs=specs,
        out_specs=tuple(pl.BlockSpec(memory_space=pltpu.VMEM) for _ in out_shapes),
        scratch_shapes=scratch,
        compiler_params=pltpu.CompilerParams(vmem_limit_bytes=VMEM_BYTES),
    )(*args)


def running_ends(len_ref):
    ends, total = [], 0
    for k in range(SEGS):
        total = total + len_ref[0, k]
        ends.append(total)
    return ends


def live_tokens(ends, count):
    total = 0
    for k in range(SEGS):
        total = jnp.where(k < count, ends[k], total)
    return total


def lookup(pos, ends, values, first):
    found = first
    for k in range(SEGS - 1):
        found = jnp.where(pos >= ends[k], values[k], found)
    return found


def token_positions():
    shape = (LEN // BLK, BLK)
    return lax.broadcasted_iota(jnp.int32, shape, 0) * BLK + lax.broadcasted_iota(
        jnp.int32, shape, 1
    )


def twice(row):
    return jnp.concatenate([row, row], axis=1)


def stacked(pair):
    lane = lax.broadcasted_iota(jnp.int32, pair.shape, 1)
    zero = jnp.zeros_like(pair)
    return jnp.concatenate(
        [jnp.where(lane < 64, pair, zero), jnp.where(lane < 64, zero, pair)], axis=0
    )


def diagonal(product):
    both = jnp.concatenate([product[:64, :BLK], product[64:, BLK:]], axis=0)
    return jnp.transpose(both)


def rms_scale(value):
    return lax.rsqrt(jnp.mean(value * value, axis=-1, keepdims=True) + EPS)


def rms_back(value, gain, grad):
    scale = rms_scale(value)
    weighted = grad * gain
    inner = jnp.mean(weighted * value, axis=-1, keepdims=True)
    unit = value * scale
    return (
        scale * weighted - unit * (scale * scale * inner),
        jnp.sum(grad * unit, axis=0, keepdims=True),
    )


def fill_bias(table_ref, bias_ref):
    key = lax.broadcasted_iota(jnp.int32, (BLK, BLK), 0)
    query = lax.broadcasted_iota(jnp.int32, (BLK, BLK), 1)
    for d in range(2):
        gap = d * BLK + query - key
        tiles = [jnp.full((BLK, BLK), table_ref[0, h], f32) for h in range(4)]
        for level in range(1, NB):
            reached = gap >= THRESHOLDS[level]
            tiles = [jnp.where(reached, table_ref[level, h], tiles[h]) for h in range(4)]
        if d == 0:
            tiles = [jnp.where(gap >= 0, tile, MASKED) for tile in tiles]
        for h in range(4):
            bias_ref[d * 2 + h // 2, :, (h % 2) * BLK : (h % 2 + 1) * BLK] = tiles[h]


def far_bias(table_ref, p):
    lane = lax.broadcasted_iota(jnp.int32, (1, 2 * BLK), 1)
    return jnp.where(lane < BLK, table_ref[NB - 1, 2 * p], table_ref[NB - 1, 2 * p + 1])


def self_scores(b, n, p, kstart, q_ref, k_ref, bias_ref, table_ref, start2):
    lanes = slice(p * BLK, (p + 1) * BLK)
    keys = k_ref[pl.ds(kstart, n * BLK), lanes]
    queries = stacked(q_ref[pl.ds(pl.multiple_of(b * BLK, BLK), BLK), lanes])
    scores = nt(keys, queries)
    parts = []
    for j in range(n):
        part = scores[j * BLK : (j + 1) * BLK]
        d = n - 1 - j
        parts.append(part + (bias_ref[2 * d + p] if d < 2 else far_bias(table_ref, p)))
    scores = jnp.concatenate(parts, axis=0) if n > 1 else parts[0]
    index = kstart + lax.broadcasted_iota(jnp.int32, (n * BLK, 2 * BLK), 0)
    return queries, keys, jnp.where(index >= start2, scores, MASKED)


def self_spans(b, ends, live):
    pos = b * BLK
    first = lax.shift_right_logical(lookup(pos, ends, ends, 0), 7)
    return pos < live, first, b - first + 1


def self_forward(half, ends, live, q_ref, k_ref, vt_ref, bias_ref, table_ref, start_ref, o_ref, lse_ref):
    def block(i, b, first, n):
        kstart = pl.multiple_of(first * BLK, BLK)
        start2 = twice(start_ref[pl.ds(b, 1), :])
        alive = (start2 < BIG).astype(f32)
        for p in range(2):
            _, _, scores = self_scores(
                b, n, p, kstart, q_ref, k_ref, bias_ref, table_ref, start2
            )
            peak = jnp.max(scores, axis=0, keepdims=True)
            raised = jnp.exp(scores - peak)
            total = jnp.sum(raised, axis=0, keepdims=True)
            mixed = nn(vt_ref[p * BLK : (p + 1) * BLK, pl.ds(kstart, n * BLK)], raised.astype(bf16))
            mixed = mixed * (alive / total)
            o_ref[pl.ds(pl.multiple_of(i * BLK, BLK), BLK), p * BLK : (p + 1) * BLK] = diagonal(
                mixed
            ).astype(bf16)
            lse_ref[p, pl.ds(i, 1), :] = peak + jnp.log(total)

    def step(i, carry):
        b = half * 4 + i
        alive, first, n = self_spans(b, ends, live)
        for m in range(1, 5):
            pl.when(alive & (n == m))(functools.partial(block, i, b, first, m))

        @pl.when(jnp.logical_not(alive))
        def _():
            o_ref[pl.ds(pl.multiple_of(i * BLK, BLK), BLK), :] = jnp.zeros((BLK, OWN), bf16)
            for p in range(2):
                lse_ref[p, pl.ds(i, 1), :] = jnp.zeros((1, 2 * BLK), f32)

        return carry

    lax.fori_loop(0, 4, step, 0)


def set_starts(ends, live, start_ref):
    pos = token_positions()
    start_ref[...] = jnp.where(pos < live, lookup(pos, ends, ends, 0), BIG)


def first_kernel(
    t_ref, len_ref, cnt_ref, table_ref,
    x_ref, gain_ref, wq_ref, wk_ref, wv_ref,
    n1_ref, q_ref, k_ref, v_ref, vt_ref, kt_ref, bias_ref, o_ref, lse_ref,
    start_ref,
):
    ends = running_ends(len_ref)
    live = live_tokens(ends, cnt_ref[0])
    set_starts(ends, live, start_ref)
    fill_bias(table_ref, bias_ref)

    def project(i, carry):
        rows = pl.ds(pl.multiple_of(i * 256, 256), 256)
        value = x_ref[rows, :].astype(f32)
        low = (value * rms_scale(value) * gain_ref[...]).astype(bf16)
        n1_ref[rows, :] = low
        q_ref[rows, :] = nn(low, wq_ref[...]).astype(bf16)
        keys = nn(low, wk_ref[...])
        k_ref[rows, :] = keys.astype(bf16)
        kt_ref[:, rows] = jnp.transpose(keys).astype(bf16)
        values = nn(low, wv_ref[...])
        v_ref[rows, :] = values.astype(bf16)
        vt_ref[:, rows] = jnp.transpose(values).astype(bf16)
        return carry

    lax.fori_loop(0, 4, project, 0)
    self_forward(
        1 - t_ref[0], ends, live, q_ref, k_ref, vt_ref, bias_ref, table_ref, start_ref, o_ref, lse_ref
    )


def second_kernel(
    t_ref, len_ref, cnt_ref, table_ref,
    q_ref, k_ref, vt_ref, bias_ref,
    o_ref, lse_ref,
    start_ref,
):
    ends = running_ends(len_ref)
    live = live_tokens(ends, cnt_ref[0])
    set_starts(ends, live, start_ref)
    self_forward(
        t_ref[0], ends, live, q_ref, k_ref, vt_ref, bias_ref, table_ref, start_ref, o_ref, lse_ref
    )


def memory_kernel(mem_ref, ck_ref, cko_ref, cv_ref, cvo_ref, mk_ref, mv_ref, mkt_ref, mvt_ref):
    def project(i, carry):
        rows = pl.ds(pl.multiple_of(i * 256, 256), 256)
        value = mem_ref[rows, :]
        for side, (wk, wv) in enumerate(((ck_ref, cv_ref), (cko_ref, cvo_ref))):
            lanes = slice(side * OWN, (side + 1) * OWN)
            keys = nn(value, wk[...])
            mk_ref[rows, lanes] = keys.astype(bf16)
            mkt_ref[lanes, rows] = jnp.transpose(keys).astype(bf16)
            values = nn(value, wv[...])
            mv_ref[rows, lanes] = values.astype(bf16)
            mvt_ref[lanes, rows] = jnp.transpose(values).astype(bf16)
        return carry

    lax.fori_loop(0, 4, project, 0)


SPANS = (1, 2, 3, 4, 6, 8)


def set_ranges(ends, mends, live, low_ref, high_ref):
    pos = token_positions()
    low_ref[...] = jnp.where(pos < live, lookup(pos, ends, mends, 0), BIG)
    high_ref[...] = lookup(pos, ends, mends[1:], mends[0])


def cross_blocks(half, ends, mends, live, block, dead):
    def step(i, carry):
        b = half * 4 + i
        pos = b * BLK
        alive = pos < live
        last = jnp.minimum(pos + BLK, live) - 1
        first = lax.shift_right_logical(lookup(pos, ends, mends, 0), 7)
        end = lax.shift_right_logical(lookup(last, ends, mends[1:], mends[0]) + BLK - 1, 7)
        n = end - first
        below = 0
        for m in SPANS:
            begin = jnp.minimum(first, LEN // BLK - m)
            pl.when(alive & (n > below) & (n <= m))(functools.partial(block, i, b, begin, m))
            below = m
        pl.when(jnp.logical_not(alive))(functools.partial(dead, i))
        return carry

    lax.fori_loop(0, 4, step, 0)


def cross_scores(i, n, lanes, kstart, q_ref, k_ref, low2, high2):
    keys = k_ref[pl.ds(kstart, n * BLK), lanes]
    queries = stacked(q_ref[pl.ds(pl.multiple_of(i * BLK, BLK), BLK), lanes])
    index = kstart + lax.broadcasted_iota(jnp.int32, (n * BLK, 2 * BLK), 0)
    allowed = (index >= low2) & (index < high2)
    return queries, keys, jnp.where(allowed, nt(keys, queries), MASKED)


def pairs(body):
    def step(g, carry):
        for k in range(2):
            p = 2 * g + k
            body(p, pl.ds(pl.multiple_of(p * BLK, BLK), BLK))
        return carry

    lax.fori_loop(0, 2, step, 0)


def third_kernel(
    t_ref, len_ref, mlen_ref, cnt_ref,
    x_ref, keep_ref, recv_ref, so_ref, soo_ref, gain2_ref, cq_ref, cqo_ref,
    mk_ref, mvt_ref, co_ref, coo_ref, gain3_ref,
    h1_ref, n2_ref, q_ref, mixed_ref, lse_ref, h2_ref, n3_ref,
    low_ref, high_ref,
):
    t = t_ref[0]
    ends, mends = running_ends(len_ref), running_ends(mlen_ref)
    live = live_tokens(ends, cnt_ref[0])
    set_ranges(ends, mends, live, low_ref, high_ref)

    def before(i, carry):
        rows = pl.ds(pl.multiple_of(i * 256, 256), 256)
        value = x_ref[pl.ds(pl.multiple_of(t * HALF + i * 256, 256), 256), :].astype(f32)
        value = value + nn(keep_ref[rows, :], so_ref[...]) + nn(recv_ref[rows, :], soo_ref[...])
        h1_ref[rows, :] = value
        low = (value * rms_scale(value) * gain2_ref[...]).astype(bf16)
        n2_ref[rows, :] = low
        q_ref[rows, :OWN] = nn(low, cq_ref[...]).astype(bf16)
        q_ref[rows, OWN:] = nn(low, cqo_ref[...]).astype(bf16)
        return carry

    lax.fori_loop(0, 2, before, 0)

    def block(i, b, first, n):
        kstart = pl.multiple_of(first * BLK, BLK)
        low2, high2 = twice(low_ref[pl.ds(b, 1), :]), twice(high_ref[pl.ds(b, 1), :])
        alive = (low2 < BIG).astype(f32)

        def pair(p, lanes):
            _, _, scores = cross_scores(i, n, lanes, kstart, q_ref, mk_ref, low2, high2)
            peak = jnp.max(scores, axis=0, keepdims=True)
            raised = jnp.exp(scores - peak)
            total = jnp.sum(raised, axis=0, keepdims=True)
            mixed = nn(mvt_ref[lanes, pl.ds(kstart, n * BLK)], raised.astype(bf16))
            mixed = mixed * (alive / total)
            mixed_ref[pl.ds(pl.multiple_of(i * BLK, BLK), BLK), lanes] = diagonal(mixed).astype(bf16)
            lse_ref[p, pl.ds(i, 1), :] = peak + jnp.log(total)

        pairs(pair)

    def dead(i):
        mixed_ref[pl.ds(pl.multiple_of(i * BLK, BLK), BLK), :] = jnp.zeros((BLK, WIDTH), bf16)
        for p in range(4):
            lse_ref[p, pl.ds(i, 1), :] = jnp.zeros((1, 2 * BLK), f32)

    cross_blocks(t, ends, mends, live, block, dead)

    def after(i, carry):
        rows = pl.ds(pl.multiple_of(i * 256, 256), 256)
        value = h1_ref[rows, :]
        value = value + nn(mixed_ref[rows, :OWN], co_ref[...]) + nn(mixed_ref[rows, OWN:], coo_ref[...])
        h2_ref[rows, :] = value
        n3_ref[rows, :] = (value * rms_scale(value) * gain3_ref[...]).astype(bf16)
        return carry

    lax.fori_loop(0, 2, after, 0)


def feed_kernel(
    half_ref, n3_ref, cot_ref, fi_ref, fo_ref,
    out_ref, gn_ref, act_ref, gp_ref,
    out_acc, gn_acc,
):
    base = half_ref[0] * HALF
    tile = 256
    n_tiles = fi_ref.shape[1] // tile

    def hidden(j, carry):
        lanes = pl.ds(pl.multiple_of(j * tile, tile), tile)
        for i in range(2):
            rows = slice(i * 256, (i + 1) * 256)
            pre = nn(n3_ref[rows, :], fi_ref[:, lanes])
            cubic = pre * pre * 0.044715
            inside = math.sqrt(2 / math.pi) * (pre + pre * cubic)
            bent = jnp.tanh(inside)
            gate = 0.5 * (1.0 + bent)
            slope = gate + 0.5 * pre * (1.0 - bent * bent) * (
                math.sqrt(2 / math.pi) * (1.0 + 3.0 * cubic)
            )
            act = (pre * gate).astype(bf16)
            act_ref[rows, lanes] = act
            grads = nt(cot_ref[pl.ds(pl.multiple_of(base + i * 256, 256), 256), :], fo_ref[lanes, :])
            grads = (grads * slope).astype(bf16)
            gp_ref[rows, lanes] = grads
            part = nn(act, fo_ref[lanes, :])
            gn_part = nt(grads, fi_ref[:, lanes])

            @pl.when(j == 0)
            def _():
                out_acc[rows, :] = part
                gn_acc[rows, :] = gn_part

            @pl.when(j > 0)
            def _():
                out_acc[rows, :] += part
                gn_acc[rows, :] += gn_part

        return carry

    lax.fori_loop(0, n_tiles, hidden, 0)
    out_ref[...] = out_acc[...].astype(bf16)
    gn_ref[...] = gn_acc[...].astype(bf16)


def feed_weights_kernel(
    t_ref, n3_ref, n3o_ref, cot_ref, act_ref, acto_ref, gp_ref, gpo_ref,
    pack_ref,
    n3t_ref,
):
    t = t_ref[0]
    mine = pl.ds(pl.multiple_of(t * HALF, HALF), HALF)
    theirs = pl.ds(pl.multiple_of((1 - t) * HALF, HALF), HALF)
    n3t_ref[:, :HALF] = jnp.transpose(n3_ref[...].astype(f32)).astype(bf16)
    n3t_ref[:, HALF:] = jnp.transpose(n3o_ref[...].astype(f32)).astype(bf16)
    for j in range(4):
        lanes = slice(j * 256, (j + 1) * 256)
        rows = slice((j // 2) * 512, (j // 2 + 1) * 512)
        cols = slice((j % 2) * 256, (j % 2 + 1) * 256)
        grads = nn(n3t_ref[:, :HALF], gp_ref[:, lanes]) + nn(n3t_ref[:, HALF:], gpo_ref[:, lanes])
        pack_ref[rows, cols] = grads.astype(bf16)
        grads = tn(act_ref[:, lanes], cot_ref[mine, :]) + tn(acto_ref[:, lanes], cot_ref[theirs, :])
        pack_ref[1024 + j * 256 : 1024 + (j + 1) * 256, :] = grads.astype(bf16)


def cross_back_kernel(
    t_ref, len_ref, mlen_ref, cnt_ref,
    gn_ref, gnr_ref, h2_ref, gain3_ref, cot_ref, co_ref, coo_ref,
    q_ref, mk_ref, mkt_ref, mv_ref, lse_ref, cq_ref, cqo_ref, h1_ref, gain2_ref, so_ref, soo_ref,
    gb2_ref, dq_ref, dk_ref, dv_ref, gh1_ref, gb1_ref, gm1_ref, gm1o_ref, gains_ref,
    low_ref, high_ref, live_ref, gm_ref, dk_acc, dv_acc, gh2_ref,
):
    t = t_ref[0]
    ends, mends = running_ends(len_ref), running_ends(mlen_ref)
    live = live_tokens(ends, cnt_ref[0])
    set_ranges(ends, mends, live, low_ref, high_ref)
    alive_rows = t * HALF + lax.broadcasted_iota(jnp.int32, (HALF, BLK), 0)
    live_ref[...] = (alive_rows < live).astype(f32)
    dk_acc[...] = jnp.zeros_like(dk_acc)
    dv_acc[...] = jnp.zeros_like(dv_acc)
    gains_ref[...] = jnp.zeros_like(gains_ref)

    for i in range(2):
        rows = slice(i * 256, (i + 1) * 256)
        grad = gn_ref[rows, :].astype(f32) + gnr_ref[rows, :].astype(f32)
        back, gain = rms_back(h2_ref[rows, :], gain3_ref[...], grad)
        gains_ref[0:1, :] += gain
        cot = cot_ref[pl.ds(pl.multiple_of(t * HALF + i * 256, 256), 256), :]
        grad = cot.astype(f32) + back
        gh2_ref[rows, :] = grad
        low = grad.astype(bf16)
        gb2_ref[rows, :] = low
        alive = live_ref[rows, 0:1]
        gm_ref[rows, :OWN] = (nt(low, co_ref[...]) * alive).astype(bf16)
        gm_ref[rows, OWN:] = (nt(low, coo_ref[...]) * alive).astype(bf16)

    def block(i, b, first, n):
        kstart = pl.multiple_of(first * BLK, BLK)
        low2, high2 = twice(low_ref[pl.ds(b, 1), :]), twice(high_ref[pl.ds(b, 1), :])
        rows = pl.ds(pl.multiple_of(i * BLK, BLK), BLK)
        span = pl.ds(kstart, n * BLK)

        def pair(p, lanes):
            queries, _, scores = cross_scores(i, n, lanes, kstart, q_ref, mk_ref, low2, high2)
            probs = jnp.exp(scores - lse_ref[p, pl.ds(i, 1), :])
            grads = stacked(gm_ref[rows, lanes])
            grad_probs = nt(mv_ref[span, lanes], grads)
            inner = jnp.sum(grad_probs * probs, axis=0, keepdims=True)
            low = (probs * (grad_probs - inner)).astype(bf16)
            dk_acc[span, lanes] += nn(low, queries)
            dv_acc[span, lanes] += nn(probs.astype(bf16), grads)
            dq_ref[rows, lanes] = diagonal(nn(mkt_ref[lanes, span], low)).astype(bf16)

        pairs(pair)

    def dead(i):
        dq_ref[pl.ds(pl.multiple_of(i * BLK, BLK), BLK), :] = jnp.zeros((BLK, WIDTH), bf16)

    cross_blocks(t, ends, mends, live, block, dead)

    for i in range(2):
        rows = slice(i * 256, (i + 1) * 256)
        grad = nt(dq_ref[rows, :OWN], cq_ref[...]) + nt(dq_ref[rows, OWN:], cqo_ref[...])
        back, gain = rms_back(h1_ref[rows, :], gain2_ref[...], grad)
        gains_ref[1:2, :] += gain
        grad = gh2_ref[rows, :] + back
        gh1_ref[rows, :] = grad
        low = grad.astype(bf16)
        gb1_ref[rows, :] = low
        alive = live_ref[rows, 0:1]
        gm1_ref[rows, :] = (nt(low, so_ref[...]) * alive).astype(bf16)
        gm1o_ref[rows, :] = (nt(low, soo_ref[...]) * alive).astype(bf16)
    dk_ref[...] = dk_acc[...].astype(bf16)
    dv_ref[...] = dv_acc[...].astype(bf16)


def cross_weights_kernel(
    mem_ref, n2_ref, mixed_ref, keep_ref, recv_ref, gb1_ref, gb2_ref, dq_ref, dk_ref, dv_ref,
    ck_ref, cko_ref, cv_ref, cvo_ref,
    own_ref, oth_ref, gmem_ref,
    memt_ref,
):
    memt_ref[...] = jnp.transpose(mem_ref[...].astype(f32)).astype(bf16)
    n2t = jnp.transpose(n2_ref[...].astype(f32)).astype(bf16)
    for side, pack in enumerate((own_ref, oth_ref)):
        lanes = slice(side * OWN, (side + 1) * OWN)
        pack[0:256, :] = tn(mixed_ref[:, lanes], gb2_ref[...]).astype(bf16)
        mixed1 = keep_ref if side == 0 else recv_ref
        pack[256:512, :] = tn(mixed1[...], gb1_ref[...]).astype(bf16)
        for k, grads in enumerate(
            (nn(n2t, dq_ref[:, lanes]), nn(memt_ref[...], dk_ref[:, lanes]), nn(memt_ref[...], dv_ref[:, lanes]))
        ):
            low = grads.astype(bf16)
            rows = slice(512 + k * 256, 768 + k * 256)
            pack[rows, :OWN] = low[:256]
            pack[rows, OWN:] = low[256:]
    for i in range(4):
        rows = slice(i * 256, (i + 1) * 256)
        grads = nt(dk_ref[rows, :OWN], ck_ref[...]) + nt(dk_ref[rows, OWN:], cko_ref[...])
        grads += nt(dv_ref[rows, :OWN], cv_ref[...]) + nt(dv_ref[rows, OWN:], cvo_ref[...])
        gmem_ref[rows, :] = grads.astype(bf16)


def self_back_kernel(
    t_ref, len_ref, cnt_ref, table_ref,
    gm_ref, gmr_ref, q_ref, k_ref, kt_ref, v_ref, bias_ref, lse_ref, lseo_ref,
    n1_ref, x_ref, gain1_ref, wq_ref, wk_ref, wv_ref,
    pack_ref, gn_ref, gno_ref, small_ref,
    start_ref, g_ref, dq_ref, dk_acc, dv_acc, near_acc, far_acc, n1t_ref,
):
    t = t_ref[0]
    ends = running_ends(len_ref)
    live = live_tokens(ends, cnt_ref[0])
    set_starts(ends, live, start_ref)
    g_ref[pl.ds(pl.multiple_of(t * HALF, HALF), HALF), :] = gm_ref[...]
    g_ref[pl.ds(pl.multiple_of((1 - t) * HALF, HALF), HALF), :] = gmr_ref[...]
    for ref in (dk_acc, dv_acc, near_acc, far_acc, small_ref):
        ref[...] = jnp.zeros_like(ref)

    def block(b, first, n):
        kstart = pl.multiple_of(first * BLK, BLK)
        start2 = twice(start_ref[pl.ds(b, 1), :])
        rows = pl.ds(pl.multiple_of(b * BLK, BLK), BLK)
        span = pl.ds(kstart, n * BLK)
        i = lax.rem(b, 4)
        mine = lax.div(b, 4) == t
        for p in range(2):
            lanes = slice(p * BLK, (p + 1) * BLK)
            queries, _, scores = self_scores(
                b, n, p, kstart, q_ref, k_ref, bias_ref, table_ref, start2
            )
            lse = jnp.where(mine, lse_ref[p, pl.ds(i, 1), :], lseo_ref[p, pl.ds(i, 1), :])
            probs = jnp.exp(scores - lse)
            grads = stacked(g_ref[rows, lanes])
            grad_probs = nt(v_ref[span, lanes], grads)
            inner = jnp.sum(grad_probs * probs, axis=0, keepdims=True)
            grad_scores = probs * (grad_probs - inner)
            near_acc[p] += grad_scores[(n - 1) * BLK :]
            if n > 1:
                near_acc[2 + p] += grad_scores[(n - 2) * BLK : (n - 1) * BLK]
            if n > 2:
                far_acc[p : p + 1, :] += jnp.sum(grad_scores[: (n - 2) * BLK], axis=0, keepdims=True)
            low = grad_scores.astype(bf16)
            dk_acc[span, lanes] += nn(low, queries)
            dv_acc[span, lanes] += nn(probs.astype(bf16), grads)
            dq_ref[rows, lanes] = diagonal(nn(kt_ref[lanes, span], low)).astype(bf16)

    def step(b, carry):
        alive, first, n = self_spans(b, ends, live)
        for m in range(1, 5):
            pl.when(alive & (n == m))(functools.partial(block, b, first, m))

        @pl.when(jnp.logical_not(alive))
        def _():
            dq_ref[pl.ds(pl.multiple_of(b * BLK, BLK), BLK), :] = jnp.zeros((BLK, OWN), bf16)

        return carry

    lax.fori_loop(0, LEN // BLK, step, 0)

    key = lax.broadcasted_iota(jnp.int32, (BLK, BLK), 0)
    query = lax.broadcasted_iota(jnp.int32, (BLK, BLK), 1)
    gaps = [query - key, BLK + query - key]
    lane4 = lax.broadcasted_iota(jnp.int32, (1, WIDTH), 1)
    for level in range(NB):
        sums = []
        for p in range(2):
            row = jnp.zeros((1, 2 * BLK), f32)
            for d in range(2):
                inside = gaps[d] >= THRESHOLDS[level]
                if level + 1 < NB:
                    inside &= gaps[d] < THRESHOLDS[level + 1]
                picked = jnp.where(twice(inside.astype(f32)) > 0, near_acc[2 * d + p], 0.0)
                row += jnp.sum(picked, axis=0, keepdims=True)
            if level == NB - 1:
                row += far_acc[p : p + 1, :]
            sums.append(row)
        small_ref[8 + level : 9 + level, :] = jnp.concatenate(sums, axis=1)

    n1t_ref[...] = jnp.transpose(n1_ref[...].astype(f32)).astype(bf16)
    low_k, low_v = dk_acc[...].astype(bf16), dv_acc[...].astype(bf16)
    for k, grads in enumerate((dq_ref[...], low_k, low_v)):
        low = nn(n1t_ref[...], grads).astype(bf16)
        rows = slice(k * 256, (k + 1) * 256)
        pack_ref[rows, :OWN] = low[:256]
        pack_ref[rows, OWN:] = low[256:]
    for i in range(4):
        rows = slice(i * 256, (i + 1) * 256)
        grads = nt(dq_ref[rows, :], wq_ref[...]) + nt(low_k[rows], wk_ref[...]) + nt(low_v[rows], wv_ref[...])
        value = x_ref[rows, :].astype(f32)
        small_ref[0:1, :] += jnp.sum(grads * (value * rms_scale(value)), axis=0, keepdims=True)
        low = grads.astype(bf16)
        out = slice((i % 2) * 256, (i % 2 + 1) * 256)

        @pl.when(t == i // 2)
        def _():
            gn_ref[out, :] = low

        @pl.when(t != i // 2)
        def _():
            gno_ref[out, :] = low


def last_kernel(t_ref, gh1_ref, x_ref, gain_ref, gn_ref, gnr_ref, gi_ref):
    base = t_ref[0] * HALF
    for i in range(2):
        rows = slice(i * 256, (i + 1) * 256)
        grad = gn_ref[rows, :].astype(f32) + gnr_ref[rows, :].astype(f32)
        value = x_ref[pl.ds(pl.multiple_of(base + i * 256, 256), 256), :].astype(f32)
        back, _ = rms_back(value, gain_ref[...], grad)
        gi_ref[rows, :] = (gh1_ref[rows, :] + back).astype(bf16)


def output_kernel(h2_ref, own_ref, recv_ref, out_ref):
    total = h2_ref[...] + own_ref[...].astype(f32) + recv_ref[...].astype(f32)
    out_ref[...] = total.astype(bf16)


def swap(value):
    return lax.ppermute(value, "tensor", [(0, 1), (1, 0)])


def unfold(rows):
    return jnp.concatenate([rows[:, :OWN], rows[:, OWN:]], axis=0)


def shards(
    inputs, memory, cotangent, dec_lengths, mem_lengths, counts,
    self_gain, self_query, self_key, self_value, self_out, rel_table,
    cross_gain, cross_query, cross_key, cross_value, cross_out,
    feed_gain, feed_in, feed_out,
):
    v = pltpu.VMEM
    i32 = jnp.int32
    t = lax.axis_index("tensor").astype(i32).reshape(1)
    gain1, gain2, gain3 = (g.reshape(1, WIDTH) for g in (self_gain, cross_gain, feed_gain))

    so_oth = swap(self_out)
    ck_oth = swap(cross_key)
    cv_oth = swap(cross_value)
    cq_oth = swap(cross_query)
    co_oth = swap(cross_out)

    tok = (LEN, WIDTH)
    half = (HALF, WIDTH)
    row_tile = v((LEN // BLK, BLK), i32)
    n1, q, k, val, vt, kt, bias, send1, lse1_oth = call(
        first_kernel,
        [(tok, bf16), ((LEN, OWN), bf16), ((LEN, OWN), bf16), ((LEN, OWN), bf16), ((OWN, LEN), bf16),
         ((OWN, LEN), bf16), ((4, BLK, 2 * BLK), f32), ((HALF, OWN), bf16), ((2, 4, 2 * BLK), f32)],
        [row_tile],
        (t, dec_lengths, counts, rel_table, inputs, gain1, self_query, self_key, self_value),
        smem=4,
    )
    mixed1_recv = swap(send1)
    mixed1_keep, lse1 = call(
        second_kernel,
        [((HALF, OWN), bf16), ((2, 4, 2 * BLK), f32)],
        [row_tile],
        (t, dec_lengths, counts, rel_table, q, k, vt, bias),
        smem=4,
    )
    mk, mv, mkt, mvt = call(
        memory_kernel,
        [(tok, bf16), (tok, bf16), ((WIDTH, LEN), bf16), ((WIDTH, LEN), bf16)],
        [],
        (memory, cross_key, ck_oth, cross_value, cv_oth),
    )
    h1, n2, cq, mixed2, lse2, h2, n3 = call(
        third_kernel,
        [(half, f32), (half, bf16), (half, bf16), (half, bf16), ((4, 4, 2 * BLK), f32), (half, f32), (half, bf16)],
        [row_tile, row_tile],
        (t, dec_lengths, mem_lengths, counts, inputs, mixed1_keep, mixed1_recv, self_out, so_oth, gain2,
         cross_query, cq_oth, mk, mvt, cross_out, co_oth, gain3),
        smem=4,
    )
    n3_recv = swap(n3)

    def feed(which, normed):
        hidden = (HALF, feed_in.shape[1])
        return call(
            feed_kernel,
            [(half, bf16), (half, bf16), (hidden, bf16), (hidden, bf16)],
            [v(half, f32), v(half, f32)],
            (which, normed, cotangent, feed_in, feed_out),
            smem=1,
        )

    out_own, gn3_own, act, gp = feed(t, n3)
    out_oth, gn3_oth, act_oth, gp_oth = feed(1 - t, n3_recv)
    gn3_recv = swap(gn3_oth)
    out_recv = swap(out_oth)
    (feed_pack,) = call(
        feed_weights_kernel,
        [((2048, WIDTH), bf16)],
        [v((WIDTH, LEN), bf16)],
        (t, n3, n3_recv, cotangent, act, act_oth, gp, gp_oth),
        smem=1,
    )
    (out_half,) = call(output_kernel, [(half, bf16)], [], (h2, out_own, out_recv))
    output = lax.all_gather(out_half, "tensor", axis=0, tiled=True)

    gb2, dcq, dmk, dmv, gh1, gb1, gm1, gm1_oth, gains = call(
        cross_back_kernel,
        [(half, bf16), (half, bf16), (tok, bf16), (tok, bf16), (half, f32), (half, bf16),
         ((HALF, OWN), bf16), ((HALF, OWN), bf16), ((8, WIDTH), f32)],
        [row_tile, row_tile, v((HALF, BLK), f32), v(half, bf16), v(tok, f32), v(tok, f32), v(half, f32)],
        (t, dec_lengths, mem_lengths, counts, gn3_own, gn3_recv, h2, gain3, cotangent, cross_out, co_oth,
         cq, mk, mkt, mv, lse2, cross_query, cq_oth, h1, gain2, self_out, so_oth),
        smem=4,
    )
    gm1_recv = swap(gm1_oth)
    cross_own, cross_oth, gmem = call(
        cross_weights_kernel,
        [((1280, WIDTH), bf16), ((1280, WIDTH), bf16), (tok, bf16)],
        [v((WIDTH, LEN), bf16)],
        (memory, n2, mixed2, mixed1_keep, mixed1_recv, gb1, gb2, dcq, dmk, dmv, cross_key, ck_oth, cross_value, cv_oth),
    )
    cross_recv = swap(cross_oth)
    grad_memory = lax.psum_scatter(gmem, "tensor", scatter_dimension=1, tiled=True)
    self_pack, gn1, gn1_oth, small = call(
        self_back_kernel,
        [((768, WIDTH), bf16), (half, bf16), (half, bf16), ((8 + NB, WIDTH), f32)],
        [row_tile, v((LEN, OWN), bf16), v((LEN, OWN), bf16), v((LEN, OWN), f32), v((LEN, OWN), f32),
         v((4, BLK, 2 * BLK), f32), v((2, 2 * BLK), f32), v((WIDTH, LEN), bf16)],
        (t, dec_lengths, counts, rel_table, gm1, gm1_recv, q, k, kt, val, bias, lse1, lse1_oth,
         n1, inputs, gain1, self_query, self_key, self_value),
        smem=4,
    )
    gn1_recv = swap(gn1_oth)
    (gi_half,) = call(last_kernel, [(half, bf16)], [], (t, gh1, inputs, gain1, gn1, gn1_recv), smem=1)
    grad_inputs = lax.all_gather(gi_half, "tensor", axis=0, tiled=True)

    cross_pack = (cross_own.astype(f32) + cross_recv.astype(f32)).astype(bf16)
    grads = jnp.concatenate([feed_pack, cross_pack, self_pack], axis=0)
    table_part = small[8:].reshape(NB, 4, BLK).sum(axis=2)
    gain_part = jnp.concatenate([small[0:1], gains[1:2], gains[0:1]], axis=0)
    small_part = jnp.concatenate(
        [gain_part, jnp.zeros((5, WIDTH), f32), jnp.pad(table_part, ((0, 0), (0, WIDTH - 4)))], axis=0
    )
    grads = lax.psum(grads, "dp").astype(f32)
    small_sum = lax.psum(small_part, "dp")
    gain_sum = small_sum[0:3]
    gain_sum = gain_sum + swap(gain_sum)
    feed_in_grad = jnp.concatenate([grads[0:512], grads[512:1024]], axis=1)
    cross = grads[2048:3328]
    own = grads[3328:]
    return (
        output,
        grad_inputs,
        grad_memory,
        gain_sum[0],
        unfold(own[0:256]),
        unfold(own[256:512]),
        unfold(own[512:768]),
        cross[256:512],
        small_sum[8:, :4],
        gain_sum[1],
        unfold(cross[512:768]),
        unfold(cross[768:1024]),
        unfold(cross[1024:1280]),
        cross[0:256],
        gain_sum[2],
        feed_in_grad,
        grads[1024:2048],
    )


def solution(mesh):
    split = P("dp", None)
    columns, rows = P(None, "tensor"), P("tensor", None)
    return jax.shard_map(
        shards,
        mesh=mesh,
        in_specs=(
            split, split, split, split, split, P("dp"),
            P(), columns, columns, columns, rows, columns,
            P(), columns, columns, columns, rows,
            P(), columns, rows,
        ),
        out_specs=(
            split, split, P("dp", "tensor"),
            P(), columns, columns, columns, rows, columns,
            P(), columns, columns, columns, rows,
            P(), columns, rows,
        ),
        check_vma=False,
    )
```

```python
import functools
import math

import jax
import jax.numpy as jnp
from jax import lax
from jax.experimental import pallas as pl
from jax.experimental.pallas import tpu as pltpu
from jax.sharding import Mesh
from jax.sharding import PartitionSpec as P

NB = 32
MAXDIST = 128
SEGS = 16
LEN = 1024
HALF = 512
WIDTH = 512
OWN = 256
BLK = 128
BIG = 1 << 30
MASKED = -1e30
EPS = 1e-06
f32 = jnp.float32
bf16 = jnp.bfloat16
ROOM = 11 * 1024 * 1024


def thresholds():
    exact = NB // 2
    edges = [
        math.ceil(exact * (MAXDIST / exact) ** (level / (NB - exact)))
        for level in range(1, NB - exact)
    ]
    return list(range(exact + 1)) + edges


THRESHOLDS = thresholds()


def nn(a, b):
    return jnp.dot(a, b, preferred_element_type=f32)


def nt(a, b):
    return lax.dot_general(a, b, (((1,), (1,)), ((), ())), preferred_element_type=f32)


def tn(a, b):
    return lax.dot_general(a, b, (((0,), (0,)), ((), ())), preferred_element_type=f32)


class Half:
    def __init__(self, array):
        self.array = array


class Near:
    def __init__(self, array):
        self.array = array


class Copies:
    def __init__(self, sems):
        self.sems, self.used, self.waits, self.out = sems, 0, {}, {}

    def start(self, source, target):
        copy = pltpu.make_async_copy(source, target, self.sems.at[self.used])
        self.used += 1
        copy.start()
        return copy

    def ready(self, *refs):
        for ref in refs:
            for copy in self.waits.pop(id(ref), ()):
                copy.wait()

    def forward(self, *pairs):
        for source, ref in pairs:
            target, _ = self.out[id(ref)]
            self.out[id(ref)] = (target, self.start(source, target))

    def done(self, *refs):
        for ref in refs:
            target, copy = self.out.get(id(ref), (None, True))
            if copy is None:
                self.out[id(ref)] = (target, self.start(ref, target))


def size_of(shape, dtype):
    return math.prod(shape) * jnp.dtype(dtype).itemsize


def call(body, outs, scratch, args, smem=1, us=3):
    tables, operands = args[:smem], args[smem:]
    arrays, in_specs, fetched = [], [], []
    hbm, vmem = pl.BlockSpec(memory_space=pltpu.HBM), pl.BlockSpec(memory_space=pltpu.VMEM)
    for operand in operands:
        if isinstance(operand, Near):
            arrays.append(operand.array)
            in_specs.append(vmem)
            continue
        array = operand.array if isinstance(operand, Half) else operand
        arrays.append(pltpu.with_memory_space_constraint(array, pltpu.HBM))
        in_specs.append(hbm)
        shape = (HALF, *array.shape[1:]) if isinstance(operand, Half) else array.shape
        fetched.append((shape, array.dtype))
    out_shapes, out_specs, sent = [], [], []
    for shape, dtype, kind in outs:
        if kind != "far":
            out_shapes.append(jax.ShapeDtypeStruct(shape, dtype))
            out_specs.append(vmem)
        if kind != "near":
            out_shapes.append(pltpu.HBM(shape, dtype))
            out_specs.append(hbm)
        if kind == "far":
            sent.append((shape, dtype))
    n_copies = len(fetched) + sum(kind != "near" for _, _, kind in outs)

    def kernel(*refs):
        refs = list(refs)

        def take(n):
            taken = refs[:n]
            del refs[:n]
            return taken

        scalars, sources, targets = take(smem), take(len(arrays)), take(len(out_shapes))
        inner, outer = take(len(fetched)), take(len(sent))
        io = Copies(take(1)[0] if n_copies else None)
        inputs, outputs = [], []
        for operand, source in zip(operands, sources, strict=True):
            if isinstance(operand, Near):
                inputs.append(source)
                continue
            ref = inner.pop(0)
            inputs.append(ref)
            if isinstance(operand, Half):
                source = source.at[pl.ds(pl.multiple_of(scalars[0][0] * HALF, HALF), HALF), :]
            io.waits[id(ref)] = [io.start(source, ref)]
        for _, _, kind in outs:
            ref = outer.pop(0) if kind == "far" else targets.pop(0)
            outputs.append(ref)
            if kind != "near":
                io.out[id(ref)] = (targets.pop(0), None)
        body(io, *scalars, *inputs, *outputs, *refs)
        io.ready(*inputs)
        io.done(*outputs)
        for _, copy in io.out.values():
            copy.wait()

    own = [pltpu.VMEM(s, d) for s, d in fetched + sent]
    used = sum(size_of(s, d) for s, d in fetched + sent) + sum(size_of(s.shape, s.dtype) for s in scratch)
    return pl.pallas_call(
        kernel,
        out_shape=tuple(out_shapes),
        in_specs=[pl.BlockSpec(memory_space=pltpu.SMEM)] * smem + in_specs,
        out_specs=tuple(out_specs),
        scratch_shapes=[*own, *([pltpu.SemaphoreType.DMA((n_copies,))] if n_copies else []), *scratch],
        compiler_params=pltpu.CompilerParams(vmem_limit_bytes=used + ROOM),
        cost_estimate=pl.CostEstimate(
            flops=us * 3_300_000_000, bytes_accessed=us * 10_000_000, transcendentals=0
        ),
    )(*tables, *arrays)


def running_ends(len_ref):
    ends, total = [], 0
    for k in range(SEGS):
        total = total + len_ref[0, k]
        ends.append(total)
    return ends


def live_tokens(ends, count):
    total = 0
    for k in range(SEGS):
        total = jnp.where(k < count, ends[k], total)
    return total


def lookup(pos, ends, values, first):
    found = first
    for k in range(SEGS - 1):
        found = jnp.where(pos >= ends[k], values[k], found)
    return found


def token_positions():
    shape = (LEN // BLK, BLK)
    return lax.broadcasted_iota(jnp.int32, shape, 0) * BLK + lax.broadcasted_iota(
        jnp.int32, shape, 1
    )


def twice(row):
    return jnp.concatenate([row, row], axis=1)


def stacked(pair):
    lane = lax.broadcasted_iota(jnp.int32, pair.shape, 1)
    zero = jnp.zeros_like(pair)
    return jnp.concatenate(
        [jnp.where(lane < 64, pair, zero), jnp.where(lane < 64, zero, pair)], axis=0
    )


def diagonal(product):
    both = jnp.concatenate([product[:64, :BLK], product[64:, BLK:]], axis=0)
    return jnp.transpose(both)


def rms_scale(value):
    return lax.rsqrt(jnp.mean(value * value, axis=-1, keepdims=True) + EPS)


def rms_back(value, gain, grad):
    scale = rms_scale(value)
    weighted = grad * gain
    inner = jnp.mean(weighted * value, axis=-1, keepdims=True)
    unit = value * scale
    return (
        scale * weighted - unit * (scale * scale * inner),
        jnp.sum(grad * unit, axis=0, keepdims=True),
    )


def fill_bias(table_ref, bias_ref):
    key = lax.broadcasted_iota(jnp.int32, (BLK, BLK), 0)
    query = lax.broadcasted_iota(jnp.int32, (BLK, BLK), 1)
    for d in range(2):
        gap = d * BLK + query - key
        tiles = [jnp.full((BLK, BLK), table_ref[h, 0], f32) for h in range(4)]
        for level in range(1, NB):
            reached = gap >= THRESHOLDS[level]
            tiles = [jnp.where(reached, table_ref[h, level], tiles[h]) for h in range(4)]
        if d == 0:
            tiles = [jnp.where(gap >= 0, tile, MASKED) for tile in tiles]
        for h in range(4):
            bias_ref[d * 2 + h // 2, :, (h % 2) * BLK : (h % 2 + 1) * BLK] = tiles[h]


def far_bias(table_ref, p):
    lane = lax.broadcasted_iota(jnp.int32, (1, 2 * BLK), 1)
    return jnp.where(lane < BLK, table_ref[2 * p, NB - 1], table_ref[2 * p + 1, NB - 1])


def self_scores(b, n, p, kstart, q_ref, k_ref, bias_ref, table_ref, start2):
    lanes = slice(p * BLK, (p + 1) * BLK)
    keys = k_ref[pl.ds(kstart, n * BLK), lanes]
    queries = stacked(q_ref[pl.ds(pl.multiple_of(b * BLK, BLK), BLK), lanes])
    scores = nt(keys, queries)
    parts = []
    for j in range(n):
        part = scores[j * BLK : (j + 1) * BLK]
        d = n - 1 - j
        parts.append(part + (bias_ref[2 * d + p] if d < 2 else far_bias(table_ref, p)))
    scores = jnp.concatenate(parts, axis=0) if n > 1 else parts[0]
    index = kstart + lax.broadcasted_iota(jnp.int32, (n * BLK, 2 * BLK), 0)
    return queries, keys, jnp.where(index >= start2, scores, MASKED)


def self_spans(b, ends, live):
    pos = b * BLK
    first = lax.shift_right_logical(lookup(pos, ends, ends, 0), 7)
    return pos < live, first, b - first + 1


def self_forward(half, ends, live, q_ref, k_ref, vt_ref, bias_ref, table_ref, start_ref, o_ref, lse_ref):
    def block(i, b, first, n):
        kstart = pl.multiple_of(first * BLK, BLK)
        start2 = twice(start_ref[pl.ds(b, 1), :])
        alive = (start2 < BIG).astype(f32)
        for p in range(2):
            _, _, scores = self_scores(
                b, n, p, kstart, q_ref, k_ref, bias_ref, table_ref, start2
            )
            peak = jnp.max(scores, axis=0, keepdims=True)
            raised = jnp.exp(scores - peak)
            total = jnp.sum(raised, axis=0, keepdims=True)
            mixed = nn(vt_ref[p * BLK : (p + 1) * BLK, pl.ds(kstart, n * BLK)], raised.astype(bf16))
            mixed = mixed * (alive / total)
            o_ref[pl.ds(pl.multiple_of(i * BLK, BLK), BLK), p * BLK : (p + 1) * BLK] = diagonal(
                mixed
            ).astype(bf16)
            lse_ref[p, pl.ds(i, 1), :] = peak + jnp.log(total)

    def step(i, carry):
        b = half * 4 + i
        alive, first, n = self_spans(b, ends, live)
        for m in range(1, 5):
            pl.when(alive & (n == m))(functools.partial(block, i, b, first, m))

        @pl.when(jnp.logical_not(alive))
        def _():
            o_ref[pl.ds(pl.multiple_of(i * BLK, BLK), BLK), :] = jnp.zeros((BLK, OWN), bf16)
            for p in range(2):
                lse_ref[p, pl.ds(i, 1), :] = jnp.zeros((1, 2 * BLK), f32)

        return carry

    lax.fori_loop(0, 4, step, 0)


def set_starts(ends, live, start_ref):
    pos = token_positions()
    start_ref[...] = jnp.where(pos < live, lookup(pos, ends, ends, 0), BIG)


def first_kernel(
    io, t_ref, len_ref, cnt_ref, table_ref,
    x_ref, gain_ref, wq_ref, wk_ref, wv_ref,
    n1_ref, q_ref, k_ref, v_ref, vt_ref, kt_ref, bias_ref, o_ref, lse_ref,
    start_ref,
):
    ends = running_ends(len_ref)
    live = live_tokens(ends, cnt_ref[0])
    set_starts(ends, live, start_ref)
    fill_bias(table_ref, bias_ref)
    io.done(bias_ref)
    io.ready(x_ref, gain_ref, wq_ref, wk_ref, wv_ref)

    def project(i, carry):
        rows = pl.ds(pl.multiple_of(i * 256, 256), 256)
        value = x_ref[rows, :].astype(f32)
        low = (value * rms_scale(value) * gain_ref[...]).astype(bf16)
        n1_ref[rows, :] = low
        q_ref[rows, :] = nn(low, wq_ref[...]).astype(bf16)
        keys = nn(low, wk_ref[...])
        k_ref[rows, :] = keys.astype(bf16)
        kt_ref[:, rows] = jnp.transpose(keys).astype(bf16)
        values = nn(low, wv_ref[...])
        v_ref[rows, :] = values.astype(bf16)
        vt_ref[:, rows] = jnp.transpose(values).astype(bf16)
        return carry

    lax.fori_loop(0, 4, project, 0)
    io.done(n1_ref, q_ref, k_ref, v_ref, vt_ref, kt_ref)
    self_forward(
        1 - t_ref[0], ends, live, q_ref, k_ref, vt_ref, bias_ref, table_ref, start_ref, o_ref, lse_ref
    )


def second_kernel(
    io, t_ref, len_ref, cnt_ref, table_ref,
    q_ref, k_ref, vt_ref, bias_ref,
    o_ref, lse_ref,
    start_ref,
):
    ends = running_ends(len_ref)
    live = live_tokens(ends, cnt_ref[0])
    set_starts(ends, live, start_ref)
    io.ready(q_ref, k_ref, vt_ref, bias_ref)
    self_forward(
        t_ref[0], ends, live, q_ref, k_ref, vt_ref, bias_ref, table_ref, start_ref, o_ref, lse_ref
    )


def memory_kernel(
    io, _, mem_ref, ck_ref, cko_ref, cv_ref, cvo_ref, mk_ref, mv_ref, mkt_ref, mvt_ref, cko_out, cvo_out
):
    io.forward((cko_ref, cko_out), (cvo_ref, cvo_out))
    io.ready(mem_ref, ck_ref, cko_ref, cv_ref, cvo_ref)

    def project(i, carry):
        rows = pl.ds(pl.multiple_of(i * 256, 256), 256)
        value = mem_ref[rows, :]
        for side, (wk, wv) in enumerate(((ck_ref, cv_ref), (cko_ref, cvo_ref))):
            lanes = slice(side * OWN, (side + 1) * OWN)
            keys = nn(value, wk[...])
            mk_ref[rows, lanes] = keys.astype(bf16)
            mkt_ref[lanes, rows] = jnp.transpose(keys).astype(bf16)
            values = nn(value, wv[...])
            mv_ref[rows, lanes] = values.astype(bf16)
            mvt_ref[lanes, rows] = jnp.transpose(values).astype(bf16)
        return carry

    lax.fori_loop(0, 4, project, 0)


SPANS = (1, 2, 3, 4, 6, 8)


def set_ranges(ends, mends, live, low_ref, high_ref):
    pos = token_positions()
    low_ref[...] = jnp.where(pos < live, lookup(pos, ends, mends, 0), BIG)
    high_ref[...] = lookup(pos, ends, mends[1:], mends[0])


def cross_blocks(half, ends, mends, live, block, dead):
    def step(i, carry):
        b = half * 4 + i
        pos = b * BLK
        alive = pos < live
        last = jnp.minimum(pos + BLK, live) - 1
        first = lax.shift_right_logical(lookup(pos, ends, mends, 0), 7)
        end = lax.shift_right_logical(lookup(last, ends, mends[1:], mends[0]) + BLK - 1, 7)
        n = end - first
        below = 0
        for m in SPANS:
            begin = jnp.minimum(first, LEN // BLK - m)
            pl.when(alive & (n > below) & (n <= m))(functools.partial(block, i, b, begin, m))
            below = m
        pl.when(jnp.logical_not(alive))(functools.partial(dead, i))
        return carry

    lax.fori_loop(0, 4, step, 0)


def cross_scores(i, n, lanes, kstart, q_ref, k_ref, low2, high2):
    keys = k_ref[pl.ds(kstart, n * BLK), lanes]
    queries = stacked(q_ref[pl.ds(pl.multiple_of(i * BLK, BLK), BLK), lanes])
    index = kstart + lax.broadcasted_iota(jnp.int32, (n * BLK, 2 * BLK), 0)
    allowed = (index >= low2) & (index < high2)
    return queries, keys, jnp.where(allowed, nt(keys, queries), MASKED)


def pairs(body):
    def step(g, carry):
        for k in range(2):
            p = 2 * g + k
            body(p, pl.ds(pl.multiple_of(p * BLK, BLK), BLK))
        return carry

    lax.fori_loop(0, 2, step, 0)


def third_kernel(
    io, t_ref, len_ref, mlen_ref, cnt_ref,
    x_ref, keep_ref, recv_ref, so_ref, soo_ref, gain2_ref, cq_ref, cqo_ref,
    mk_ref, mvt_ref, co_ref, coo_ref, gain3_ref,
    h1_ref, n2_ref, q_ref, mixed_ref, lse_ref, h2_ref, n3_ref, recv_out, soo_out, cqo_out, coo_out,
    low_ref, high_ref,
):
    t = t_ref[0]
    io.forward((recv_ref, recv_out), (soo_ref, soo_out), (cqo_ref, cqo_out), (coo_ref, coo_out))
    ends, mends = running_ends(len_ref), running_ends(mlen_ref)
    live = live_tokens(ends, cnt_ref[0])
    set_ranges(ends, mends, live, low_ref, high_ref)

    io.ready(x_ref, keep_ref, recv_ref, so_ref, soo_ref, gain2_ref, cq_ref, cqo_ref)

    def before(i, carry):
        rows = pl.ds(pl.multiple_of(i * 256, 256), 256)
        value = x_ref[rows, :].astype(f32)
        value = value + nn(keep_ref[rows, :], so_ref[...]) + nn(recv_ref[rows, :], soo_ref[...])
        h1_ref[rows, :] = value
        low = (value * rms_scale(value) * gain2_ref[...]).astype(bf16)
        n2_ref[rows, :] = low
        q_ref[rows, :OWN] = nn(low, cq_ref[...]).astype(bf16)
        q_ref[rows, OWN:] = nn(low, cqo_ref[...]).astype(bf16)
        return carry

    lax.fori_loop(0, 2, before, 0)
    io.done(h1_ref, n2_ref, q_ref)
    io.ready(mk_ref, mvt_ref)

    def block(i, b, first, n):
        kstart = pl.multiple_of(first * BLK, BLK)
        low2, high2 = twice(low_ref[pl.ds(b, 1), :]), twice(high_ref[pl.ds(b, 1), :])
        alive = (low2 < BIG).astype(f32)

        def pair(p, lanes):
            _, _, scores = cross_scores(i, n, lanes, kstart, q_ref, mk_ref, low2, high2)
            peak = jnp.max(scores, axis=0, keepdims=True)
            raised = jnp.exp(scores - peak)
            total = jnp.sum(raised, axis=0, keepdims=True)
            mixed = nn(mvt_ref[lanes, pl.ds(kstart, n * BLK)], raised.astype(bf16))
            mixed = mixed * (alive / total)
            mixed_ref[pl.ds(pl.multiple_of(i * BLK, BLK), BLK), lanes] = diagonal(mixed).astype(bf16)
            lse_ref[p, pl.ds(i, 1), :] = peak + jnp.log(total)

        pairs(pair)

    def dead(i):
        mixed_ref[pl.ds(pl.multiple_of(i * BLK, BLK), BLK), :] = jnp.zeros((BLK, WIDTH), bf16)
        for p in range(4):
            lse_ref[p, pl.ds(i, 1), :] = jnp.zeros((1, 2 * BLK), f32)

    cross_blocks(t, ends, mends, live, block, dead)

    io.done(mixed_ref, lse_ref)
    io.ready(co_ref, coo_ref, gain3_ref)

    def after(i, carry):
        rows = pl.ds(pl.multiple_of(i * 256, 256), 256)
        value = h1_ref[rows, :]
        value = value + nn(mixed_ref[rows, :OWN], co_ref[...]) + nn(mixed_ref[rows, OWN:], coo_ref[...])
        h2_ref[rows, :] = value
        n3_ref[rows, :] = (value * rms_scale(value) * gain3_ref[...]).astype(bf16)
        return carry

    lax.fori_loop(0, 2, after, 0)


def feed_kernel(
    io, place_ref, n3_ref, fi_ref, cot_ref, fo_ref,
    out_ref, gn_ref, act_ref, gp_ref,
):
    tile = 256
    n_tiles = fi_ref.shape[1] // tile
    root = math.sqrt(2 / math.pi)
    base = place_ref[0] * HALF
    io.ready(n3_ref, fi_ref, cot_ref, fo_ref)

    def hidden(j, carry):
        lanes = pl.ds(pl.multiple_of(j * tile, tile), tile)
        for i in range(2):
            rows = slice(i * 256, (i + 1) * 256)
            pre = nn(n3_ref[rows, :], fi_ref[:, lanes])
            square = pre * pre
            bent = jnp.tanh(pre * (root + (root * 0.044715) * square))
            gate = 0.5 + 0.5 * bent
            slope = gate + pre * (0.5 - 0.5 * bent * bent) * (root + (root * 0.134145) * square)
            act_ref[rows, lanes] = (pre * gate).astype(bf16)
            grads = nt(cot_ref[pl.ds(pl.multiple_of(base + i * 256, 256), 256), :], fo_ref[lanes, :])
            gp_ref[rows, lanes] = (grads * slope).astype(bf16)
        return carry

    lax.fori_loop(0, n_tiles, hidden, 0)
    io.done(act_ref, gp_ref)

    def outward(i, carry):
        rows = pl.ds(pl.multiple_of(i * 256, 256), 256)
        out_ref[rows, :] = nn(act_ref[rows, :], fo_ref[...]).astype(bf16)
        gn_ref[rows, :] = nt(gp_ref[rows, :], fi_ref[...]).astype(bf16)
        return carry

    lax.fori_loop(0, 2, outward, 0)


def feed_weights_kernel(
    io, t_ref, h2_ref, own_ref, oth_ref, n3_ref, gp_ref, n3o_ref, gpo_ref, act_ref, cot_ref, acto_ref,
    fi_ref, fo_ref, out_ref,
    n3t_ref,
):
    t = t_ref[0]
    mine = pl.ds(pl.multiple_of(t * HALF, HALF), HALF)
    theirs = pl.ds(pl.multiple_of((1 - t) * HALF, HALF), HALF)
    io.ready(n3_ref, gp_ref, n3o_ref, gpo_ref)
    n3t_ref[:, :HALF] = jnp.transpose(n3_ref[...].astype(f32)).astype(bf16)
    n3t_ref[:, HALF:] = jnp.transpose(n3o_ref[...].astype(f32)).astype(bf16)
    n_tiles = fi_ref.shape[1] // 256
    for j in range(n_tiles):
        lanes = slice(j * 256, (j + 1) * 256)
        grads = nn(n3t_ref[:, :HALF], gp_ref[:, lanes]) + nn(n3t_ref[:, HALF:], gpo_ref[:, lanes])
        fi_ref[:, lanes] = grads.astype(bf16)
    io.done(fi_ref)
    io.ready(act_ref, cot_ref, acto_ref)
    for j in range(n_tiles):
        lanes = slice(j * 256, (j + 1) * 256)
        grads = tn(act_ref[:, lanes], cot_ref[mine, :]) + tn(acto_ref[:, lanes], cot_ref[theirs, :])
        fo_ref[lanes, :] = grads.astype(bf16)
    io.done(fo_ref)
    io.ready(h2_ref, own_ref, oth_ref)
    out_ref[mine, :] = (h2_ref[...] + own_ref[...].astype(f32)).astype(bf16)
    out_ref[theirs, :] = oth_ref[...]


def cross_back_kernel(
    io, t_ref, len_ref, mlen_ref, cnt_ref,
    gn_ref, gnr_ref, h2_ref, gain3_ref, cot_ref, co_ref, coo_ref,
    q_ref, mk_ref, mkt_ref, mv_ref, lse_ref, cq_ref, cqo_ref, h1_ref, gain2_ref, so_ref, soo_ref,
    gb2_ref, dq_ref, dk_ref, dv_ref, gh1_ref, gb1_ref, gm1_ref, gm1o_ref, gains_ref,
    low_ref, high_ref, live_ref, gm_ref, dk_acc, dv_acc, gh2_ref,
):
    t = t_ref[0]
    ends, mends = running_ends(len_ref), running_ends(mlen_ref)
    live = live_tokens(ends, cnt_ref[0])
    set_ranges(ends, mends, live, low_ref, high_ref)
    alive_rows = t * HALF + lax.broadcasted_iota(jnp.int32, (HALF, BLK), 0)
    live_ref[...] = (alive_rows < live).astype(f32)
    dk_acc[...] = jnp.zeros_like(dk_acc)
    dv_acc[...] = jnp.zeros_like(dv_acc)
    gains_ref[...] = jnp.zeros_like(gains_ref)

    io.ready(gn_ref, gnr_ref, h2_ref, gain3_ref, cot_ref, co_ref, coo_ref)
    for i in range(2):
        rows = slice(i * 256, (i + 1) * 256)
        grad = gn_ref[rows, :].astype(f32) + gnr_ref[rows, :].astype(f32)
        back, gain = rms_back(h2_ref[rows, :], gain3_ref[...], grad)
        gains_ref[0:1, :] += gain
        grad = cot_ref[rows, :].astype(f32) + back
        gh2_ref[rows, :] = grad
        low = grad.astype(bf16)
        gb2_ref[rows, :] = low
        alive = live_ref[rows, 0:1]
        gm_ref[rows, :OWN] = (nt(low, co_ref[...]) * alive).astype(bf16)
        gm_ref[rows, OWN:] = (nt(low, coo_ref[...]) * alive).astype(bf16)
    io.done(gb2_ref)
    io.ready(q_ref, mk_ref, mkt_ref, mv_ref, lse_ref)

    def block(i, b, first, n):
        kstart = pl.multiple_of(first * BLK, BLK)
        low2, high2 = twice(low_ref[pl.ds(b, 1), :]), twice(high_ref[pl.ds(b, 1), :])
        rows = pl.ds(pl.multiple_of(i * BLK, BLK), BLK)
        span = pl.ds(kstart, n * BLK)

        def pair(p, lanes):
            queries, _, scores = cross_scores(i, n, lanes, kstart, q_ref, mk_ref, low2, high2)
            probs = jnp.exp(scores - lse_ref[p, pl.ds(i, 1), :])
            grads = stacked(gm_ref[rows, lanes])
            grad_probs = nt(mv_ref[span, lanes], grads)
            inner = jnp.sum(grad_probs * probs, axis=0, keepdims=True)
            low = (probs * (grad_probs - inner)).astype(bf16)
            dk_acc[span, lanes] += nn(low, queries)
            dv_acc[span, lanes] += nn(probs.astype(bf16), grads)
            dq_ref[rows, lanes] = diagonal(nn(mkt_ref[lanes, span], low)).astype(bf16)

        pairs(pair)

    def dead(i):
        dq_ref[pl.ds(pl.multiple_of(i * BLK, BLK), BLK), :] = jnp.zeros((BLK, WIDTH), bf16)

    cross_blocks(t, ends, mends, live, block, dead)

    dk_ref[...] = dk_acc[...].astype(bf16)
    dv_ref[...] = dv_acc[...].astype(bf16)
    io.done(dq_ref, dk_ref, dv_ref)
    io.ready(cq_ref, cqo_ref, h1_ref, gain2_ref, so_ref, soo_ref)
    for i in range(2):
        rows = slice(i * 256, (i + 1) * 256)
        grad = nt(dq_ref[rows, :OWN], cq_ref[...]) + nt(dq_ref[rows, OWN:], cqo_ref[...])
        back, gain = rms_back(h1_ref[rows, :], gain2_ref[...], grad)
        gains_ref[1:2, :] += gain
        grad = gh2_ref[rows, :] + back
        gh1_ref[rows, :] = grad
        low = grad.astype(bf16)
        gb1_ref[rows, :] = low
        alive = live_ref[rows, 0:1]
        gm1_ref[rows, :] = (nt(low, so_ref[...]) * alive).astype(bf16)
        gm1o_ref[rows, :] = (nt(low, soo_ref[...]) * alive).astype(bf16)


def cross_weights_kernel(
    io, place_ref, mem_ref, dk_ref, dv_ref, n2_ref, dq_ref, mixed_ref, gb2_ref, keep_ref, gb1_ref, recv_ref,
    ck_ref, cko_ref, cv_ref, cvo_ref,
    hold_ref, holdo_ref, send_ref, gmem_ref, gmems_ref,
    memt_ref, fold_ref,
):
    t, c = place_ref[0], place_ref[1]
    io.ready(mem_ref, dk_ref, dv_ref, n2_ref, dq_ref, mixed_ref, gb2_ref, keep_ref, gb1_ref, recv_ref)
    memt_ref[...] = jnp.transpose(mem_ref[...].astype(f32)).astype(bf16)
    n2t = jnp.transpose(n2_ref[...].astype(f32)).astype(bf16)
    for side in range(2):
        lanes = slice(side * OWN, (side + 1) * OWN)
        mixed1 = keep_ref if side == 0 else recv_ref
        fold_ref[0] = tn(mixed_ref[:, lanes], gb2_ref[...]).astype(bf16)
        fold_ref[1] = tn(mixed1[...], gb1_ref[...]).astype(bf16)
        fold(fold_ref, 2, nn(n2t, dq_ref[:, lanes]))
        fold(fold_ref, 3, nn(memt_ref[...], dk_ref[:, lanes]))
        fold(fold_ref, 4, nn(memt_ref[...], dv_ref[:, lanes]))
        deal(c, fold_ref, hold_ref if side == 0 else holdo_ref, send_ref, side * 640)
    io.done(hold_ref, holdo_ref, send_ref)
    io.ready(ck_ref, cko_ref, cv_ref, cvo_ref)
    for i in range(4):
        rows = slice(i * 256, (i + 1) * 256)
        grads = nt(dk_ref[rows, :OWN], ck_ref[...]) + nt(dk_ref[rows, OWN:], cko_ref[...])
        grads += nt(dv_ref[rows, :OWN], cv_ref[...]) + nt(dv_ref[rows, OWN:], cvo_ref[...])
        low = grads.astype(bf16)

        @pl.when(t == 0)
        def _():
            gmem_ref[rows, :] = low[:, :OWN]
            gmems_ref[rows, :] = low[:, OWN:]

        @pl.when(t != 0)
        def _():
            gmem_ref[rows, :] = low[:, OWN:]
            gmems_ref[rows, :] = low[:, :OWN]


def fold(fold_ref, k, weight):
    low = weight.astype(bf16)
    fold_ref[k, :, :OWN] = low[:256]
    fold_ref[k, :, OWN:] = low[256:]


def deal(c, fold_ref, hold_ref, send_ref, base):
    for k in range(fold_ref.shape[0]):
        rows = slice(k * BLK, (k + 1) * BLK)
        hold_ref[rows, :] = fold_ref[k, pl.ds(pl.multiple_of(c * BLK, BLK), BLK), :]
        rows = slice(base + k * BLK, base + (k + 1) * BLK)
        send_ref[rows, :] = fold_ref[k, pl.ds(pl.multiple_of((1 - c) * BLK, BLK), BLK), :]


def self_back_kernel(
    io, place_ref, len_ref, cnt_ref, table_ref,
    gm_ref, gmr_ref, q_ref, k_ref, kt_ref, v_ref, bias_ref, lse_ref, lseo_ref,
    n1_ref, x_ref, gh1_ref, gain1_ref, gains_ref, wq_ref, wk_ref, wv_ref,
    hold_ref, send_ref, gi_ref, small_ref,
    start_ref, g_ref, dq_ref, dk_acc, dv_acc, near_acc, far_acc, n1t_ref, fold_ref, sums_ref,
):
    t = place_ref[0]
    ends = running_ends(len_ref)
    live = live_tokens(ends, cnt_ref[0])
    set_starts(ends, live, start_ref)
    io.ready(gm_ref, gmr_ref)
    g_ref[pl.ds(pl.multiple_of(t * HALF, HALF), HALF), :] = gm_ref[...]
    g_ref[pl.ds(pl.multiple_of((1 - t) * HALF, HALF), HALF), :] = gmr_ref[...]
    for ref in (dk_acc, dv_acc, near_acc, far_acc, small_ref):
        ref[...] = jnp.zeros_like(ref)
    io.ready(q_ref, k_ref, kt_ref, v_ref, bias_ref, lse_ref, lseo_ref)

    def block(b, first, n):
        kstart = pl.multiple_of(first * BLK, BLK)
        start2 = twice(start_ref[pl.ds(b, 1), :])
        rows = pl.ds(pl.multiple_of(b * BLK, BLK), BLK)
        span = pl.ds(kstart, n * BLK)
        i = lax.rem(b, 4)
        mine = lax.div(b, 4) == t
        for p in range(2):
            lanes = slice(p * BLK, (p + 1) * BLK)
            queries, _, scores = self_scores(
                b, n, p, kstart, q_ref, k_ref, bias_ref, table_ref, start2
            )
            lse = jnp.where(mine, lse_ref[p, pl.ds(i, 1), :], lseo_ref[p, pl.ds(i, 1), :])
            probs = jnp.exp(scores - lse)
            grads = stacked(g_ref[rows, lanes])
            grad_probs = nt(v_ref[span, lanes], grads)
            inner = jnp.sum(grad_probs * probs, axis=0, keepdims=True)
            grad_scores = probs * (grad_probs - inner)
            near_acc[p] += grad_scores[(n - 1) * BLK :]
            if n > 1:
                near_acc[2 + p] += grad_scores[(n - 2) * BLK : (n - 1) * BLK]
            if n > 2:
                far_acc[p : p + 1, :] += jnp.sum(grad_scores[: (n - 2) * BLK], axis=0, keepdims=True)
            low = grad_scores.astype(bf16)
            dk_acc[span, lanes] += nn(low, queries)
            dv_acc[span, lanes] += nn(probs.astype(bf16), grads)
            dq_ref[rows, lanes] = diagonal(nn(kt_ref[lanes, span], low)).astype(bf16)

    def step(b, carry):
        alive, first, n = self_spans(b, ends, live)
        for m in range(1, 5):
            pl.when(alive & (n == m))(functools.partial(block, b, first, m))

        @pl.when(jnp.logical_not(alive))
        def _():
            dq_ref[pl.ds(pl.multiple_of(b * BLK, BLK), BLK), :] = jnp.zeros((BLK, OWN), bf16)

        return carry

    lax.fori_loop(0, LEN // BLK, step, 0)

    io.ready(n1_ref)
    n1t_ref[...] = jnp.transpose(n1_ref[...].astype(f32)).astype(bf16)
    low_k, low_v = dk_acc[...].astype(bf16), dv_acc[...].astype(bf16)
    for k, grads in enumerate((dq_ref[...], low_k, low_v)):
        fold(fold_ref, k, nn(n1t_ref[...], grads))
    deal(place_ref[1], fold_ref, hold_ref, send_ref, 0)
    io.done(hold_ref, send_ref)
    io.ready(x_ref, gh1_ref, gain1_ref, gains_ref, wq_ref, wk_ref, wv_ref)
    gain1 = jnp.zeros((1, WIDTH), f32)
    for i in range(4):
        rows = slice(i * 256, (i + 1) * 256)
        grads = nt(dq_ref[rows, :], wq_ref[...]) + nt(low_k[rows], wk_ref[...]) + nt(low_v[rows], wv_ref[...])
        back, gain = rms_back(x_ref[rows, :].astype(f32), gain1_ref[...], grads)
        gain1 += gain
        mine = (t == i // 2).astype(f32)
        back += mine * gh1_ref[(i % 2) * 256 : (i % 2 + 1) * 256, :]
        gi_ref[rows, :] = back.astype(bf16)
    io.done(gi_ref)
    key = lax.broadcasted_iota(jnp.int32, (BLK, BLK), 0)
    query = lax.broadcasted_iota(jnp.int32, (BLK, BLK), 1)
    gaps = [query - key, BLK + query - key]
    for level in range(NB):
        for p in range(2):
            row = jnp.zeros((1, 2 * BLK), f32)
            for d in range(2):
                inside = gaps[d] >= THRESHOLDS[level]
                if level + 1 < NB:
                    inside &= gaps[d] < THRESHOLDS[level + 1]
                picked = jnp.where(twice(inside.astype(f32)) > 0, near_acc[2 * d + p], 0.0)
                row += jnp.sum(picked, axis=0, keepdims=True)
            if level == NB - 1:
                row += far_acc[p : p + 1, :]
            sums_ref[level : level + 1, p * 256 : (p + 1) * 256] = row
    lane = lax.broadcasted_iota(jnp.int32, (NB, BLK), 1)
    table = jnp.zeros((NB, BLK), f32)
    for h in range(4):
        total = jnp.sum(sums_ref[:, h * BLK : (h + 1) * BLK], axis=1, keepdims=True)
        table = jnp.where(lane == h, total, table)
    small_ref[16:48, :] = table

    for k, gain in enumerate((gain1, gains_ref[1:2, :], gains_ref[0:1, :])):
        for j in range(4):
            small_ref[4 * k + j : 4 * k + j + 1, :] = gain[:, j * BLK : (j + 1) * BLK]


def join_kernel(io, place_ref, own_ref, got_ref, recv_ref, mine_ref, theirs_ref, hold_ref, send_ref):
    x = place_ref[2]
    io.ready(own_ref, got_ref, recv_ref, mine_ref, theirs_ref)
    for k in range(8):
        if k < 5:
            rows = slice(k * BLK, (k + 1) * BLK)
            total = own_ref[rows, :].astype(f32) + got_ref[rows, :].astype(f32) + recv_ref[rows, :].astype(f32)
        else:
            rows = slice((k - 5) * BLK, (k - 4) * BLK)
            total = mine_ref[rows, :].astype(f32) + theirs_ref[rows, :].astype(f32)
        low = total.astype(bf16)
        rows = slice((k % 4) * BLK, (k % 4 + 1) * BLK)

        @pl.when(x == k // 4)
        def _():
            hold_ref[rows, :] = low

        @pl.when(x != k // 4)
        def _():
            send_ref[rows, :] = low


def pieces_kernel(io, _, in_ref, out_ref):
    io.ready(in_ref)
    total = in_ref[0].astype(f32)
    for k in range(1, in_ref.shape[0]):
        total += in_ref[k].astype(f32)
    total = total.astype(bf16)
    for k in range(in_ref.shape[0]):
        out_ref[k] = total


def unfold_kernel(
    io, place_ref, own_ref, pair_ref, core_ref, both_ref,
    co_ref, so_ref, cq_ref, ck_ref, cv_ref, wq_ref, wk_ref, wv_ref,
):
    c, x = place_ref[1], place_ref[2]
    outs = (co_ref, so_ref, cq_ref, ck_ref, cv_ref, wq_ref, wk_ref, wv_ref)

    def spread(ref, core, bit):
        low = pl.ds(pl.multiple_of(core * BLK, BLK), BLK)
        high = pl.ds(pl.multiple_of(256 + core * BLK, BLK), BLK)
        for k, out in enumerate(outs):
            rows = slice((k % 4) * BLK, (k % 4 + 1) * BLK)

            @pl.when(bit == k // 4)
            def _():
                if k < 2:
                    out[low, :] = ref[rows, :].astype(f32)
                else:
                    out[low, :] = ref[rows, :OWN].astype(f32)
                    out[high, :] = ref[rows, OWN:].astype(f32)

    for ref, core, bit in ((own_ref, c, x), (pair_ref, c, 1 - x), (core_ref, 1 - c, x), (both_ref, 1 - c, 1 - x)):
        io.ready(ref)
        spread(ref, core, bit)


def swap(value, axis="tensor"):
    return lax.ppermute(value, axis, [(0, 1), (1, 0)])


def shards(
    inputs, memory, cotangent, dec_lengths, mem_lengths, counts,
    self_gain, self_query, self_key, self_value, self_out, rel_table,
    cross_gain, cross_query, cross_key, cross_value, cross_out,
    feed_gain, feed_in, feed_out,
):
    v = pltpu.VMEM
    i32 = jnp.int32
    t, c, x = (lax.axis_index(name).astype(i32) for name in ("tensor", "core", "pair"))
    ring = lax.axis_size("ring")
    place = jnp.stack([t, c, x])
    place_oth = jnp.stack([1 - t, c, x])
    gain1, gain2, gain3 = (g.reshape(1, WIDTH) for g in (self_gain, cross_gain, feed_gain))
    table = rel_table.T

    so_oth = swap(self_out)
    ck_oth = swap(cross_key)
    cv_oth = swap(cross_value)
    cq_oth = swap(cross_query)
    co_oth = swap(cross_out)

    tok = (LEN, WIDTH)
    half = (HALF, WIDTH)
    heads, heads_t, part = (LEN, OWN), (OWN, LEN), (HALF, OWN)
    row_tile = v((LEN // BLK, BLK), i32)
    n1, q, q_far, k, k_far, val, vt, kt, bias, bias_far, send1, lse1_oth = call(
        first_kernel,
        [(tok, bf16, "far"), (heads, bf16, "both"), (heads, bf16, "both"), (heads, bf16, "far"),
         (heads_t, bf16, "near"), (heads_t, bf16, "far"), ((4, BLK, 2 * BLK), f32, "both"), (part, bf16, "near"),
         ((2, 4, 2 * BLK), f32, "far")],
        [row_tile],
        (place, dec_lengths, counts, table, inputs, gain1, self_query, self_key, self_value),
        smem=4, us=6,
    )
    mixed1_recv = swap(send1)
    mixed1_keep, keep_far, lse1 = call(
        second_kernel,
        [(part, bf16, "both"), ((2, 4, 2 * BLK), f32, "far")],
        [row_tile],
        (place, dec_lengths, counts, table, Near(q), Near(k), Near(vt), Near(bias)),
        smem=4, us=4,
    )
    mk, mk_far, mv, mkt, mvt, ck_oth, cv_oth = call(
        memory_kernel,
        [(tok, bf16, "both"), (tok, bf16, "far"), ((WIDTH, LEN), bf16, "far"), ((WIDTH, LEN), bf16, "near"),
         ((WIDTH, OWN), bf16, "far"), ((WIDTH, OWN), bf16, "far")],
        [],
        (place, memory, cross_key, Near(ck_oth), cross_value, Near(cv_oth)),
    )
    h1, n2, cq, mixed2, lse2, h2, n3, n3_far, recv_far, so_oth, cq_oth, co_oth = call(
        third_kernel,
        [(half, f32, "far"), (half, bf16, "far"), (half, bf16, "far"), (half, bf16, "far"),
         ((4, 4, 2 * BLK), f32, "far"), (half, f32, "far"), (half, bf16, "both"), (part, bf16, "far"),
         ((OWN, WIDTH), bf16, "far"), ((WIDTH, OWN), bf16, "far"), ((OWN, WIDTH), bf16, "far")],
        [row_tile, row_tile],
        (place, dec_lengths, mem_lengths, counts, Half(inputs), Near(mixed1_keep), Near(mixed1_recv), self_out,
         Near(so_oth), gain2, cross_query, Near(cq_oth), Near(mk), Near(mvt), cross_out, Near(co_oth), gain3),
        smem=4, us=9,
    )
    n3_recv = swap(n3)

    hidden = feed_in.shape[1]
    units = (HALF, hidden)
    out_own, gn3_own, act, gp = call(
        feed_kernel,
        [(half, bf16, "far"), (half, bf16, "far"), (units, bf16, "far"), (units, bf16, "far")],
        [],
        (place, Near(n3), Near(feed_in), Near(cotangent), Near(feed_out)),
        us=5,
    )
    n3_recv, act = lax.optimization_barrier((n3_recv, act))
    out_oth, gn3_oth, act_oth, gp_oth = call(
        feed_kernel,
        [(half, bf16, "near"), (half, bf16, "near"), (units, bf16, "near"), (units, bf16, "near")],
        [],
        (place_oth, Near(n3_recv), Near(feed_in), Near(cotangent), Near(feed_out)),
        us=5,
    )
    gn3_recv = swap(gn3_oth)
    feed_in_grad, feed_out_grad, out_part = call(
        feed_weights_kernel,
        [((WIDTH, hidden), bf16, "far"), ((hidden, WIDTH), bf16, "far"), (tok, bf16, "far")],
        [v((WIDTH, LEN), bf16)],
        (place, h2, out_own, Near(out_oth), n3_far, gp, Near(n3_recv), Near(gp_oth), act, cotangent, Near(act_oth)),
        us=5,
    )
    gn3_recv, out_part, feed_in_grad, feed_out_grad = lax.optimization_barrier(
        (gn3_recv, out_part, feed_in_grad, feed_out_grad)
    )
    dp = ("ring", "pair", "core")
    feed_in_grad, feed_out_grad = lax.psum((feed_in_grad, feed_out_grad), dp)

    def later():
        gb2, dcq, dmk, dmv, gh1, gb1, gm1, gm1_oth, gains = call(
            cross_back_kernel,
            [(half, bf16, "near"), (half, bf16, "near"), (tok, bf16, "near"), (tok, bf16, "near"), (half, f32, "far"),
             (half, bf16, "near"), (part, bf16, "near"), (part, bf16, "near"), ((8, WIDTH), f32, "far")],
            [row_tile, row_tile, v((HALF, BLK), f32), v(half, bf16), v(tok, f32), v(tok, f32), v(half, f32)],
            (place, dec_lengths, mem_lengths, counts, gn3_own, Near(gn3_recv), h2, gain3, Half(cotangent),
             cross_out, co_oth, cq, mk_far, mkt, mv, lse2, cross_query, cq_oth, h1, gain2, self_out, so_oth),
            smem=4, us=11,
        )
        gm1_recv = swap(gm1_oth)
        cross_hold, cross_hold_oth, cross_send, gmem, gmem_send = call(
            cross_weights_kernel,
            [((640, WIDTH), bf16, "near"), ((640, WIDTH), bf16, "near"), ((1280, WIDTH), bf16, "near"),
             (heads, bf16, "far"), (heads, bf16, "far")],
            [v((WIDTH, LEN), bf16), v((5, 256, WIDTH), bf16)],
            (place, memory, Near(dmk), Near(dmv), n2, Near(dcq), mixed2, Near(gb2), keep_far, Near(gb1), recv_far,
             cross_key, ck_oth, cross_value, cv_oth),
            us=5,
        )
        cross_got = swap(cross_send, "core")
        cross_recv = swap((cross_hold_oth.astype(f32) + cross_got[640:].astype(f32)).astype(bf16))
        self_hold, self_send, gi_part, small = call(
            self_back_kernel,
            [((384, WIDTH), bf16, "near"), ((384, WIDTH), bf16, "near"), (tok, bf16, "far"), ((48, BLK), f32, "near")],
            [row_tile, v((LEN, OWN), bf16), v((LEN, OWN), bf16), v((LEN, OWN), f32), v((LEN, OWN), f32),
             v((4, BLK, 2 * BLK), f32), v((2, 2 * BLK), f32), v((WIDTH, LEN), bf16), v((3, 256, WIDTH), bf16),
             v((NB, WIDTH), f32)],
            (place, dec_lengths, counts, table, Near(gm1), Near(gm1_recv), q_far, k_far, kt, val, bias_far, lse1, lse1_oth,
             n1, inputs, gh1, gain1, gains, self_query, self_key, self_value),
            smem=4, us=9,
        )
        self_got = swap(self_send, "core")
        gi_recv = swap(gi_part)

        hold, send = call(
            join_kernel,
            [(half, bf16, "near"), (half, bf16, "near")],
            [],
            (place, *map(Near, (cross_hold, cross_got, cross_recv, self_hold, self_got))),
            us=2,
        )
        small = jnp.broadcast_to(small[None], (4 * ring, 48, BLK))
        small = jnp.sum(lax.all_to_all(small, dp, 0, 0), axis=0)
        gmem_recv = swap(gmem_send)
        summed = (hold.astype(f32) + swap(send, "pair").astype(f32)).astype(bf16)
        summed, small, gmem_recv = lax.optimization_barrier((summed, small, gmem_recv))
        pieces = (ring, HALF // ring, WIDTH)
        taken = lax.all_to_all(summed.reshape(pieces), "ring", 0, 0)
        (summed,) = call(pieces_kernel, [(pieces, bf16, "near")], [], (place, Near(taken)), us=2)
        summed, gi_recv = lax.optimization_barrier((summed, gi_recv))
        out_recv = swap(out_part)
        own = lax.all_to_all(summed, "ring", 0, 0).reshape(half)
        pair = swap(own, "pair")
        narrow, wide = ((OWN, WIDTH), f32, "far"), ((WIDTH, OWN), f32, "far")
        co_grad, so_grad, cq_grad, ck_grad, cv_grad, wq_grad, wk_grad, wv_grad = call(
            unfold_kernel,
            [narrow] * 2 + [wide] * 6,
            [],
            (place, *map(Near, (own, pair, swap(own, "core"), swap(pair, "core")))),
        )
        gain_grads = (small + swap(small))[:12]

        def both(part, other):
            return (part.astype(f32) + other.astype(f32)).astype(bf16)

        output, grad_inputs, grad_memory = both(out_part, out_recv), both(gi_part, gi_recv), both(gmem, gmem_recv)
        return (
            output,
            grad_inputs,
            grad_memory,
            gain_grads,
            small[16:, :4],
            co_grad,
            so_grad,
            cq_grad,
            ck_grad,
            cv_grad,
            wq_grad,
            wk_grad,
            wv_grad,
        )

    def never():
        shapes = jax.eval_shape(later)
        return tuple(jnp.zeros(shape.shape, shape.dtype) for shape in shapes)

    (
        output,
        grad_inputs,
        grad_memory,
        gain_grads,
        table_grad,
        co_grad,
        so_grad,
        cq_grad,
        ck_grad,
        cv_grad,
        wq_grad,
        wk_grad,
        wv_grad,
    ) = lax.cond(counts[0] > 0, later, never)
    gain_grads = gain_grads.reshape(3, WIDTH)
    return (
        output,
        grad_inputs,
        grad_memory,
        gain_grads[0],
        wq_grad,
        wk_grad,
        wv_grad,
        so_grad,
        table_grad,
        gain_grads[1],
        cq_grad,
        ck_grad,
        cv_grad,
        co_grad,
        gain_grads[2],
        feed_in_grad.astype(f32),
        feed_out_grad.astype(f32),
    )


def solution(mesh):
    devices = mesh.devices
    rows, tensor = devices.shape
    mesh = Mesh(devices.reshape(rows // 4, 2, 2, tensor), ("ring", "pair", "core", "tensor"))
    dp = ("ring", "pair", "core")
    split = P(dp, None)
    columns, rows = P(None, "tensor"), P("tensor", None)
    return jax.shard_map(
        shards,
        mesh=mesh,
        in_specs=(
            split, split, split, split, split, P(dp),
            P(), columns, columns, columns, rows, columns,
            P(), columns, columns, columns, rows,
            P(), columns, rows,
        ),
        out_specs=(
            split, split, P(dp, "tensor"),
            P(), columns, columns, columns, rows, columns,
            P(), columns, columns, columns, rows,
            P(), columns, rows,
        ),
        check_vma=False,
    )
```

```python
import functools
import math

import jax
import jax.numpy as jnp
from jax import lax
from jax.experimental import pallas as pl
from jax.experimental.pallas import tpu as pltpu
from jax.sharding import Mesh
from jax.sharding import PartitionSpec as P

NB = 32
MAXDIST = 128
SEGS = 16
LEN = 1024
HALF = 512
WIDTH = 512
OWN = 256
BLK = 128
BIG = 1 << 30
MASKED = -1e30
EPS = 1e-06
f32 = jnp.float32
bf16 = jnp.bfloat16
ROOM = 11 * 1024 * 1024
SHORT = 0.05


def thresholds():
    exact = NB // 2
    edges = [
        math.ceil(exact * (MAXDIST / exact) ** (level / (NB - exact)))
        for level in range(1, NB - exact)
    ]
    return list(range(exact + 1)) + edges


THRESHOLDS = thresholds()


def nn(a, b):
    return jnp.dot(a, b, preferred_element_type=f32)


def nt(a, b):
    return lax.dot_general(a, b, (((1,), (1,)), ((), ())), preferred_element_type=f32)


def tn(a, b):
    return lax.dot_general(a, b, (((0,), (0,)), ((), ())), preferred_element_type=f32)


class Half:
    def __init__(self, array):
        self.array = array


class Near:
    def __init__(self, array):
        self.array = array


PACKED = 640


def packed_parts(core):
    def at(start, size):
        return pl.ds(pl.multiple_of(start, BLK), size)

    left, right, all_lanes = slice(0, OWN), slice(OWN, WIDTH), slice(0, WIDTH)
    return (
        [(at(core * BLK, BLK), (slice(0, 128), all_lanes))],
        [(at(core * BLK, BLK), (slice(128, 256), all_lanes))],
        [(at(core * 256, 256), (slice(256, 512), left))],
        [(at(core * 256, 256), (slice(256, 512), right))],
        [(at(core * 256, BLK), (slice(512, 640), left)), (at(core * 256 + BLK, BLK), (slice(512, 640), right))],
    )


def pack_kernel(place_ref, *refs):
    *weights, pack_ref, sems = refs
    copies = []
    for ref, parts in zip(weights, packed_parts(place_ref[1]), strict=True):
        for rows, where in parts:
            copy = pltpu.make_async_copy(ref.at[rows, :], pack_ref.at[where], sems.at[len(copies)])
            copy.start()
            copies.append(copy)
    for copy in copies:
        copy.wait()


def pack_weights(place, *weights):
    return pl.pallas_call(
        pack_kernel,
        out_shape=jax.ShapeDtypeStruct((PACKED, WIDTH), bf16),
        in_specs=[pl.BlockSpec(memory_space=pltpu.SMEM)] + [pl.BlockSpec(memory_space=pltpu.HBM)] * 5,
        out_specs=pl.BlockSpec(memory_space=pltpu.VMEM),
        scratch_shapes=[pltpu.SemaphoreType.DMA((6,))],
        compiler_params=pltpu.CompilerParams(vmem_limit_bytes=ROOM),
        cost_estimate=pl.CostEstimate(flops=1000, bytes_accessed=1000, transcendentals=0),
    )(place, *(pltpu.with_memory_space_constraint(w, pltpu.HBM) for w in weights))


class Copies:
    def __init__(self, sems):
        self.sems, self.used, self.waits, self.out = sems, 0, {}, {}

    def start(self, source, target):
        copy = pltpu.make_async_copy(source, target, self.sems.at[self.used])
        self.used += 1
        copy.start()
        return copy

    def ready(self, *refs):
        for ref in refs:
            for copy in self.waits.pop(id(ref), ()):
                copy.wait()

    def forward(self, *pairs):
        for source, ref in pairs:
            target, _ = self.out[id(ref)]
            self.out[id(ref)] = (target, self.start(source, target))

    def done(self, *refs):
        for ref in refs:
            target, copy = self.out.get(id(ref), (None, True))
            if copy is None:
                self.out[id(ref)] = (target, self.start(ref, target))


def size_of(shape, dtype):
    return math.prod(shape) * jnp.dtype(dtype).itemsize


def call(body, outs, scratch, args, smem=1, us=3):
    tables, operands = args[:smem], args[smem:]
    arrays, in_specs, fetched = [], [], []
    hbm, vmem = pl.BlockSpec(memory_space=pltpu.HBM), pl.BlockSpec(memory_space=pltpu.VMEM)
    for operand in operands:
        if isinstance(operand, Near):
            arrays.append(operand.array)
            in_specs.append(vmem)
            continue
        array = operand.array if isinstance(operand, Half) else operand
        arrays.append(pltpu.with_memory_space_constraint(array, pltpu.HBM))
        in_specs.append(hbm)
        shape = (HALF, *array.shape[1:]) if isinstance(operand, Half) else array.shape
        fetched.append((shape, array.dtype))
    out_shapes, out_specs, sent = [], [], []
    for shape, dtype, kind in outs:
        if kind != "far":
            out_shapes.append(jax.ShapeDtypeStruct(shape, dtype))
            out_specs.append(vmem)
        if kind != "near":
            out_shapes.append(pltpu.HBM(shape, dtype))
            out_specs.append(hbm)
        if kind == "far":
            sent.append((shape, dtype))
    n_copies = len(fetched) + sum(kind != "near" for _, _, kind in outs)

    def kernel(*refs):
        refs = list(refs)

        def take(n):
            taken = refs[:n]
            del refs[:n]
            return taken

        scalars, sources, targets = take(smem), take(len(arrays)), take(len(out_shapes))
        inner, outer = take(len(fetched)), take(len(sent))
        io = Copies(take(1)[0] if n_copies else None)
        inputs, outputs = [], []
        for operand, source in zip(operands, sources, strict=True):
            if isinstance(operand, Near):
                inputs.append(source)
                continue
            ref = inner.pop(0)
            inputs.append(ref)
            if isinstance(operand, Half):
                source = source.at[pl.ds(pl.multiple_of(scalars[0][0] * HALF, HALF), HALF), :]
            io.waits[id(ref)] = [io.start(source, ref)]
        for _, _, kind in outs:
            ref = outer.pop(0) if kind == "far" else targets.pop(0)
            outputs.append(ref)
            if kind != "near":
                io.out[id(ref)] = (targets.pop(0), None)
        body(io, *scalars, *inputs, *outputs, *refs)
        io.ready(*inputs)
        io.done(*outputs)
        for _, copy in io.out.values():
            copy.wait()

    own = [pltpu.VMEM(s, d) for s, d in fetched + sent]
    used = sum(size_of(s, d) for s, d in fetched + sent) + sum(size_of(s.shape, s.dtype) for s in scratch)
    return pl.pallas_call(
        kernel,
        out_shape=tuple(out_shapes),
        in_specs=[pl.BlockSpec(memory_space=pltpu.SMEM)] * smem + in_specs,
        out_specs=tuple(out_specs),
        scratch_shapes=[*own, *([pltpu.SemaphoreType.DMA((n_copies,))] if n_copies else []), *scratch],
        compiler_params=pltpu.CompilerParams(vmem_limit_bytes=used + ROOM),
        cost_estimate=pl.CostEstimate(
            flops=int(us * 3.3e9), bytes_accessed=int(us * 1e7), transcendentals=0
        ),
    )(*tables, *arrays)


def running_ends(len_ref):
    ends, total = [], 0
    for k in range(SEGS):
        total = total + len_ref[0, k]
        ends.append(total)
    return ends


def live_tokens(ends, count):
    total = 0
    for k in range(SEGS):
        total = jnp.where(k < count, ends[k], total)
    return total


def lookup(pos, ends, values, first):
    found = first
    for k in range(SEGS - 1):
        found = jnp.where(pos >= ends[k], values[k], found)
    return found


def token_positions():
    shape = (LEN // BLK, BLK)
    return lax.broadcasted_iota(jnp.int32, shape, 0) * BLK + lax.broadcasted_iota(
        jnp.int32, shape, 1
    )


def twice(row):
    return jnp.concatenate([row, row], axis=1)


def stacked(pair):
    lane = lax.broadcasted_iota(jnp.int32, pair.shape, 1)
    zero = jnp.zeros_like(pair)
    return jnp.concatenate(
        [jnp.where(lane < 64, pair, zero), jnp.where(lane < 64, zero, pair)], axis=0
    )


def diagonal(product):
    both = jnp.concatenate([product[:64, :BLK], product[64:, BLK:]], axis=0)
    return jnp.transpose(both)


def rms_scale(value):
    return lax.rsqrt(jnp.mean(value * value, axis=-1, keepdims=True) + EPS)


def rms_back(value, gain, grad):
    scale = rms_scale(value)
    weighted = grad * gain
    inner = jnp.mean(weighted * value, axis=-1, keepdims=True)
    unit = value * scale
    return (
        scale * weighted - unit * (scale * scale * inner),
        jnp.sum(grad * unit, axis=0, keepdims=True),
    )


def fill_bias(table_ref, bias_ref):
    key = lax.broadcasted_iota(jnp.int32, (BLK, BLK), 0)
    query = lax.broadcasted_iota(jnp.int32, (BLK, BLK), 1)
    for d in range(2):
        gap = d * BLK + query - key
        tiles = [jnp.full((BLK, BLK), table_ref[h, 0], f32) for h in range(4)]
        for level in range(1, NB):
            reached = gap >= THRESHOLDS[level]
            tiles = [jnp.where(reached, table_ref[h, level], tiles[h]) for h in range(4)]
        if d == 0:
            tiles = [jnp.where(gap >= 0, tile, MASKED) for tile in tiles]
        for h in range(4):
            bias_ref[d * 2 + h // 2, :, (h % 2) * BLK : (h % 2 + 1) * BLK] = tiles[h]


def far_bias(table_ref, p):
    lane = lax.broadcasted_iota(jnp.int32, (1, 2 * BLK), 1)
    return jnp.where(lane < BLK, table_ref[2 * p, NB - 1], table_ref[2 * p + 1, NB - 1])


def self_scores(b, n, p, kstart, q_ref, k_ref, bias_ref, table_ref, start2):
    lanes = slice(p * BLK, (p + 1) * BLK)
    keys = k_ref[pl.ds(kstart, n * BLK), lanes]
    queries = stacked(q_ref[pl.ds(pl.multiple_of(b * BLK, BLK), BLK), lanes])
    scores = nt(keys, queries)
    parts = []
    for j in range(n):
        part = scores[j * BLK : (j + 1) * BLK]
        d = n - 1 - j
        parts.append(part + (bias_ref[2 * d + p] if d < 2 else far_bias(table_ref, p)))
    scores = jnp.concatenate(parts, axis=0) if n > 1 else parts[0]
    index = kstart + lax.broadcasted_iota(jnp.int32, (n * BLK, 2 * BLK), 0)
    return queries, keys, jnp.where(index >= start2, scores, MASKED)


def self_spans(b, ends, live):
    pos = b * BLK
    first = lax.shift_right_logical(lookup(pos, ends, ends, 0), 7)
    return pos < live, first, b - first + 1


def self_forward(half, ends, live, q_ref, k_ref, vt_ref, bias_ref, table_ref, start_ref, o_ref, lse_ref):
    def block(i, b, first, n):
        kstart = pl.multiple_of(first * BLK, BLK)
        start2 = twice(start_ref[pl.ds(b, 1), :])
        alive = (start2 < BIG).astype(f32)
        for p in range(2):
            _, _, scores = self_scores(
                b, n, p, kstart, q_ref, k_ref, bias_ref, table_ref, start2
            )
            peak = jnp.max(scores, axis=0, keepdims=True)
            raised = jnp.exp(scores - peak)
            total = jnp.sum(raised, axis=0, keepdims=True)
            mixed = nn(vt_ref[p * BLK : (p + 1) * BLK, pl.ds(kstart, n * BLK)], raised.astype(bf16))
            mixed = mixed * (alive / total)
            o_ref[pl.ds(pl.multiple_of(i * BLK, BLK), BLK), p * BLK : (p + 1) * BLK] = diagonal(
                mixed
            ).astype(bf16)
            lse_ref[p, pl.ds(i, 1), :] = peak + jnp.log(total)

    def step(i, carry):
        b = half * 4 + i
        alive, first, n = self_spans(b, ends, live)
        for m in range(1, 5):
            pl.when(alive & (n == m))(functools.partial(block, i, b, first, m))

        @pl.when(jnp.logical_not(alive))
        def _():
            o_ref[pl.ds(pl.multiple_of(i * BLK, BLK), BLK), :] = jnp.zeros((BLK, OWN), bf16)
            for p in range(2):
                lse_ref[p, pl.ds(i, 1), :] = jnp.zeros((1, 2 * BLK), f32)

        return carry

    lax.fori_loop(0, 4, step, 0)


def set_starts(ends, live, start_ref):
    pos = token_positions()
    start_ref[...] = jnp.where(pos < live, lookup(pos, ends, ends, 0), BIG)


def first_kernel(
    io, t_ref, len_ref, cnt_ref, table_ref,
    x_ref, gain_ref, wq_ref, wk_ref, wv_ref,
    n1_ref, q_ref, k_ref, v_ref, vt_ref, kt_ref, bias_ref, o_ref, lse_ref,
    start_ref,
):
    ends = running_ends(len_ref)
    live = live_tokens(ends, cnt_ref[0])
    set_starts(ends, live, start_ref)
    fill_bias(table_ref, bias_ref)
    io.done(bias_ref)
    io.ready(x_ref, gain_ref, wq_ref, wk_ref, wv_ref)

    def project(i, carry):
        rows = pl.ds(pl.multiple_of(i * 256, 256), 256)
        value = x_ref[rows, :].astype(f32)
        low = (value * rms_scale(value) * gain_ref[...]).astype(bf16)
        n1_ref[rows, :] = low
        q_ref[rows, :] = nn(low, wq_ref[...]).astype(bf16)
        keys = nn(low, wk_ref[...])
        k_ref[rows, :] = keys.astype(bf16)
        kt_ref[:, rows] = jnp.transpose(keys).astype(bf16)
        values = nn(low, wv_ref[...])
        v_ref[rows, :] = values.astype(bf16)
        vt_ref[:, rows] = jnp.transpose(values).astype(bf16)
        return carry

    lax.fori_loop(0, 4, project, 0)
    io.done(n1_ref, q_ref, k_ref, v_ref, vt_ref, kt_ref)
    self_forward(
        1 - t_ref[0], ends, live, q_ref, k_ref, vt_ref, bias_ref, table_ref, start_ref, o_ref, lse_ref
    )


def second_kernel(
    io, t_ref, len_ref, cnt_ref, table_ref,
    q_ref, k_ref, vt_ref, bias_ref,
    o_ref, lse_ref,
    start_ref,
):
    ends = running_ends(len_ref)
    live = live_tokens(ends, cnt_ref[0])
    set_starts(ends, live, start_ref)
    io.ready(q_ref, k_ref, vt_ref, bias_ref)
    self_forward(
        t_ref[0], ends, live, q_ref, k_ref, vt_ref, bias_ref, table_ref, start_ref, o_ref, lse_ref
    )


def memory_kernel(
    io, place_ref, mem_ref, ck_ref, cv_ref, pack_ref, packo_ref,
    mk_ref, mv_ref, mkt_ref, mvt_ref, so_out, co_out, cq_out, cko_ref, cvo_ref,
):
    for core, pack in ((place_ref[1], pack_ref), (1 - place_ref[1], packo_ref)):
        for ref, parts in zip((so_out, co_out, cq_out, cko_ref, cvo_ref), packed_parts(core), strict=True):
            for rows, where in parts:
                ref[rows, :] = pack[where]
    io.done(so_out, co_out, cq_out, cko_ref, cvo_ref)
    io.ready(mem_ref, ck_ref, cv_ref)

    def project(i, carry):
        rows = pl.ds(pl.multiple_of(i * 256, 256), 256)
        value = mem_ref[rows, :]
        for side, (wk, wv) in enumerate(((ck_ref, cv_ref), (cko_ref, cvo_ref))):
            lanes = slice(side * OWN, (side + 1) * OWN)
            keys = nn(value, wk[...])
            mk_ref[rows, lanes] = keys.astype(bf16)
            mkt_ref[lanes, rows] = jnp.transpose(keys).astype(bf16)
            values = nn(value, wv[...])
            mv_ref[rows, lanes] = values.astype(bf16)
            mvt_ref[lanes, rows] = jnp.transpose(values).astype(bf16)
        return carry

    lax.fori_loop(0, 4, project, 0)


SPANS = (1, 2, 3, 4, 6, 8)


def set_ranges(ends, mends, live, low_ref, high_ref):
    pos = token_positions()
    low_ref[...] = jnp.where(pos < live, lookup(pos, ends, mends, 0), BIG)
    high_ref[...] = lookup(pos, ends, mends[1:], mends[0])


def cross_blocks(half, ends, mends, live, block, dead):
    def step(i, carry):
        b = half * 4 + i
        pos = b * BLK
        alive = pos < live
        last = jnp.minimum(pos + BLK, live) - 1
        first = lax.shift_right_logical(lookup(pos, ends, mends, 0), 7)
        end = lax.shift_right_logical(lookup(last, ends, mends[1:], mends[0]) + BLK - 1, 7)
        n = end - first
        below = 0
        for m in SPANS:
            begin = jnp.minimum(first, LEN // BLK - m)
            pl.when(alive & (n > below) & (n <= m))(functools.partial(block, i, b, begin, m))
            below = m
        pl.when(jnp.logical_not(alive))(functools.partial(dead, i))
        return carry

    lax.fori_loop(0, 4, step, 0)


def cross_scores(i, n, lanes, kstart, q_ref, k_ref, low2, high2):
    keys = k_ref[pl.ds(kstart, n * BLK), lanes]
    queries = stacked(q_ref[pl.ds(pl.multiple_of(i * BLK, BLK), BLK), lanes])
    index = kstart + lax.broadcasted_iota(jnp.int32, (n * BLK, 2 * BLK), 0)
    allowed = (index >= low2) & (index < high2)
    return queries, keys, jnp.where(allowed, nt(keys, queries), MASKED)


def pairs(body):
    def step(g, carry):
        for k in range(2):
            p = 2 * g + k
            body(p, pl.ds(pl.multiple_of(p * BLK, BLK), BLK))
        return carry

    lax.fori_loop(0, 2, step, 0)


def third_kernel(
    io, t_ref, len_ref, mlen_ref, cnt_ref,
    x_ref, keep_ref, recv_ref, so_ref, soo_ref, gain2_ref, cq_ref, cqo_ref,
    mk_ref, mvt_ref, co_ref, coo_ref, gain3_ref,
    h1_ref, n2_ref, q_ref, mixed_ref, lse_ref, h2_ref, n3_ref, recv_out,
    low_ref, high_ref,
):
    t = t_ref[0]
    io.forward((recv_ref, recv_out))
    ends, mends = running_ends(len_ref), running_ends(mlen_ref)
    live = live_tokens(ends, cnt_ref[0])
    set_ranges(ends, mends, live, low_ref, high_ref)

    io.ready(x_ref, keep_ref, recv_ref, so_ref, soo_ref, gain2_ref, cq_ref, cqo_ref)

    def before(i, carry):
        rows = pl.ds(pl.multiple_of(i * 256, 256), 256)
        value = x_ref[rows, :].astype(f32)
        value = value + nn(keep_ref[rows, :], so_ref[...]) + nn(recv_ref[rows, :], soo_ref[...])
        h1_ref[rows, :] = value
        low = (value * rms_scale(value) * gain2_ref[...]).astype(bf16)
        n2_ref[rows, :] = low
        q_ref[rows, :OWN] = nn(low, cq_ref[...]).astype(bf16)
        q_ref[rows, OWN:] = nn(low, cqo_ref[...]).astype(bf16)
        return carry

    lax.fori_loop(0, 2, before, 0)
    io.done(h1_ref, n2_ref, q_ref)
    io.ready(mk_ref, mvt_ref)

    def block(i, b, first, n):
        kstart = pl.multiple_of(first * BLK, BLK)
        low2, high2 = twice(low_ref[pl.ds(b, 1), :]), twice(high_ref[pl.ds(b, 1), :])
        alive = (low2 < BIG).astype(f32)

        def pair(p, lanes):
            _, _, scores = cross_scores(i, n, lanes, kstart, q_ref, mk_ref, low2, high2)
            peak = jnp.max(scores, axis=0, keepdims=True)
            raised = jnp.exp(scores - peak)
            total = jnp.sum(raised, axis=0, keepdims=True)
            mixed = nn(mvt_ref[lanes, pl.ds(kstart, n * BLK)], raised.astype(bf16))
            mixed = mixed * (alive / total)
            mixed_ref[pl.ds(pl.multiple_of(i * BLK, BLK), BLK), lanes] = diagonal(mixed).astype(bf16)
            lse_ref[p, pl.ds(i, 1), :] = peak + jnp.log(total)

        pairs(pair)

    def dead(i):
        mixed_ref[pl.ds(pl.multiple_of(i * BLK, BLK), BLK), :] = jnp.zeros((BLK, WIDTH), bf16)
        for p in range(4):
            lse_ref[p, pl.ds(i, 1), :] = jnp.zeros((1, 2 * BLK), f32)

    cross_blocks(t, ends, mends, live, block, dead)

    io.done(mixed_ref, lse_ref)
    io.ready(co_ref, coo_ref, gain3_ref)

    def after(i, carry):
        rows = pl.ds(pl.multiple_of(i * 256, 256), 256)
        value = h1_ref[rows, :]
        value = value + nn(mixed_ref[rows, :OWN], co_ref[...]) + nn(mixed_ref[rows, OWN:], coo_ref[...])
        h2_ref[rows, :] = value
        n3_ref[rows, :] = (value * rms_scale(value) * gain3_ref[...]).astype(bf16)
        return carry

    lax.fori_loop(0, 2, after, 0)


def feed_kernel(
    io, place_ref, n3_ref, fi_ref, cot_ref, fo_ref,
    out_ref, gn_ref, act_ref, gp_ref,
):
    tile = 256
    n_tiles = fi_ref.shape[1] // tile
    root = math.sqrt(2 / math.pi)
    base = place_ref[0] * HALF
    io.ready(n3_ref, fi_ref, cot_ref, fo_ref)

    def hidden(j, carry):
        lanes = pl.ds(pl.multiple_of(j * tile, tile), tile)
        for i in range(2):
            rows = slice(i * 256, (i + 1) * 256)
            pre = nn(n3_ref[rows, :], fi_ref[:, lanes])
            square = pre * pre
            bent = jnp.tanh(pre * (root + (root * 0.044715) * square))
            gate = 0.5 + 0.5 * bent
            slope = gate + pre * (0.5 - 0.5 * bent * bent) * (root + (root * 0.134145) * square)
            act_ref[rows, lanes] = (pre * gate).astype(bf16)
            grads = nt(cot_ref[pl.ds(pl.multiple_of(base + i * 256, 256), 256), :], fo_ref[lanes, :])
            gp_ref[rows, lanes] = (grads * slope).astype(bf16)
        return carry

    lax.fori_loop(0, n_tiles, hidden, 0)
    io.done(act_ref, gp_ref)

    def outward(i, carry):
        rows = pl.ds(pl.multiple_of(i * 256, 256), 256)
        out_ref[rows, :] = nn(act_ref[rows, :], fo_ref[...]).astype(bf16)
        gn_ref[rows, :] = nt(gp_ref[rows, :], fi_ref[...]).astype(bf16)
        return carry

    lax.fori_loop(0, 2, outward, 0)


def feed_weights_kernel(
    io, t_ref, h2_ref, own_ref, oth_ref, n3_ref, gp_ref, n3o_ref, gpo_ref, act_ref, cot_ref, acto_ref,
    fi_ref, fo_ref, out_ref,
    n3t_ref,
):
    t = t_ref[0]
    mine = pl.ds(pl.multiple_of(t * HALF, HALF), HALF)
    theirs = pl.ds(pl.multiple_of((1 - t) * HALF, HALF), HALF)
    io.ready(n3_ref, gp_ref, n3o_ref, gpo_ref)
    n3t_ref[:, :HALF] = jnp.transpose(n3_ref[...].astype(f32)).astype(bf16)
    n3t_ref[:, HALF:] = jnp.transpose(n3o_ref[...].astype(f32)).astype(bf16)
    n_tiles = fi_ref.shape[1] // 256
    for j in range(n_tiles):
        lanes = slice(j * 256, (j + 1) * 256)
        grads = nn(n3t_ref[:, :HALF], gp_ref[:, lanes]) + nn(n3t_ref[:, HALF:], gpo_ref[:, lanes])
        fi_ref[:, lanes] = grads.astype(bf16)
    io.done(fi_ref)
    io.ready(act_ref, cot_ref, acto_ref)
    for j in range(n_tiles):
        lanes = slice(j * 256, (j + 1) * 256)
        grads = tn(act_ref[:, lanes], cot_ref[mine, :]) + tn(acto_ref[:, lanes], cot_ref[theirs, :])
        fo_ref[lanes, :] = grads.astype(bf16)
    io.done(fo_ref)
    io.ready(h2_ref, own_ref, oth_ref)
    out_ref[mine, :] = (h2_ref[...] + own_ref[...].astype(f32)).astype(bf16)
    out_ref[theirs, :] = oth_ref[...]


def cross_back_kernel(
    io, t_ref, len_ref, mlen_ref, cnt_ref,
    gn_ref, gnr_ref, h2_ref, gain3_ref, cot_ref, co_ref, coo_ref,
    q_ref, mk_ref, mkt_ref, mv_ref, lse_ref, cq_ref, cqo_ref, h1_ref, gain2_ref, so_ref, soo_ref,
    gb2_ref, dq_ref, dk_ref, dv_ref, gh1_ref, gb1_ref, gm1_ref, gm1o_ref, gains_ref,
    low_ref, high_ref, live_ref, gm_ref, dk_acc, dv_acc, gh2_ref,
):
    t = t_ref[0]
    ends, mends = running_ends(len_ref), running_ends(mlen_ref)
    live = live_tokens(ends, cnt_ref[0])
    set_ranges(ends, mends, live, low_ref, high_ref)
    alive_rows = t * HALF + lax.broadcasted_iota(jnp.int32, (HALF, BLK), 0)
    live_ref[...] = (alive_rows < live).astype(f32)
    dk_acc[...] = jnp.zeros_like(dk_acc)
    dv_acc[...] = jnp.zeros_like(dv_acc)
    gains_ref[...] = jnp.zeros_like(gains_ref)

    io.ready(gn_ref, gnr_ref, h2_ref, gain3_ref, cot_ref, co_ref, coo_ref)
    for i in range(2):
        rows = slice(i * 256, (i + 1) * 256)
        grad = gn_ref[rows, :].astype(f32) + gnr_ref[rows, :].astype(f32)
        back, gain = rms_back(h2_ref[rows, :], gain3_ref[...], grad)
        gains_ref[0:1, :] += gain
        grad = cot_ref[rows, :].astype(f32) + back
        gh2_ref[rows, :] = grad
        low = grad.astype(bf16)
        gb2_ref[rows, :] = low
        alive = live_ref[rows, 0:1]
        gm_ref[rows, :OWN] = (nt(low, co_ref[...]) * alive).astype(bf16)
        gm_ref[rows, OWN:] = (nt(low, coo_ref[...]) * alive).astype(bf16)
    io.done(gb2_ref)
    io.ready(q_ref, mk_ref, mkt_ref, mv_ref, lse_ref)

    def block(i, b, first, n):
        kstart = pl.multiple_of(first * BLK, BLK)
        low2, high2 = twice(low_ref[pl.ds(b, 1), :]), twice(high_ref[pl.ds(b, 1), :])
        rows = pl.ds(pl.multiple_of(i * BLK, BLK), BLK)
        span = pl.ds(kstart, n * BLK)

        def pair(p, lanes):
            queries, _, scores = cross_scores(i, n, lanes, kstart, q_ref, mk_ref, low2, high2)
            probs = jnp.exp(scores - lse_ref[p, pl.ds(i, 1), :])
            grads = stacked(gm_ref[rows, lanes])
            grad_probs = nt(mv_ref[span, lanes], grads)
            inner = jnp.sum(grad_probs * probs, axis=0, keepdims=True)
            low = (probs * (grad_probs - inner)).astype(bf16)
            dk_acc[span, lanes] += nn(low, queries)
            dv_acc[span, lanes] += nn(probs.astype(bf16), grads)
            dq_ref[rows, lanes] = diagonal(nn(mkt_ref[lanes, span], low)).astype(bf16)

        pairs(pair)

    def dead(i):
        dq_ref[pl.ds(pl.multiple_of(i * BLK, BLK), BLK), :] = jnp.zeros((BLK, WIDTH), bf16)

    cross_blocks(t, ends, mends, live, block, dead)

    dk_ref[...] = dk_acc[...].astype(bf16)
    dv_ref[...] = dv_acc[...].astype(bf16)
    io.done(dq_ref, dk_ref, dv_ref)
    io.ready(cq_ref, cqo_ref, h1_ref, gain2_ref, so_ref, soo_ref)
    for i in range(2):
        rows = slice(i * 256, (i + 1) * 256)
        grad = nt(dq_ref[rows, :OWN], cq_ref[...]) + nt(dq_ref[rows, OWN:], cqo_ref[...])
        back, gain = rms_back(h1_ref[rows, :], gain2_ref[...], grad)
        gains_ref[1:2, :] += gain
        grad = gh2_ref[rows, :] + back
        gh1_ref[rows, :] = grad
        low = grad.astype(bf16)
        gb1_ref[rows, :] = low
        alive = live_ref[rows, 0:1]
        gm1_ref[rows, :] = (nt(low, so_ref[...]) * alive).astype(bf16)
        gm1o_ref[rows, :] = (nt(low, soo_ref[...]) * alive).astype(bf16)


def cross_weights_kernel(
    io, place_ref, mem_ref, dk_ref, dv_ref, n2_ref, dq_ref, mixed_ref, gb2_ref, keep_ref, gb1_ref, recv_ref,
    ck_ref, cko_ref, cv_ref, cvo_ref,
    hold_ref, holdo_ref, send_ref, gmem_ref, gmems_ref,
    memt_ref, fold_ref,
):
    t, c = place_ref[0], place_ref[1]
    io.ready(mem_ref, dk_ref, dv_ref, n2_ref, dq_ref, mixed_ref, gb2_ref, keep_ref, gb1_ref, recv_ref)
    memt_ref[...] = jnp.transpose(mem_ref[...].astype(f32)).astype(bf16)
    n2t = jnp.transpose(n2_ref[...].astype(f32)).astype(bf16)
    for side in range(2):
        lanes = slice(side * OWN, (side + 1) * OWN)
        mixed1 = keep_ref if side == 0 else recv_ref
        fold_ref[0] = tn(mixed_ref[:, lanes], gb2_ref[...]).astype(bf16)
        fold_ref[1] = tn(mixed1[...], gb1_ref[...]).astype(bf16)
        fold(fold_ref, 2, nn(n2t, dq_ref[:, lanes]))
        fold(fold_ref, 3, nn(memt_ref[...], dk_ref[:, lanes]))
        fold(fold_ref, 4, nn(memt_ref[...], dv_ref[:, lanes]))
        deal(c, fold_ref, hold_ref if side == 0 else holdo_ref, send_ref, side * 640)
    io.done(hold_ref, holdo_ref, send_ref)
    io.ready(ck_ref, cko_ref, cv_ref, cvo_ref)
    for i in range(4):
        rows = slice(i * 256, (i + 1) * 256)
        grads = nt(dk_ref[rows, :OWN], ck_ref[...]) + nt(dk_ref[rows, OWN:], cko_ref[...])
        grads += nt(dv_ref[rows, :OWN], cv_ref[...]) + nt(dv_ref[rows, OWN:], cvo_ref[...])
        low = grads.astype(bf16)

        @pl.when(t == 0)
        def _():
            gmem_ref[rows, :] = low[:, :OWN]
            gmems_ref[rows, :] = low[:, OWN:]

        @pl.when(t != 0)
        def _():
            gmem_ref[rows, :] = low[:, OWN:]
            gmems_ref[rows, :] = low[:, :OWN]


def fold(fold_ref, k, weight):
    low = weight.astype(bf16)
    fold_ref[k, :, :OWN] = low[:256]
    fold_ref[k, :, OWN:] = low[256:]


def deal(c, fold_ref, hold_ref, send_ref, base):
    for k in range(fold_ref.shape[0]):
        rows = slice(k * BLK, (k + 1) * BLK)
        hold_ref[rows, :] = fold_ref[k, pl.ds(pl.multiple_of(c * BLK, BLK), BLK), :]
        rows = slice(base + k * BLK, base + (k + 1) * BLK)
        send_ref[rows, :] = fold_ref[k, pl.ds(pl.multiple_of((1 - c) * BLK, BLK), BLK), :]


def self_back_blocks(
    half, ends, live, start_ref, table_ref, g_ref, q_ref, k_ref, kt_ref, v_ref, bias_ref, lse_ref,
    dq_ref, dk_acc, dv_acc, near_acc, far_acc,
):
    def block(i, b, first, n):
        kstart = pl.multiple_of(first * BLK, BLK)
        start2 = twice(start_ref[pl.ds(b, 1), :])
        rows = pl.ds(pl.multiple_of(i * BLK, BLK), BLK)
        span = pl.ds(kstart, n * BLK)
        for p in range(2):
            lanes = slice(p * BLK, (p + 1) * BLK)
            queries, _, scores = self_scores(
                b, n, p, kstart, q_ref, k_ref, bias_ref, table_ref, start2
            )
            probs = jnp.exp(scores - lse_ref[p, pl.ds(i, 1), :])
            grads = stacked(g_ref[rows, lanes])
            grad_probs = nt(v_ref[span, lanes], grads)
            inner = jnp.sum(grad_probs * probs, axis=0, keepdims=True)
            grad_scores = probs * (grad_probs - inner)
            near_acc[p] += grad_scores[(n - 1) * BLK :]
            if n > 1:
                near_acc[2 + p] += grad_scores[(n - 2) * BLK : (n - 1) * BLK]
            if n > 2:
                far_acc[p : p + 1, :] += jnp.sum(grad_scores[: (n - 2) * BLK], axis=0, keepdims=True)
            low = grad_scores.astype(bf16)
            dk_acc[span, lanes] += nn(low, queries)
            dv_acc[span, lanes] += nn(probs.astype(bf16), grads)
            dq_ref[rows, lanes] = diagonal(nn(kt_ref[lanes, span], low)).astype(bf16)

    def step(i, carry):
        b = half * 4 + i
        alive, first, n = self_spans(b, ends, live)
        for m in range(1, 5):
            pl.when(alive & (n == m))(functools.partial(block, i, b, first, m))

        @pl.when(jnp.logical_not(alive))
        def _():
            dq_ref[pl.ds(pl.multiple_of(i * BLK, BLK), BLK), :] = jnp.zeros((BLK, OWN), bf16)

        return carry

    lax.fori_loop(0, 4, step, 0)


def self_back_own_kernel(
    io, place_ref, len_ref, cnt_ref, table_ref,
    gm_ref, q_ref, k_ref, kt_ref, v_ref, bias_ref, lse_ref,
    dq_ref, dk_acc, dv_acc, near_acc, far_acc,
    start_ref,
):
    ends = running_ends(len_ref)
    live = live_tokens(ends, cnt_ref[0])
    set_starts(ends, live, start_ref)
    for ref in (dk_acc, dv_acc, near_acc, far_acc):
        ref[...] = jnp.zeros_like(ref)
    io.ready(gm_ref, q_ref, k_ref, kt_ref, v_ref, bias_ref, lse_ref)
    self_back_blocks(
        place_ref[0], ends, live, start_ref, table_ref, gm_ref, q_ref, k_ref, kt_ref, v_ref, bias_ref, lse_ref,
        dq_ref, dk_acc, dv_acc, near_acc, far_acc,
    )


def self_back_kernel(
    io, place_ref, len_ref, cnt_ref, table_ref,
    gmr_ref, dqm_ref, dkm_ref, dvm_ref, nearm_ref, farm_ref, q_ref, k_ref, kt_ref, v_ref, bias_ref, lse_ref,
    n1_ref, x_ref, gh1_ref, gain1_ref, gains_ref, wq_ref, wk_ref, wv_ref,
    hold_ref, send_ref, gi_ref, small_ref,
    start_ref, dqo_ref, dq_ref, dk_acc, dv_acc, near_acc, far_acc, n1t_ref, fold_ref, sums_ref,
):
    t = place_ref[0]
    ends = running_ends(len_ref)
    live = live_tokens(ends, cnt_ref[0])
    set_starts(ends, live, start_ref)
    small_ref[...] = jnp.zeros_like(small_ref)
    for ref, so_far in ((dk_acc, dkm_ref), (dv_acc, dvm_ref), (near_acc, nearm_ref), (far_acc, farm_ref)):
        ref[...] = so_far[...]
    io.ready(q_ref, k_ref, kt_ref, v_ref, bias_ref, lse_ref)
    self_back_blocks(
        1 - t, ends, live, start_ref, table_ref, gmr_ref, q_ref, k_ref, kt_ref, v_ref, bias_ref, lse_ref,
        dqo_ref, dk_acc, dv_acc, near_acc, far_acc,
    )
    dq_ref[pl.ds(pl.multiple_of(t * HALF, HALF), HALF), :] = dqm_ref[...]
    dq_ref[pl.ds(pl.multiple_of((1 - t) * HALF, HALF), HALF), :] = dqo_ref[...]

    io.ready(n1_ref)
    n1t_ref[...] = jnp.transpose(n1_ref[...].astype(f32)).astype(bf16)
    low_k, low_v = dk_acc[...].astype(bf16), dv_acc[...].astype(bf16)
    for k, grads in enumerate((dq_ref[...], low_k, low_v)):
        fold(fold_ref, k, nn(n1t_ref[...], grads))
    deal(place_ref[1], fold_ref, hold_ref, send_ref, 0)
    io.done(hold_ref, send_ref)
    io.ready(x_ref, gh1_ref, gain1_ref, gains_ref, wq_ref, wk_ref, wv_ref)
    gain1 = jnp.zeros((1, WIDTH), f32)
    for i in range(4):
        rows = slice(i * 256, (i + 1) * 256)
        grads = nt(dq_ref[rows, :], wq_ref[...]) + nt(low_k[rows], wk_ref[...]) + nt(low_v[rows], wv_ref[...])
        back, gain = rms_back(x_ref[rows, :].astype(f32), gain1_ref[...], grads)
        gain1 += gain
        mine = (t == i // 2).astype(f32)
        back += mine * gh1_ref[(i % 2) * 256 : (i % 2 + 1) * 256, :]
        gi_ref[rows, :] = back.astype(bf16)
    io.done(gi_ref)
    key = lax.broadcasted_iota(jnp.int32, (BLK, BLK), 0)
    query = lax.broadcasted_iota(jnp.int32, (BLK, BLK), 1)
    gaps = [query - key, BLK + query - key]
    for level in range(NB):
        for p in range(2):
            row = jnp.zeros((1, 2 * BLK), f32)
            for d in range(2):
                inside = gaps[d] >= THRESHOLDS[level]
                if level + 1 < NB:
                    inside &= gaps[d] < THRESHOLDS[level + 1]
                picked = jnp.where(twice(inside.astype(f32)) > 0, near_acc[2 * d + p], 0.0)
                row += jnp.sum(picked, axis=0, keepdims=True)
            if level == NB - 1:
                row += far_acc[p : p + 1, :]
            sums_ref[level : level + 1, p * 256 : (p + 1) * 256] = row
    lane = lax.broadcasted_iota(jnp.int32, (NB, BLK), 1)
    table = jnp.zeros((NB, BLK), f32)
    for h in range(4):
        total = jnp.sum(sums_ref[:, h * BLK : (h + 1) * BLK], axis=1, keepdims=True)
        table = jnp.where(lane == h, total, table)
    small_ref[16:48, :] = table

    for k, gain in enumerate((gain1, gains_ref[1:2, :], gains_ref[0:1, :])):
        for j in range(4):
            small_ref[4 * k + j : 4 * k + j + 1, :] = gain[:, j * BLK : (j + 1) * BLK]


def join_kernel(io, place_ref, own_ref, got_ref, recv_ref, mine_ref, theirs_ref, hold_ref, send_ref):
    x = place_ref[2]
    io.ready(own_ref, got_ref, recv_ref, mine_ref, theirs_ref)
    for k in range(8):
        if k < 5:
            rows = slice(k * BLK, (k + 1) * BLK)
            total = own_ref[rows, :].astype(f32) + got_ref[rows, :].astype(f32) + recv_ref[rows, :].astype(f32)
        else:
            rows = slice((k - 5) * BLK, (k - 4) * BLK)
            total = mine_ref[rows, :].astype(f32) + theirs_ref[rows, :].astype(f32)
        low = total.astype(bf16)
        rows = slice((k % 4) * BLK, (k % 4 + 1) * BLK)

        @pl.when(x == k // 4)
        def _():
            hold_ref[rows, :] = low

        @pl.when(x != k // 4)
        def _():
            send_ref[rows, :] = low


def pieces_kernel(io, _, in_ref, out_ref):
    io.ready(in_ref)
    total = in_ref[0].astype(f32)
    for k in range(1, in_ref.shape[0]):
        total += in_ref[k].astype(f32)
    total = total.astype(bf16)
    for k in range(in_ref.shape[0]):
        out_ref[k] = total


def unfold_kernel(
    io, place_ref, own_ref, pair_ref, core_ref, both_ref,
    co_ref, so_ref, cq_ref, ck_ref, cv_ref, wq_ref, wk_ref, wv_ref,
):
    c, x = place_ref[1], place_ref[2]
    outs = (co_ref, so_ref, cq_ref, ck_ref, cv_ref, wq_ref, wk_ref, wv_ref)

    def spread(ref, core, bit):
        low = pl.ds(pl.multiple_of(core * BLK, BLK), BLK)
        high = pl.ds(pl.multiple_of(256 + core * BLK, BLK), BLK)
        for k, out in enumerate(outs):
            rows = slice((k % 4) * BLK, (k % 4 + 1) * BLK)

            @pl.when(bit == k // 4)
            def _():
                if k < 2:
                    out[low, :] = ref[rows, :].astype(f32)
                else:
                    out[low, :] = ref[rows, :OWN].astype(f32)
                    out[high, :] = ref[rows, OWN:].astype(f32)

    for ref, core, bit in ((own_ref, c, x), (pair_ref, c, 1 - x), (core_ref, 1 - c, x), (both_ref, 1 - c, 1 - x)):
        io.ready(ref)
        spread(ref, core, bit)


def swap(value, axis="tensor"):
    return lax.ppermute(value, axis, [(0, 1), (1, 0)])


def shards(
    inputs, memory, cotangent, dec_lengths, mem_lengths, counts,
    self_gain, self_query, self_key, self_value, self_out, rel_table,
    cross_gain, cross_query, cross_key, cross_value, cross_out,
    feed_gain, feed_in, feed_out,
):
    v = pltpu.VMEM
    i32 = jnp.int32
    t, c, x = (lax.axis_index(name).astype(i32) for name in ("tensor", "core", "pair"))
    ring = lax.axis_size("ring")
    place = jnp.stack([t, c, x])
    place_oth = jnp.stack([1 - t, c, x])
    gain1, gain2, gain3 = (g.reshape(1, WIDTH) for g in (self_gain, cross_gain, feed_gain))
    table = rel_table.T

    pack = swap(pack_weights(place, self_out, cross_out, cross_query, cross_key, cross_value))

    tok = (LEN, WIDTH)
    half = (HALF, WIDTH)
    heads, heads_t, part = (LEN, OWN), (OWN, LEN), (HALF, OWN)
    row_tile = v((LEN // BLK, BLK), i32)
    n1, q, q_far, k, k_far, val, vt, kt, bias, bias_far, send1, lse1_oth = call(
        first_kernel,
        [(tok, bf16, "far"), (heads, bf16, "both"), (heads, bf16, "both"), (heads, bf16, "far"),
         (heads_t, bf16, "near"), (heads_t, bf16, "far"), ((4, BLK, 2 * BLK), f32, "both"), (part, bf16, "near"),
         ((2, 4, 2 * BLK), f32, "far")],
        [row_tile],
        (place, dec_lengths, counts, table, inputs, gain1, self_query, self_key, self_value),
        smem=4, us=6,
    )
    pack, send1 = lax.optimization_barrier((pack, send1))
    pack_core = swap(pack, "core")
    mixed1_recv = swap(send1)
    mixed1_keep, keep_far, lse1 = call(
        second_kernel,
        [(part, bf16, "both"), ((2, 4, 2 * BLK), f32, "far")],
        [row_tile],
        (place, dec_lengths, counts, table, Near(q), Near(k), Near(vt), Near(bias)),
        smem=4, us=SHORT,
    )
    narrow, wide = (OWN, WIDTH), (WIDTH, OWN)
    mk, mk_far, mv, mkt, mvt, so_near, so_oth, co_near, co_oth, cq_near, cq_oth, ck_oth, cv_oth = call(
        memory_kernel,
        [(tok, bf16, "both"), (tok, bf16, "far"), ((WIDTH, LEN), bf16, "far"), ((WIDTH, LEN), bf16, "near"),
         (narrow, bf16, "both"), (narrow, bf16, "both"), (wide, bf16, "both"), (wide, bf16, "far"), (wide, bf16, "far")],
        [],
        (place, memory, cross_key, cross_value, Near(pack), Near(pack_core)),
        us=SHORT,
    )
    h1, n2, cq, mixed2, lse2, h2, n3, n3_far, recv_far = call(
        third_kernel,
        [(half, f32, "far"), (half, bf16, "far"), (half, bf16, "far"), (half, bf16, "far"),
         ((4, 4, 2 * BLK), f32, "far"), (half, f32, "far"), (half, bf16, "both"), (part, bf16, "far")],
        [row_tile, row_tile],
        (place, dec_lengths, mem_lengths, counts, Half(inputs), Near(mixed1_keep), Near(mixed1_recv), self_out,
         Near(so_near), gain2, cross_query, Near(cq_near), Near(mk), Near(mvt), cross_out, Near(co_near), gain3),
        smem=4, us=9,
    )
    n3_recv = swap(n3)

    hidden = feed_in.shape[1]
    units = (HALF, hidden)
    out_own, gn3_own, act, gp = call(
        feed_kernel,
        [(half, bf16, "far"), (half, bf16, "far"), (units, bf16, "far"), (units, bf16, "far")],
        [],
        (place, Near(n3), Near(feed_in), Near(cotangent), Near(feed_out)),
        us=5,
    )
    n3_recv, act = lax.optimization_barrier((n3_recv, act))
    out_oth, gn3_oth, act_oth, gp_oth = call(
        feed_kernel,
        [(half, bf16, "near"), (half, bf16, "near"), (units, bf16, "near"), (units, bf16, "near")],
        [],
        (place_oth, Near(n3_recv), Near(feed_in), Near(cotangent), Near(feed_out)),
        us=5,
    )
    gn3_recv = swap(gn3_oth)
    feed_in_grad, feed_out_grad, out_part = call(
        feed_weights_kernel,
        [((WIDTH, hidden), bf16, "far"), ((hidden, WIDTH), bf16, "far"), (tok, bf16, "far")],
        [v((WIDTH, LEN), bf16)],
        (place, h2, out_own, Near(out_oth), n3_far, gp, Near(n3_recv), Near(gp_oth), act, cotangent, Near(act_oth)),
        us=5,
    )
    gn3_recv, out_part, feed_in_grad, feed_out_grad = lax.optimization_barrier(
        (gn3_recv, out_part, feed_in_grad, feed_out_grad)
    )
    dp = ("ring", "pair", "core")
    feed_in_grad, feed_out_grad = lax.psum((feed_in_grad, feed_out_grad), dp)

    def later():
        gb2, dcq, dmk, dmv, gh1, gb1, gm1, gm1_oth, gains = call(
            cross_back_kernel,
            [(half, bf16, "near"), (half, bf16, "near"), (tok, bf16, "near"), (tok, bf16, "near"), (half, f32, "far"),
             (half, bf16, "near"), (part, bf16, "near"), (part, bf16, "near"), ((8, WIDTH), f32, "far")],
            [row_tile, row_tile, v((HALF, BLK), f32), v(half, bf16), v(tok, f32), v(tok, f32), v(half, f32)],
            (place, dec_lengths, mem_lengths, counts, gn3_own, Near(gn3_recv), h2, gain3, Half(cotangent),
             cross_out, co_oth, cq, mk_far, mkt, mv, lse2, cross_query, cq_oth, h1, gain2, self_out, so_oth),
            smem=4, us=SHORT,
        )
        gm1_recv = swap(gm1_oth)
        cross_hold, cross_hold_oth, cross_send, gmem, gmem_send = call(
            cross_weights_kernel,
            [((640, WIDTH), bf16, "near"), ((640, WIDTH), bf16, "near"), ((1280, WIDTH), bf16, "near"),
             (heads, bf16, "far"), (heads, bf16, "far")],
            [v((WIDTH, LEN), bf16), v((5, 256, WIDTH), bf16)],
            (place, memory, Near(dmk), Near(dmv), n2, Near(dcq), mixed2, Near(gb2), keep_far, Near(gb1), recv_far,
             cross_key, ck_oth, cross_value, cv_oth),
            us=3,
        )
        cross_got = swap(cross_send, "core")
        acc, tiles = ((LEN, OWN), f32), ((4, BLK, 2 * BLK), f32)
        dq1, dk1, dv1, near1, far1 = call(
            self_back_own_kernel,
            [(part, bf16, "near"), (*acc, "near"), (*acc, "near"), (*tiles, "near"), ((8, 2 * BLK), f32, "near")],
            [row_tile],
            (place, dec_lengths, counts, table, Near(gm1), q_far, k_far, kt, val, bias_far, lse1),
            smem=4, us=3,
        )
        cross_recv = swap((cross_hold_oth.astype(f32) + cross_got[640:].astype(f32)).astype(bf16))
        self_hold, self_send, gi_part, small = call(
            self_back_kernel,
            [((384, WIDTH), bf16, "near"), ((384, WIDTH), bf16, "near"), (tok, bf16, "far"), ((48, BLK), f32, "near")],
            [row_tile, v(part, bf16), v(heads, bf16), v(*acc), v(*acc), v(*tiles), v((8, 2 * BLK), f32),
             v((WIDTH, LEN), bf16), v((3, 256, WIDTH), bf16), v((NB, WIDTH), f32)],
            (place, dec_lengths, counts, table, Near(gm1_recv), Near(dq1), Near(dk1), Near(dv1), Near(near1), Near(far1),
             q_far, k_far, kt, val, bias_far, lse1_oth, n1, inputs, gh1, gain1, gains, self_query, self_key, self_value),
            smem=4, us=3,
        )
        self_got = swap(self_send, "core")
        gi_recv = swap(gi_part)

        hold, send = call(
            join_kernel,
            [(half, bf16, "near"), (half, bf16, "near")],
            [],
            (place, *map(Near, (cross_hold, cross_got, cross_recv, self_hold, self_got))),
            us=2,
        )
        small, hold = lax.optimization_barrier((small, hold))
        small = jnp.broadcast_to(small[None], (4 * ring, 48, BLK))
        small = jnp.sum(lax.all_to_all(small, dp, 0, 0), axis=0)
        gmem_recv = swap(gmem_send)
        summed = (hold.astype(f32) + swap(send, "pair").astype(f32)).astype(bf16)
        summed, small, gmem_recv, out_late = lax.optimization_barrier((summed, small, gmem_recv, out_part))
        out_recv = swap(out_late)
        pieces = (ring, HALF // ring, WIDTH)
        taken = lax.all_to_all(summed.reshape(pieces), "ring", 0, 0)
        (summed,) = call(pieces_kernel, [(pieces, bf16, "near")], [], (place, Near(taken)), us=SHORT)
        summed, gi_recv = lax.optimization_barrier((summed, gi_recv))
        own = lax.all_to_all(summed, "ring", 0, 0).reshape(half)
        return own, small, gi_part, gi_recv, out_recv, gmem, gmem_recv

    def last(own, small, gi_part, gi_recv, out_recv, gmem, gmem_recv, feed_in_grad, feed_out_grad):
        def both(part, other):
            return (part.astype(f32) + other.astype(f32)).astype(bf16)

        pair, core_own = swap(own, "pair"), swap(own, "core")
        gain_grads = small + swap(small)
        ready = (
            both(out_part, out_recv), both(gi_part, gi_recv), both(gmem, gmem_recv),
            *(gain_grads[4 * k : 4 * k + 4].reshape(WIDTH) for k in range(3)), small[16:, :4],
            feed_in_grad.astype(f32), feed_out_grad.astype(f32),
        )
        pair, *ready = lax.optimization_barrier((pair, *ready))
        narrows, wides = (narrow, f32, "far"), (wide, f32, "far")
        grads = call(
            unfold_kernel,
            [narrows] * 2 + [wides] * 6,
            [],
            (place, *map(Near, (own, pair, core_own, swap(pair, "core")))),
        )
        return *ready, *grads

    def always(branch, *operands):
        def never(*operands):
            shapes = jax.eval_shape(branch, *operands)
            return tuple(jnp.zeros(shape.shape, shape.dtype) for shape in shapes)

        return lax.cond(counts[0] > 0, branch, never, *operands)

    results = always(later)
    output, grad_inputs, grad_memory, *gain_grads, table_grad, feed_in_grad, feed_out_grad = (
        results := always(last, *results, feed_in_grad, feed_out_grad)
    )[:9]
    co_grad, so_grad, cq_grad, ck_grad, cv_grad, wq_grad, wk_grad, wv_grad = results[9:]
    return (
        output,
        grad_inputs,
        grad_memory,
        gain_grads[0],
        wq_grad,
        wk_grad,
        wv_grad,
        so_grad,
        table_grad,
        gain_grads[1],
        cq_grad,
        ck_grad,
        cv_grad,
        co_grad,
        gain_grads[2],
        feed_in_grad,
        feed_out_grad,
    )


def solution(mesh):
    devices = mesh.devices
    rows, tensor = devices.shape
    mesh = Mesh(devices.reshape(rows // 4, 2, 2, tensor), ("ring", "pair", "core", "tensor"))
    dp = ("ring", "pair", "core")
    split = P(dp, None)
    columns, rows = P(None, "tensor"), P("tensor", None)
    return jax.shard_map(
        shards,
        mesh=mesh,
        in_specs=(
            split, split, split, split, split, P(dp),
            P(), columns, columns, columns, rows, columns,
            P(), columns, columns, columns, rows,
            P(), columns, rows,
        ),
        out_specs=(
            split, split, P(dp, "tensor"),
            P(), columns, columns, columns, rows, columns,
            P(), columns, columns, columns, rows,
            P(), columns, rows,
        ),
        check_vma=False,
    )
```

```python
import functools
import math

import jax
import jax.numpy as jnp
from jax import lax
from jax.experimental import pallas as pl
from jax.experimental.pallas import tpu as pltpu
from jax.sharding import Mesh
from jax.sharding import PartitionSpec as P

NB = 32
MAXDIST = 128
SEGS = 16
LEN = 1024
HALF = 512
WIDTH = 512
OWN = 256
BLK = 128
BIG = 1 << 30
MASKED = -1e30
EPS = 1e-06
f32 = jnp.float32
bf16 = jnp.bfloat16
ROOM = 11 * 1024 * 1024
SHORT = 0.05


def thresholds():
    exact = NB // 2
    edges = [
        math.ceil(exact * (MAXDIST / exact) ** (level / (NB - exact)))
        for level in range(1, NB - exact)
    ]
    return list(range(exact + 1)) + edges


THRESHOLDS = thresholds()


def nn(a, b):
    return jnp.dot(a, b, preferred_element_type=f32)


def nt(a, b):
    return lax.dot_general(a, b, (((1,), (1,)), ((), ())), preferred_element_type=f32)


def tn(a, b):
    return lax.dot_general(a, b, (((0,), (0,)), ((), ())), preferred_element_type=f32)


class Half:
    def __init__(self, array):
        self.array = array


class Near:
    def __init__(self, array):
        self.array = array


class Raw:
    def __init__(self, array):
        self.array = array


PACKED = 640


def packed_parts(core):
    def at(start, size):
        return pl.ds(pl.multiple_of(start, BLK), size)

    left, right, all_lanes = slice(0, OWN), slice(OWN, WIDTH), slice(0, WIDTH)
    return (
        [(at(core * BLK, BLK), (slice(0, 128), all_lanes))],
        [(at(core * BLK, BLK), (slice(128, 256), all_lanes))],
        [(at(core * 256, 256), (slice(256, 512), left))],
        [(at(core * 256, 256), (slice(256, 512), right))],
        [(at(core * 256, BLK), (slice(512, 640), left)), (at(core * 256 + BLK, BLK), (slice(512, 640), right))],
    )


def pack_kernel(io, place_ref, *refs):
    *weights, pack_ref, sems = refs
    copies = []
    for ref, parts in zip(weights, packed_parts(place_ref[1]), strict=True):
        for rows, where in parts:
            copy = pltpu.make_async_copy(ref.at[rows, :], pack_ref.at[where], sems.at[len(copies)])
            copy.start()
            copies.append(copy)
    for copy in copies:
        copy.wait()


class Copies:
    def __init__(self, sems):
        self.sems, self.used, self.waits, self.out = sems, 0, {}, {}

    def start(self, source, target):
        copy = pltpu.make_async_copy(source, target, self.sems.at[self.used])
        self.used += 1
        copy.start()
        return copy

    def ready(self, *refs):
        for ref in refs:
            for copy in self.waits.pop(id(ref), ()):
                copy.wait()

    def done(self, *refs):
        for ref in refs:
            target, copy = self.out.get(id(ref), (None, True))
            if copy is None:
                self.out[id(ref)] = (target, self.start(ref, target))


def size_of(shape, dtype):
    return math.prod(shape) * jnp.dtype(dtype).itemsize


def call(body, outs, scratch, args, smem=1, us=3, fetch=(), forward=()):
    tables, operands = args[:smem], args[smem:]
    arrays, in_specs, fetched = [], [], []
    hbm, vmem = pl.BlockSpec(memory_space=pltpu.HBM), pl.BlockSpec(memory_space=pltpu.VMEM)

    def shape_of(operand):
        if isinstance(operand, Half):
            return (HALF, *operand.array.shape[1:]), operand.array.dtype
        return operand.shape, operand.dtype

    for operand in (*operands, *fetch, *map(Near, forward)):
        array = operand.array if isinstance(operand, (Near, Raw, Half)) else operand
        near = isinstance(operand, Near)
        arrays.append(array if near else pltpu.with_memory_space_constraint(array, pltpu.HBM))
        in_specs.append(vmem if near else hbm)
    fetched = [shape_of(o) for o in operands if not isinstance(o, (Near, Raw))]
    out_shapes, out_specs, sent = [], [], []
    extra = [(*shape_of(o), "near") for o in fetch] + [(o.shape, o.dtype, "far") for o in forward]
    for k, (shape, dtype, kind) in enumerate([*outs, *extra]):
        if kind != "far":
            out_shapes.append(jax.ShapeDtypeStruct(shape, dtype))
            out_specs.append(vmem)
        if kind != "near":
            out_shapes.append(pltpu.HBM(shape, dtype))
            out_specs.append(hbm)
        if kind == "far" and k < len(outs):
            sent.append((shape, dtype))
    n_copies = len(fetched) + sum(kind != "near" for _, _, kind in outs) + len(extra)

    def kernel(*refs):
        refs = list(refs)

        def take(n):
            taken = refs[:n]
            del refs[:n]
            return taken

        scalars, sources = take(smem), take(len(operands))
        extra_sources = take(len(extra))
        targets = take(len(out_shapes) - len(extra))
        extra_targets = take(len(extra))
        inner, outer = take(len(fetched)), take(len(sent))
        io = Copies(take(1)[0] if n_copies else None)
        inputs, outputs = [], []

        def source_of(operand, source):
            if isinstance(operand, Half):
                return source.at[pl.ds(pl.multiple_of(scalars[0][0] * HALF, HALF), HALF), :]
            return source

        for operand, source in zip(operands, sources, strict=True):
            if isinstance(operand, (Near, Raw)):
                inputs.append(source)
                continue
            ref = inner.pop(0)
            inputs.append(ref)
            io.waits[id(ref)] = [io.start(source_of(operand, source), ref)]
        moved = [
            io.start(source_of(operand, source), target)
            for operand, source, target in zip((*fetch, *forward), extra_sources, extra_targets, strict=True)
        ]
        for _, _, kind in outs:
            ref = outer.pop(0) if kind == "far" else targets.pop(0)
            outputs.append(ref)
            if kind != "near":
                io.out[id(ref)] = (targets.pop(0), None)
        body(io, *scalars, *inputs, *outputs, *refs)
        io.ready(*inputs)
        io.done(*outputs)
        for copy in (*(copy for _, copy in io.out.values()), *moved):
            copy.wait()

    own = [pltpu.VMEM(s, d) for s, d in fetched + sent]
    used = sum(size_of(s, d) for s, d in fetched + sent) + sum(
        size_of(s.shape, s.dtype) for s in scratch if s.memory_space == pltpu.VMEM
    )
    return pl.pallas_call(
        kernel,
        out_shape=tuple(out_shapes),
        in_specs=[pl.BlockSpec(memory_space=pltpu.SMEM)] * smem + in_specs,
        out_specs=tuple(out_specs),
        scratch_shapes=[*own, *([pltpu.SemaphoreType.DMA((n_copies,))] if n_copies else []), *scratch],
        compiler_params=pltpu.CompilerParams(vmem_limit_bytes=used + ROOM),
        cost_estimate=pl.CostEstimate(flops=int(us * 3.3e9), bytes_accessed=int(us * 1e7), transcendentals=0),
    )(*tables, *arrays)


def running_ends(len_ref):
    ends, total = [], 0
    for k in range(SEGS):
        total = total + len_ref[0, k]
        ends.append(total)
    return ends


def live_tokens(ends, count):
    total = 0
    for k in range(SEGS):
        total = jnp.where(k < count, ends[k], total)
    return total


def lookup(pos, ends, values, first):
    found = first
    for k in range(SEGS - 1):
        found = jnp.where(pos >= ends[k], values[k], found)
    return found


def token_positions():
    shape = (LEN // BLK, BLK)
    return lax.broadcasted_iota(jnp.int32, shape, 0) * BLK + lax.broadcasted_iota(
        jnp.int32, shape, 1
    )


def twice(row):
    return jnp.concatenate([row, row], axis=1)


def stacked(pair):
    lane = lax.broadcasted_iota(jnp.int32, pair.shape, 1)
    zero = jnp.zeros_like(pair)
    return jnp.concatenate(
        [jnp.where(lane < 64, pair, zero), jnp.where(lane < 64, zero, pair)], axis=0
    )


def diagonal(product):
    both = jnp.concatenate([product[:64, :BLK], product[64:, BLK:]], axis=0)
    return jnp.transpose(both)


def rms_scale(value):
    return lax.rsqrt(jnp.mean(value * value, axis=-1, keepdims=True) + EPS)


def rms_back(value, gain, grad):
    scale = rms_scale(value)
    weighted = grad * gain
    inner = jnp.mean(weighted * value, axis=-1, keepdims=True)
    unit = value * scale
    return (
        scale * weighted - unit * (scale * scale * inner),
        jnp.sum(grad * unit, axis=0, keepdims=True),
    )


def fill_bias(table_ref, bias_ref):
    key = lax.broadcasted_iota(jnp.int32, (BLK, BLK), 0)
    query = lax.broadcasted_iota(jnp.int32, (BLK, BLK), 1)
    for d in range(2):
        gap = d * BLK + query - key
        tiles = [jnp.full((BLK, BLK), table_ref[h, 0], f32) for h in range(4)]
        for level in range(1, NB):
            reached = gap >= THRESHOLDS[level]
            tiles = [jnp.where(reached, table_ref[h, level], tiles[h]) for h in range(4)]
        if d == 0:
            tiles = [jnp.where(gap >= 0, tile, MASKED) for tile in tiles]
        for h in range(4):
            bias_ref[d * 2 + h // 2, :, (h % 2) * BLK : (h % 2 + 1) * BLK] = tiles[h]


def far_bias(table_ref, p):
    lane = lax.broadcasted_iota(jnp.int32, (1, 2 * BLK), 1)
    return jnp.where(lane < BLK, table_ref[2 * p, NB - 1], table_ref[2 * p + 1, NB - 1])


def self_scores(b, n, p, kstart, q_ref, k_ref, bias_ref, table_ref, start2):
    lanes = slice(p * BLK, (p + 1) * BLK)
    keys = k_ref[pl.ds(kstart, n * BLK), lanes]
    queries = stacked(q_ref[pl.ds(pl.multiple_of(b * BLK, BLK), BLK), lanes])
    scores = nt(keys, queries)
    parts = []
    for j in range(n):
        part = scores[j * BLK : (j + 1) * BLK]
        d = n - 1 - j
        parts.append(part + (bias_ref[2 * d + p] if d < 2 else far_bias(table_ref, p)))
    scores = jnp.concatenate(parts, axis=0) if n > 1 else parts[0]
    index = kstart + lax.broadcasted_iota(jnp.int32, (n * BLK, 2 * BLK), 0)
    return queries, keys, jnp.where(index >= start2, scores, MASKED)


def self_spans(b, ends, live):
    pos = b * BLK
    first = lax.shift_right_logical(lookup(pos, ends, ends, 0), 7)
    return pos < live, first, b - first + 1


def self_forward(half, ends, live, q_ref, k_ref, vt_ref, bias_ref, table_ref, start_ref, o_ref, lse_ref):
    def block(i, b, first, n):
        kstart = pl.multiple_of(first * BLK, BLK)
        start2 = twice(start_ref[pl.ds(b, 1), :])
        alive = (start2 < BIG).astype(f32)
        for p in range(2):
            _, _, scores = self_scores(
                b, n, p, kstart, q_ref, k_ref, bias_ref, table_ref, start2
            )
            peak = jnp.max(scores, axis=0, keepdims=True)
            raised = jnp.exp(scores - peak)
            total = jnp.sum(raised, axis=0, keepdims=True)
            mixed = nn(vt_ref[p * BLK : (p + 1) * BLK, pl.ds(kstart, n * BLK)], raised.astype(bf16))
            mixed = mixed * (alive / total)
            o_ref[pl.ds(pl.multiple_of(i * BLK, BLK), BLK), p * BLK : (p + 1) * BLK] = diagonal(
                mixed
            ).astype(bf16)
            lse_ref[p, pl.ds(i, 1), :] = peak + jnp.log(total)

    def step(i, carry):
        b = half * 4 + i
        alive, first, n = self_spans(b, ends, live)
        for m in range(1, 5):
            pl.when(alive & (n == m))(functools.partial(block, i, b, first, m))

        @pl.when(jnp.logical_not(alive))
        def _():
            o_ref[pl.ds(pl.multiple_of(i * BLK, BLK), BLK), :] = jnp.zeros((BLK, OWN), bf16)
            for p in range(2):
                lse_ref[p, pl.ds(i, 1), :] = jnp.zeros((1, 2 * BLK), f32)

        return carry

    lax.fori_loop(0, 4, step, 0)


def set_starts(ends, live, start_ref):
    pos = token_positions()
    start_ref[...] = jnp.where(pos < live, lookup(pos, ends, ends, 0), BIG)


def first_kernel(
    io, t_ref, len_ref, cnt_ref, table_ref,
    x_ref, gain_ref, wq_ref, wk_ref, wv_ref,
    n1_ref, q_ref, k_ref, v_ref, vt_ref, kt_ref, bias_ref, o_ref, lse_ref,
    start_ref,
):
    ends = running_ends(len_ref)
    live = live_tokens(ends, cnt_ref[0])
    set_starts(ends, live, start_ref)
    fill_bias(table_ref, bias_ref)
    io.done(bias_ref)
    io.ready(x_ref, gain_ref, wq_ref, wk_ref, wv_ref)

    def project(i, carry):
        rows = pl.ds(pl.multiple_of(i * 256, 256), 256)
        value = x_ref[rows, :].astype(f32)
        low = (value * rms_scale(value) * gain_ref[...]).astype(bf16)
        n1_ref[rows, :] = low
        q_ref[rows, :] = nn(low, wq_ref[...]).astype(bf16)
        keys = nn(low, wk_ref[...])
        k_ref[rows, :] = keys.astype(bf16)
        kt_ref[:, rows] = jnp.transpose(keys).astype(bf16)
        values = nn(low, wv_ref[...])
        v_ref[rows, :] = values.astype(bf16)
        vt_ref[:, rows] = jnp.transpose(values).astype(bf16)
        return carry

    lax.fori_loop(0, 4, project, 0)
    io.done(n1_ref, q_ref, k_ref, v_ref, vt_ref, kt_ref)
    self_forward(
        1 - t_ref[0], ends, live, q_ref, k_ref, vt_ref, bias_ref, table_ref, start_ref, o_ref, lse_ref
    )


def second_kernel(
    io, t_ref, len_ref, cnt_ref, table_ref,
    q_ref, k_ref, vt_ref, bias_ref,
    o_ref, lse_ref,
    start_ref,
):
    ends = running_ends(len_ref)
    live = live_tokens(ends, cnt_ref[0])
    set_starts(ends, live, start_ref)
    io.ready(q_ref, k_ref, vt_ref, bias_ref)
    self_forward(
        t_ref[0], ends, live, q_ref, k_ref, vt_ref, bias_ref, table_ref, start_ref, o_ref, lse_ref
    )


def memory_kernel(
    io, place_ref, mem_ref, ck_ref, cv_ref, pack_ref, packo_ref,
    mk_ref, mv_ref, mkt_ref, mvt_ref, so_out, co_out, cq_out, cko_ref, cvo_ref,
):
    for core, pack in ((place_ref[1], pack_ref), (1 - place_ref[1], packo_ref)):
        for ref, parts in zip((so_out, co_out, cq_out, cko_ref, cvo_ref), packed_parts(core), strict=True):
            for rows, where in parts:
                ref[rows, :] = pack[where]
    io.done(so_out, co_out, cq_out, cko_ref, cvo_ref)
    io.ready(mem_ref, ck_ref, cv_ref)

    def project(i, carry):
        rows = pl.ds(pl.multiple_of(i * 256, 256), 256)
        value = mem_ref[rows, :]
        for side, (wk, wv) in enumerate(((ck_ref, cv_ref), (cko_ref, cvo_ref))):
            lanes = slice(side * OWN, (side + 1) * OWN)
            keys = nn(value, wk[...])
            mk_ref[rows, lanes] = keys.astype(bf16)
            mkt_ref[lanes, rows] = jnp.transpose(keys).astype(bf16)
            values = nn(value, wv[...])
            mv_ref[rows, lanes] = values.astype(bf16)
            mvt_ref[lanes, rows] = jnp.transpose(values).astype(bf16)
        return carry

    lax.fori_loop(0, 4, project, 0)


SPANS = (1, 2, 3, 4, 6, 8)


def set_ranges(ends, mends, live, low_ref, high_ref):
    pos = token_positions()
    low_ref[...] = jnp.where(pos < live, lookup(pos, ends, mends, 0), BIG)
    high_ref[...] = lookup(pos, ends, mends[1:], mends[0])


def cross_blocks(half, ends, mends, live, block, dead):
    def step(i, carry):
        b = half * 4 + i
        pos = b * BLK
        alive = pos < live
        last = jnp.minimum(pos + BLK, live) - 1
        first = lax.shift_right_logical(lookup(pos, ends, mends, 0), 7)
        end = lax.shift_right_logical(lookup(last, ends, mends[1:], mends[0]) + BLK - 1, 7)
        n = end - first
        below = 0
        for m in SPANS:
            begin = jnp.minimum(first, LEN // BLK - m)
            pl.when(alive & (n > below) & (n <= m))(functools.partial(block, i, b, begin, m))
            below = m
        pl.when(jnp.logical_not(alive))(functools.partial(dead, i))
        return carry

    lax.fori_loop(0, 4, step, 0)


def cross_scores(i, n, lanes, kstart, q_ref, k_ref, low2, high2):
    keys = k_ref[pl.ds(kstart, n * BLK), lanes]
    queries = stacked(q_ref[pl.ds(pl.multiple_of(i * BLK, BLK), BLK), lanes])
    index = kstart + lax.broadcasted_iota(jnp.int32, (n * BLK, 2 * BLK), 0)
    allowed = (index >= low2) & (index < high2)
    return queries, keys, jnp.where(allowed, nt(keys, queries), MASKED)


def pairs(body):
    for p in range(4):
        body(p, slice(p * BLK, (p + 1) * BLK))


def third_kernel(
    io, t_ref, len_ref, mlen_ref, cnt_ref,
    x_ref, keep_ref, recv_ref, so_ref, soo_ref, gain2_ref, cq_ref, cqo_ref,
    mk_ref, mvt_ref, co_ref, coo_ref, gain3_ref,
    h1_ref, n2_ref, q_ref, mixed_ref, lse_ref, h2_ref, n3_ref,
    low_ref, high_ref,
):
    t = t_ref[0]
    ends, mends = running_ends(len_ref), running_ends(mlen_ref)
    live = live_tokens(ends, cnt_ref[0])
    set_ranges(ends, mends, live, low_ref, high_ref)

    io.ready(x_ref, keep_ref, recv_ref, so_ref, soo_ref, gain2_ref, cq_ref, cqo_ref)

    def before(i, carry):
        rows = pl.ds(pl.multiple_of(i * 256, 256), 256)
        value = x_ref[rows, :].astype(f32)
        value = value + nn(keep_ref[rows, :], so_ref[...]) + nn(recv_ref[rows, :], soo_ref[...])
        h1_ref[rows, :] = value
        low = (value * rms_scale(value) * gain2_ref[...]).astype(bf16)
        n2_ref[rows, :] = low
        q_ref[rows, :OWN] = nn(low, cq_ref[...]).astype(bf16)
        q_ref[rows, OWN:] = nn(low, cqo_ref[...]).astype(bf16)
        return carry

    lax.fori_loop(0, 2, before, 0)
    io.done(h1_ref, n2_ref, q_ref)
    io.ready(mk_ref, mvt_ref)

    def block(i, b, first, n):
        kstart = pl.multiple_of(first * BLK, BLK)
        low2, high2 = twice(low_ref[pl.ds(b, 1), :]), twice(high_ref[pl.ds(b, 1), :])
        alive = (low2 < BIG).astype(f32)

        def pair(p, lanes):
            _, _, scores = cross_scores(i, n, lanes, kstart, q_ref, mk_ref, low2, high2)
            peak = jnp.max(scores, axis=0, keepdims=True)
            raised = jnp.exp(scores - peak)
            total = jnp.sum(raised, axis=0, keepdims=True)
            mixed = nn(mvt_ref[lanes, pl.ds(kstart, n * BLK)], raised.astype(bf16))
            mixed = mixed * (alive / total)
            mixed_ref[pl.ds(pl.multiple_of(i * BLK, BLK), BLK), lanes] = diagonal(mixed).astype(bf16)
            lse_ref[p, pl.ds(i, 1), :] = peak + jnp.log(total)

        pairs(pair)

    def dead(i):
        mixed_ref[pl.ds(pl.multiple_of(i * BLK, BLK), BLK), :] = jnp.zeros((BLK, WIDTH), bf16)
        for p in range(4):
            lse_ref[p, pl.ds(i, 1), :] = jnp.zeros((1, 2 * BLK), f32)

    cross_blocks(t, ends, mends, live, block, dead)

    io.done(mixed_ref, lse_ref)
    io.ready(co_ref, coo_ref, gain3_ref)

    def after(i, carry):
        rows = pl.ds(pl.multiple_of(i * 256, 256), 256)
        value = h1_ref[rows, :]
        value = value + nn(mixed_ref[rows, :OWN], co_ref[...]) + nn(mixed_ref[rows, OWN:], coo_ref[...])
        h2_ref[rows, :] = value
        n3_ref[rows, :] = (value * rms_scale(value) * gain3_ref[...]).astype(bf16)
        return carry

    lax.fori_loop(0, 2, after, 0)


def feed_kernel(
    io, place_ref, n3_ref, fi_ref, cot_ref, fo_ref,
    out_ref, gn_ref, act_ref, gp_ref,
):
    tile = 256
    n_tiles = fi_ref.shape[1] // tile
    root = math.sqrt(2 / math.pi)
    base = place_ref[0] * HALF
    io.ready(n3_ref, fi_ref, cot_ref, fo_ref)

    def hidden(j, carry):
        lanes = pl.ds(pl.multiple_of(j * tile, tile), tile)
        for i in range(2):
            rows = slice(i * 256, (i + 1) * 256)
            pre = nn(n3_ref[rows, :], fi_ref[:, lanes])
            square = pre * pre
            bent = jnp.tanh(pre * (root + (root * 0.044715) * square))
            gate = 0.5 + 0.5 * bent
            slope = gate + pre * (0.5 - 0.5 * bent * bent) * (root + (root * 0.134145) * square)
            act_ref[rows, lanes] = (pre * gate).astype(bf16)
            grads = nt(cot_ref[pl.ds(pl.multiple_of(base + i * 256, 256), 256), :], fo_ref[lanes, :])
            gp_ref[rows, lanes] = (grads * slope).astype(bf16)
        return carry

    lax.fori_loop(0, n_tiles, hidden, 0)
    io.done(act_ref, gp_ref)

    def outward(i, carry):
        rows = pl.ds(pl.multiple_of(i * 256, 256), 256)
        out_ref[rows, :] = nn(act_ref[rows, :], fo_ref[...]).astype(bf16)
        gn_ref[rows, :] = nt(gp_ref[rows, :], fi_ref[...]).astype(bf16)
        return carry

    lax.fori_loop(0, 2, outward, 0)


def feed_weights_kernel(
    io, t_ref, h2_ref, own_ref, oth_ref, n3_ref, gp_ref, n3o_ref, gpo_ref, act_ref, cot_ref, acto_ref,
    fi_ref, fo_ref, out_ref,
    n3t_ref,
):
    t = t_ref[0]
    mine = pl.ds(pl.multiple_of(t * HALF, HALF), HALF)
    theirs = pl.ds(pl.multiple_of((1 - t) * HALF, HALF), HALF)
    io.ready(n3_ref, gp_ref, n3o_ref, gpo_ref)
    n3t_ref[:, :HALF] = jnp.transpose(n3_ref[...].astype(f32)).astype(bf16)
    n3t_ref[:, HALF:] = jnp.transpose(n3o_ref[...].astype(f32)).astype(bf16)
    n_tiles = fi_ref.shape[1] // 256
    for j in range(n_tiles):
        lanes = slice(j * 256, (j + 1) * 256)
        grads = nn(n3t_ref[:, :HALF], gp_ref[:, lanes]) + nn(n3t_ref[:, HALF:], gpo_ref[:, lanes])
        fi_ref[:, lanes] = grads.astype(bf16)
    io.done(fi_ref)
    io.ready(act_ref, cot_ref, acto_ref)
    for j in range(n_tiles):
        lanes = slice(j * 256, (j + 1) * 256)
        grads = tn(act_ref[:, lanes], cot_ref[mine, :]) + tn(acto_ref[:, lanes], cot_ref[theirs, :])
        fo_ref[lanes, :] = grads.astype(bf16)
    io.done(fo_ref)
    io.ready(h2_ref, own_ref, oth_ref)
    out_ref[mine, :] = (h2_ref[...] + own_ref[...].astype(f32)).astype(bf16)
    out_ref[theirs, :] = oth_ref[...]


def cross_back_kernel(
    io, t_ref, len_ref, mlen_ref, cnt_ref,
    gn_ref, gnr_ref, h2_ref, gain3_ref, cot_ref, co_ref, coo_ref,
    q_ref, mk_ref, mkt_ref, mv_ref, lse_ref, cq_ref, cqo_ref, h1_ref, gain2_ref, so_ref, soo_ref,
    gb2_ref, dq_ref, dk_ref, dv_ref, gh1_ref, gb1_ref, gm1_ref, gm1o_ref, gains_ref,
    low_ref, high_ref, live_ref, gm_ref, dk_acc, dv_acc, gh2_ref,
):
    t = t_ref[0]
    ends, mends = running_ends(len_ref), running_ends(mlen_ref)
    live = live_tokens(ends, cnt_ref[0])
    set_ranges(ends, mends, live, low_ref, high_ref)
    alive_rows = t * HALF + lax.broadcasted_iota(jnp.int32, (HALF, BLK), 0)
    live_ref[...] = (alive_rows < live).astype(f32)
    dk_acc[...] = jnp.zeros_like(dk_acc)
    dv_acc[...] = jnp.zeros_like(dv_acc)
    gains_ref[...] = jnp.zeros_like(gains_ref)

    io.ready(gn_ref, gnr_ref, h2_ref, gain3_ref, cot_ref, co_ref, coo_ref)
    for i in range(2):
        rows = slice(i * 256, (i + 1) * 256)
        grad = gn_ref[rows, :].astype(f32) + gnr_ref[rows, :].astype(f32)
        back, gain = rms_back(h2_ref[rows, :], gain3_ref[...], grad)
        gains_ref[0:1, :] += gain
        grad = cot_ref[rows, :].astype(f32) + back
        gh2_ref[rows, :] = grad
        low = grad.astype(bf16)
        gb2_ref[rows, :] = low
        alive = live_ref[rows, 0:1]
        gm_ref[rows, :OWN] = (nt(low, co_ref[...]) * alive).astype(bf16)
        gm_ref[rows, OWN:] = (nt(low, coo_ref[...]) * alive).astype(bf16)
    io.done(gb2_ref)
    io.ready(q_ref, mk_ref, mkt_ref, mv_ref, lse_ref)

    def block(i, b, first, n):
        kstart = pl.multiple_of(first * BLK, BLK)
        low2, high2 = twice(low_ref[pl.ds(b, 1), :]), twice(high_ref[pl.ds(b, 1), :])
        rows = pl.ds(pl.multiple_of(i * BLK, BLK), BLK)
        span = pl.ds(kstart, n * BLK)

        def pair(p, lanes):
            queries, _, scores = cross_scores(i, n, lanes, kstart, q_ref, mk_ref, low2, high2)
            probs = jnp.exp(scores - lse_ref[p, pl.ds(i, 1), :])
            grads = stacked(gm_ref[rows, lanes])
            grad_probs = nt(mv_ref[span, lanes], grads)
            inner = jnp.sum(grad_probs * probs, axis=0, keepdims=True)
            low = (probs * (grad_probs - inner)).astype(bf16)
            dk_acc[span, lanes] += nn(low, queries)
            dv_acc[span, lanes] += nn(probs.astype(bf16), grads)
            dq_ref[rows, lanes] = diagonal(nn(mkt_ref[lanes, span], low)).astype(bf16)

        pairs(pair)

    def dead(i):
        dq_ref[pl.ds(pl.multiple_of(i * BLK, BLK), BLK), :] = jnp.zeros((BLK, WIDTH), bf16)

    cross_blocks(t, ends, mends, live, block, dead)

    dk_ref[...] = dk_acc[...].astype(bf16)
    dv_ref[...] = dv_acc[...].astype(bf16)
    io.done(dq_ref, dk_ref, dv_ref)
    io.ready(cq_ref, cqo_ref, h1_ref, gain2_ref, so_ref, soo_ref)
    for i in range(2):
        rows = slice(i * 256, (i + 1) * 256)
        grad = nt(dq_ref[rows, :OWN], cq_ref[...]) + nt(dq_ref[rows, OWN:], cqo_ref[...])
        back, gain = rms_back(h1_ref[rows, :], gain2_ref[...], grad)
        gains_ref[1:2, :] += gain
        grad = gh2_ref[rows, :] + back
        gh1_ref[rows, :] = grad
        low = grad.astype(bf16)
        gb1_ref[rows, :] = low
        alive = live_ref[rows, 0:1]
        gm1_ref[rows, :] = (nt(low, so_ref[...]) * alive).astype(bf16)
        gm1o_ref[rows, :] = (nt(low, soo_ref[...]) * alive).astype(bf16)


def cross_weights_kernel(
    io, place_ref, mem_ref, dk_ref, dv_ref, n2_ref, dq_ref, mixed_ref, gb2_ref, keep_ref, gb1_ref, recv_ref,
    hold_ref, holdo_ref, send_ref,
    memt_ref, fold_ref,
):
    c = place_ref[1]
    io.ready(mem_ref, dk_ref, dv_ref, n2_ref, dq_ref, mixed_ref, gb2_ref, keep_ref, gb1_ref, recv_ref)
    memt_ref[...] = jnp.transpose(mem_ref[...].astype(f32)).astype(bf16)
    n2t = jnp.transpose(n2_ref[...].astype(f32)).astype(bf16)
    for side in range(2):
        lanes = slice(side * OWN, (side + 1) * OWN)
        mixed1 = keep_ref if side == 0 else recv_ref
        fold_ref[0] = tn(mixed_ref[:, lanes], gb2_ref[...]).astype(bf16)
        fold_ref[1] = tn(mixed1[...], gb1_ref[...]).astype(bf16)
        fold(fold_ref, 2, nn(n2t, dq_ref[:, lanes]))
        fold(fold_ref, 3, nn(memt_ref[...], dk_ref[:, lanes]))
        fold(fold_ref, 4, nn(memt_ref[...], dv_ref[:, lanes]))
        deal(c, fold_ref, hold_ref if side == 0 else holdo_ref, send_ref, side * 640)


def memory_back_kernel(
    io, place_ref, dk_ref, ck_ref, cko_ref, dv_ref, cv_ref, cvo_ref, gmem_ref, gmems_ref
):
    t = place_ref[0]
    io.ready(dk_ref, ck_ref, cko_ref, dv_ref, cv_ref, cvo_ref)
    for i in range(4):
        rows = slice(i * 256, (i + 1) * 256)
        grads = nt(dk_ref[rows, :OWN], ck_ref[...]) + nt(dk_ref[rows, OWN:], cko_ref[...])
        grads += nt(dv_ref[rows, :OWN], cv_ref[...]) + nt(dv_ref[rows, OWN:], cvo_ref[...])
        low = grads.astype(bf16)

        @pl.when(t == 0)
        def _():
            gmem_ref[rows, :] = low[:, :OWN]
            gmems_ref[rows, :] = low[:, OWN:]

        @pl.when(t != 0)
        def _():
            gmem_ref[rows, :] = low[:, OWN:]
            gmems_ref[rows, :] = low[:, :OWN]


def fold(fold_ref, k, weight):
    low = weight.astype(bf16)
    fold_ref[k, :, :OWN] = low[:256]
    fold_ref[k, :, OWN:] = low[256:]


def deal(c, fold_ref, hold_ref, send_ref, base):
    for k in range(fold_ref.shape[0]):
        rows = slice(k * BLK, (k + 1) * BLK)
        hold_ref[rows, :] = fold_ref[k, pl.ds(pl.multiple_of(c * BLK, BLK), BLK), :]
        rows = slice(base + k * BLK, base + (k + 1) * BLK)
        send_ref[rows, :] = fold_ref[k, pl.ds(pl.multiple_of((1 - c) * BLK, BLK), BLK), :]


def self_back_blocks(
    half, ends, live, start_ref, table_ref, g_ref, q_ref, k_ref, kt_ref, v_ref, bias_ref, lse_ref,
    dq_ref, dk_acc, dv_acc, near_acc, far_acc,
):
    def block(i, b, first, n):
        kstart = pl.multiple_of(first * BLK, BLK)
        start2 = twice(start_ref[pl.ds(b, 1), :])
        rows = pl.ds(pl.multiple_of(i * BLK, BLK), BLK)
        span = pl.ds(kstart, n * BLK)
        for p in range(2):
            lanes = slice(p * BLK, (p + 1) * BLK)
            queries, _, scores = self_scores(
                b, n, p, kstart, q_ref, k_ref, bias_ref, table_ref, start2
            )
            probs = jnp.exp(scores - lse_ref[p, pl.ds(i, 1), :])
            grads = stacked(g_ref[rows, lanes])
            grad_probs = nt(v_ref[span, lanes], grads)
            inner = jnp.sum(grad_probs * probs, axis=0, keepdims=True)
            grad_scores = probs * (grad_probs - inner)
            near_acc[p] += grad_scores[(n - 1) * BLK :]
            if n > 1:
                near_acc[2 + p] += grad_scores[(n - 2) * BLK : (n - 1) * BLK]
            if n > 2:
                far_acc[p : p + 1, :] += jnp.sum(grad_scores[: (n - 2) * BLK], axis=0, keepdims=True)
            low = grad_scores.astype(bf16)
            dk_acc[span, lanes] += nn(low, queries)
            dv_acc[span, lanes] += nn(probs.astype(bf16), grads)
            dq_ref[rows, lanes] = diagonal(nn(kt_ref[lanes, span], low)).astype(bf16)

    def step(i, carry):
        b = half * 4 + i
        alive, first, n = self_spans(b, ends, live)
        for m in range(1, 5):
            pl.when(alive & (n == m))(functools.partial(block, i, b, first, m))

        @pl.when(jnp.logical_not(alive))
        def _():
            dq_ref[pl.ds(pl.multiple_of(i * BLK, BLK), BLK), :] = jnp.zeros((BLK, OWN), bf16)

        return carry

    lax.fori_loop(0, 4, step, 0)


def self_back_own_kernel(
    io, place_ref, len_ref, cnt_ref, table_ref,
    gm_ref, q_ref, k_ref, kt_ref, v_ref, bias_ref, lse_ref,
    dq_ref, dk_acc, dv_acc, near_acc, far_acc,
    start_ref,
):
    ends = running_ends(len_ref)
    live = live_tokens(ends, cnt_ref[0])
    set_starts(ends, live, start_ref)
    for ref in (dk_acc, dv_acc, near_acc, far_acc):
        ref[...] = jnp.zeros_like(ref)
    io.ready(gm_ref, q_ref, k_ref, kt_ref, v_ref, bias_ref, lse_ref)
    self_back_blocks(
        place_ref[0], ends, live, start_ref, table_ref, gm_ref, q_ref, k_ref, kt_ref, v_ref, bias_ref, lse_ref,
        dq_ref, dk_acc, dv_acc, near_acc, far_acc,
    )


def self_back_kernel(
    io, place_ref, len_ref, cnt_ref, table_ref,
    gmr_ref, dqm_ref, dkm_ref, dvm_ref, nearm_ref, farm_ref, q_ref, k_ref, kt_ref, v_ref, bias_ref, lse_ref,
    n1_ref, x_ref, gh1_ref, gain1_ref, gains_ref, wq_ref, wk_ref, wv_ref,
    hold_ref, send_ref, gi_ref, small_ref,
    start_ref, dqo_ref, dq_ref, dk_acc, dv_acc, near_acc, far_acc, n1t_ref, fold_ref, sums_ref,
):
    t = place_ref[0]
    ends = running_ends(len_ref)
    live = live_tokens(ends, cnt_ref[0])
    set_starts(ends, live, start_ref)
    small_ref[...] = jnp.zeros_like(small_ref)
    for ref, so_far in ((dk_acc, dkm_ref), (dv_acc, dvm_ref), (near_acc, nearm_ref), (far_acc, farm_ref)):
        ref[...] = so_far[...]
    io.ready(q_ref, k_ref, kt_ref, v_ref, bias_ref, lse_ref)
    self_back_blocks(
        1 - t, ends, live, start_ref, table_ref, gmr_ref, q_ref, k_ref, kt_ref, v_ref, bias_ref, lse_ref,
        dqo_ref, dk_acc, dv_acc, near_acc, far_acc,
    )
    dq_ref[pl.ds(pl.multiple_of(t * HALF, HALF), HALF), :] = dqm_ref[...]
    dq_ref[pl.ds(pl.multiple_of((1 - t) * HALF, HALF), HALF), :] = dqo_ref[...]

    io.ready(n1_ref)
    n1t_ref[...] = jnp.transpose(n1_ref[...].astype(f32)).astype(bf16)
    low_k, low_v = dk_acc[...].astype(bf16), dv_acc[...].astype(bf16)
    for k, grads in enumerate((dq_ref[...], low_k, low_v)):
        fold(fold_ref, k, nn(n1t_ref[...], grads))
    deal(place_ref[1], fold_ref, hold_ref, send_ref, 0)
    io.done(hold_ref, send_ref)
    io.ready(x_ref, gh1_ref, gain1_ref, gains_ref, wq_ref, wk_ref, wv_ref)
    gain1 = jnp.zeros((1, WIDTH), f32)
    for i in range(4):
        rows = slice(i * 256, (i + 1) * 256)
        grads = nt(dq_ref[rows, :], wq_ref[...]) + nt(low_k[rows], wk_ref[...]) + nt(low_v[rows], wv_ref[...])
        back, gain = rms_back(x_ref[rows, :].astype(f32), gain1_ref[...], grads)
        gain1 += gain
        mine = (t == i // 2).astype(f32)
        back += mine * gh1_ref[(i % 2) * 256 : (i % 2 + 1) * 256, :]
        gi_ref[rows, :] = back.astype(bf16)
    io.done(gi_ref)
    key = lax.broadcasted_iota(jnp.int32, (BLK, BLK), 0)
    query = lax.broadcasted_iota(jnp.int32, (BLK, BLK), 1)
    gaps = [query - key, BLK + query - key]
    for level in range(NB):
        for p in range(2):
            row = jnp.zeros((1, 2 * BLK), f32)
            for d in range(2):
                inside = gaps[d] >= THRESHOLDS[level]
                if level + 1 < NB:
                    inside &= gaps[d] < THRESHOLDS[level + 1]
                picked = jnp.where(twice(inside.astype(f32)) > 0, near_acc[2 * d + p], 0.0)
                row += jnp.sum(picked, axis=0, keepdims=True)
            if level == NB - 1:
                row += far_acc[p : p + 1, :]
            sums_ref[level : level + 1, p * 256 : (p + 1) * 256] = row
    lane = lax.broadcasted_iota(jnp.int32, (NB, BLK), 1)
    table = jnp.zeros((NB, BLK), f32)
    for h in range(4):
        total = jnp.sum(sums_ref[:, h * BLK : (h + 1) * BLK], axis=1, keepdims=True)
        table = jnp.where(lane == h, total, table)
    small_ref[16:48, :] = table

    for k, gain in enumerate((gain1, gains_ref[1:2, :], gains_ref[0:1, :])):
        for j in range(4):
            small_ref[4 * k + j : 4 * k + j + 1, :] = gain[:, j * BLK : (j + 1) * BLK]


def join_kernel(io, place_ref, own_ref, got_ref, recv_ref, mine_ref, theirs_ref, hold_ref, send_ref):
    x = place_ref[2]
    io.ready(own_ref, got_ref, recv_ref, mine_ref, theirs_ref)
    for k in range(8):
        if k < 5:
            rows = slice(k * BLK, (k + 1) * BLK)
            total = own_ref[rows, :].astype(f32) + got_ref[rows, :].astype(f32) + recv_ref[rows, :].astype(f32)
        else:
            rows = slice((k - 5) * BLK, (k - 4) * BLK)
            total = mine_ref[rows, :].astype(f32) + theirs_ref[rows, :].astype(f32)
        low = total.astype(bf16)
        rows = slice((k % 4) * BLK, (k % 4 + 1) * BLK)

        @pl.when(x == k // 4)
        def _():
            hold_ref[rows, :] = low

        @pl.when(x != k // 4)
        def _():
            send_ref[rows, :] = low


def pieces_kernel(io, _, in_ref, out_ref):
    io.ready(in_ref)
    total = in_ref[0].astype(f32)
    for k in range(1, in_ref.shape[0]):
        total += in_ref[k].astype(f32)
    total = total.astype(bf16)
    for k in range(in_ref.shape[0]):
        out_ref[k] = total


def unfold_kernel(
    io, place_ref, own_ref, pair_ref, core_ref, both_ref,
    co_ref, so_ref, cq_ref, ck_ref, cv_ref, wq_ref, wk_ref, wv_ref,
):
    c, x = place_ref[1], place_ref[2]
    outs = (co_ref, so_ref, cq_ref, ck_ref, cv_ref, wq_ref, wk_ref, wv_ref)

    def spread(ref, core, bit):
        low = pl.ds(pl.multiple_of(core * BLK, BLK), BLK)
        high = pl.ds(pl.multiple_of(256 + core * BLK, BLK), BLK)
        for k, out in enumerate(outs):
            rows = slice((k % 4) * BLK, (k % 4 + 1) * BLK)

            @pl.when(bit == k // 4)
            def _():
                if k < 2:
                    out[low, :] = ref[rows, :].astype(f32)
                else:
                    out[low, :] = ref[rows, :OWN].astype(f32)
                    out[high, :] = ref[rows, OWN:].astype(f32)

    for ref, core, bit in ((own_ref, c, x), (pair_ref, c, 1 - x), (core_ref, 1 - c, x), (both_ref, 1 - c, 1 - x)):
        io.ready(ref)
        spread(ref, core, bit)


def swap(value, axis="tensor"):
    return lax.ppermute(value, axis, [(0, 1), (1, 0)])


def shards(
    inputs, memory, cotangent, dec_lengths, mem_lengths, counts,
    self_gain, self_query, self_key, self_value, self_out, rel_table,
    cross_gain, cross_query, cross_key, cross_value, cross_out,
    feed_gain, feed_in, feed_out,
):
    v = pltpu.VMEM
    i32 = jnp.int32
    t, c, x = (lax.axis_index(name).astype(i32) for name in ("tensor", "core", "pair"))
    ring = lax.axis_size("ring")
    place = jnp.stack([t, c, x])
    place_oth = jnp.stack([1 - t, c, x])
    gain1, gain2, gain3 = (g.reshape(1, WIDTH) for g in (self_gain, cross_gain, feed_gain))
    table = rel_table.T

    tok = (LEN, WIDTH)
    half = (HALF, WIDTH)
    heads, heads_t, part = (LEN, OWN), (OWN, LEN), (HALF, OWN)
    narrow, wide = (OWN, WIDTH), (WIDTH, OWN)
    row_tile = v((LEN // BLK, BLK), i32)

    pack, x_near, gain1_near, wq, wk, wv = call(
        pack_kernel,
        [((PACKED, WIDTH), bf16, "near")],
        [pltpu.SemaphoreType.DMA((6,))],
        (place, *map(Raw, (self_out, cross_out, cross_query, cross_key, cross_value))),
        us=SHORT, fetch=(inputs, gain1, self_query, self_key, self_value),
    )
    pack = swap(pack)
    n1, q, q_far, k, k_far, val, vt, kt, bias, bias_far, send1, lse1_oth = call(
        first_kernel,
        [(tok, bf16, "far"), (heads, bf16, "both"), (heads, bf16, "both"), (heads, bf16, "far"),
         (heads_t, bf16, "near"), (heads_t, bf16, "far"), ((4, BLK, 2 * BLK), f32, "both"), (part, bf16, "near"),
         ((2, 4, 2 * BLK), f32, "near")],
        [row_tile],
        (place, dec_lengths, counts, table, *map(Near, (x_near, gain1_near, wq, wk, wv))),
        smem=4, us=6,
    )
    pack, send1 = lax.optimization_barrier((pack, send1))
    pack_core = swap(pack, "core")
    mixed1_recv = swap(send1)
    mixed1_keep, lse1, memory_near, ck, cv, lse1_oth = call(
        second_kernel,
        [(part, bf16, "near"), ((2, 4, 2 * BLK), f32, "near")],
        [row_tile],
        (place, dec_lengths, counts, table, Near(q), Near(k), Near(vt), Near(bias)),
        smem=4, us=SHORT, fetch=(memory, cross_key, cross_value), forward=(lse1_oth,),
    )
    mk, mv, mkt, mvt, so_oth, co_oth, cq_oth, ck_oth, cv_oth, x_half, so, gain2_near, cq_w, co, gain3_near, keep_far, lse1 = call(
        memory_kernel,
        [(tok, bf16, "near"), (tok, bf16, "near"), ((WIDTH, LEN), bf16, "near"), ((WIDTH, LEN), bf16, "near"),
         (narrow, bf16, "near"), (narrow, bf16, "near"), (wide, bf16, "near"), (wide, bf16, "near"), (wide, bf16, "near")],
        [],
        (place, *map(Near, (memory_near, ck, cv, pack, pack_core))),
        us=SHORT, fetch=(Half(inputs), self_out, gain2, cross_query, cross_out, gain3), forward=(mixed1_keep, lse1),
    )
    (h1, n2, cq, mixed2, lse2, h2, n3, fi, cot, fo,
     mk, mv, mkt, so_oth_far, co_oth_far, cq_oth_far, ck_oth, cv_oth, recv_far) = call(
        third_kernel,
        [(half, f32, "far"), (half, bf16, "far"), (half, bf16, "far"), (half, bf16, "far"),
         ((4, 4, 2 * BLK), f32, "far"), (half, f32, "near"), (half, bf16, "near")],
        [row_tile, row_tile],
        (place, dec_lengths, mem_lengths, counts,
         *map(Near, (x_half, mixed1_keep, mixed1_recv, so, so_oth, gain2_near, cq_w, cq_oth, mk, mvt, co, co_oth, gain3_near))),
        smem=4, us=9,
        fetch=(feed_in, cotangent, feed_out),
        forward=(mk, mv, mkt, so_oth, co_oth, cq_oth, ck_oth, cv_oth, mixed1_recv),
    )
    n3_recv = swap(n3)

    hidden = feed_in.shape[1]
    units = (HALF, hidden)
    out_own, gn3_own, act, gp, h2_far, n3_far = call(
        feed_kernel,
        [(half, bf16, "far"), (half, bf16, "far"), (units, bf16, "far"), (units, bf16, "far")],
        [],
        (place, *map(Near, (n3, fi, cot, fo))),
        us=5, forward=(h2, n3),
    )
    h2 = h2_far
    n3_recv, act = lax.optimization_barrier((n3_recv, act))
    out_oth, gn3_oth, act_oth, gp_oth = call(
        feed_kernel,
        [(half, bf16, "near"), (half, bf16, "near"), (units, bf16, "near"), (units, bf16, "near")],
        [],
        (place_oth, *map(Near, (n3_recv, fi, cot, fo))),
        us=5,
    )
    gn3_recv = swap(gn3_oth)
    feed_in_grad, feed_out_grad, out_part = call(
        feed_weights_kernel,
        [((WIDTH, hidden), bf16, "far"), ((hidden, WIDTH), bf16, "far"), (tok, bf16, "far")],
        [v((WIDTH, LEN), bf16)],
        (place, h2, out_own, Near(out_oth), n3_far, gp, Near(n3_recv), Near(gp_oth), act, Near(cot), Near(act_oth)),
        us=5,
    )
    gn3_recv, out_part, feed_in_grad, feed_out_grad = lax.optimization_barrier(
        (gn3_recv, out_part, feed_in_grad, feed_out_grad)
    )
    dp = ("ring", "pair", "core")
    feed_in_grad, feed_out_grad = lax.psum((feed_in_grad, feed_out_grad), dp)

    def later():
        (gb2, dcq, dmk, dmv, gh1, gb1, gm1, gm1_oth, gains, memory_near, n2_near, mixed2_near, keep, recv) = call(
            cross_back_kernel,
            [(half, bf16, "near"), (half, bf16, "near"), (tok, bf16, "near"), (tok, bf16, "near"), (half, f32, "near"),
             (half, bf16, "near"), (part, bf16, "near"), (part, bf16, "near"), ((8, WIDTH), f32, "near")],
            [row_tile, row_tile, v((HALF, BLK), f32), v(half, bf16), v(tok, f32), v(tok, f32), v(half, f32)],
            (place, dec_lengths, mem_lengths, counts, gn3_own, Near(gn3_recv), h2, gain3, Half(cotangent),
             cross_out, co_oth_far, cq, mk, mkt, mv, lse2, cross_query, cq_oth_far, h1, gain2, self_out, so_oth_far),
            smem=4, us=SHORT, fetch=(memory, n2, mixed2, keep_far, recv_far),
        )
        gm1_recv = swap(gm1_oth)
        cross_hold, cross_hold_oth, cross_send, q, k, kt_near, v_near, bias, lse1_near, lse1_oth_near, dmk, dmv = call(
            cross_weights_kernel,
            [((640, WIDTH), bf16, "near"), ((640, WIDTH), bf16, "near"), ((1280, WIDTH), bf16, "near")],
            [v((WIDTH, LEN), bf16), v((5, 256, WIDTH), bf16)],
            (place, *map(Near, (memory_near, dmk, dmv, n2_near, dcq, mixed2_near, gb2, keep, gb1, recv))),
            us=3, fetch=(q_far, k_far, kt, val, bias_far, lse1, lse1_oth), forward=(dmk, dmv),
        )
        cross_got = swap(cross_send, "core")
        acc, tiles = ((LEN, OWN), f32), ((4, BLK, 2 * BLK), f32)
        dq1, dk1, dv1, near1, far1, n1_near, x_near, gain1_near, wq, wk, wv = call(
            self_back_own_kernel,
            [(part, bf16, "near"), (*acc, "near"), (*acc, "near"), (*tiles, "near"), ((8, 2 * BLK), f32, "near")],
            [row_tile],
            (place, dec_lengths, counts, table, *map(Near, (gm1, q, k, kt_near, v_near, bias, lse1_near))),
            smem=4, us=3, fetch=(n1, inputs, gain1, self_query, self_key, self_value),
        )
        cross_recv = swap((cross_hold_oth.astype(f32) + cross_got[640:].astype(f32)).astype(bf16))
        self_hold, self_send, gi_part, small = call(
            self_back_kernel,
            [((384, WIDTH), bf16, "near"), ((384, WIDTH), bf16, "near"), (tok, bf16, "far"), ((48, BLK), f32, "near")],
            [row_tile, v(part, bf16), v(heads, bf16), v(*acc), v(*acc), v(*tiles), v((8, 2 * BLK), f32),
             v((WIDTH, LEN), bf16), v((3, 256, WIDTH), bf16), v((NB, WIDTH), f32)],
            (place, dec_lengths, counts, table,
             *map(Near, (gm1_recv, dq1, dk1, dv1, near1, far1, q, k, kt_near, v_near, bias, lse1_oth_near,
                         n1_near, x_near, gh1, gain1_near, gains, wq, wk, wv))),
            smem=4, us=3,
        )
        self_got = swap(self_send, "core")
        gi_recv = swap(gi_part)

        hold, send = call(
            join_kernel,
            [(half, bf16, "near"), (half, bf16, "near")],
            [],
            (place, *map(Near, (cross_hold, cross_got, cross_recv, self_hold, self_got))),
            us=2,
        )
        small, hold = lax.optimization_barrier((small, hold))
        small = jnp.broadcast_to(small[None], (4 * ring, 48, BLK))
        small = jnp.sum(lax.all_to_all(small, dp, 0, 0), axis=0)
        dmk, hold = lax.optimization_barrier((dmk, hold))
        gmem, gmem_send = call(
            memory_back_kernel,
            [(heads, bf16, "far"), (heads, bf16, "near")],
            [],
            (place, dmk, cross_key, ck_oth, dmv, cross_value, cv_oth),
            us=SHORT,
        )
        gmem_recv = swap(gmem_send)
        summed = (hold.astype(f32) + swap(send, "pair").astype(f32)).astype(bf16)
        summed, small, gmem_send, out_late = lax.optimization_barrier((summed, small, gmem_send, out_part))
        out_recv = swap(out_late)
        pieces = (ring, HALF // ring, WIDTH)
        taken = lax.all_to_all(summed.reshape(pieces), "ring", 0, 0)
        (summed,) = call(pieces_kernel, [(pieces, bf16, "near")], [], (place, Near(taken)), us=SHORT)
        summed, gi_recv = lax.optimization_barrier((summed, gi_recv))
        own = lax.all_to_all(summed, "ring", 0, 0).reshape(half)
        return own, small, gi_part, gi_recv, out_recv, gmem, gmem_recv

    def last(own, small, gi_part, gi_recv, out_recv, gmem, gmem_recv, feed_in_grad, feed_out_grad):
        def both(part, other):
            return (part.astype(f32) + other.astype(f32)).astype(bf16)

        pair, core_own = swap(own, "pair"), swap(own, "core")
        gain_grads = small + swap(small)
        ready = (
            both(out_part, out_recv), both(gi_part, gi_recv), both(gmem, gmem_recv),
            *(gain_grads[4 * k : 4 * k + 4].reshape(WIDTH) for k in range(3)), small[16:, :4],
            feed_in_grad.astype(f32), feed_out_grad.astype(f32),
        )
        pair, *ready = lax.optimization_barrier((pair, *ready))
        narrows, wides = (narrow, f32, "far"), (wide, f32, "far")
        grads = call(
            unfold_kernel,
            [narrows] * 2 + [wides] * 6,
            [],
            (place, *map(Near, (own, pair, core_own, swap(pair, "core")))),
        )
        return *ready, *grads

    def always(branch, *operands):
        def never(*operands):
            shapes = jax.eval_shape(branch, *operands)
            return tuple(jnp.zeros(shape.shape, shape.dtype) for shape in shapes)

        return lax.cond(counts[0] > 0, branch, never, *operands)

    results = always(later)
    output, grad_inputs, grad_memory, *gain_grads, table_grad, feed_in_grad, feed_out_grad = (
        results := always(last, *results, feed_in_grad, feed_out_grad)
    )[:9]
    co_grad, so_grad, cq_grad, ck_grad, cv_grad, wq_grad, wk_grad, wv_grad = results[9:]
    return (
        output,
        grad_inputs,
        grad_memory,
        gain_grads[0],
        wq_grad,
        wk_grad,
        wv_grad,
        so_grad,
        table_grad,
        gain_grads[1],
        cq_grad,
        ck_grad,
        cv_grad,
        co_grad,
        gain_grads[2],
        feed_in_grad,
        feed_out_grad,
    )


def solution(mesh):
    devices = mesh.devices
    rows, tensor = devices.shape
    mesh = Mesh(devices.reshape(rows // 4, 2, 2, tensor), ("ring", "pair", "core", "tensor"))
    dp = ("ring", "pair", "core")
    split = P(dp, None)
    columns, rows = P(None, "tensor"), P("tensor", None)
    return jax.shard_map(
        shards,
        mesh=mesh,
        in_specs=(
            split, split, split, split, split, P(dp),
            P(), columns, columns, columns, rows, columns,
            P(), columns, columns, columns, rows,
            P(), columns, rows,
        ),
        out_specs=(
            split, split, P(dp, "tensor"),
            P(), columns, columns, columns, rows, columns,
            P(), columns, columns, columns, rows,
            P(), columns, rows,
        ),
        check_vma=False,
    )
```

```python
import functools
import math

import jax
import jax.numpy as jnp
from jax import lax
from jax.experimental import pallas as pl
from jax.experimental.pallas import tpu as pltpu
from jax.sharding import Mesh
from jax.sharding import PartitionSpec as P

NB = 32
MAXDIST = 128
SEGS = 16
LEN = 1024
HALF = 512
WIDTH = 512
OWN = 256
BLK = 128
BIG = 1 << 30
MASKED = -1e30
EPS = 1e-06
f32 = jnp.float32
bf16 = jnp.bfloat16
ROOM = 11 * 1024 * 1024
SHORT = 0.05


def thresholds():
    exact = NB // 2
    edges = [
        math.ceil(exact * (MAXDIST / exact) ** (level / (NB - exact)))
        for level in range(1, NB - exact)
    ]
    return list(range(exact + 1)) + edges


THRESHOLDS = thresholds()


def nn(a, b):
    return jnp.dot(a, b, preferred_element_type=f32)


def nt(a, b):
    return lax.dot_general(a, b, (((1,), (1,)), ((), ())), preferred_element_type=f32)


def tn(a, b):
    return lax.dot_general(a, b, (((0,), (0,)), ((), ())), preferred_element_type=f32)


class Half:
    def __init__(self, array):
        self.array = array


class Near:
    def __init__(self, array):
        self.array = array


class Raw:
    def __init__(self, array):
        self.array = array


PACKED = 640
SMALL = 16


def packed_parts(core):
    def at(start, size):
        return pl.ds(pl.multiple_of(start, BLK), size)

    left, right, all_lanes = slice(0, OWN), slice(OWN, WIDTH), slice(0, WIDTH)
    return (
        [(at(core * BLK, BLK), (slice(0, 128), all_lanes))],
        [(at(core * BLK, BLK), (slice(128, 256), all_lanes))],
        [(at(core * 256, 256), (slice(256, 512), left))],
        [(at(core * 256, 256), (slice(256, 512), right))],
        [(at(core * 256, BLK), (slice(512, 640), left)), (at(core * 256 + BLK, BLK), (slice(512, 640), right))],
    )


def pack_kernel(io, place_ref, *refs):
    *weights, pack_ref, sems = refs
    copies = []
    for ref, parts in zip(weights, packed_parts(place_ref[1]), strict=True):
        for rows, where in parts:
            copy = pltpu.make_async_copy(ref.at[rows, :], pack_ref.at[where], sems.at[len(copies)])
            copy.start()
            copies.append(copy)
    for copy in copies:
        copy.wait()


class Copies:
    def __init__(self, sems):
        self.sems, self.used, self.waits, self.out = sems, 0, {}, {}

    def start(self, source, target):
        copy = pltpu.make_async_copy(source, target, self.sems.at[self.used])
        self.used += 1
        copy.start()
        return copy

    def ready(self, *refs):
        for ref in refs:
            for copy in self.waits.pop(id(ref), ()):
                copy.wait()

    def done(self, *refs):
        for ref in refs:
            target, copy = self.out.get(id(ref), (None, True))
            if copy is None:
                self.out[id(ref)] = (target, self.start(ref, target))


def size_of(shape, dtype):
    return math.prod(shape) * jnp.dtype(dtype).itemsize


def call(body, outs, scratch, args, smem=1, us=3, fetch=(), forward=()):
    tables, operands = args[:smem], args[smem:]
    arrays, in_specs, fetched = [], [], []
    hbm, vmem = pl.BlockSpec(memory_space=pltpu.HBM), pl.BlockSpec(memory_space=pltpu.VMEM)

    def shape_of(operand):
        if isinstance(operand, Half):
            return (HALF, *operand.array.shape[1:]), operand.array.dtype
        return operand.shape, operand.dtype

    for operand in (*operands, *fetch, *map(Near, forward)):
        array = operand.array if isinstance(operand, (Near, Raw, Half)) else operand
        near = isinstance(operand, Near)
        arrays.append(array if near else pltpu.with_memory_space_constraint(array, pltpu.HBM))
        in_specs.append(vmem if near else hbm)
    fetched = [shape_of(o) for o in operands if not isinstance(o, (Near, Raw))]
    out_shapes, out_specs, sent = [], [], []
    extra = [(*shape_of(o), "near") for o in fetch] + [(o.shape, o.dtype, "far") for o in forward]
    for k, (shape, dtype, kind) in enumerate([*outs, *extra]):
        if kind != "far":
            out_shapes.append(jax.ShapeDtypeStruct(shape, dtype))
            out_specs.append(vmem)
        if kind != "near":
            out_shapes.append(pltpu.HBM(shape, dtype))
            out_specs.append(hbm)
        if kind == "far" and k < len(outs):
            sent.append((shape, dtype))
    n_copies = len(fetched) + sum(kind != "near" for _, _, kind in outs) + len(extra)

    def kernel(*refs):
        refs = list(refs)

        def take(n):
            taken = refs[:n]
            del refs[:n]
            return taken

        scalars, sources = take(smem), take(len(operands))
        extra_sources = take(len(extra))
        targets = take(len(out_shapes) - len(extra))
        extra_targets = take(len(extra))
        inner, outer = take(len(fetched)), take(len(sent))
        io = Copies(take(1)[0] if n_copies else None)
        inputs, outputs = [], []

        def source_of(operand, source):
            if isinstance(operand, Half):
                return source.at[pl.ds(pl.multiple_of(scalars[0][0] * HALF, HALF), HALF), :]
            return source

        for operand, source in zip(operands, sources, strict=True):
            if isinstance(operand, (Near, Raw)):
                inputs.append(source)
                continue
            ref = inner.pop(0)
            inputs.append(ref)
            io.waits[id(ref)] = [io.start(source_of(operand, source), ref)]
        moved = [
            io.start(source_of(operand, source), target)
            for operand, source, target in zip((*fetch, *forward), extra_sources, extra_targets, strict=True)
        ]
        for _, _, kind in outs:
            ref = outer.pop(0) if kind == "far" else targets.pop(0)
            outputs.append(ref)
            if kind != "near":
                io.out[id(ref)] = (targets.pop(0), None)
        body(io, *scalars, *inputs, *outputs, *refs)
        io.ready(*inputs)
        io.done(*outputs)
        for copy in (*(copy for _, copy in io.out.values()), *moved):
            copy.wait()

    own = [pltpu.VMEM(s, d) for s, d in fetched + sent]
    used = sum(size_of(s, d) for s, d in fetched + sent) + sum(
        size_of(s.shape, s.dtype) for s in scratch if s.memory_space == pltpu.VMEM
    )
    return pl.pallas_call(
        kernel,
        out_shape=tuple(out_shapes),
        in_specs=[pl.BlockSpec(memory_space=pltpu.SMEM)] * smem + in_specs,
        out_specs=tuple(out_specs),
        scratch_shapes=[*own, *([pltpu.SemaphoreType.DMA((n_copies,))] if n_copies else []), *scratch],
        compiler_params=pltpu.CompilerParams(vmem_limit_bytes=used + ROOM),
        cost_estimate=pl.CostEstimate(flops=int(us * 3.3e9), bytes_accessed=int(us * 1e7), transcendentals=0),
    )(*tables, *arrays)


def running_ends(len_ref):
    ends, total = [], 0
    for k in range(SEGS):
        total = total + len_ref[0, k]
        ends.append(total)
    return ends


def live_tokens(ends, count):
    total = 0
    for k in range(SEGS):
        total = jnp.where(k < count, ends[k], total)
    return total


def lookup(pos, ends, values, first):
    found = first
    for k in range(SEGS - 1):
        found = jnp.where(pos >= ends[k], values[k], found)
    return found


def token_positions():
    shape = (LEN // BLK, BLK)
    return lax.broadcasted_iota(jnp.int32, shape, 0) * BLK + lax.broadcasted_iota(
        jnp.int32, shape, 1
    )


def twice(row):
    return jnp.concatenate([row, row], axis=1)


def stacked(pair):
    lane = lax.broadcasted_iota(jnp.int32, pair.shape, 1)
    zero = jnp.zeros_like(pair)
    return jnp.concatenate(
        [jnp.where(lane < 64, pair, zero), jnp.where(lane < 64, zero, pair)], axis=0
    )


def diagonal(product):
    return jnp.concatenate([product[:64, :BLK], product[64:, BLK:]], axis=0)


def own_rows(row):
    return jnp.concatenate(
        [jnp.broadcast_to(row[:, :BLK], (64, BLK)), jnp.broadcast_to(row[:, BLK:], (64, BLK))], axis=0
    )


def in_chunks(n, body):
    def four(j, carry):
        body(4 * j, 4)
        return carry

    lax.fori_loop(0, lax.shift_right_logical(n, 2), four, 0)
    pl.when((n & 2) != 0)(lambda: body(n & ~3, 2))
    pl.when((n & 1) != 0)(lambda: body(n & ~1, 1))


def reset(m_ref, l_ref, acc_ref):
    m_ref[...] = jnp.full(m_ref.shape, MASKED, f32)
    l_ref[...] = jnp.zeros(l_ref.shape, f32)
    acc_ref[...] = jnp.zeros(acc_ref.shape, f32)


def soften(p, scores, values_t, m_ref, l_ref, acc_ref):
    before = m_ref[p, 0:1, :]
    peak = jnp.maximum(before, jnp.max(scores, axis=0, keepdims=True))
    shrink = jnp.exp(before - peak)
    raised = jnp.exp(scores - peak)
    m_ref[p, 0:1, :] = peak
    l_ref[p, 0:1, :] = l_ref[p, 0:1, :] * shrink + jnp.sum(raised, axis=0, keepdims=True)
    acc_ref[p] = acc_ref[p] * own_rows(shrink) + diagonal(nn(values_t, raised.astype(bf16)))


def settle(p, alive, m_ref, l_ref, acc_ref):
    total = l_ref[p, 0:1, :]
    mixed = jnp.transpose(acc_ref[p] * own_rows(alive / total))
    return mixed.astype(bf16), m_ref[p, 0:1, :] + jnp.log(total)


def inner_row(grads, mixed):
    product = jnp.transpose(grads.astype(f32) * mixed.astype(f32))
    return jnp.concatenate(
        [jnp.sum(product[:64], axis=0, keepdims=True), jnp.sum(product[64:], axis=0, keepdims=True)], axis=1
    )


def rms_scale(value):
    return lax.rsqrt(jnp.mean(value * value, axis=-1, keepdims=True) + EPS)


def rms_back(value, gain, grad):
    scale = rms_scale(value)
    weighted = grad * gain
    inner = jnp.mean(weighted * value, axis=-1, keepdims=True)
    unit = value * scale
    return (
        scale * weighted - unit * (scale * scale * inner),
        jnp.sum(grad * unit, axis=0, keepdims=True),
    )


def fill_bias(table_ref, bias_ref):
    key = lax.broadcasted_iota(jnp.int32, (BLK, BLK), 0)
    query = lax.broadcasted_iota(jnp.int32, (BLK, BLK), 1)
    for d in range(2):
        gap = d * BLK + query - key
        tiles = [jnp.full((BLK, BLK), table_ref[h, 0], f32) for h in range(4)]
        for level in range(1, NB):
            reached = gap >= THRESHOLDS[level]
            tiles = [jnp.where(reached, table_ref[h, level], tiles[h]) for h in range(4)]
        if d == 0:
            tiles = [jnp.where(gap >= 0, tile, MASKED) for tile in tiles]
        for h in range(4):
            bias_ref[d * 2 + h // 2, :, (h % 2) * BLK : (h % 2 + 1) * BLK] = tiles[h]
    for h in range(4):
        far = jnp.full((BLK, BLK), table_ref[h, NB - 1], f32)
        bias_ref[4 + h // 2, :, (h % 2) * BLK : (h % 2 + 1) * BLK] = far


def self_scores(distances, p, kstart, qs_ref, k_ref, bias_ref, start2):
    m = len(distances)
    keys = k_ref[pl.ds(kstart, m * BLK), p * BLK : (p + 1) * BLK]
    scores = nt(keys, qs_ref[p])
    parts = [scores[k * BLK : (k + 1) * BLK] + bias_ref[2 * d + p] for k, d in enumerate(distances)]
    index = kstart + lax.broadcasted_iota(jnp.int32, (m * BLK, 2 * BLK), 0)
    return jnp.where(index >= start2, jnp.concatenate(parts, axis=0) if m > 1 else parts[0], MASKED)


def self_spans(b, ends, live):
    pos = b * BLK
    first = lax.shift_right_logical(lookup(pos, ends, ends, 0), 7)
    return pos < live, first, b - first + 1


def self_forward(half, ends, live, q_ref, k_ref, vt_ref, bias_ref, start_ref, o_ref, lse_ref, qs_ref, m_ref, l_ref, acc_ref):
    def step(i, carry):
        b = half * 4 + i
        alive, first, n = self_spans(b, ends, live)
        rows = pl.ds(pl.multiple_of(i * BLK, BLK), BLK)

        @pl.when(alive)
        def _():
            start2 = twice(start_ref[pl.ds(b, 1), :])
            for p in range(2):
                lanes = slice(p * BLK, (p + 1) * BLK)
                qs_ref[p] = stacked(q_ref[pl.ds(pl.multiple_of(b * BLK, BLK), BLK), lanes])
            reset(m_ref, l_ref, acc_ref)

            def chunk(j, m):
                kstart = pl.multiple_of((first + j) * BLK, BLK)
                distances = [jnp.minimum(n - 1 - j - k, 2) for k in range(m)]
                for p in range(2):
                    scores = self_scores(distances, p, kstart, qs_ref, k_ref, bias_ref, start2)
                    values_t = vt_ref[p * BLK : (p + 1) * BLK, pl.ds(kstart, m * BLK)]
                    soften(p, scores, values_t, m_ref, l_ref, acc_ref)

            in_chunks(n, chunk)
            for p in range(2):
                mixed, lse = settle(p, (start2 < BIG).astype(f32), m_ref, l_ref, acc_ref)
                o_ref[rows, p * BLK : (p + 1) * BLK] = mixed
                lse_ref[p, pl.ds(i, 1), :] = lse

        @pl.when(jnp.logical_not(alive))
        def _():
            o_ref[rows, :] = jnp.zeros((BLK, OWN), bf16)
            for p in range(2):
                lse_ref[p, pl.ds(i, 1), :] = jnp.zeros((1, 2 * BLK), f32)

        return carry

    lax.fori_loop(0, 4, step, 0)


def set_starts(ends, live, start_ref):
    pos = token_positions()
    start_ref[...] = jnp.where(pos < live, lookup(pos, ends, ends, 0), BIG)


def first_kernel(
    io, t_ref, len_ref, cnt_ref, table_ref,
    x_ref, gain_ref, wq_ref, wk_ref, wv_ref,
    n1_ref, q_ref, k_ref, v_ref, vt_ref, kt_ref, bias_ref, o_ref, lse_ref,
    start_ref, *work,
):
    ends = running_ends(len_ref)
    live = live_tokens(ends, cnt_ref[0])
    set_starts(ends, live, start_ref)
    fill_bias(table_ref, bias_ref)
    io.done(bias_ref)
    io.ready(x_ref, gain_ref, wq_ref, wk_ref, wv_ref)

    def project(i, carry):
        rows = pl.ds(pl.multiple_of(i * 256, 256), 256)
        value = x_ref[rows, :].astype(f32)
        low = (value * rms_scale(value) * gain_ref[...]).astype(bf16)
        n1_ref[rows, :] = low
        q_ref[rows, :] = nn(low, wq_ref[...]).astype(bf16)
        keys = nn(low, wk_ref[...])
        k_ref[rows, :] = keys.astype(bf16)
        kt_ref[:, rows] = jnp.transpose(keys).astype(bf16)
        values = nn(low, wv_ref[...])
        v_ref[rows, :] = values.astype(bf16)
        vt_ref[:, rows] = jnp.transpose(values).astype(bf16)
        return carry

    lax.fori_loop(0, 4, project, 0)
    io.done(n1_ref, q_ref, k_ref, v_ref, vt_ref, kt_ref)
    self_forward(
        1 - t_ref[0], ends, live, q_ref, k_ref, vt_ref, bias_ref, start_ref, o_ref, lse_ref, *work
    )


def second_kernel(
    io, t_ref, len_ref, cnt_ref,
    q_ref, k_ref, vt_ref, bias_ref,
    o_ref, lse_ref,
    start_ref, *work,
):
    ends = running_ends(len_ref)
    live = live_tokens(ends, cnt_ref[0])
    set_starts(ends, live, start_ref)
    io.ready(q_ref, k_ref, vt_ref, bias_ref)
    self_forward(
        t_ref[0], ends, live, q_ref, k_ref, vt_ref, bias_ref, start_ref, o_ref, lse_ref, *work
    )


def memory_kernel(
    io, place_ref, mem_ref, ck_ref, cv_ref, pack_ref, packo_ref,
    mk_ref, mv_ref, mkt_ref, mvt_ref, so_out, co_out, cq_out, cko_ref, cvo_ref,
):
    for core, pack in ((place_ref[1], pack_ref), (1 - place_ref[1], packo_ref)):
        for ref, parts in zip((so_out, co_out, cq_out, cko_ref, cvo_ref), packed_parts(core), strict=True):
            for rows, where in parts:
                ref[rows, :] = pack[where]
    io.done(so_out, co_out, cq_out, cko_ref, cvo_ref)
    io.ready(mem_ref, ck_ref, cv_ref)

    def project(i, carry):
        rows = pl.ds(pl.multiple_of(i * 256, 256), 256)
        value = mem_ref[rows, :]
        for side, (wk, wv) in enumerate(((ck_ref, cv_ref), (cko_ref, cvo_ref))):
            lanes = slice(side * OWN, (side + 1) * OWN)
            keys = nn(value, wk[...])
            mk_ref[rows, lanes] = keys.astype(bf16)
            mkt_ref[lanes, rows] = jnp.transpose(keys).astype(bf16)
            values = nn(value, wv[...])
            mv_ref[rows, lanes] = values.astype(bf16)
            mvt_ref[lanes, rows] = jnp.transpose(values).astype(bf16)
        return carry

    lax.fori_loop(0, 4, project, 0)


def set_ranges(ends, mends, live, low_ref, high_ref):
    pos = token_positions()
    low_ref[...] = jnp.where(pos < live, lookup(pos, ends, mends, 0), BIG)
    high_ref[...] = lookup(pos, ends, mends[1:], mends[0])


def cross_blocks(half, ends, mends, live, block, dead):
    def step(i, carry):
        b = half * 4 + i
        pos = b * BLK
        alive = pos < live
        last = jnp.minimum(pos + BLK, live) - 1
        first = lax.shift_right_logical(lookup(pos, ends, mends, 0), 7)
        end = lax.shift_right_logical(lookup(last, ends, mends[1:], mends[0]) + BLK - 1, 7)
        pl.when(alive)(lambda: block(i, b, first, end - first))
        pl.when(jnp.logical_not(alive))(lambda: dead(i))
        return carry

    lax.fori_loop(0, 4, step, 0)


def cross_allowed(kstart, m, low2, high2):
    index = kstart + lax.broadcasted_iota(jnp.int32, (m * BLK, 2 * BLK), 0)
    return (index >= low2) & (index < high2)


def third_kernel(
    io, t_ref, len_ref, mlen_ref, cnt_ref,
    x_ref, keep_ref, recv_ref, so_ref, soo_ref, gain2_ref, cq_ref, cqo_ref,
    mk_ref, mvt_ref, co_ref, coo_ref, gain3_ref,
    h1_ref, n2_ref, q_ref, mixed_ref, lse_ref, h2_ref, n3_ref,
    low_ref, high_ref, qs_ref, m_ref, l_ref, acc_ref,
):
    t = t_ref[0]
    ends, mends = running_ends(len_ref), running_ends(mlen_ref)
    live = live_tokens(ends, cnt_ref[0])
    set_ranges(ends, mends, live, low_ref, high_ref)

    io.ready(x_ref, keep_ref, recv_ref, so_ref, soo_ref, gain2_ref, cq_ref, cqo_ref)

    def before(i, carry):
        rows = pl.ds(pl.multiple_of(i * 256, 256), 256)
        value = x_ref[rows, :].astype(f32)
        value = value + nn(keep_ref[rows, :], so_ref[...]) + nn(recv_ref[rows, :], soo_ref[...])
        h1_ref[rows, :] = value
        low = (value * rms_scale(value) * gain2_ref[...]).astype(bf16)
        n2_ref[rows, :] = low
        q_ref[rows, :OWN] = nn(low, cq_ref[...]).astype(bf16)
        q_ref[rows, OWN:] = nn(low, cqo_ref[...]).astype(bf16)
        return carry

    lax.fori_loop(0, 2, before, 0)
    io.done(h1_ref, n2_ref, q_ref)
    io.ready(mk_ref, mvt_ref)

    def block(i, b, first, n):
        low2, high2 = twice(low_ref[pl.ds(b, 1), :]), twice(high_ref[pl.ds(b, 1), :])
        rows = pl.ds(pl.multiple_of(i * BLK, BLK), BLK)
        for p in range(4):
            qs_ref[p] = stacked(q_ref[rows, p * BLK : (p + 1) * BLK])
        reset(m_ref, l_ref, acc_ref)

        def chunk(j, m):
            kstart = pl.multiple_of((first + j) * BLK, BLK)
            span = pl.ds(kstart, m * BLK)
            allowed = cross_allowed(kstart, m, low2, high2)
            for p in range(4):
                lanes = slice(p * BLK, (p + 1) * BLK)
                scores = jnp.where(allowed, nt(mk_ref[span, lanes], qs_ref[p]), MASKED)
                soften(p, scores, mvt_ref[lanes, span], m_ref, l_ref, acc_ref)

        in_chunks(n, chunk)
        for p in range(4):
            mixed, lse = settle(p, (low2 < BIG).astype(f32), m_ref, l_ref, acc_ref)
            mixed_ref[rows, p * BLK : (p + 1) * BLK] = mixed
            lse_ref[p, pl.ds(i, 1), :] = lse

    def dead(i):
        mixed_ref[pl.ds(pl.multiple_of(i * BLK, BLK), BLK), :] = jnp.zeros((BLK, WIDTH), bf16)
        for p in range(4):
            lse_ref[p, pl.ds(i, 1), :] = jnp.zeros((1, 2 * BLK), f32)

    cross_blocks(t, ends, mends, live, block, dead)

    io.done(mixed_ref, lse_ref)
    io.ready(co_ref, coo_ref, gain3_ref)

    def after(i, carry):
        rows = pl.ds(pl.multiple_of(i * 256, 256), 256)
        value = h1_ref[rows, :]
        value = value + nn(mixed_ref[rows, :OWN], co_ref[...]) + nn(mixed_ref[rows, OWN:], coo_ref[...])
        h2_ref[rows, :] = value
        n3_ref[rows, :] = (value * rms_scale(value) * gain3_ref[...]).astype(bf16)
        return carry

    lax.fori_loop(0, 2, after, 0)


def feed_kernel(
    io, place_ref, n3_ref, fi_ref, cot_ref, fo_ref,
    out_ref, gn_ref, act_ref, gp_ref,
):
    tile = 256
    n_tiles = fi_ref.shape[1] // tile
    root = math.sqrt(2 / math.pi)
    base = place_ref[0] * HALF
    io.ready(n3_ref, fi_ref, cot_ref, fo_ref)

    def hidden(j, carry):
        lanes = pl.ds(pl.multiple_of(j * tile, tile), tile)
        for i in range(2):
            rows = slice(i * 256, (i + 1) * 256)
            pre = nn(n3_ref[rows, :], fi_ref[:, lanes])
            square = pre * pre
            bent = jnp.tanh(pre * (root + (root * 0.044715) * square))
            gate = 0.5 + 0.5 * bent
            slope = gate + pre * (0.5 - 0.5 * bent * bent) * (root + (root * 0.134145) * square)
            act_ref[rows, lanes] = (pre * gate).astype(bf16)
            grads = nt(cot_ref[pl.ds(pl.multiple_of(base + i * 256, 256), 256), :], fo_ref[lanes, :])
            gp_ref[rows, lanes] = (grads * slope).astype(bf16)
        return carry

    lax.fori_loop(0, n_tiles, hidden, 0)
    io.done(act_ref, gp_ref)

    def outward(i, carry):
        rows = pl.ds(pl.multiple_of(i * 256, 256), 256)
        out_ref[rows, :] = nn(act_ref[rows, :], fo_ref[...]).astype(bf16)
        gn_ref[rows, :] = nt(gp_ref[rows, :], fi_ref[...]).astype(bf16)
        return carry

    lax.fori_loop(0, 2, outward, 0)


def feed_weights_kernel(
    io, place_ref, h2_ref, own_ref, oth_ref, n3_ref, gp_ref, n3o_ref, gpo_ref, act_ref, cot_ref, acto_ref,
    hold_ref, send_ref, outa_ref, outb_ref,
    n3t_ref,
):
    t, c = place_ref[0], place_ref[1]

    def put(core, rows, lanes, grads):
        low = grads.astype(bf16)

        @pl.when(c == core)
        def _():
            hold_ref[rows, lanes] = low

        @pl.when(c != core)
        def _():
            send_ref[rows, lanes] = low

    mine = pl.ds(pl.multiple_of(t * HALF, HALF), HALF)
    theirs = pl.ds(pl.multiple_of((1 - t) * HALF, HALF), HALF)
    io.ready(n3_ref, gp_ref, n3o_ref, gpo_ref)
    n3t_ref[:, :HALF] = jnp.transpose(n3_ref[...].astype(f32)).astype(bf16)
    n3t_ref[:, HALF:] = jnp.transpose(n3o_ref[...].astype(f32)).astype(bf16)
    n_tiles = gp_ref.shape[1] // 256
    for j in range(n_tiles):
        lanes = slice(j * 256, (j + 1) * 256)
        grads = nn(n3t_ref[:, :HALF], gp_ref[:, lanes]) + nn(n3t_ref[:, HALF:], gpo_ref[:, lanes])
        put(0, slice((j // 2) * WIDTH, (j // 2 + 1) * WIDTH), slice((j % 2) * 256, (j % 2 + 1) * 256), grads)
    io.ready(act_ref, cot_ref, acto_ref)
    for j in range(n_tiles):
        lanes = slice(j * 256, (j + 1) * 256)
        grads = tn(act_ref[:, lanes], cot_ref[mine, :]) + tn(acto_ref[:, lanes], cot_ref[theirs, :])
        put(1, lanes, slice(0, WIDTH), grads)
    io.ready(h2_ref, own_ref, oth_ref)
    own = (h2_ref[...] + own_ref[...].astype(f32)).astype(bf16)
    for k, out_ref in enumerate((outa_ref, outb_ref)):

        @pl.when(t == k)
        def _():
            out_ref[...] = own

        @pl.when(t != k)
        def _():
            out_ref[...] = oth_ref[...]


def cross_back_kernel(
    io, t_ref, len_ref, mlen_ref, cnt_ref,
    gn_ref, gnr_ref, h2_ref, gain3_ref, cot_ref, co_ref, coo_ref,
    q_ref, mk_ref, mkt_ref, mv_ref, lse_ref, mixed_ref, cq_ref, cqo_ref, h1_ref, gain2_ref, so_ref, soo_ref,
    gb2_ref, dq_ref, dk_ref, dv_ref, gh1_ref, gb1_ref, gm1_ref, gm1o_ref, gains_ref,
    low_ref, high_ref, live_ref, gm_ref, dk_acc, dv_acc, gh2_ref, qs_ref, gs_ref, acc_ref,
):
    t = t_ref[0]
    ends, mends = running_ends(len_ref), running_ends(mlen_ref)
    live = live_tokens(ends, cnt_ref[0])
    set_ranges(ends, mends, live, low_ref, high_ref)
    alive_rows = t * HALF + lax.broadcasted_iota(jnp.int32, (HALF, BLK), 0)
    live_ref[...] = (alive_rows < live).astype(f32)
    dk_acc[...] = jnp.zeros_like(dk_acc)
    dv_acc[...] = jnp.zeros_like(dv_acc)
    gains_ref[...] = jnp.zeros_like(gains_ref)

    io.ready(gn_ref, gnr_ref, h2_ref, gain3_ref, cot_ref, co_ref, coo_ref)
    for i in range(2):
        rows = slice(i * 256, (i + 1) * 256)
        grad = gn_ref[rows, :].astype(f32) + gnr_ref[rows, :].astype(f32)
        back, gain = rms_back(h2_ref[rows, :], gain3_ref[...], grad)
        gains_ref[0:1, :] += gain
        grad = cot_ref[rows, :].astype(f32) + back
        gh2_ref[rows, :] = grad
        low = grad.astype(bf16)
        gb2_ref[rows, :] = low
        alive = live_ref[rows, 0:1]
        gm_ref[rows, :OWN] = (nt(low, co_ref[...]) * alive).astype(bf16)
        gm_ref[rows, OWN:] = (nt(low, coo_ref[...]) * alive).astype(bf16)
    io.done(gb2_ref)
    io.ready(q_ref, mk_ref, mkt_ref, mv_ref, lse_ref, mixed_ref)

    def block(i, b, first, n):
        low2, high2 = twice(low_ref[pl.ds(b, 1), :]), twice(high_ref[pl.ds(b, 1), :])
        rows = pl.ds(pl.multiple_of(i * BLK, BLK), BLK)
        inner = []
        for p in range(4):
            lanes = slice(p * BLK, (p + 1) * BLK)
            qs_ref[p] = stacked(q_ref[rows, lanes])
            gs_ref[p] = stacked(gm_ref[rows, lanes])
            inner.append(inner_row(gm_ref[rows, lanes], mixed_ref[rows, lanes]))
        acc_ref[...] = jnp.zeros(acc_ref.shape, f32)

        def chunk(j, m):
            kstart = pl.multiple_of((first + j) * BLK, BLK)
            span = pl.ds(kstart, m * BLK)
            allowed = cross_allowed(kstart, m, low2, high2)
            for p in range(4):
                lanes = slice(p * BLK, (p + 1) * BLK)
                scores = jnp.where(allowed, nt(mk_ref[span, lanes], qs_ref[p]), MASKED)
                probs = jnp.exp(scores - lse_ref[p, pl.ds(i, 1), :])
                low = (probs * (nt(mv_ref[span, lanes], gs_ref[p]) - inner[p])).astype(bf16)
                dk_acc[span, lanes] += nn(low, qs_ref[p])
                dv_acc[span, lanes] += nn(probs.astype(bf16), gs_ref[p])
                acc_ref[p] += diagonal(nn(mkt_ref[lanes, span], low))

        in_chunks(n, chunk)
        for p in range(4):
            dq_ref[rows, p * BLK : (p + 1) * BLK] = jnp.transpose(acc_ref[p]).astype(bf16)

    def dead(i):
        dq_ref[pl.ds(pl.multiple_of(i * BLK, BLK), BLK), :] = jnp.zeros((BLK, WIDTH), bf16)

    cross_blocks(t, ends, mends, live, block, dead)

    dk_ref[...] = dk_acc[...].astype(bf16)
    dv_ref[...] = dv_acc[...].astype(bf16)
    io.done(dq_ref, dk_ref, dv_ref)
    io.ready(cq_ref, cqo_ref, h1_ref, gain2_ref, so_ref, soo_ref)
    for i in range(2):
        rows = slice(i * 256, (i + 1) * 256)
        grad = nt(dq_ref[rows, :OWN], cq_ref[...]) + nt(dq_ref[rows, OWN:], cqo_ref[...])
        back, gain = rms_back(h1_ref[rows, :], gain2_ref[...], grad)
        gains_ref[1:2, :] += gain
        grad = gh2_ref[rows, :] + back
        gh1_ref[rows, :] = grad
        low = grad.astype(bf16)
        gb1_ref[rows, :] = low
        alive = live_ref[rows, 0:1]
        gm1_ref[rows, :] = (nt(low, so_ref[...]) * alive).astype(bf16)
        gm1o_ref[rows, :] = (nt(low, soo_ref[...]) * alive).astype(bf16)


def cross_weights_kernel(
    io, place_ref, mem_ref, dk_ref, dv_ref, n2_ref, dq_ref, mixed_ref, gb2_ref, keep_ref, gb1_ref, recv_ref,
    hold_ref, holdo_ref, send_ref,
    memt_ref, fold_ref,
):
    c = place_ref[1]
    io.ready(mem_ref, dk_ref, dv_ref, n2_ref, dq_ref, mixed_ref, gb2_ref, keep_ref, gb1_ref, recv_ref)
    memt_ref[...] = jnp.transpose(mem_ref[...].astype(f32)).astype(bf16)
    n2t = jnp.transpose(n2_ref[...].astype(f32)).astype(bf16)
    for side in range(2):
        lanes = slice(side * OWN, (side + 1) * OWN)
        mixed1 = keep_ref if side == 0 else recv_ref
        fold_ref[0] = tn(mixed_ref[:, lanes], gb2_ref[...]).astype(bf16)
        fold_ref[1] = tn(mixed1[...], gb1_ref[...]).astype(bf16)
        fold(fold_ref, 2, nn(n2t, dq_ref[:, lanes]))
        fold(fold_ref, 3, nn(memt_ref[...], dk_ref[:, lanes]))
        fold(fold_ref, 4, nn(memt_ref[...], dv_ref[:, lanes]))
        deal(c, fold_ref, hold_ref if side == 0 else holdo_ref, send_ref, side * 640)


def memory_back_kernel(
    io, place_ref, dk_ref, ck_ref, cko_ref, dv_ref, cv_ref, cvo_ref, gmem_ref, gmems_ref
):
    t = place_ref[0]
    io.ready(dk_ref, ck_ref, cko_ref, dv_ref, cv_ref, cvo_ref)
    for i in range(4):
        rows = slice(i * 256, (i + 1) * 256)
        grads = nt(dk_ref[rows, :OWN], ck_ref[...]) + nt(dk_ref[rows, OWN:], cko_ref[...])
        grads += nt(dv_ref[rows, :OWN], cv_ref[...]) + nt(dv_ref[rows, OWN:], cvo_ref[...])
        low = grads.astype(bf16)

        @pl.when(t == 0)
        def _():
            gmem_ref[rows, :] = low[:, :OWN]
            gmems_ref[rows, :] = low[:, OWN:]

        @pl.when(t != 0)
        def _():
            gmem_ref[rows, :] = low[:, OWN:]
            gmems_ref[rows, :] = low[:, :OWN]


def fold(fold_ref, k, weight):
    low = weight.astype(bf16)
    fold_ref[k, :, :OWN] = low[:256]
    fold_ref[k, :, OWN:] = low[256:]


def deal(c, fold_ref, hold_ref, send_ref, base):
    for k in range(fold_ref.shape[0]):
        rows = slice(k * BLK, (k + 1) * BLK)
        hold_ref[rows, :] = fold_ref[k, pl.ds(pl.multiple_of(c * BLK, BLK), BLK), :]
        rows = slice(base + k * BLK, base + (k + 1) * BLK)
        send_ref[rows, :] = fold_ref[k, pl.ds(pl.multiple_of((1 - c) * BLK, BLK), BLK), :]


def self_back_blocks(
    half, ends, live, start_ref, g_ref, mixed_ref, q_ref, k_ref, kt_ref, v_ref, bias_ref, lse_ref,
    dq_ref, dk_acc, dv_acc, near_acc, qs_ref, gs_ref, acc_ref,
):
    def step(i, carry):
        b = half * 4 + i
        alive, first, n = self_spans(b, ends, live)
        rows = pl.ds(pl.multiple_of(i * BLK, BLK), BLK)

        @pl.when(alive)
        def _():
            start2 = twice(start_ref[pl.ds(b, 1), :])
            inner = []
            for p in range(2):
                lanes = slice(p * BLK, (p + 1) * BLK)
                qs_ref[p] = stacked(q_ref[pl.ds(pl.multiple_of(b * BLK, BLK), BLK), lanes])
                gs_ref[p] = stacked(g_ref[rows, lanes])
                inner.append(inner_row(g_ref[rows, lanes], mixed_ref[rows, lanes]))
            acc_ref[...] = jnp.zeros(acc_ref.shape, f32)

            def chunk(j, m):
                kstart = pl.multiple_of((first + j) * BLK, BLK)
                span = pl.ds(kstart, m * BLK)
                distances = [jnp.minimum(n - 1 - j - k, 2) for k in range(m)]
                for p in range(2):
                    lanes = slice(p * BLK, (p + 1) * BLK)
                    scores = self_scores(distances, p, kstart, qs_ref, k_ref, bias_ref, start2)
                    probs = jnp.exp(scores - lse_ref[p, pl.ds(i, 1), :])
                    grad_scores = probs * (nt(v_ref[span, lanes], gs_ref[p]) - inner[p])
                    for k, d in enumerate(distances):
                        near_acc[2 * d + p] += grad_scores[k * BLK : (k + 1) * BLK]
                    low = grad_scores.astype(bf16)
                    dk_acc[span, lanes] += nn(low, qs_ref[p])
                    dv_acc[span, lanes] += nn(probs.astype(bf16), gs_ref[p])
                    acc_ref[p] += diagonal(nn(kt_ref[lanes, span], low))

            in_chunks(n, chunk)
            for p in range(2):
                dq_ref[rows, p * BLK : (p + 1) * BLK] = jnp.transpose(acc_ref[p]).astype(bf16)

        @pl.when(jnp.logical_not(alive))
        def _():
            dq_ref[rows, :] = jnp.zeros((BLK, OWN), bf16)

        return carry

    lax.fori_loop(0, 4, step, 0)


def self_back_own_kernel(
    io, place_ref, len_ref, cnt_ref,
    gm_ref, mixed_ref, q_ref, k_ref, kt_ref, v_ref, bias_ref, lse_ref,
    dq_ref, dk_acc, dv_acc, near_acc,
    start_ref, *work,
):
    ends = running_ends(len_ref)
    live = live_tokens(ends, cnt_ref[0])
    set_starts(ends, live, start_ref)
    for ref in (dk_acc, dv_acc, near_acc):
        ref[...] = jnp.zeros_like(ref)
    io.ready(gm_ref, mixed_ref, q_ref, k_ref, kt_ref, v_ref, bias_ref, lse_ref)
    self_back_blocks(
        place_ref[0], ends, live, start_ref, gm_ref, mixed_ref, q_ref, k_ref, kt_ref, v_ref, bias_ref, lse_ref,
        dq_ref, dk_acc, dv_acc, near_acc, *work,
    )


def self_back_kernel(
    io, place_ref, len_ref, cnt_ref,
    gmr_ref, mixed_ref, dqm_ref, dkm_ref, dvm_ref, nearm_ref, q_ref, k_ref, kt_ref, v_ref, bias_ref, lse_ref,
    n1_ref, x_ref, gh1_ref, gain1_ref, gains_ref, wq_ref, wk_ref, wv_ref,
    hold_ref, send_ref, gia_ref, gib_ref,
    start_ref, dqo_ref, dq_ref, dk_acc, dv_acc, near_acc, n1t_ref, fold_ref, sums_ref, small_ref, *work,
):
    t = place_ref[0]
    ends = running_ends(len_ref)
    live = live_tokens(ends, cnt_ref[0])
    set_starts(ends, live, start_ref)
    small_ref[...] = jnp.zeros_like(small_ref)
    for ref, so_far in ((dk_acc, dkm_ref), (dv_acc, dvm_ref), (near_acc, nearm_ref)):
        ref[...] = so_far[...]
    io.ready(mixed_ref, q_ref, k_ref, kt_ref, v_ref, bias_ref, lse_ref)
    self_back_blocks(
        1 - t, ends, live, start_ref, gmr_ref, mixed_ref, q_ref, k_ref, kt_ref, v_ref, bias_ref, lse_ref,
        dqo_ref, dk_acc, dv_acc, near_acc, *work,
    )
    dq_ref[pl.ds(pl.multiple_of(t * HALF, HALF), HALF), :] = dqm_ref[...]
    dq_ref[pl.ds(pl.multiple_of((1 - t) * HALF, HALF), HALF), :] = dqo_ref[...]

    io.ready(n1_ref)
    n1t_ref[...] = jnp.transpose(n1_ref[...].astype(f32)).astype(bf16)
    low_k, low_v = dk_acc[...].astype(bf16), dv_acc[...].astype(bf16)
    for k, grads in enumerate((dq_ref[...], low_k, low_v)):
        fold(fold_ref, k, nn(n1t_ref[...], grads))
    deal(place_ref[1], fold_ref, hold_ref, send_ref, 0)
    io.ready(x_ref, gh1_ref, gain1_ref, gains_ref, wq_ref, wk_ref, wv_ref)
    gain1 = jnp.zeros((1, WIDTH), f32)
    for i in range(4):
        rows = slice(i * 256, (i + 1) * 256)
        grads = nt(dq_ref[rows, :], wq_ref[...]) + nt(low_k[rows], wk_ref[...]) + nt(low_v[rows], wv_ref[...])
        back, gain = rms_back(x_ref[rows, :].astype(f32), gain1_ref[...], grads)
        gain1 += gain
        mine = (t == i // 2).astype(f32)
        back += mine * gh1_ref[(i % 2) * 256 : (i % 2 + 1) * 256, :]
        (gia_ref if i < 2 else gib_ref)[(i % 2) * 256 : (i % 2 + 1) * 256, :] = back.astype(bf16)
    io.done(gia_ref, gib_ref)
    key = lax.broadcasted_iota(jnp.int32, (BLK, BLK), 0)
    query = lax.broadcasted_iota(jnp.int32, (BLK, BLK), 1)
    gaps = [query - key, BLK + query - key]
    for level in range(NB):
        for p in range(2):
            row = jnp.zeros((1, 2 * BLK), f32)
            for d in range(2):
                inside = gaps[d] >= THRESHOLDS[level]
                if level + 1 < NB:
                    inside &= gaps[d] < THRESHOLDS[level + 1]
                picked = jnp.where(twice(inside.astype(f32)) > 0, near_acc[2 * d + p], 0.0)
                row += jnp.sum(picked, axis=0, keepdims=True)
            if level == NB - 1:
                row += jnp.sum(near_acc[4 + p], axis=0, keepdims=True)
            sums_ref[level : level + 1, p * 256 : (p + 1) * 256] = row
    for h in range(4):
        lanes = jnp.transpose(sums_ref[:, h * BLK : (h + 1) * BLK])
        small_ref[3 + h : 4 + h, :NB] = jnp.sum(lanes, axis=0, keepdims=True)
    for k, gain in enumerate((gain1, gains_ref[1:2, :], gains_ref[0:1, :])):
        small_ref[k : k + 1, :] = gain
    low = small_ref[...].astype(bf16)
    hold_ref[384:, :] = low
    send_ref[384:, :] = low


def join_kernel(io, place_ref, own_ref, got_ref, recv_ref, mine_ref, theirs_ref, hold_ref, send_ref):
    x = place_ref[2]
    io.ready(own_ref, got_ref, recv_ref, mine_ref, theirs_ref)
    for k in range(8):
        if k < 5:
            rows = slice(k * BLK, (k + 1) * BLK)
            total = own_ref[rows, :].astype(f32) + got_ref[rows, :].astype(f32) + recv_ref[rows, :].astype(f32)
        else:
            rows = slice((k - 5) * BLK, (k - 4) * BLK)
            total = mine_ref[rows, :].astype(f32) + theirs_ref[rows, :].astype(f32)
        low = total.astype(bf16)
        rows = slice((k % 4) * BLK, (k % 4 + 1) * BLK)

        @pl.when(x == k // 4)
        def _():
            hold_ref[rows, :] = low

        @pl.when(x != k // 4)
        def _():
            send_ref[rows, :] = low

    low = (mine_ref[384:, :].astype(f32) + theirs_ref[384:, :].astype(f32)).astype(bf16)
    hold_ref[HALF:, :] = low
    send_ref[HALF:, :] = low


def halve_kernel(slot, every, io, place_ref, hold_ref, got_ref, keep_ref, send_ref):
    bit, size = place_ref[slot], keep_ref.shape[0] - every
    io.ready(hold_ref, got_ref)
    for k in range(2):
        rows = slice(k * size, (k + 1) * size)
        low = (hold_ref[rows, :].astype(f32) + got_ref[rows, :].astype(f32)).astype(bf16)

        @pl.when(bit == k)
        def _():
            keep_ref[:size, :] = low

        @pl.when(bit != k)
        def _():
            send_ref[:size, :] = low

    if every:
        low = (hold_ref[2 * size :, :].astype(f32) + got_ref[2 * size :, :].astype(f32)).astype(bf16)
        keep_ref[size:, :] = low
        send_ref[size:, :] = low


def total_kernel(io, _, hold_ref, got_ref, out_ref, *small_refs):
    io.ready(hold_ref, got_ref)
    total = hold_ref[...].astype(f32) + got_ref[...].astype(f32)
    out_ref[...] = total[: out_ref.shape[0]].astype(bf16)
    for small_ref in small_refs:
        small_ref[...] = total[out_ref.shape[0] :]


def merge_kernel(slot, io, place_ref, own_ref, got_ref, out_ref):
    bit, size = place_ref[slot], own_ref.shape[0]
    io.ready(own_ref, got_ref)
    out_ref[pl.ds(pl.multiple_of(bit * size, size), size), :] = own_ref[...]
    out_ref[pl.ds(pl.multiple_of((1 - bit) * size, size), size), :] = got_ref[...]


def feed_unfold_kernel(io, place_ref, own_ref, pair_ref, core_ref, both_ref, fi_ref, fo_ref):
    c, x = place_ref[1], place_ref[2]
    io.ready(own_ref, pair_ref, core_ref, both_ref)
    for ref, core, bit in ((own_ref, c, x), (pair_ref, c, 1 - x), (core_ref, 1 - c, x), (both_ref, 1 - c, 1 - x)):
        at = pl.ds(pl.multiple_of(bit * WIDTH, WIDTH), WIDTH)

        @pl.when(core == 0)
        def _():
            fi_ref[:, at] = ref[...].astype(f32)

        @pl.when(core != 0)
        def _():
            fo_ref[at, :] = ref[...].astype(f32)


def unfold_kernel(
    io, place_ref, own_ref, pair_ref, core_ref, both_ref,
    co_ref, so_ref, cq_ref, ck_ref, cv_ref, wq_ref, wk_ref, wv_ref,
):
    c, x = place_ref[1], place_ref[2]
    outs = (co_ref, so_ref, cq_ref, ck_ref, cv_ref, wq_ref, wk_ref, wv_ref)

    def spread(ref, core, bit):
        low = pl.ds(pl.multiple_of(core * BLK, BLK), BLK)
        high = pl.ds(pl.multiple_of(256 + core * BLK, BLK), BLK)
        for k, out in enumerate(outs):
            rows = slice((k % 4) * BLK, (k % 4 + 1) * BLK)

            @pl.when(bit == k // 4)
            def _():
                if k < 2:
                    out[low, :] = ref[rows, :].astype(f32)
                else:
                    out[low, :] = ref[rows, :OWN].astype(f32)
                    out[high, :] = ref[rows, OWN:].astype(f32)

    for ref, core, bit in ((own_ref, c, x), (pair_ref, c, 1 - x), (core_ref, 1 - c, x), (both_ref, 1 - c, 1 - x)):
        io.ready(ref)
        spread(ref, core, bit)


def swap(value, axis="tensor", bit=0):
    return lax.ppermute(value, axis, [(i, i ^ (1 << bit)) for i in range(lax.axis_size(axis))])


def shards(
    inputs, memory, cotangent, dec_lengths, mem_lengths, counts,
    self_gain, self_query, self_key, self_value, self_out, rel_table,
    cross_gain, cross_query, cross_key, cross_value, cross_out,
    feed_gain, feed_in, feed_out,
):
    v = pltpu.VMEM
    i32 = jnp.int32
    t, c, x = (lax.axis_index(name).astype(i32) for name in ("tensor", "core", "pair"))
    ring = lax.axis_size("ring")
    at_ring = lax.axis_index("ring").astype(i32)
    bits = range(ring.bit_length() - 1)
    ring_bits = [lax.shift_right_logical(at_ring, k) & 1 for k in bits]
    place = jnp.stack([t, c, x, *ring_bits])
    place_oth = jnp.stack([1 - t, c, x, *ring_bits])

    def halve(hold, got, slot, every=0):
        shape = (((hold.shape[0] - every) // 2 + every, WIDTH), bf16, "near")
        return call(
            functools.partial(halve_kernel, slot, every), [shape, shape], [], (place, Near(hold), Near(got)), us=SHORT
        )

    def merge(own, got, slot):
        shape = ((2 * own.shape[0], WIDTH), bf16, "near")
        return call(functools.partial(merge_kernel, slot), [shape], [], (place, Near(own), Near(got)), us=SHORT)[0]

    def tie(*arrays):
        return lax.optimization_barrier(arrays)
    gain1, gain2, gain3 = (g.reshape(1, WIDTH) for g in (self_gain, cross_gain, feed_gain))
    table = rel_table.T

    tok = (LEN, WIDTH)
    half = (HALF, WIDTH)
    heads, heads_t, part = (LEN, OWN), (OWN, LEN), (HALF, OWN)
    narrow, wide = (OWN, WIDTH), (WIDTH, OWN)
    row_tile = v((LEN // BLK, BLK), i32)
    tiles = ((6, BLK, 2 * BLK), f32)

    def forward_work(n):
        rows = v((n, 8, 2 * BLK), f32)
        return [v((n, 2 * BLK, BLK), bf16), rows, rows, v((n, BLK, BLK), f32)]

    def backward_work(n):
        return [v((n, 2 * BLK, BLK), bf16), v((n, 2 * BLK, BLK), bf16), v((n, BLK, BLK), f32)]

    pack, x_near, gain1_near, wq, wk, wv = call(
        pack_kernel,
        [((PACKED, WIDTH), bf16, "near")],
        [pltpu.SemaphoreType.DMA((6,))],
        (place, *map(Raw, (self_out, cross_out, cross_query, cross_key, cross_value))),
        us=SHORT, fetch=(inputs, gain1, self_query, self_key, self_value),
    )
    pack = swap(pack)
    n1, q, q_far, k, k_far, val, vt, kt, bias, bias_far, send1, lse1_oth = call(
        first_kernel,
        [(tok, bf16, "far"), (heads, bf16, "both"), (heads, bf16, "both"), (heads, bf16, "far"),
         (heads_t, bf16, "near"), (heads_t, bf16, "far"), (*tiles, "both"), (part, bf16, "near"),
         ((2, 4, 2 * BLK), f32, "near")],
        [row_tile, *forward_work(2)],
        (place, dec_lengths, counts, table, *map(Near, (x_near, gain1_near, wq, wk, wv))),
        smem=4, us=6,
    )
    mixed1_recv = swap(send1)
    mixed1_keep, lse1, memory_near, ck, cv, lse1_oth, send_far = call(
        second_kernel,
        [(part, bf16, "near"), ((2, 4, 2 * BLK), f32, "near")],
        [row_tile, *forward_work(2)],
        (place, dec_lengths, counts, Near(q), Near(k), Near(vt), Near(bias)),
        smem=3, us=SHORT, fetch=(memory, cross_key, cross_value), forward=(lse1_oth, send1),
    )
    pack, mixed1_keep = lax.optimization_barrier((pack, mixed1_keep))
    pack_core = swap(pack, "core")
    mk, mv, mkt, mvt, so_oth, co_oth, cq_oth, ck_oth, cv_oth, x_half, so, gain2_near, cq_w, co, gain3_near, keep_far, lse1 = call(
        memory_kernel,
        [(tok, bf16, "near"), (tok, bf16, "near"), ((WIDTH, LEN), bf16, "near"), ((WIDTH, LEN), bf16, "near"),
         (narrow, bf16, "near"), (narrow, bf16, "near"), (wide, bf16, "near"), (wide, bf16, "near"), (wide, bf16, "near")],
        [],
        (place, *map(Near, (memory_near, ck, cv, pack, pack_core))),
        us=SHORT, fetch=(Half(inputs), self_out, gain2, cross_query, cross_out, gain3), forward=(mixed1_keep, lse1),
    )
    (h1, n2, cq, mixed2, lse2, h2, n3, fi, cot, fo,
     mk, mv, mkt, so_oth_far, co_oth_far, cq_oth_far, ck_oth, cv_oth, recv_far) = call(
        third_kernel,
        [(half, f32, "far"), (half, bf16, "far"), (half, bf16, "far"), (half, bf16, "far"),
         ((4, 4, 2 * BLK), f32, "far"), (half, f32, "near"), (half, bf16, "near")],
        [row_tile, row_tile, *forward_work(4)],
        (place, dec_lengths, mem_lengths, counts,
         *map(Near, (x_half, mixed1_keep, mixed1_recv, so, so_oth, gain2_near, cq_w, cq_oth, mk, mvt, co, co_oth, gain3_near))),
        smem=4, us=9,
        fetch=(feed_in, cotangent, feed_out),
        forward=(mk, mv, mkt, so_oth, co_oth, cq_oth, ck_oth, cv_oth, mixed1_recv),
    )
    n3_recv = swap(n3)

    hidden = feed_in.shape[1]
    units = (HALF, hidden)
    out_own, gn3_own, act, gp, h2_far, n3_far = call(
        feed_kernel,
        [(half, bf16, "far"), (half, bf16, "far"), (units, bf16, "far"), (units, bf16, "far")],
        [],
        (place, *map(Near, (n3, fi, cot, fo))),
        us=5, forward=(h2, n3),
    )
    h2 = h2_far
    n3_recv, act = lax.optimization_barrier((n3_recv, act))
    out_oth, gn3_oth, act_oth, gp_oth = call(
        feed_kernel,
        [(half, bf16, "near"), (half, bf16, "near"), (units, bf16, "near"), (units, bf16, "near")],
        [],
        (place_oth, *map(Near, (n3_recv, fi, cot, fo))),
        us=5,
    )
    gn3_recv = swap(gn3_oth)
    blocks = ((2 * WIDTH, WIDTH), bf16, "near")
    feed_hold, feed_send, out_a, out_b = call(
        feed_weights_kernel,
        [blocks, blocks, (half, bf16, "far"), (half, bf16, "far")],
        [v((WIDTH, LEN), bf16)],
        (place, h2, out_own, Near(out_oth), n3_far, gp, Near(n3_recv), Near(gp_oth), act, Near(cot), Near(act_oth)),
        us=5,
    )
    feed_got = swap(feed_send, "core")

    (gb2, dcq, dmk, dmv, gh1, gb1, gm1, gm1_oth, gains, memory_near, n2_near, mixed2_near, keep, recv) = call(
        cross_back_kernel,
        [(half, bf16, "near"), (half, bf16, "near"), (tok, bf16, "near"), (tok, bf16, "near"), (half, f32, "near"),
         (half, bf16, "near"), (part, bf16, "near"), (part, bf16, "near"), ((8, WIDTH), f32, "near")],
        [row_tile, row_tile, v((HALF, BLK), f32), v(half, bf16), v(tok, f32), v(tok, f32), v(half, f32), *backward_work(4)],
        (place, dec_lengths, mem_lengths, counts, gn3_own, Near(gn3_recv), h2, gain3, Half(cotangent),
         cross_out, co_oth_far, cq, mk, mkt, mv, lse2, mixed2, cross_query, cq_oth_far, h1, gain2, self_out, so_oth_far),
        smem=4, us=12, fetch=(memory, n2, mixed2, keep_far, recv_far),
    )
    feed_hold, feed_send = halve(feed_hold, feed_got, 2)
    out_a_recv = swap(out_a)
    gb2, feed_send, out_a_recv = tie(gb2, feed_send, out_a_recv)
    feed_got = swap(feed_send, "pair")
    gm1_recv = swap(gm1_oth)
    (cross_hold, cross_hold_oth, cross_send, q, k, kt_near, v_near, bias, lse1_near, lse1_oth_near, sent,
     dmk, dmv) = call(
        cross_weights_kernel,
        [((640, WIDTH), bf16, "near"), ((640, WIDTH), bf16, "near"), ((1280, WIDTH), bf16, "near")],
        [v((WIDTH, LEN), bf16), v((5, 256, WIDTH), bf16)],
        (place, *map(Near, (memory_near, dmk, dmv, n2_near, dcq, mixed2_near, gb2, keep, gb1, recv))),
        us=3, fetch=(q_far, k_far, kt, val, bias_far, lse1, lse1_oth, send_far), forward=(dmk, dmv),
    )
    cross_got = swap(cross_send, "core")
    acc = ((LEN, OWN), f32)
    dq1, dk1, dv1, near1, n1_near, x_near, gain1_near, wq, wk, wv = call(
        self_back_own_kernel,
        [(part, bf16, "near"), (*acc, "near"), (*acc, "near"), (*tiles, "near")],
        [row_tile, *backward_work(2)],
        (place, dec_lengths, counts, *map(Near, (gm1, keep, q, k, kt_near, v_near, bias, lse1_near))),
        smem=3, us=3, fetch=(n1, inputs, gain1, self_query, self_key, self_value),
    )
    cross_recv = swap((cross_hold_oth.astype(f32) + cross_got[640:].astype(f32)).astype(bf16))
    self_hold, self_send, gi_a, gi_b = call(
        self_back_kernel,
        [((384 + SMALL, WIDTH), bf16, "near"), ((384 + SMALL, WIDTH), bf16, "near"),
         (half, bf16, "far"), (half, bf16, "far")],
        [row_tile, v(part, bf16), v(heads, bf16), v(*acc), v(*acc), v(*tiles),
         v((WIDTH, LEN), bf16), v((3, 256, WIDTH), bf16), v((NB, WIDTH), f32), v((SMALL, WIDTH), f32), *backward_work(2)],
        (place, dec_lengths, counts,
         *map(Near, (gm1_recv, sent, dq1, dk1, dv1, near1, q, k, kt_near, v_near, bias, lse1_oth_near,
                     n1_near, x_near, gh1, gain1_near, gains, wq, wk, wv))),
        smem=3, us=3,
    )
    self_got = swap(self_send, "core")
    feed_hold, feed_send = halve(feed_hold, feed_got, 3)
    self_hold, feed_send = tie(self_hold, feed_send)
    feed_got = swap(feed_send, "ring")
    for k in bits[1:]:
        feed_hold, feed_send = halve(feed_hold, feed_got, 3 + k)
        cross_recv, feed_send = tie(cross_recv, feed_send)
        feed_got = swap(feed_send, "ring", k)

    joined = ((HALF + SMALL, WIDTH), bf16, "near")
    hold, send = call(
        join_kernel,
        [joined, joined],
        [],
        (place, *map(Near, (cross_hold, cross_got, cross_recv, self_hold, self_got))),
        us=SHORT,
    )
    got, gi_a_recv = swap(send, "pair"), swap(gi_a)
    (feed_own,) = call(
        total_kernel, [((feed_hold.shape[0], WIDTH), bf16, "near")], [], (place, Near(feed_hold), Near(feed_got)), us=SHORT
    )
    got, feed_own, gi_a_recv = tie(got, feed_own, gi_a_recv)
    hold, send = halve(hold, got, 3, SMALL)
    for k in reversed(bits[1:]):
        feed_own = merge(feed_own, swap(feed_own, "ring", k), 3 + k)
    send, dmk = tie(send, dmk)
    gmem, gmem_send = call(
        memory_back_kernel,
        [(heads, bf16, "far"), (heads, bf16, "near")],
        [],
        (place, dmk, cross_key, ck_oth, dmv, cross_value, cv_oth),
        us=SHORT,
    )
    gi_b_recv, out_b_recv, gmem_recv = swap(gi_b), swap(out_b), swap(gmem_send)
    for k in bits[1:]:
        got = swap(send, "ring", k - 1)
        if k == 1:
            got, gmem_send, feed_own, gi_b_recv = tie(got, gmem_send, feed_own, gi_b_recv)
        hold, send = halve(hold, got, 3 + k, SMALL)
    feed_own = merge(feed_own, swap(feed_own, "ring"), 3)
    got = swap(send, "ring", bits[-1])
    got, feed_own, out_b_recv = tie(got, feed_own, out_b_recv)
    feed_pair, feed_core = swap(feed_own, "pair"), swap(feed_own, "core")
    own, small = call(
        total_kernel,
        [((hold.shape[0] - SMALL, WIDTH), bf16, "near"), ((SMALL, WIDTH), f32, "near")],
        [],
        (place, Near(hold), Near(got)),
        us=SHORT,
    )
    for k in reversed(bits):
        own = merge(own, swap(own, "ring", k), 3 + k)
    own, feed_pair, gmem_recv = tie(own, feed_pair, gmem_recv)
    pair, core_own = swap(own, "pair"), swap(own, "core")
    gain_grads = small[:8] + swap(small[:8])

    def both(part, other):
        return (part.astype(f32) + other.astype(f32)).astype(bf16)

    output = jnp.concatenate([both(out_a, out_a_recv), both(out_b, out_b_recv)])
    grad_inputs = jnp.concatenate([both(gi_a, gi_a_recv), both(gi_b, gi_b_recv)])
    grad_memory = both(gmem, gmem_recv)
    wide_hidden, tall_hidden = ((WIDTH, hidden), f32, "far"), ((hidden, WIDTH), f32, "far")
    feed_in_grad, feed_out_grad = call(
        feed_unfold_kernel,
        [wide_hidden, tall_hidden],
        [],
        (place, *map(Near, (feed_own, feed_pair, feed_core, swap(feed_pair, "core")))),
        us=SHORT,
    )
    pair, output, grad_inputs, grad_memory, feed_in_grad, feed_out_grad = lax.optimization_barrier(
        (pair, output, grad_inputs, grad_memory, feed_in_grad, feed_out_grad)
    )
    narrows, wides = (narrow, f32, "far"), (wide, f32, "far")
    co_grad, so_grad, cq_grad, ck_grad, cv_grad, wq_grad, wk_grad, wv_grad = call(
        unfold_kernel,
        [narrows] * 2 + [wides] * 6,
        [],
        (place, *map(Near, (own, pair, core_own, swap(pair, "core")))),
    )
    return (
        output,
        grad_inputs,
        grad_memory,
        gain_grads[0],
        wq_grad,
        wk_grad,
        wv_grad,
        so_grad,
        small[3:7, :NB].T,
        gain_grads[1],
        cq_grad,
        ck_grad,
        cv_grad,
        co_grad,
        gain_grads[2],
        feed_in_grad,
        feed_out_grad,
    )


def solution(mesh):
    devices = mesh.devices
    rows, tensor = devices.shape
    mesh = Mesh(devices.reshape(rows // 4, 2, 2, tensor), ("ring", "pair", "core", "tensor"))
    dp = ("ring", "pair", "core")
    split = P(dp, None)
    columns, rows = P(None, "tensor"), P("tensor", None)
    return jax.shard_map(
        shards,
        mesh=mesh,
        in_specs=(
            split, split, split, split, split, P(dp),
            P(), columns, columns, columns, rows, columns,
            P(), columns, columns, columns, rows,
            P(), columns, rows,
        ),
        out_specs=(
            split, split, P(dp, "tensor"),
            P(), columns, columns, columns, rows, columns,
            P(), columns, columns, columns, rows,
            P(), columns, rows,
        ),
        check_vma=False,
    )
```

```python
import functools
import math

import jax
import jax.numpy as jnp
from jax import lax
from jax.experimental import pallas as pl
from jax.experimental.pallas import tpu as pltpu
from jax.sharding import Mesh
from jax.sharding import PartitionSpec as P

NB = 32
MAXDIST = 128
SEGS = 16
LEN = 1024
HALF = 512
WIDTH = 512
OWN = 256
BLK = 128
BIG = 1 << 30
MASKED = -1e30
EPS = 1e-06
f32 = jnp.float32
bf16 = jnp.bfloat16
ROOM = 11 * 1024 * 1024
SHORT = 0.05


def thresholds():
    exact = NB // 2
    edges = [
        math.ceil(exact * (MAXDIST / exact) ** (level / (NB - exact)))
        for level in range(1, NB - exact)
    ]
    return list(range(exact + 1)) + edges


THRESHOLDS = thresholds()


def nn(a, b):
    return jnp.dot(a, b, preferred_element_type=f32)


def nt(a, b):
    return lax.dot_general(a, b, (((1,), (1,)), ((), ())), preferred_element_type=f32)


def tn(a, b):
    return lax.dot_general(a, b, (((0,), (0,)), ((), ())), preferred_element_type=f32)


class Half:
    def __init__(self, array):
        self.array = array


class Near:
    def __init__(self, array):
        self.array = array


class Raw:
    def __init__(self, array):
        self.array = array


PACKED = 640
SMALL = 16


def packed_parts(core):
    def at(start, size):
        return pl.ds(pl.multiple_of(start, BLK), size)

    left, right, all_lanes = slice(0, OWN), slice(OWN, WIDTH), slice(0, WIDTH)
    return (
        [(at(core * BLK, BLK), (slice(0, 128), all_lanes))],
        [(at(core * BLK, BLK), (slice(128, 256), all_lanes))],
        [(at(core * 256, 256), (slice(256, 512), left))],
        [(at(core * 256, 256), (slice(256, 512), right))],
        [(at(core * 256, BLK), (slice(512, 640), left)), (at(core * 256 + BLK, BLK), (slice(512, 640), right))],
    )


def pack_kernel(io, place_ref, *refs):
    *weights, pack_ref, sems = refs
    copies = []
    for ref, parts in zip(weights, packed_parts(place_ref[1]), strict=True):
        for rows, where in parts:
            copy = pltpu.make_async_copy(ref.at[rows, :], pack_ref.at[where], sems.at[len(copies)])
            copy.start()
            copies.append(copy)
    for copy in copies:
        copy.wait()


class Copies:
    def __init__(self, sems):
        self.sems, self.used, self.waits, self.out = sems, 0, {}, {}

    def start(self, source, target):
        copy = pltpu.make_async_copy(source, target, self.sems.at[self.used])
        self.used += 1
        copy.start()
        return copy

    def ready(self, *refs):
        for ref in refs:
            for copy in self.waits.pop(id(ref), ()):
                copy.wait()

    def done(self, *refs):
        for ref in refs:
            target, copy = self.out.get(id(ref), (None, True))
            if copy is None:
                self.out[id(ref)] = (target, self.start(ref, target))


def size_of(shape, dtype):
    return math.prod(shape) * jnp.dtype(dtype).itemsize


def call(body, outs, scratch, args, smem=1, us=3, fetch=(), forward=()):
    tables, operands = args[:smem], args[smem:]
    arrays, in_specs, fetched = [], [], []
    hbm, vmem = pl.BlockSpec(memory_space=pltpu.HBM), pl.BlockSpec(memory_space=pltpu.VMEM)

    def shape_of(operand):
        if isinstance(operand, Half):
            return (HALF, *operand.array.shape[1:]), operand.array.dtype
        return operand.shape, operand.dtype

    for operand in (*operands, *fetch, *map(Near, forward)):
        array = operand.array if isinstance(operand, (Near, Raw, Half)) else operand
        near = isinstance(operand, Near)
        arrays.append(array if near else pltpu.with_memory_space_constraint(array, pltpu.HBM))
        in_specs.append(vmem if near else hbm)
    fetched = [shape_of(o) for o in operands if not isinstance(o, (Near, Raw))]
    out_shapes, out_specs, sent = [], [], []
    extra = [(*shape_of(o), "near") for o in fetch] + [(o.shape, o.dtype, "far") for o in forward]
    for k, (shape, dtype, kind) in enumerate([*outs, *extra]):
        if kind != "far":
            out_shapes.append(jax.ShapeDtypeStruct(shape, dtype))
            out_specs.append(vmem)
        if kind != "near":
            out_shapes.append(pltpu.HBM(shape, dtype))
            out_specs.append(hbm)
        if kind == "far" and k < len(outs):
            sent.append((shape, dtype))
    n_copies = len(fetched) + sum(kind != "near" for _, _, kind in outs) + len(extra)

    def kernel(*refs):
        refs = list(refs)

        def take(n):
            taken = refs[:n]
            del refs[:n]
            return taken

        scalars, sources = take(smem), take(len(operands))
        extra_sources = take(len(extra))
        targets = take(len(out_shapes) - len(extra))
        extra_targets = take(len(extra))
        inner, outer = take(len(fetched)), take(len(sent))
        io = Copies(take(1)[0] if n_copies else None)
        inputs, outputs = [], []

        def source_of(operand, source):
            if isinstance(operand, Half):
                return source.at[pl.ds(pl.multiple_of(scalars[0][0] * HALF, HALF), HALF), :]
            return source

        for operand, source in zip(operands, sources, strict=True):
            if isinstance(operand, (Near, Raw)):
                inputs.append(source)
                continue
            ref = inner.pop(0)
            inputs.append(ref)
            io.waits[id(ref)] = [io.start(source_of(operand, source), ref)]
        moved = [
            io.start(source_of(operand, source), target)
            for operand, source, target in zip((*fetch, *forward), extra_sources, extra_targets, strict=True)
        ]
        for _, _, kind in outs:
            ref = outer.pop(0) if kind == "far" else targets.pop(0)
            outputs.append(ref)
            if kind != "near":
                io.out[id(ref)] = (targets.pop(0), None)
        body(io, *scalars, *inputs, *outputs, *refs)
        io.ready(*inputs)
        io.done(*outputs)
        for copy in (*(copy for _, copy in io.out.values()), *moved):
            copy.wait()

    own = [pltpu.VMEM(s, d) for s, d in fetched + sent]
    used = sum(size_of(s, d) for s, d in fetched + sent) + sum(
        size_of(s.shape, s.dtype) for s in scratch if s.memory_space == pltpu.VMEM
    )
    return pl.pallas_call(
        kernel,
        out_shape=tuple(out_shapes),
        in_specs=[pl.BlockSpec(memory_space=pltpu.SMEM)] * smem + in_specs,
        out_specs=tuple(out_specs),
        scratch_shapes=[*own, *([pltpu.SemaphoreType.DMA((n_copies,))] if n_copies else []), *scratch],
        compiler_params=pltpu.CompilerParams(vmem_limit_bytes=used + ROOM),
        cost_estimate=pl.CostEstimate(flops=int(us * 3.3e9), bytes_accessed=int(us * 1e7), transcendentals=0),
    )(*tables, *arrays)


def running_ends(len_ref):
    ends, total = [], 0
    for k in range(SEGS):
        total = total + len_ref[0, k]
        ends.append(total)
    return ends


def live_tokens(ends, count):
    total = 0
    for k in range(SEGS):
        total = jnp.where(k < count, ends[k], total)
    return total


def lookup(pos, ends, values, first):
    found = first
    for k in range(SEGS - 1):
        found = jnp.where(pos >= ends[k], values[k], found)
    return found


def token_positions():
    shape = (LEN // BLK, BLK)
    return lax.broadcasted_iota(jnp.int32, shape, 0) * BLK + lax.broadcasted_iota(
        jnp.int32, shape, 1
    )


def twice(row):
    return jnp.concatenate([row, row], axis=1)


def stacked(pair):
    lane = lax.broadcasted_iota(jnp.int32, pair.shape, 1)
    zero = jnp.zeros_like(pair)
    return jnp.concatenate(
        [jnp.where(lane < 64, pair, zero), jnp.where(lane < 64, zero, pair)], axis=0
    )


def diagonal(product):
    return jnp.concatenate([product[:64, :BLK], product[64:, BLK:]], axis=0)


def own_rows(row):
    return jnp.concatenate(
        [jnp.broadcast_to(row[:, :BLK], (64, BLK)), jnp.broadcast_to(row[:, BLK:], (64, BLK))], axis=0
    )


def in_chunks(n, body):
    def four(j, carry):
        body(4 * j, 4)
        return carry

    lax.fori_loop(0, lax.shift_right_logical(n, 2), four, 0)
    pl.when((n & 2) != 0)(lambda: body(n & ~3, 2))
    pl.when((n & 1) != 0)(lambda: body(n & ~1, 1))


def reset(m_ref, l_ref, acc_ref):
    m_ref[...] = jnp.full(m_ref.shape, MASKED, f32)
    l_ref[...] = jnp.zeros(l_ref.shape, f32)
    acc_ref[...] = jnp.zeros(acc_ref.shape, f32)


def soften(p, scores, values_t, m_ref, l_ref, acc_ref):
    before = m_ref[p, 0:1, :]
    peak = jnp.maximum(before, jnp.max(scores, axis=0, keepdims=True))
    shrink = jnp.exp(before - peak)
    raised = jnp.exp(scores - peak)
    m_ref[p, 0:1, :] = peak
    l_ref[p, 0:1, :] = l_ref[p, 0:1, :] * shrink + jnp.sum(raised, axis=0, keepdims=True)
    acc_ref[p] = acc_ref[p] * own_rows(shrink) + diagonal(nn(values_t, raised.astype(bf16)))


def settle(p, alive, m_ref, l_ref, acc_ref):
    total = l_ref[p, 0:1, :]
    mixed = jnp.transpose(acc_ref[p] * own_rows(alive / total))
    return mixed.astype(bf16), m_ref[p, 0:1, :] + jnp.log(total)


def inner_row(grads, mixed):
    product = jnp.transpose(grads.astype(f32) * mixed.astype(f32))
    return jnp.concatenate(
        [jnp.sum(product[:64], axis=0, keepdims=True), jnp.sum(product[64:], axis=0, keepdims=True)], axis=1
    )


def rms_scale(value):
    return lax.rsqrt(jnp.mean(value * value, axis=-1, keepdims=True) + EPS)


def rms_back(value, gain, grad):
    scale = rms_scale(value)
    weighted = grad * gain
    inner = jnp.mean(weighted * value, axis=-1, keepdims=True)
    unit = value * scale
    return (
        scale * weighted - unit * (scale * scale * inner),
        jnp.sum(grad * unit, axis=0, keepdims=True),
    )


def fill_bias(table_ref, bias_ref):
    key = lax.broadcasted_iota(jnp.int32, (BLK, BLK), 0)
    query = lax.broadcasted_iota(jnp.int32, (BLK, BLK), 1)
    for d in range(2):
        gap = d * BLK + query - key
        tiles = [jnp.full((BLK, BLK), table_ref[h, 0], f32) for h in range(4)]
        for level in range(1, NB):
            reached = gap >= THRESHOLDS[level]
            tiles = [jnp.where(reached, table_ref[h, level], tiles[h]) for h in range(4)]
        if d == 0:
            tiles = [jnp.where(gap >= 0, tile, MASKED) for tile in tiles]
        for h in range(4):
            bias_ref[d * 2 + h // 2, :, (h % 2) * BLK : (h % 2 + 1) * BLK] = tiles[h]
    for h in range(4):
        far = jnp.full((BLK, BLK), table_ref[h, NB - 1], f32)
        bias_ref[4 + h // 2, :, (h % 2) * BLK : (h % 2 + 1) * BLK] = far


def self_scores(distances, p, kstart, qs_ref, k_ref, bias_ref, start2):
    m = len(distances)
    keys = k_ref[pl.ds(kstart, m * BLK), p * BLK : (p + 1) * BLK]
    scores = nt(keys, qs_ref[p])
    parts = [scores[k * BLK : (k + 1) * BLK] + bias_ref[2 * d + p] for k, d in enumerate(distances)]
    index = kstart + lax.broadcasted_iota(jnp.int32, (m * BLK, 2 * BLK), 0)
    return jnp.where(index >= start2, jnp.concatenate(parts, axis=0) if m > 1 else parts[0], MASKED)


def self_spans(b, ends, live):
    pos = b * BLK
    first = lax.shift_right_logical(lookup(pos, ends, ends, 0), 7)
    return pos < live, first, b - first + 1


def self_forward(half, ends, live, q_ref, k_ref, vt_ref, bias_ref, start_ref, o_ref, lse_ref, qs_ref, m_ref, l_ref, acc_ref):
    def step(i, carry):
        b = half * 4 + i
        alive, first, n = self_spans(b, ends, live)
        rows = pl.ds(pl.multiple_of(i * BLK, BLK), BLK)

        @pl.when(alive)
        def _():
            start2 = twice(start_ref[pl.ds(b, 1), :])
            for p in range(2):
                lanes = slice(p * BLK, (p + 1) * BLK)
                qs_ref[p] = stacked(q_ref[pl.ds(pl.multiple_of(b * BLK, BLK), BLK), lanes])
            reset(m_ref, l_ref, acc_ref)

            def chunk(j, m):
                kstart = pl.multiple_of((first + j) * BLK, BLK)
                distances = [jnp.minimum(n - 1 - j - k, 2) for k in range(m)]
                for p in range(2):
                    scores = self_scores(distances, p, kstart, qs_ref, k_ref, bias_ref, start2)
                    values_t = vt_ref[p * BLK : (p + 1) * BLK, pl.ds(kstart, m * BLK)]
                    soften(p, scores, values_t, m_ref, l_ref, acc_ref)

            in_chunks(n, chunk)
            for p in range(2):
                mixed, lse = settle(p, (start2 < BIG).astype(f32), m_ref, l_ref, acc_ref)
                o_ref[rows, p * BLK : (p + 1) * BLK] = mixed
                lse_ref[p, pl.ds(i, 1), :] = lse

        @pl.when(jnp.logical_not(alive))
        def _():
            o_ref[rows, :] = jnp.zeros((BLK, OWN), bf16)
            for p in range(2):
                lse_ref[p, pl.ds(i, 1), :] = jnp.zeros((1, 2 * BLK), f32)

        return carry

    lax.fori_loop(0, 4, step, 0)


def set_starts(ends, live, start_ref):
    pos = token_positions()
    start_ref[...] = jnp.where(pos < live, lookup(pos, ends, ends, 0), BIG)


def first_kernel(
    io, t_ref, len_ref, cnt_ref, table_ref,
    x_ref, gain_ref, wq_ref, wk_ref, wv_ref,
    n1_ref, q_ref, k_ref, v_ref, vt_ref, kt_ref, bias_ref, o_ref, lse_ref,
    start_ref, *work,
):
    ends = running_ends(len_ref)
    live = live_tokens(ends, cnt_ref[0])
    set_starts(ends, live, start_ref)
    fill_bias(table_ref, bias_ref)
    io.done(bias_ref)
    io.ready(x_ref, gain_ref, wq_ref, wk_ref, wv_ref)

    def project(i, carry):
        rows = pl.ds(pl.multiple_of(i * 256, 256), 256)
        value = x_ref[rows, :].astype(f32)
        low = (value * rms_scale(value) * gain_ref[...]).astype(bf16)
        n1_ref[rows, :] = low
        q_ref[rows, :] = nn(low, wq_ref[...]).astype(bf16)
        keys = nn(low, wk_ref[...])
        k_ref[rows, :] = keys.astype(bf16)
        kt_ref[:, rows] = jnp.transpose(keys).astype(bf16)
        values = nn(low, wv_ref[...])
        v_ref[rows, :] = values.astype(bf16)
        vt_ref[:, rows] = jnp.transpose(values).astype(bf16)
        return carry

    lax.fori_loop(0, 4, project, 0)
    io.done(n1_ref, q_ref, k_ref, v_ref, vt_ref, kt_ref)
    self_forward(
        1 - t_ref[0], ends, live, q_ref, k_ref, vt_ref, bias_ref, start_ref, o_ref, lse_ref, *work
    )


def second_kernel(
    io, t_ref, len_ref, cnt_ref,
    q_ref, k_ref, vt_ref, bias_ref,
    o_ref, lse_ref,
    start_ref, *work,
):
    ends = running_ends(len_ref)
    live = live_tokens(ends, cnt_ref[0])
    set_starts(ends, live, start_ref)
    io.ready(q_ref, k_ref, vt_ref, bias_ref)
    self_forward(
        t_ref[0], ends, live, q_ref, k_ref, vt_ref, bias_ref, start_ref, o_ref, lse_ref, *work
    )


def memory_kernel(
    io, place_ref, mem_ref, ck_ref, cv_ref, pack_ref, packo_ref,
    mk_ref, mv_ref, mkt_ref, mvt_ref, so_out, co_out, cq_out, cko_ref, cvo_ref,
):
    for core, pack in ((place_ref[1], pack_ref), (1 - place_ref[1], packo_ref)):
        for ref, parts in zip((so_out, co_out, cq_out, cko_ref, cvo_ref), packed_parts(core), strict=True):
            for rows, where in parts:
                ref[rows, :] = pack[where]
    io.done(so_out, co_out, cq_out, cko_ref, cvo_ref)
    io.ready(mem_ref, ck_ref, cv_ref)

    def project(i, carry):
        rows = pl.ds(pl.multiple_of(i * 256, 256), 256)
        value = mem_ref[rows, :]
        for side, (wk, wv) in enumerate(((ck_ref, cv_ref), (cko_ref, cvo_ref))):
            lanes = slice(side * OWN, (side + 1) * OWN)
            keys = nn(value, wk[...])
            mk_ref[rows, lanes] = keys.astype(bf16)
            mkt_ref[lanes, rows] = jnp.transpose(keys).astype(bf16)
            values = nn(value, wv[...])
            mv_ref[rows, lanes] = values.astype(bf16)
            mvt_ref[lanes, rows] = jnp.transpose(values).astype(bf16)
        return carry

    lax.fori_loop(0, 4, project, 0)


def set_ranges(ends, mends, live, low_ref, high_ref):
    pos = token_positions()
    low_ref[...] = jnp.where(pos < live, lookup(pos, ends, mends, 0), BIG)
    high_ref[...] = lookup(pos, ends, mends[1:], mends[0])


def cross_blocks(half, ends, mends, live, block, dead):
    def step(i, carry):
        b = half * 4 + i
        pos = b * BLK
        alive = pos < live
        last = jnp.minimum(pos + BLK, live) - 1
        first = lax.shift_right_logical(lookup(pos, ends, mends, 0), 7)
        end = lax.shift_right_logical(lookup(last, ends, mends[1:], mends[0]) + BLK - 1, 7)
        pl.when(alive)(lambda: block(i, b, first, end - first))
        pl.when(jnp.logical_not(alive))(lambda: dead(i))
        return carry

    lax.fori_loop(0, 4, step, 0)


def cross_allowed(kstart, m, low2, high2):
    index = kstart + lax.broadcasted_iota(jnp.int32, (m * BLK, 2 * BLK), 0)
    return (index >= low2) & (index < high2)


def third_kernel(
    io, t_ref, len_ref, mlen_ref, cnt_ref,
    x_ref, keep_ref, recv_ref, so_ref, soo_ref, gain2_ref, cq_ref, cqo_ref,
    mk_ref, mvt_ref, co_ref, coo_ref, gain3_ref,
    h1_ref, n2_ref, q_ref, mixed_ref, lse_ref, h2_ref, n3_ref,
    low_ref, high_ref, qs_ref, m_ref, l_ref, acc_ref,
):
    t = t_ref[0]
    ends, mends = running_ends(len_ref), running_ends(mlen_ref)
    live = live_tokens(ends, cnt_ref[0])
    set_ranges(ends, mends, live, low_ref, high_ref)

    io.ready(x_ref, keep_ref, recv_ref, so_ref, soo_ref, gain2_ref, cq_ref, cqo_ref)

    def before(i, carry):
        rows = pl.ds(pl.multiple_of(i * 256, 256), 256)
        value = x_ref[rows, :].astype(f32)
        value = value + nn(keep_ref[rows, :], so_ref[...]) + nn(recv_ref[rows, :], soo_ref[...])
        h1_ref[rows, :] = value
        low = (value * rms_scale(value) * gain2_ref[...]).astype(bf16)
        n2_ref[rows, :] = low
        q_ref[rows, :OWN] = nn(low, cq_ref[...]).astype(bf16)
        q_ref[rows, OWN:] = nn(low, cqo_ref[...]).astype(bf16)
        return carry

    lax.fori_loop(0, 2, before, 0)
    io.done(h1_ref, n2_ref, q_ref)
    io.ready(mk_ref, mvt_ref)

    def block(i, b, first, n):
        low2, high2 = twice(low_ref[pl.ds(b, 1), :]), twice(high_ref[pl.ds(b, 1), :])
        rows = pl.ds(pl.multiple_of(i * BLK, BLK), BLK)
        for p in range(4):
            qs_ref[p] = stacked(q_ref[rows, p * BLK : (p + 1) * BLK])
        reset(m_ref, l_ref, acc_ref)

        def chunk(j, m):
            kstart = pl.multiple_of((first + j) * BLK, BLK)
            span = pl.ds(kstart, m * BLK)
            allowed = cross_allowed(kstart, m, low2, high2)
            for p in range(4):
                lanes = slice(p * BLK, (p + 1) * BLK)
                scores = jnp.where(allowed, nt(mk_ref[span, lanes], qs_ref[p]), MASKED)
                soften(p, scores, mvt_ref[lanes, span], m_ref, l_ref, acc_ref)

        in_chunks(n, chunk)
        for p in range(4):
            mixed, lse = settle(p, (low2 < BIG).astype(f32), m_ref, l_ref, acc_ref)
            mixed_ref[rows, p * BLK : (p + 1) * BLK] = mixed
            lse_ref[p, pl.ds(i, 1), :] = lse

    def dead(i):
        mixed_ref[pl.ds(pl.multiple_of(i * BLK, BLK), BLK), :] = jnp.zeros((BLK, WIDTH), bf16)
        for p in range(4):
            lse_ref[p, pl.ds(i, 1), :] = jnp.zeros((1, 2 * BLK), f32)

    cross_blocks(t, ends, mends, live, block, dead)

    io.done(mixed_ref, lse_ref)
    io.ready(co_ref, coo_ref, gain3_ref)

    def after(i, carry):
        rows = pl.ds(pl.multiple_of(i * 256, 256), 256)
        value = h1_ref[rows, :]
        value = value + nn(mixed_ref[rows, :OWN], co_ref[...]) + nn(mixed_ref[rows, OWN:], coo_ref[...])
        h2_ref[rows, :] = value
        n3_ref[rows, :] = (value * rms_scale(value) * gain3_ref[...]).astype(bf16)
        return carry

    lax.fori_loop(0, 2, after, 0)


def feed_kernel(
    io, place_ref, n3_ref, fi_ref, cot_ref, fo_ref,
    out_ref, gn_ref, act_ref, gp_ref,
):
    tile = 256
    n_tiles = fi_ref.shape[1] // tile
    root = math.sqrt(2 / math.pi)
    base = place_ref[0] * HALF
    io.ready(n3_ref, fi_ref, cot_ref, fo_ref)

    def hidden(j, carry):
        lanes = pl.ds(pl.multiple_of(j * tile, tile), tile)
        for i in range(2):
            rows = slice(i * 256, (i + 1) * 256)
            pre = nn(n3_ref[rows, :], fi_ref[:, lanes])
            square = pre * pre
            bent = jnp.tanh(pre * (root + (root * 0.044715) * square))
            gate = 0.5 + 0.5 * bent
            slope = gate + pre * (0.5 - 0.5 * bent * bent) * (root + (root * 0.134145) * square)
            act_ref[rows, lanes] = (pre * gate).astype(bf16)
            grads = nt(cot_ref[pl.ds(pl.multiple_of(base + i * 256, 256), 256), :], fo_ref[lanes, :])
            gp_ref[rows, lanes] = (grads * slope).astype(bf16)
        return carry

    lax.fori_loop(0, n_tiles, hidden, 0)
    io.done(act_ref, gp_ref)

    def outward(i, carry):
        rows = pl.ds(pl.multiple_of(i * 256, 256), 256)
        out_ref[rows, :] = nn(act_ref[rows, :], fo_ref[...]).astype(bf16)
        gn_ref[rows, :] = nt(gp_ref[rows, :], fi_ref[...]).astype(bf16)
        return carry

    lax.fori_loop(0, 2, outward, 0)


def feed_weights_kernel(
    io, place_ref, h2_ref, own_ref, oth_ref, n3_ref, gp_ref, n3o_ref, gpo_ref, act_ref, cot_ref, acto_ref,
    hold_ref, senda_ref, sendb_ref, sendc_ref, sendd_ref, outa_ref, outb_ref,
    n3t_ref,
):
    t, c = place_ref[0], place_ref[1]

    parts = (senda_ref, sendb_ref, sendc_ref, sendd_ref)

    def put(core, start, lanes, grads):
        low = grads.astype(bf16)

        @pl.when(c == core)
        def _():
            hold_ref[start : start + low.shape[0], lanes] = low

        @pl.when(c != core)
        def _():
            for k in range(low.shape[0] // 256):
                parts[start // 256 + k][:, lanes] = low[k * 256 : (k + 1) * 256]

    mine = pl.ds(pl.multiple_of(t * HALF, HALF), HALF)
    theirs = pl.ds(pl.multiple_of((1 - t) * HALF, HALF), HALF)
    io.ready(n3_ref, gp_ref, n3o_ref, gpo_ref)
    n3t_ref[:, :HALF] = jnp.transpose(n3_ref[...].astype(f32)).astype(bf16)
    n3t_ref[:, HALF:] = jnp.transpose(n3o_ref[...].astype(f32)).astype(bf16)
    n_tiles = gp_ref.shape[1] // 256
    for j in range(n_tiles):
        lanes = slice(j * 256, (j + 1) * 256)
        grads = nn(n3t_ref[:, :HALF], gp_ref[:, lanes]) + nn(n3t_ref[:, HALF:], gpo_ref[:, lanes])
        put(0, (j // 2) * WIDTH, slice((j % 2) * 256, (j % 2 + 1) * 256), grads)
    io.ready(act_ref, cot_ref, acto_ref)
    for j in range(n_tiles):
        lanes = slice(j * 256, (j + 1) * 256)
        grads = tn(act_ref[:, lanes], cot_ref[mine, :]) + tn(acto_ref[:, lanes], cot_ref[theirs, :])
        put(1, j * 256, slice(0, WIDTH), grads)
    io.ready(h2_ref, own_ref, oth_ref)
    own = (h2_ref[...] + own_ref[...].astype(f32)).astype(bf16)
    for k, out_ref in enumerate((outa_ref, outb_ref)):

        @pl.when(t == k)
        def _():
            out_ref[...] = own

        @pl.when(t != k)
        def _():
            out_ref[...] = oth_ref[...]


def cross_back_kernel(
    io, t_ref, len_ref, mlen_ref, cnt_ref,
    gn_ref, gnr_ref, h2_ref, gain3_ref, cot_ref, co_ref, coo_ref,
    q_ref, mk_ref, mkt_ref, mv_ref, lse_ref, mixed_ref, cq_ref, cqo_ref, h1_ref, gain2_ref, so_ref, soo_ref,
    gb2_ref, dq_ref, dk_ref, dv_ref, gh1_ref, gb1_ref, gm1_ref, gm1o_ref, gains_ref,
    low_ref, high_ref, live_ref, gm_ref, dk_acc, dv_acc, gh2_ref, qs_ref, gs_ref, acc_ref,
):
    t = t_ref[0]
    ends, mends = running_ends(len_ref), running_ends(mlen_ref)
    live = live_tokens(ends, cnt_ref[0])
    set_ranges(ends, mends, live, low_ref, high_ref)
    alive_rows = t * HALF + lax.broadcasted_iota(jnp.int32, (HALF, BLK), 0)
    live_ref[...] = (alive_rows < live).astype(f32)
    dk_acc[...] = jnp.zeros_like(dk_acc)
    dv_acc[...] = jnp.zeros_like(dv_acc)
    gains_ref[...] = jnp.zeros_like(gains_ref)

    io.ready(gn_ref, gnr_ref, h2_ref, gain3_ref, cot_ref, co_ref, coo_ref)
    for i in range(2):
        rows = slice(i * 256, (i + 1) * 256)
        grad = gn_ref[rows, :].astype(f32) + gnr_ref[rows, :].astype(f32)
        back, gain = rms_back(h2_ref[rows, :], gain3_ref[...], grad)
        gains_ref[0:1, :] += gain
        grad = cot_ref[rows, :].astype(f32) + back
        gh2_ref[rows, :] = grad
        low = grad.astype(bf16)
        gb2_ref[rows, :] = low
        alive = live_ref[rows, 0:1]
        gm_ref[rows, :OWN] = (nt(low, co_ref[...]) * alive).astype(bf16)
        gm_ref[rows, OWN:] = (nt(low, coo_ref[...]) * alive).astype(bf16)
    io.done(gb2_ref)
    io.ready(q_ref, mk_ref, mkt_ref, mv_ref, lse_ref, mixed_ref)

    def block(i, b, first, n):
        low2, high2 = twice(low_ref[pl.ds(b, 1), :]), twice(high_ref[pl.ds(b, 1), :])
        rows = pl.ds(pl.multiple_of(i * BLK, BLK), BLK)
        inner = []
        for p in range(4):
            lanes = slice(p * BLK, (p + 1) * BLK)
            qs_ref[p] = stacked(q_ref[rows, lanes])
            gs_ref[p] = stacked(gm_ref[rows, lanes])
            inner.append(inner_row(gm_ref[rows, lanes], mixed_ref[rows, lanes]))
        acc_ref[...] = jnp.zeros(acc_ref.shape, f32)

        def chunk(j, m):
            kstart = pl.multiple_of((first + j) * BLK, BLK)
            span = pl.ds(kstart, m * BLK)
            allowed = cross_allowed(kstart, m, low2, high2)
            for p in range(4):
                lanes = slice(p * BLK, (p + 1) * BLK)
                scores = jnp.where(allowed, nt(mk_ref[span, lanes], qs_ref[p]), MASKED)
                probs = jnp.exp(scores - lse_ref[p, pl.ds(i, 1), :])
                low = (probs * (nt(mv_ref[span, lanes], gs_ref[p]) - inner[p])).astype(bf16)
                dk_acc[span, lanes] += nn(low, qs_ref[p])
                dv_acc[span, lanes] += nn(probs.astype(bf16), gs_ref[p])
                acc_ref[p] += diagonal(nn(mkt_ref[lanes, span], low))

        in_chunks(n, chunk)
        for p in range(4):
            dq_ref[rows, p * BLK : (p + 1) * BLK] = jnp.transpose(acc_ref[p]).astype(bf16)

    def dead(i):
        dq_ref[pl.ds(pl.multiple_of(i * BLK, BLK), BLK), :] = jnp.zeros((BLK, WIDTH), bf16)

    cross_blocks(t, ends, mends, live, block, dead)

    dk_ref[...] = dk_acc[...].astype(bf16)
    dv_ref[...] = dv_acc[...].astype(bf16)
    io.done(dq_ref, dk_ref, dv_ref)
    io.ready(cq_ref, cqo_ref, h1_ref, gain2_ref, so_ref, soo_ref)
    for i in range(2):
        rows = slice(i * 256, (i + 1) * 256)
        grad = nt(dq_ref[rows, :OWN], cq_ref[...]) + nt(dq_ref[rows, OWN:], cqo_ref[...])
        back, gain = rms_back(h1_ref[rows, :], gain2_ref[...], grad)
        gains_ref[1:2, :] += gain
        grad = gh2_ref[rows, :] + back
        gh1_ref[rows, :] = grad
        low = grad.astype(bf16)
        gb1_ref[rows, :] = low
        alive = live_ref[rows, 0:1]
        gm1_ref[rows, :] = (nt(low, so_ref[...]) * alive).astype(bf16)
        gm1o_ref[rows, :] = (nt(low, soo_ref[...]) * alive).astype(bf16)


def cross_weights_kernel(
    io, place_ref, mem_ref, dk_ref, dv_ref, n2_ref, dq_ref, mixed_ref, gb2_ref, keep_ref, gb1_ref, recv_ref,
    hold_ref, holdo_ref, send_ref,
    memt_ref, fold_ref,
):
    c = place_ref[1]
    io.ready(mem_ref, dk_ref, dv_ref, n2_ref, dq_ref, mixed_ref, gb2_ref, keep_ref, gb1_ref, recv_ref)
    memt_ref[...] = jnp.transpose(mem_ref[...].astype(f32)).astype(bf16)
    n2t = jnp.transpose(n2_ref[...].astype(f32)).astype(bf16)
    for side in range(2):
        lanes = slice(side * OWN, (side + 1) * OWN)
        mixed1 = keep_ref if side == 0 else recv_ref
        fold_ref[0] = tn(mixed_ref[:, lanes], gb2_ref[...]).astype(bf16)
        fold_ref[1] = tn(mixed1[...], gb1_ref[...]).astype(bf16)
        fold(fold_ref, 2, nn(n2t, dq_ref[:, lanes]))
        fold(fold_ref, 3, nn(memt_ref[...], dk_ref[:, lanes]))
        fold(fold_ref, 4, nn(memt_ref[...], dv_ref[:, lanes]))
        deal(c, fold_ref, hold_ref if side == 0 else holdo_ref, send_ref, side * 640)


def memory_back_kernel(
    io, place_ref, dk_ref, ck_ref, cko_ref, dv_ref, cv_ref, cvo_ref, gmem_ref, gmems_ref
):
    t = place_ref[0]
    io.ready(dk_ref, ck_ref, cko_ref, dv_ref, cv_ref, cvo_ref)
    for i in range(4):
        rows = slice(i * 256, (i + 1) * 256)
        grads = nt(dk_ref[rows, :OWN], ck_ref[...]) + nt(dk_ref[rows, OWN:], cko_ref[...])
        grads += nt(dv_ref[rows, :OWN], cv_ref[...]) + nt(dv_ref[rows, OWN:], cvo_ref[...])
        low = grads.astype(bf16)

        @pl.when(t == 0)
        def _():
            gmem_ref[rows, :] = low[:, :OWN]
            gmems_ref[rows, :] = low[:, OWN:]

        @pl.when(t != 0)
        def _():
            gmem_ref[rows, :] = low[:, OWN:]
            gmems_ref[rows, :] = low[:, :OWN]


def fold(fold_ref, k, weight):
    low = weight.astype(bf16)
    fold_ref[k, :, :OWN] = low[:256]
    fold_ref[k, :, OWN:] = low[256:]


def deal(c, fold_ref, hold_ref, send_ref, base):
    for k in range(fold_ref.shape[0]):
        rows = slice(k * BLK, (k + 1) * BLK)
        hold_ref[rows, :] = fold_ref[k, pl.ds(pl.multiple_of(c * BLK, BLK), BLK), :]
        rows = slice(base + k * BLK, base + (k + 1) * BLK)
        send_ref[rows, :] = fold_ref[k, pl.ds(pl.multiple_of((1 - c) * BLK, BLK), BLK), :]


def self_back_blocks(
    half, ends, live, start_ref, g_ref, mixed_ref, q_ref, k_ref, kt_ref, v_ref, bias_ref, lse_ref,
    dq_ref, dk_acc, dv_acc, near_acc, qs_ref, gs_ref, acc_ref,
):
    def step(i, carry):
        b = half * 4 + i
        alive, first, n = self_spans(b, ends, live)
        rows = pl.ds(pl.multiple_of(i * BLK, BLK), BLK)

        @pl.when(alive)
        def _():
            start2 = twice(start_ref[pl.ds(b, 1), :])
            inner = []
            for p in range(2):
                lanes = slice(p * BLK, (p + 1) * BLK)
                qs_ref[p] = stacked(q_ref[pl.ds(pl.multiple_of(b * BLK, BLK), BLK), lanes])
                gs_ref[p] = stacked(g_ref[rows, lanes])
                inner.append(inner_row(g_ref[rows, lanes], mixed_ref[rows, lanes]))
            acc_ref[...] = jnp.zeros(acc_ref.shape, f32)

            def chunk(j, m):
                kstart = pl.multiple_of((first + j) * BLK, BLK)
                span = pl.ds(kstart, m * BLK)
                distances = [jnp.minimum(n - 1 - j - k, 2) for k in range(m)]
                for p in range(2):
                    lanes = slice(p * BLK, (p + 1) * BLK)
                    scores = self_scores(distances, p, kstart, qs_ref, k_ref, bias_ref, start2)
                    probs = jnp.exp(scores - lse_ref[p, pl.ds(i, 1), :])
                    grad_scores = probs * (nt(v_ref[span, lanes], gs_ref[p]) - inner[p])
                    for k, d in enumerate(distances):
                        near_acc[2 * d + p] += grad_scores[k * BLK : (k + 1) * BLK]
                    low = grad_scores.astype(bf16)
                    dk_acc[span, lanes] += nn(low, qs_ref[p])
                    dv_acc[span, lanes] += nn(probs.astype(bf16), gs_ref[p])
                    acc_ref[p] += diagonal(nn(kt_ref[lanes, span], low))

            in_chunks(n, chunk)
            for p in range(2):
                dq_ref[rows, p * BLK : (p + 1) * BLK] = jnp.transpose(acc_ref[p]).astype(bf16)

        @pl.when(jnp.logical_not(alive))
        def _():
            dq_ref[rows, :] = jnp.zeros((BLK, OWN), bf16)

        return carry

    lax.fori_loop(0, 4, step, 0)


def self_back_own_kernel(
    io, place_ref, len_ref, cnt_ref,
    gm_ref, mixed_ref, q_ref, k_ref, kt_ref, v_ref, bias_ref, lse_ref,
    dq_ref, dk_acc, dv_acc, near_acc,
    start_ref, *work,
):
    ends = running_ends(len_ref)
    live = live_tokens(ends, cnt_ref[0])
    set_starts(ends, live, start_ref)
    for ref in (dk_acc, dv_acc, near_acc):
        ref[...] = jnp.zeros_like(ref)
    io.ready(gm_ref, mixed_ref, q_ref, k_ref, kt_ref, v_ref, bias_ref, lse_ref)
    self_back_blocks(
        place_ref[0], ends, live, start_ref, gm_ref, mixed_ref, q_ref, k_ref, kt_ref, v_ref, bias_ref, lse_ref,
        dq_ref, dk_acc, dv_acc, near_acc, *work,
    )


def self_back_kernel(
    io, place_ref, len_ref, cnt_ref,
    gmr_ref, mixed_ref, dqm_ref, dkm_ref, dvm_ref, nearm_ref, q_ref, k_ref, kt_ref, v_ref, bias_ref, lse_ref,
    n1_ref, x_ref, gh1_ref, gain1_ref, gains_ref, wq_ref, wk_ref, wv_ref,
    hold_ref, send_ref, gia_ref, gib_ref,
    start_ref, dqo_ref, dq_ref, dk_acc, dv_acc, near_acc, n1t_ref, fold_ref, sums_ref, small_ref, *work,
):
    t = place_ref[0]
    ends = running_ends(len_ref)
    live = live_tokens(ends, cnt_ref[0])
    set_starts(ends, live, start_ref)
    small_ref[...] = jnp.zeros_like(small_ref)
    for ref, so_far in ((dk_acc, dkm_ref), (dv_acc, dvm_ref), (near_acc, nearm_ref)):
        ref[...] = so_far[...]
    io.ready(mixed_ref, q_ref, k_ref, kt_ref, v_ref, bias_ref, lse_ref)
    self_back_blocks(
        1 - t, ends, live, start_ref, gmr_ref, mixed_ref, q_ref, k_ref, kt_ref, v_ref, bias_ref, lse_ref,
        dqo_ref, dk_acc, dv_acc, near_acc, *work,
    )
    dq_ref[pl.ds(pl.multiple_of(t * HALF, HALF), HALF), :] = dqm_ref[...]
    dq_ref[pl.ds(pl.multiple_of((1 - t) * HALF, HALF), HALF), :] = dqo_ref[...]

    io.ready(n1_ref)
    n1t_ref[...] = jnp.transpose(n1_ref[...].astype(f32)).astype(bf16)
    low_k, low_v = dk_acc[...].astype(bf16), dv_acc[...].astype(bf16)
    for k, grads in enumerate((dq_ref[...], low_k, low_v)):
        fold(fold_ref, k, nn(n1t_ref[...], grads))
    deal(place_ref[1], fold_ref, hold_ref, send_ref, 0)
    io.ready(x_ref, gh1_ref, gain1_ref, gains_ref, wq_ref, wk_ref, wv_ref)
    gain1 = jnp.zeros((1, WIDTH), f32)
    for i in range(4):
        rows = slice(i * 256, (i + 1) * 256)
        grads = nt(dq_ref[rows, :], wq_ref[...]) + nt(low_k[rows], wk_ref[...]) + nt(low_v[rows], wv_ref[...])
        back, gain = rms_back(x_ref[rows, :].astype(f32), gain1_ref[...], grads)
        gain1 += gain
        mine = (t == i // 2).astype(f32)
        back += mine * gh1_ref[(i % 2) * 256 : (i % 2 + 1) * 256, :]
        (gia_ref if i < 2 else gib_ref)[(i % 2) * 256 : (i % 2 + 1) * 256, :] = back.astype(bf16)
    io.done(gia_ref, gib_ref)
    key = lax.broadcasted_iota(jnp.int32, (BLK, BLK), 0)
    query = lax.broadcasted_iota(jnp.int32, (BLK, BLK), 1)
    gaps = [query - key, BLK + query - key]
    for level in range(NB):
        for p in range(2):
            row = jnp.zeros((1, 2 * BLK), f32)
            for d in range(2):
                inside = gaps[d] >= THRESHOLDS[level]
                if level + 1 < NB:
                    inside &= gaps[d] < THRESHOLDS[level + 1]
                picked = jnp.where(twice(inside.astype(f32)) > 0, near_acc[2 * d + p], 0.0)
                row += jnp.sum(picked, axis=0, keepdims=True)
            if level == NB - 1:
                row += jnp.sum(near_acc[4 + p], axis=0, keepdims=True)
            sums_ref[level : level + 1, p * 256 : (p + 1) * 256] = row
    for h in range(4):
        lanes = jnp.transpose(sums_ref[:, h * BLK : (h + 1) * BLK])
        small_ref[3 + h : 4 + h, :NB] = jnp.sum(lanes, axis=0, keepdims=True)
    for k, gain in enumerate((gain1, gains_ref[1:2, :], gains_ref[0:1, :])):
        small_ref[k : k + 1, :] = gain
    low = small_ref[...].astype(bf16)
    hold_ref[384:, :] = low
    send_ref[384:, :] = low


def join_kernel(io, place_ref, own_ref, got_ref, recv_ref, mine_ref, theirs_ref, hold_ref, send_ref):
    x = place_ref[2]
    io.ready(own_ref, got_ref, recv_ref, mine_ref, theirs_ref)
    for k in range(8):
        if k < 5:
            rows = slice(k * BLK, (k + 1) * BLK)
            total = own_ref[rows, :].astype(f32) + got_ref[rows, :].astype(f32) + recv_ref[rows, :].astype(f32)
        else:
            rows = slice((k - 5) * BLK, (k - 4) * BLK)
            total = mine_ref[rows, :].astype(f32) + theirs_ref[rows, :].astype(f32)
        low = total.astype(bf16)
        rows = slice((k % 4) * BLK, (k % 4 + 1) * BLK)

        @pl.when(x == k // 4)
        def _():
            hold_ref[rows, :] = low

        @pl.when(x != k // 4)
        def _():
            send_ref[rows, :] = low

    low = (mine_ref[384:, :].astype(f32) + theirs_ref[384:, :].astype(f32)).astype(bf16)
    hold_ref[HALF:, :] = low
    send_ref[HALF:, :] = low


def feed_halve_kernel(io, place_ref, hold_ref, gota_ref, gotb_ref, gotc_ref, gotd_ref, keep_ref, send_ref):
    x = place_ref[2]
    for k, got_ref in enumerate((gota_ref, gotb_ref, gotc_ref, gotd_ref)):
        rows, to = slice(k * 256, (k + 1) * 256), slice((k % 2) * 256, (k % 2 + 1) * 256)
        low = (hold_ref[rows, :].astype(f32) + got_ref[...].astype(f32)).astype(bf16)

        @pl.when(x == k // 2)
        def _():
            keep_ref[to, :] = low

        @pl.when(x != k // 2)
        def _():
            send_ref[to, :] = low


def halve_kernel(slot, every, io, place_ref, hold_ref, got_ref, keep_ref, send_ref):
    bit, size = place_ref[slot], keep_ref.shape[0] - every
    io.ready(hold_ref, got_ref)
    for k in range(2):
        rows = slice(k * size, (k + 1) * size)
        low = (hold_ref[rows, :].astype(f32) + got_ref[rows, :].astype(f32)).astype(bf16)

        @pl.when(bit == k)
        def _():
            keep_ref[:size, :] = low

        @pl.when(bit != k)
        def _():
            send_ref[:size, :] = low

    if every:
        low = (hold_ref[2 * size :, :].astype(f32) + got_ref[2 * size :, :].astype(f32)).astype(bf16)
        keep_ref[size:, :] = low
        send_ref[size:, :] = low


def total_kernel(io, _, hold_ref, got_ref, out_ref, *small_refs):
    io.ready(hold_ref, got_ref)
    total = hold_ref[...].astype(f32) + got_ref[...].astype(f32)
    out_ref[...] = total[: out_ref.shape[0]].astype(bf16)
    for small_ref in small_refs:
        small_ref[...] = total[out_ref.shape[0] :]


def merge_kernel(slot, io, place_ref, own_ref, got_ref, out_ref):
    bit, size = place_ref[slot], own_ref.shape[0]
    io.ready(own_ref, got_ref)
    out_ref[pl.ds(pl.multiple_of(bit * size, size), size), :] = own_ref[...]
    out_ref[pl.ds(pl.multiple_of((1 - bit) * size, size), size), :] = got_ref[...]


def feed_unfold_kernel(io, place_ref, own_ref, pair_ref, core_ref, both_ref, fi_ref, fo_ref):
    c, x = place_ref[1], place_ref[2]
    io.ready(own_ref, pair_ref, core_ref, both_ref)
    for ref, core, bit in ((own_ref, c, x), (pair_ref, c, 1 - x), (core_ref, 1 - c, x), (both_ref, 1 - c, 1 - x)):
        at = pl.ds(pl.multiple_of(bit * WIDTH, WIDTH), WIDTH)

        @pl.when(core == 0)
        def _():
            fi_ref[:, at] = ref[...].astype(f32)

        @pl.when(core != 0)
        def _():
            fo_ref[at, :] = ref[...].astype(f32)


def unfold_kernel(
    io, place_ref, own_ref, pair_ref, core_ref, both_ref,
    co_ref, so_ref, cq_ref, ck_ref, cv_ref, wq_ref, wk_ref, wv_ref,
):
    c, x = place_ref[1], place_ref[2]
    outs = (co_ref, so_ref, cq_ref, ck_ref, cv_ref, wq_ref, wk_ref, wv_ref)

    def spread(ref, core, bit):
        low = pl.ds(pl.multiple_of(core * BLK, BLK), BLK)
        high = pl.ds(pl.multiple_of(256 + core * BLK, BLK), BLK)
        for k, out in enumerate(outs):
            rows = slice((k % 4) * BLK, (k % 4 + 1) * BLK)

            @pl.when(bit == k // 4)
            def _():
                if k < 2:
                    out[low, :] = ref[rows, :].astype(f32)
                else:
                    out[low, :] = ref[rows, :OWN].astype(f32)
                    out[high, :] = ref[rows, OWN:].astype(f32)

    for ref, core, bit in ((own_ref, c, x), (pair_ref, c, 1 - x), (core_ref, 1 - c, x), (both_ref, 1 - c, 1 - x)):
        io.ready(ref)
        spread(ref, core, bit)


def swap(value, axis="tensor", bit=0):
    return lax.ppermute(value, axis, [(i, i ^ (1 << bit)) for i in range(lax.axis_size(axis))])


def shards(
    inputs, memory, cotangent, dec_lengths, mem_lengths, counts,
    self_gain, self_query, self_key, self_value, self_out, rel_table,
    cross_gain, cross_query, cross_key, cross_value, cross_out,
    feed_gain, feed_in, feed_out,
):
    v = pltpu.VMEM
    i32 = jnp.int32
    t, c, x = (lax.axis_index(name).astype(i32) for name in ("tensor", "core", "pair"))
    ring = lax.axis_size("ring")
    at_ring = lax.axis_index("ring").astype(i32)
    bits = range(ring.bit_length() - 1)
    ring_bits = [lax.shift_right_logical(at_ring, k) & 1 for k in bits]
    place = jnp.stack([t, c, x, *ring_bits])
    place_oth = jnp.stack([1 - t, c, x, *ring_bits])

    def halve(hold, got, slot, every=0):
        shape = (((hold.shape[0] - every) // 2 + every, WIDTH), bf16, "near")
        return call(
            functools.partial(halve_kernel, slot, every), [shape, shape], [], (place, Near(hold), Near(got)), us=SHORT
        )

    def merge(own, got, slot):
        shape = ((2 * own.shape[0], WIDTH), bf16, "near")
        return call(functools.partial(merge_kernel, slot), [shape], [], (place, Near(own), Near(got)), us=SHORT)[0]

    def tie(*arrays):
        return lax.optimization_barrier(arrays)
    gain1, gain2, gain3 = (g.reshape(1, WIDTH) for g in (self_gain, cross_gain, feed_gain))
    table = rel_table.T

    tok = (LEN, WIDTH)
    half = (HALF, WIDTH)
    heads, heads_t, part = (LEN, OWN), (OWN, LEN), (HALF, OWN)
    narrow, wide = (OWN, WIDTH), (WIDTH, OWN)
    row_tile = v((LEN // BLK, BLK), i32)
    tiles = ((6, BLK, 2 * BLK), f32)

    def forward_work(n):
        rows = v((n, 8, 2 * BLK), f32)
        return [v((n, 2 * BLK, BLK), bf16), rows, rows, v((n, BLK, BLK), f32)]

    def backward_work(n):
        return [v((n, 2 * BLK, BLK), bf16), v((n, 2 * BLK, BLK), bf16), v((n, BLK, BLK), f32)]

    pack, x_near, gain1_near, wq, wk, wv = call(
        pack_kernel,
        [((PACKED, WIDTH), bf16, "near")],
        [pltpu.SemaphoreType.DMA((6,))],
        (place, *map(Raw, (self_out, cross_out, cross_query, cross_key, cross_value))),
        us=SHORT, fetch=(inputs, gain1, self_query, self_key, self_value),
    )
    pack = swap(pack)
    n1, q, q_far, k, k_far, val, vt, kt, bias, bias_far, send1, lse1_oth = call(
        first_kernel,
        [(tok, bf16, "far"), (heads, bf16, "both"), (heads, bf16, "both"), (heads, bf16, "far"),
         (heads_t, bf16, "near"), (heads_t, bf16, "far"), (*tiles, "both"), (part, bf16, "near"),
         ((2, 4, 2 * BLK), f32, "near")],
        [row_tile, *forward_work(2)],
        (place, dec_lengths, counts, table, *map(Near, (x_near, gain1_near, wq, wk, wv))),
        smem=4, us=6,
    )
    mixed1_recv = swap(send1)
    mixed1_keep, lse1, memory_near, ck, cv, lse1_oth, send_far = call(
        second_kernel,
        [(part, bf16, "near"), ((2, 4, 2 * BLK), f32, "near")],
        [row_tile, *forward_work(2)],
        (place, dec_lengths, counts, Near(q), Near(k), Near(vt), Near(bias)),
        smem=3, us=SHORT, fetch=(memory, cross_key, cross_value), forward=(lse1_oth, send1),
    )
    pack, mixed1_keep = lax.optimization_barrier((pack, mixed1_keep))
    pack_core = swap(pack, "core")
    mk, mv, mkt, mvt, so_oth, co_oth, cq_oth, ck_oth, cv_oth, x_half, so, gain2_near, cq_w, co, gain3_near, keep_far, lse1 = call(
        memory_kernel,
        [(tok, bf16, "near"), (tok, bf16, "near"), ((WIDTH, LEN), bf16, "near"), ((WIDTH, LEN), bf16, "near"),
         (narrow, bf16, "near"), (narrow, bf16, "near"), (wide, bf16, "near"), (wide, bf16, "near"), (wide, bf16, "near")],
        [],
        (place, *map(Near, (memory_near, ck, cv, pack, pack_core))),
        us=SHORT, fetch=(Half(inputs), self_out, gain2, cross_query, cross_out, gain3), forward=(mixed1_keep, lse1),
    )
    (h1, n2, cq, mixed2, lse2, h2, n3, fi, cot, fo,
     mk, mv, mkt, so_oth_far, co_oth_far, cq_oth_far, ck_oth, cv_oth, recv_far) = call(
        third_kernel,
        [(half, f32, "far"), (half, bf16, "far"), (half, bf16, "far"), (half, bf16, "far"),
         ((4, 4, 2 * BLK), f32, "far"), (half, f32, "near"), (half, bf16, "near")],
        [row_tile, row_tile, *forward_work(4)],
        (place, dec_lengths, mem_lengths, counts,
         *map(Near, (x_half, mixed1_keep, mixed1_recv, so, so_oth, gain2_near, cq_w, cq_oth, mk, mvt, co, co_oth, gain3_near))),
        smem=4, us=9,
        fetch=(feed_in, cotangent, feed_out),
        forward=(mk, mv, mkt, so_oth, co_oth, cq_oth, ck_oth, cv_oth, mixed1_recv),
    )
    n3_recv = swap(n3)

    hidden = feed_in.shape[1]
    units = (HALF, hidden)
    out_own, gn3_own, act, gp, h2_far, n3_far = call(
        feed_kernel,
        [(half, bf16, "far"), (half, bf16, "far"), (units, bf16, "far"), (units, bf16, "far")],
        [],
        (place, *map(Near, (n3, fi, cot, fo))),
        us=5, forward=(h2, n3),
    )
    h2 = h2_far
    n3_recv, act = lax.optimization_barrier((n3_recv, act))
    out_oth, gn3_oth, act_oth, gp_oth = call(
        feed_kernel,
        [(half, bf16, "near"), (half, bf16, "near"), (units, bf16, "near"), (units, bf16, "near")],
        [],
        (place_oth, *map(Near, (n3_recv, fi, cot, fo))),
        us=5,
    )
    gn3_recv = swap(gn3_oth)
    quarter = ((256, WIDTH), bf16, "near")
    feed_hold, *feed_send, out_a, out_b = call(
        feed_weights_kernel,
        [((2 * WIDTH, WIDTH), bf16, "near"), *[quarter] * 4, (half, bf16, "far"), (half, bf16, "far")],
        [v((WIDTH, LEN), bf16)],
        (place, h2, out_own, Near(out_oth), n3_far, gp, Near(n3_recv), Near(gp_oth), act, Near(cot), Near(act_oth)),
        us=5,
    )
    feed_hold, feed_send = call(
        feed_halve_kernel,
        [(half, bf16, "near")] * 2,
        [],
        (place, Near(feed_hold), *(Near(swap(part, "core")) for part in feed_send)),
        us=SHORT,
    )
    gn3_recv, feed_send = tie(gn3_recv, feed_send)
    feed_got = swap(feed_send, "pair")

    (gb2, dcq, dmk, dmv, gh1, gb1, gm1, gm1_oth, gains, memory_near, n2_near, mixed2_near, keep, recv) = call(
        cross_back_kernel,
        [(half, bf16, "near"), (half, bf16, "near"), (tok, bf16, "near"), (tok, bf16, "near"), (half, f32, "near"),
         (half, bf16, "near"), (part, bf16, "near"), (part, bf16, "near"), ((8, WIDTH), f32, "near")],
        [row_tile, row_tile, v((HALF, BLK), f32), v(half, bf16), v(tok, f32), v(tok, f32), v(half, f32), *backward_work(4)],
        (place, dec_lengths, mem_lengths, counts, gn3_own, Near(gn3_recv), h2, gain3, Half(cotangent),
         cross_out, co_oth_far, cq, mk, mkt, mv, lse2, mixed2, cross_query, cq_oth_far, h1, gain2, self_out, so_oth_far),
        smem=4, us=12, fetch=(memory, n2, mixed2, keep_far, recv_far),
    )
    out_a_recv = swap(out_a)
    feed_hold, feed_send = halve(feed_hold, feed_got, 3)
    gb2, feed_send, out_a_recv = tie(gb2, feed_send, out_a_recv)
    feed_got = swap(feed_send, "ring")
    gm1_recv = swap(gm1_oth)
    (cross_hold, cross_hold_oth, cross_send, q, k, kt_near, v_near, bias, lse1_near, lse1_oth_near, sent,
     dmk, dmv) = call(
        cross_weights_kernel,
        [((640, WIDTH), bf16, "near"), ((640, WIDTH), bf16, "near"), ((1280, WIDTH), bf16, "near")],
        [v((WIDTH, LEN), bf16), v((5, 256, WIDTH), bf16)],
        (place, *map(Near, (memory_near, dmk, dmv, n2_near, dcq, mixed2_near, gb2, keep, gb1, recv))),
        us=3, fetch=(q_far, k_far, kt, val, bias_far, lse1, lse1_oth, send_far), forward=(dmk, dmv),
    )
    cross_got = swap(cross_send, "core")
    acc = ((LEN, OWN), f32)
    dq1, dk1, dv1, near1, n1_near, x_near, gain1_near, wq, wk, wv = call(
        self_back_own_kernel,
        [(part, bf16, "near"), (*acc, "near"), (*acc, "near"), (*tiles, "near")],
        [row_tile, *backward_work(2)],
        (place, dec_lengths, counts, *map(Near, (gm1, keep, q, k, kt_near, v_near, bias, lse1_near))),
        smem=3, us=3, fetch=(n1, inputs, gain1, self_query, self_key, self_value),
    )
    cross_recv = swap((cross_hold_oth.astype(f32) + cross_got[640:].astype(f32)).astype(bf16))
    for bit in bits[1:]:
        feed_hold, feed_send = halve(feed_hold, feed_got, 3 + bit)
        gm1_recv, feed_send = tie(gm1_recv, feed_send)
        feed_got = swap(feed_send, "ring", bit)
    self_hold, self_send, gi_a, gi_b = call(
        self_back_kernel,
        [((384 + SMALL, WIDTH), bf16, "near"), ((384 + SMALL, WIDTH), bf16, "near"),
         (half, bf16, "far"), (half, bf16, "far")],
        [row_tile, v(part, bf16), v(heads, bf16), v(*acc), v(*acc), v(*tiles),
         v((WIDTH, LEN), bf16), v((3, 256, WIDTH), bf16), v((NB, WIDTH), f32), v((SMALL, WIDTH), f32), *backward_work(2)],
        (place, dec_lengths, counts,
         *map(Near, (gm1_recv, sent, dq1, dk1, dv1, near1, q, k, kt_near, v_near, bias, lse1_oth_near,
                     n1_near, x_near, gh1, gain1_near, gains, wq, wk, wv))),
        smem=3, us=3,
    )
    self_got = swap(self_send, "core")
    (feed_own,) = call(
        total_kernel, [((feed_hold.shape[0], WIDTH), bf16, "near")], [], (place, Near(feed_hold), Near(feed_got)), us=SHORT
    )
    joined = ((HALF + SMALL, WIDTH), bf16, "near")
    hold, send = call(
        join_kernel,
        [joined, joined],
        [],
        (place, *map(Near, (cross_hold, cross_got, cross_recv, self_hold, self_got))),
        us=SHORT,
    )
    got, gi_a_recv = swap(send, "pair"), swap(gi_a)
    got, feed_own, gi_a_recv = tie(got, feed_own, gi_a_recv)
    hold, send = halve(hold, got, 3, SMALL)
    for k in reversed(bits[1:]):
        feed_own = merge(feed_own, swap(feed_own, "ring", k), 3 + k)
    send, dmk = tie(send, dmk)
    gmem, gmem_send = call(
        memory_back_kernel,
        [(heads, bf16, "far"), (heads, bf16, "near")],
        [],
        (place, dmk, cross_key, ck_oth, dmv, cross_value, cv_oth),
        us=SHORT,
    )
    gi_b_recv, out_b_recv, gmem_recv = swap(gi_b), swap(out_b), swap(gmem_send)
    for k in bits[1:]:
        got = swap(send, "ring", k - 1)
        if k == 1:
            got, gmem_send, feed_own, gi_b_recv = tie(got, gmem_send, feed_own, gi_b_recv)
        hold, send = halve(hold, got, 3 + k, SMALL)
    feed_own = merge(feed_own, swap(feed_own, "ring"), 3)
    got = swap(send, "ring", bits[-1])
    got, out_b_recv, feed_own = tie(got, out_b_recv, feed_own)
    feed_pair, feed_core = swap(feed_own, "pair"), swap(feed_own, "core")
    own, small = call(
        total_kernel,
        [((hold.shape[0] - SMALL, WIDTH), bf16, "near"), ((SMALL, WIDTH), f32, "near")],
        [],
        (place, Near(hold), Near(got)),
        us=SHORT,
    )
    for k in reversed(bits):
        got = swap(own, "ring", k)
        if k == 0:
            got, feed_pair = tie(got, feed_pair)
        own = merge(own, got, 3 + k)
    own, gmem_recv = tie(own, gmem_recv)
    pair, core_own = swap(own, "pair"), swap(own, "core")
    gain_grads = small[:8] + swap(small[:8])

    def both(part, other):
        return (part.astype(f32) + other.astype(f32)).astype(bf16)

    output = jnp.concatenate([both(out_a, out_a_recv), both(out_b, out_b_recv)])
    grad_inputs = jnp.concatenate([both(gi_a, gi_a_recv), both(gi_b, gi_b_recv)])
    grad_memory = both(gmem, gmem_recv)
    wide_hidden, tall_hidden = ((WIDTH, hidden), f32, "far"), ((hidden, WIDTH), f32, "far")
    feed_in_grad, feed_out_grad = call(
        feed_unfold_kernel,
        [wide_hidden, tall_hidden],
        [],
        (place, *map(Near, (feed_own, feed_pair, feed_core, swap(feed_pair, "core")))),
        us=SHORT,
    )
    pair, output, grad_inputs, grad_memory, feed_in_grad, feed_out_grad = lax.optimization_barrier(
        (pair, output, grad_inputs, grad_memory, feed_in_grad, feed_out_grad)
    )
    narrows, wides = (narrow, f32, "far"), (wide, f32, "far")
    co_grad, so_grad, cq_grad, ck_grad, cv_grad, wq_grad, wk_grad, wv_grad = call(
        unfold_kernel,
        [narrows] * 2 + [wides] * 6,
        [],
        (place, *map(Near, (own, pair, core_own, swap(pair, "core")))),
    )
    return (
        output,
        grad_inputs,
        grad_memory,
        gain_grads[0],
        wq_grad,
        wk_grad,
        wv_grad,
        so_grad,
        small[3:7, :NB].T,
        gain_grads[1],
        cq_grad,
        ck_grad,
        cv_grad,
        co_grad,
        gain_grads[2],
        feed_in_grad,
        feed_out_grad,
    )


def solution(mesh):
    devices = mesh.devices
    rows, tensor = devices.shape
    mesh = Mesh(devices.reshape(rows // 4, 2, 2, tensor), ("ring", "pair", "core", "tensor"))
    dp = ("ring", "pair", "core")
    split = P(dp, None)
    columns, rows = P(None, "tensor"), P("tensor", None)
    return jax.shard_map(
        shards,
        mesh=mesh,
        in_specs=(
            split, split, split, split, split, P(dp),
            P(), columns, columns, columns, rows, columns,
            P(), columns, columns, columns, rows,
            P(), columns, rows,
        ),
        out_specs=(
            split, split, P(dp, "tensor"),
            P(), columns, columns, columns, rows, columns,
            P(), columns, columns, columns, rows,
            P(), columns, rows,
        ),
        check_vma=False,
    )
```

```python
import functools
import math

import jax
import jax.numpy as jnp
from jax import lax
from jax.experimental import pallas as pl
from jax.experimental.pallas import tpu as pltpu
from jax.sharding import Mesh
from jax.sharding import PartitionSpec as P

NB = 32
MAXDIST = 128
SEGS = 16
LEN = 1024
HALF = 512
WIDTH = 512
OWN = 256
BLK = 128
BIG = 1 << 30
MASKED = -1e30
EPS = 1e-06
f32 = jnp.float32
bf16 = jnp.bfloat16
ROOM = 11 * 1024 * 1024
SHORT = 0.05


def thresholds():
    exact = NB // 2
    edges = [
        math.ceil(exact * (MAXDIST / exact) ** (level / (NB - exact)))
        for level in range(1, NB - exact)
    ]
    return list(range(exact + 1)) + edges


THRESHOLDS = thresholds()


def nn(a, b):
    return jnp.dot(a, b, preferred_element_type=f32)


def nt(a, b):
    return lax.dot_general(a, b, (((1,), (1,)), ((), ())), preferred_element_type=f32)


def tn(a, b):
    return lax.dot_general(a, b, (((0,), (0,)), ((), ())), preferred_element_type=f32)


class Half:
    def __init__(self, array):
        self.array = array


class Near:
    def __init__(self, array):
        self.array = array


class Raw:
    def __init__(self, array):
        self.array = array


PACKED = 640
SMALL = 16


def packed_parts(core):
    def at(start, size):
        return pl.ds(pl.multiple_of(start, BLK), size)

    left, right, all_lanes = slice(0, OWN), slice(OWN, WIDTH), slice(0, WIDTH)
    return (
        [(at(core * BLK, BLK), (slice(0, 128), all_lanes))],
        [(at(core * BLK, BLK), (slice(128, 256), all_lanes))],
        [(at(core * 256, 256), (slice(256, 512), left))],
        [(at(core * 256, 256), (slice(256, 512), right))],
        [(at(core * 256, BLK), (slice(512, 640), left)), (at(core * 256 + BLK, BLK), (slice(512, 640), right))],
    )


def pack_kernel(io, place_ref, *refs):
    *weights, pack_ref, sems = refs
    copies = []
    for ref, parts in zip(weights, packed_parts(place_ref[1]), strict=True):
        for rows, where in parts:
            copy = pltpu.make_async_copy(ref.at[rows, :], pack_ref.at[where], sems.at[len(copies)])
            copy.start()
            copies.append(copy)
    for copy in copies:
        copy.wait()


class Copies:
    def __init__(self, sems):
        self.sems, self.used, self.waits, self.out = sems, 0, {}, {}

    def start(self, source, target):
        copy = pltpu.make_async_copy(source, target, self.sems.at[self.used])
        self.used += 1
        copy.start()
        return copy

    def ready(self, *refs):
        for ref in refs:
            for copy in self.waits.pop(id(ref), ()):
                copy.wait()

    def done(self, *refs):
        for ref in refs:
            target, copy = self.out.get(id(ref), (None, True))
            if copy is None:
                self.out[id(ref)] = (target, self.start(ref, target))


def size_of(shape, dtype):
    return math.prod(shape) * jnp.dtype(dtype).itemsize


def call(body, outs, scratch, args, smem=1, us=3, fetch=(), forward=()):
    tables, operands = args[:smem], args[smem:]
    arrays, in_specs, fetched = [], [], []
    hbm, vmem = pl.BlockSpec(memory_space=pltpu.HBM), pl.BlockSpec(memory_space=pltpu.VMEM)

    def shape_of(operand):
        if isinstance(operand, Half):
            return (HALF, *operand.array.shape[1:]), operand.array.dtype
        return operand.shape, operand.dtype

    for operand in (*operands, *fetch, *map(Near, forward)):
        array = operand.array if isinstance(operand, (Near, Raw, Half)) else operand
        near = isinstance(operand, Near)
        arrays.append(array if near else pltpu.with_memory_space_constraint(array, pltpu.HBM))
        in_specs.append(vmem if near else hbm)
    fetched = [shape_of(o) for o in operands if not isinstance(o, (Near, Raw))]
    out_shapes, out_specs, sent = [], [], []
    extra = [(*shape_of(o), "near") for o in fetch] + [(o.shape, o.dtype, "far") for o in forward]
    for k, (shape, dtype, kind) in enumerate([*outs, *extra]):
        if kind != "far":
            out_shapes.append(jax.ShapeDtypeStruct(shape, dtype))
            out_specs.append(vmem)
        if kind != "near":
            out_shapes.append(pltpu.HBM(shape, dtype))
            out_specs.append(hbm)
        if kind == "far" and k < len(outs):
            sent.append((shape, dtype))
    n_copies = len(fetched) + sum(kind != "near" for _, _, kind in outs) + len(extra)

    def kernel(*refs):
        refs = list(refs)

        def take(n):
            taken = refs[:n]
            del refs[:n]
            return taken

        scalars, sources = take(smem), take(len(operands))
        extra_sources = take(len(extra))
        targets = take(len(out_shapes) - len(extra))
        extra_targets = take(len(extra))
        inner, outer = take(len(fetched)), take(len(sent))
        io = Copies(take(1)[0] if n_copies else None)
        inputs, outputs = [], []

        def source_of(operand, source):
            if isinstance(operand, Half):
                return source.at[pl.ds(pl.multiple_of(scalars[0][0] * HALF, HALF), HALF), :]
            return source

        for operand, source in zip(operands, sources, strict=True):
            if isinstance(operand, (Near, Raw)):
                inputs.append(source)
                continue
            ref = inner.pop(0)
            inputs.append(ref)
            io.waits[id(ref)] = [io.start(source_of(operand, source), ref)]
        moved = [
            io.start(source_of(operand, source), target)
            for operand, source, target in zip((*fetch, *forward), extra_sources, extra_targets, strict=True)
        ]
        for _, _, kind in outs:
            ref = outer.pop(0) if kind == "far" else targets.pop(0)
            outputs.append(ref)
            if kind != "near":
                io.out[id(ref)] = (targets.pop(0), None)
        body(io, *scalars, *inputs, *outputs, *refs)
        io.ready(*inputs)
        io.done(*outputs)
        for copy in (*(copy for _, copy in io.out.values()), *moved):
            copy.wait()

    own = [pltpu.VMEM(s, d) for s, d in fetched + sent]
    used = sum(size_of(s, d) for s, d in fetched + sent) + sum(
        size_of(s.shape, s.dtype) for s in scratch if s.memory_space == pltpu.VMEM
    )
    return pl.pallas_call(
        kernel,
        out_shape=tuple(out_shapes),
        in_specs=[pl.BlockSpec(memory_space=pltpu.SMEM)] * smem + in_specs,
        out_specs=tuple(out_specs),
        scratch_shapes=[*own, *([pltpu.SemaphoreType.DMA((n_copies,))] if n_copies else []), *scratch],
        compiler_params=pltpu.CompilerParams(vmem_limit_bytes=used + ROOM),
        cost_estimate=pl.CostEstimate(flops=int(us * 3.3e9), bytes_accessed=int(us * 1e7), transcendentals=0),
    )(*tables, *arrays)


def running_ends(len_ref):
    ends, total = [], 0
    for k in range(SEGS):
        total = total + len_ref[0, k]
        ends.append(total)
    return ends


def live_tokens(ends, count):
    total = 0
    for k in range(SEGS):
        total = jnp.where(k < count, ends[k], total)
    return total


def lookup(pos, ends, values, first):
    found = first
    for k in range(SEGS - 1):
        found = jnp.where(pos >= ends[k], values[k], found)
    return found


def token_positions():
    shape = (LEN // BLK, BLK)
    return lax.broadcasted_iota(jnp.int32, shape, 0) * BLK + lax.broadcasted_iota(
        jnp.int32, shape, 1
    )


def twice(row):
    return jnp.concatenate([row, row], axis=1)


def stacked(pair):
    lane = lax.broadcasted_iota(jnp.int32, pair.shape, 1)
    zero = jnp.zeros_like(pair)
    return jnp.concatenate(
        [jnp.where(lane < 64, pair, zero), jnp.where(lane < 64, zero, pair)], axis=0
    )


def diagonal(product):
    return jnp.concatenate([product[:64, :BLK], product[64:, BLK:]], axis=0)


def own_rows(row):
    return jnp.concatenate(
        [jnp.broadcast_to(row[:, :BLK], (64, BLK)), jnp.broadcast_to(row[:, BLK:], (64, BLK))], axis=0
    )


def in_chunks(n, body):
    def four(j, carry):
        body(4 * j, 4)
        return carry

    lax.fori_loop(0, lax.shift_right_logical(n, 2), four, 0)
    for rest in (3, 2, 1):
        pl.when((n & 3) == rest)(functools.partial(body, n & ~3, rest))


def reset(m_ref, l_ref, acc_ref):
    m_ref[...] = jnp.full(m_ref.shape, MASKED, f32)
    l_ref[...] = jnp.zeros(l_ref.shape, f32)
    acc_ref[...] = jnp.zeros(acc_ref.shape, f32)


def soften(p, scores, values_t, m_ref, l_ref, acc_ref):
    before = m_ref[p, 0:1, :]
    peak = jnp.maximum(before, jnp.max(scores, axis=0, keepdims=True))
    shrink = jnp.exp(before - peak)
    raised = jnp.exp(scores - peak)
    m_ref[p, 0:1, :] = peak
    l_ref[p, 0:1, :] = l_ref[p, 0:1, :] * shrink + jnp.sum(raised, axis=0, keepdims=True)
    acc_ref[p] = acc_ref[p] * own_rows(shrink) + diagonal(nn(values_t, raised.astype(bf16)))


def settle(p, alive, m_ref, l_ref, acc_ref):
    total = l_ref[p, 0:1, :]
    mixed = jnp.transpose(acc_ref[p] * own_rows(alive / total))
    return mixed.astype(bf16), m_ref[p, 0:1, :] + jnp.log(total)


def inner_row(grads, mixed):
    product = jnp.transpose(grads.astype(f32) * mixed.astype(f32))
    return jnp.concatenate(
        [jnp.sum(product[:64], axis=0, keepdims=True), jnp.sum(product[64:], axis=0, keepdims=True)], axis=1
    )


def rms_scale(value):
    return lax.rsqrt(jnp.mean(value * value, axis=-1, keepdims=True) + EPS)


def rms_back(value, gain, grad):
    scale = rms_scale(value)
    weighted = grad * gain
    inner = jnp.mean(weighted * value, axis=-1, keepdims=True)
    unit = value * scale
    return (
        scale * weighted - unit * (scale * scale * inner),
        jnp.sum(grad * unit, axis=0, keepdims=True),
    )


def fill_bias(table_ref, bias_ref):
    key = lax.broadcasted_iota(jnp.int32, (BLK, BLK), 0)
    query = lax.broadcasted_iota(jnp.int32, (BLK, BLK), 1)
    for d in range(2):
        gap = d * BLK + query - key
        tiles = [jnp.full((BLK, BLK), table_ref[h, 0], f32) for h in range(4)]
        for level in range(1, NB):
            reached = gap >= THRESHOLDS[level]
            tiles = [jnp.where(reached, table_ref[h, level], tiles[h]) for h in range(4)]
        if d == 0:
            tiles = [jnp.where(gap >= 0, tile, MASKED) for tile in tiles]
        for h in range(4):
            bias_ref[d * 2 + h // 2, :, (h % 2) * BLK : (h % 2 + 1) * BLK] = tiles[h]
    for h in range(4):
        far = jnp.full((BLK, BLK), table_ref[h, NB - 1], f32)
        bias_ref[4 + h // 2, :, (h % 2) * BLK : (h % 2 + 1) * BLK] = far


def self_scores(distances, p, kstart, qs_ref, k_ref, bias_ref, start2):
    m = len(distances)
    keys = k_ref[pl.ds(kstart, m * BLK), p * BLK : (p + 1) * BLK]
    scores = nt(keys, qs_ref[p])
    parts = [scores[k * BLK : (k + 1) * BLK] + bias_ref[2 * d + p] for k, d in enumerate(distances)]
    index = kstart + lax.broadcasted_iota(jnp.int32, (m * BLK, 2 * BLK), 0)
    return jnp.where(index >= start2, jnp.concatenate(parts, axis=0) if m > 1 else parts[0], MASKED)


def self_spans(b, ends, live):
    pos = b * BLK
    first = lax.shift_right_logical(lookup(pos, ends, ends, 0), 7)
    return pos < live, first, b - first + 1


def self_forward(half, ends, live, q_ref, k_ref, vt_ref, bias_ref, start_ref, o_ref, lse_ref, qs_ref, m_ref, l_ref, acc_ref):
    def step(i, carry):
        b = half * 4 + i
        alive, first, n = self_spans(b, ends, live)
        rows = pl.ds(pl.multiple_of(i * BLK, BLK), BLK)

        @pl.when(alive)
        def _():
            start2 = twice(start_ref[pl.ds(b, 1), :])
            for p in range(2):
                lanes = slice(p * BLK, (p + 1) * BLK)
                qs_ref[p] = stacked(q_ref[pl.ds(pl.multiple_of(b * BLK, BLK), BLK), lanes])
            reset(m_ref, l_ref, acc_ref)

            def chunk(j, m):
                kstart = pl.multiple_of((first + j) * BLK, BLK)
                distances = [jnp.minimum(n - 1 - j - k, 2) for k in range(m)]
                for p in range(2):
                    scores = self_scores(distances, p, kstart, qs_ref, k_ref, bias_ref, start2)
                    values_t = vt_ref[p * BLK : (p + 1) * BLK, pl.ds(kstart, m * BLK)]
                    soften(p, scores, values_t, m_ref, l_ref, acc_ref)

            in_chunks(n, chunk)
            for p in range(2):
                mixed, lse = settle(p, (start2 < BIG).astype(f32), m_ref, l_ref, acc_ref)
                o_ref[rows, p * BLK : (p + 1) * BLK] = mixed
                lse_ref[p, pl.ds(i, 1), :] = lse

        @pl.when(jnp.logical_not(alive))
        def _():
            o_ref[rows, :] = jnp.zeros((BLK, OWN), bf16)
            for p in range(2):
                lse_ref[p, pl.ds(i, 1), :] = jnp.zeros((1, 2 * BLK), f32)

        return carry

    lax.fori_loop(0, 4, step, 0)


def set_starts(ends, live, start_ref):
    pos = token_positions()
    start_ref[...] = jnp.where(pos < live, lookup(pos, ends, ends, 0), BIG)


def first_kernel(
    io, t_ref, len_ref, cnt_ref, table_ref,
    x_ref, gain_ref, wq_ref, wk_ref, wv_ref,
    n1_ref, q_ref, k_ref, v_ref, vt_ref, kt_ref, bias_ref, o_ref, lse_ref,
    start_ref, *work,
):
    ends = running_ends(len_ref)
    live = live_tokens(ends, cnt_ref[0])
    set_starts(ends, live, start_ref)
    fill_bias(table_ref, bias_ref)
    io.done(bias_ref)
    io.ready(x_ref, gain_ref, wq_ref, wk_ref, wv_ref)

    def project(i, carry):
        rows = pl.ds(pl.multiple_of(i * 256, 256), 256)
        value = x_ref[rows, :].astype(f32)
        low = (value * rms_scale(value) * gain_ref[...]).astype(bf16)
        n1_ref[rows, :] = low
        q_ref[rows, :] = nn(low, wq_ref[...]).astype(bf16)
        keys = nn(low, wk_ref[...])
        k_ref[rows, :] = keys.astype(bf16)
        kt_ref[:, rows] = jnp.transpose(keys).astype(bf16)
        values = nn(low, wv_ref[...])
        v_ref[rows, :] = values.astype(bf16)
        vt_ref[:, rows] = jnp.transpose(values).astype(bf16)
        return carry

    lax.fori_loop(0, 4, project, 0)
    io.done(n1_ref, q_ref, k_ref, v_ref, vt_ref, kt_ref)
    self_forward(
        1 - t_ref[0], ends, live, q_ref, k_ref, vt_ref, bias_ref, start_ref, o_ref, lse_ref, *work
    )


def second_kernel(
    io, t_ref, len_ref, cnt_ref,
    q_ref, k_ref, vt_ref, bias_ref,
    o_ref, lse_ref,
    start_ref, *work,
):
    ends = running_ends(len_ref)
    live = live_tokens(ends, cnt_ref[0])
    set_starts(ends, live, start_ref)
    io.ready(q_ref, k_ref, vt_ref, bias_ref)
    self_forward(
        t_ref[0], ends, live, q_ref, k_ref, vt_ref, bias_ref, start_ref, o_ref, lse_ref, *work
    )


def memory_kernel(
    io, place_ref, mem_ref, ck_ref, cv_ref, pack_ref, packo_ref,
    mk_ref, mv_ref, mkt_ref, mvt_ref, so_out, co_out, cq_out, cko_ref, cvo_ref,
):
    for core, pack in ((place_ref[1], pack_ref), (1 - place_ref[1], packo_ref)):
        for ref, parts in zip((so_out, co_out, cq_out, cko_ref, cvo_ref), packed_parts(core), strict=True):
            for rows, where in parts:
                ref[rows, :] = pack[where]
    io.done(so_out, co_out, cq_out, cko_ref, cvo_ref)
    io.ready(mem_ref, ck_ref, cv_ref)

    def project(i, carry):
        rows = pl.ds(pl.multiple_of(i * 256, 256), 256)
        value = mem_ref[rows, :]
        for side, (wk, wv) in enumerate(((ck_ref, cv_ref), (cko_ref, cvo_ref))):
            lanes = slice(side * OWN, (side + 1) * OWN)
            keys = nn(value, wk[...])
            mk_ref[rows, lanes] = keys.astype(bf16)
            mkt_ref[lanes, rows] = jnp.transpose(keys).astype(bf16)
            values = nn(value, wv[...])
            mv_ref[rows, lanes] = values.astype(bf16)
            mvt_ref[lanes, rows] = jnp.transpose(values).astype(bf16)
        return carry

    lax.fori_loop(0, 4, project, 0)


def set_ranges(ends, mends, live, low_ref, high_ref):
    pos = token_positions()
    low_ref[...] = jnp.where(pos < live, lookup(pos, ends, mends, 0), BIG)
    high_ref[...] = lookup(pos, ends, mends[1:], mends[0])


def cross_blocks(half, ends, mends, live, block, dead):
    def step(i, carry):
        b = half * 4 + i
        pos = b * BLK
        alive = pos < live
        last = jnp.minimum(pos + BLK, live) - 1
        first = lax.shift_right_logical(lookup(pos, ends, mends, 0), 7)
        end = lax.shift_right_logical(lookup(last, ends, mends[1:], mends[0]) + BLK - 1, 7)
        pl.when(alive)(lambda: block(i, b, first, end - first))
        pl.when(jnp.logical_not(alive))(lambda: dead(i))
        return carry

    lax.fori_loop(0, 4, step, 0)


def cross_allowed(kstart, m, low2, high2):
    index = kstart + lax.broadcasted_iota(jnp.int32, (m * BLK, 2 * BLK), 0)
    return (index >= low2) & (index < high2)


def third_kernel(
    io, t_ref, len_ref, mlen_ref, cnt_ref,
    x_ref, keep_ref, recv_ref, so_ref, soo_ref, gain2_ref, cq_ref, cqo_ref,
    mk_ref, mvt_ref, co_ref, coo_ref, gain3_ref,
    h1_ref, n2_ref, q_ref, mixed_ref, lse_ref, h2_ref, n3_ref,
    low_ref, high_ref, qs_ref, m_ref, l_ref, acc_ref,
):
    t = t_ref[0]
    ends, mends = running_ends(len_ref), running_ends(mlen_ref)
    live = live_tokens(ends, cnt_ref[0])
    set_ranges(ends, mends, live, low_ref, high_ref)

    io.ready(x_ref, keep_ref, recv_ref, so_ref, soo_ref, gain2_ref, cq_ref, cqo_ref)

    def before(i, carry):
        rows = pl.ds(pl.multiple_of(i * 256, 256), 256)
        value = x_ref[rows, :].astype(f32)
        value = value + nn(keep_ref[rows, :], so_ref[...]) + nn(recv_ref[rows, :], soo_ref[...])
        h1_ref[rows, :] = value
        low = (value * rms_scale(value) * gain2_ref[...]).astype(bf16)
        n2_ref[rows, :] = low
        q_ref[rows, :OWN] = nn(low, cq_ref[...]).astype(bf16)
        q_ref[rows, OWN:] = nn(low, cqo_ref[...]).astype(bf16)
        return carry

    lax.fori_loop(0, 2, before, 0)
    io.done(h1_ref, n2_ref, q_ref)
    io.ready(mk_ref, mvt_ref)

    def block(i, b, first, n):
        low2, high2 = twice(low_ref[pl.ds(b, 1), :]), twice(high_ref[pl.ds(b, 1), :])
        rows = pl.ds(pl.multiple_of(i * BLK, BLK), BLK)
        for p in range(4):
            qs_ref[p] = stacked(q_ref[rows, p * BLK : (p + 1) * BLK])
        reset(m_ref, l_ref, acc_ref)

        def chunk(j, m):
            kstart = pl.multiple_of((first + j) * BLK, BLK)
            span = pl.ds(kstart, m * BLK)
            allowed = cross_allowed(kstart, m, low2, high2)
            for p in range(4):
                lanes = slice(p * BLK, (p + 1) * BLK)
                scores = jnp.where(allowed, nt(mk_ref[span, lanes], qs_ref[p]), MASKED)
                soften(p, scores, mvt_ref[lanes, span], m_ref, l_ref, acc_ref)

        in_chunks(n, chunk)
        for p in range(4):
            mixed, lse = settle(p, (low2 < BIG).astype(f32), m_ref, l_ref, acc_ref)
            mixed_ref[rows, p * BLK : (p + 1) * BLK] = mixed
            lse_ref[p, pl.ds(i, 1), :] = lse

    def dead(i):
        mixed_ref[pl.ds(pl.multiple_of(i * BLK, BLK), BLK), :] = jnp.zeros((BLK, WIDTH), bf16)
        for p in range(4):
            lse_ref[p, pl.ds(i, 1), :] = jnp.zeros((1, 2 * BLK), f32)

    cross_blocks(t, ends, mends, live, block, dead)

    io.done(mixed_ref, lse_ref)
    io.ready(co_ref, coo_ref, gain3_ref)

    def after(i, carry):
        rows = pl.ds(pl.multiple_of(i * 256, 256), 256)
        value = h1_ref[rows, :]
        value = value + nn(mixed_ref[rows, :OWN], co_ref[...]) + nn(mixed_ref[rows, OWN:], coo_ref[...])
        h2_ref[rows, :] = value
        n3_ref[rows, :] = (value * rms_scale(value) * gain3_ref[...]).astype(bf16)
        return carry

    lax.fori_loop(0, 2, after, 0)


def feed_kernel(
    io, place_ref, n3_ref, fi_ref, cot_ref, fo_ref,
    out_ref, gn_ref, act_ref, gp_ref,
):
    tile = 256
    n_tiles = fi_ref.shape[1] // tile
    root = math.sqrt(2 / math.pi)
    base = place_ref[0] * HALF
    io.ready(n3_ref, fi_ref, cot_ref, fo_ref)

    def hidden(j, carry):
        lanes = pl.ds(pl.multiple_of(j * tile, tile), tile)
        for i in range(2):
            rows = slice(i * 256, (i + 1) * 256)
            pre = nn(n3_ref[rows, :], fi_ref[:, lanes])
            square = pre * pre
            bent = jnp.tanh(pre * (root + (root * 0.044715) * square))
            gate = 0.5 + 0.5 * bent
            slope = gate + pre * (0.5 - 0.5 * bent * bent) * (root + (root * 0.134145) * square)
            act_ref[rows, lanes] = (pre * gate).astype(bf16)
            grads = nt(cot_ref[pl.ds(pl.multiple_of(base + i * 256, 256), 256), :], fo_ref[lanes, :])
            gp_ref[rows, lanes] = (grads * slope).astype(bf16)
        return carry

    lax.fori_loop(0, n_tiles, hidden, 0)
    io.done(act_ref, gp_ref)

    def outward(i, carry):
        rows = pl.ds(pl.multiple_of(i * 256, 256), 256)
        out_ref[rows, :] = nn(act_ref[rows, :], fo_ref[...]).astype(bf16)
        gn_ref[rows, :] = nt(gp_ref[rows, :], fi_ref[...]).astype(bf16)
        return carry

    lax.fori_loop(0, 2, outward, 0)


def feed_weights_kernel(
    io, place_ref, h2_ref, own_ref, oth_ref, n3_ref, gp_ref, n3o_ref, gpo_ref, act_ref, cot_ref, acto_ref,
    hold_ref, senda_ref, sendb_ref, sendc_ref, sendd_ref, outa_ref, outb_ref,
    n3t_ref,
):
    t, c = place_ref[0], place_ref[1]

    parts = (senda_ref, sendb_ref, sendc_ref, sendd_ref)

    def put(core, start, lanes, grads):
        low = grads.astype(bf16)

        @pl.when(c == core)
        def _():
            hold_ref[start : start + low.shape[0], lanes] = low

        @pl.when(c != core)
        def _():
            for k in range(low.shape[0] // 256):
                parts[start // 256 + k][:, lanes] = low[k * 256 : (k + 1) * 256]

    mine = pl.ds(pl.multiple_of(t * HALF, HALF), HALF)
    theirs = pl.ds(pl.multiple_of((1 - t) * HALF, HALF), HALF)
    io.ready(n3_ref, gp_ref, n3o_ref, gpo_ref)
    n3t_ref[:, :HALF] = jnp.transpose(n3_ref[...].astype(f32)).astype(bf16)
    n3t_ref[:, HALF:] = jnp.transpose(n3o_ref[...].astype(f32)).astype(bf16)
    n_tiles = gp_ref.shape[1] // 256
    for j in range(n_tiles):
        lanes = slice(j * 256, (j + 1) * 256)
        grads = nn(n3t_ref[:, :HALF], gp_ref[:, lanes]) + nn(n3t_ref[:, HALF:], gpo_ref[:, lanes])
        put(0, (j // 2) * WIDTH, slice((j % 2) * 256, (j % 2 + 1) * 256), grads)
    io.ready(act_ref, cot_ref, acto_ref)
    for j in range(n_tiles):
        lanes = slice(j * 256, (j + 1) * 256)
        grads = tn(act_ref[:, lanes], cot_ref[mine, :]) + tn(acto_ref[:, lanes], cot_ref[theirs, :])
        put(1, j * 256, slice(0, WIDTH), grads)
    io.ready(h2_ref, own_ref, oth_ref)
    own = (h2_ref[...] + own_ref[...].astype(f32)).astype(bf16)
    for k, out_ref in enumerate((outa_ref, outb_ref)):

        @pl.when(t == k)
        def _():
            out_ref[...] = own

        @pl.when(t != k)
        def _():
            out_ref[...] = oth_ref[...]


def cross_back_kernel(
    io, t_ref, len_ref, mlen_ref, cnt_ref,
    gn_ref, gnr_ref, h2_ref, gain3_ref, cot_ref, co_ref, coo_ref,
    q_ref, mk_ref, mkt_ref, mv_ref, lse_ref, mixed_ref, cq_ref, cqo_ref, h1_ref, gain2_ref, so_ref, soo_ref,
    gb2_ref, dq_ref, dk_ref, dv_ref, gh1_ref, gb1_ref, gm1_ref, gm1o_ref, gains_ref,
    low_ref, high_ref, live_ref, gm_ref, dk_acc, dv_acc, gh2_ref, qs_ref, gs_ref, acc_ref,
):
    t = t_ref[0]
    ends, mends = running_ends(len_ref), running_ends(mlen_ref)
    live = live_tokens(ends, cnt_ref[0])
    set_ranges(ends, mends, live, low_ref, high_ref)
    alive_rows = t * HALF + lax.broadcasted_iota(jnp.int32, (HALF, BLK), 0)
    live_ref[...] = (alive_rows < live).astype(f32)
    dk_acc[...] = jnp.zeros_like(dk_acc)
    dv_acc[...] = jnp.zeros_like(dv_acc)
    gains_ref[...] = jnp.zeros_like(gains_ref)

    io.ready(gn_ref, gnr_ref, h2_ref, gain3_ref, cot_ref, co_ref, coo_ref)
    for i in range(2):
        rows = slice(i * 256, (i + 1) * 256)
        grad = gn_ref[rows, :].astype(f32) + gnr_ref[rows, :].astype(f32)
        back, gain = rms_back(h2_ref[rows, :], gain3_ref[...], grad)
        gains_ref[0:1, :] += gain
        grad = cot_ref[rows, :].astype(f32) + back
        gh2_ref[rows, :] = grad
        low = grad.astype(bf16)
        gb2_ref[rows, :] = low
        alive = live_ref[rows, 0:1]
        gm_ref[rows, :OWN] = (nt(low, co_ref[...]) * alive).astype(bf16)
        gm_ref[rows, OWN:] = (nt(low, coo_ref[...]) * alive).astype(bf16)
    io.done(gb2_ref)
    io.ready(q_ref, mk_ref, mkt_ref, mv_ref, lse_ref, mixed_ref)

    def block(i, b, first, n):
        low2, high2 = twice(low_ref[pl.ds(b, 1), :]), twice(high_ref[pl.ds(b, 1), :])
        rows = pl.ds(pl.multiple_of(i * BLK, BLK), BLK)
        inner = []
        for p in range(4):
            lanes = slice(p * BLK, (p + 1) * BLK)
            qs_ref[p] = stacked(q_ref[rows, lanes])
            gs_ref[p] = stacked(gm_ref[rows, lanes])
            inner.append(inner_row(gm_ref[rows, lanes], mixed_ref[rows, lanes]))
        acc_ref[...] = jnp.zeros(acc_ref.shape, f32)

        def chunk(j, m):
            kstart = pl.multiple_of((first + j) * BLK, BLK)
            span = pl.ds(kstart, m * BLK)
            allowed = cross_allowed(kstart, m, low2, high2)
            for p in range(4):
                lanes = slice(p * BLK, (p + 1) * BLK)
                scores = jnp.where(allowed, nt(mk_ref[span, lanes], qs_ref[p]), MASKED)
                probs = jnp.exp(scores - lse_ref[p, pl.ds(i, 1), :])
                low = (probs * (nt(mv_ref[span, lanes], gs_ref[p]) - inner[p])).astype(bf16)
                dk_acc[span, lanes] += nn(low, qs_ref[p])
                dv_acc[span, lanes] += nn(probs.astype(bf16), gs_ref[p])
                acc_ref[p] += diagonal(nn(mkt_ref[lanes, span], low))

        in_chunks(n, chunk)
        for p in range(4):
            dq_ref[rows, p * BLK : (p + 1) * BLK] = jnp.transpose(acc_ref[p]).astype(bf16)

    def dead(i):
        dq_ref[pl.ds(pl.multiple_of(i * BLK, BLK), BLK), :] = jnp.zeros((BLK, WIDTH), bf16)

    cross_blocks(t, ends, mends, live, block, dead)

    dk_ref[...] = dk_acc[...].astype(bf16)
    dv_ref[...] = dv_acc[...].astype(bf16)
    io.done(dq_ref, dk_ref, dv_ref)
    io.ready(cq_ref, cqo_ref, h1_ref, gain2_ref, so_ref, soo_ref)
    for i in range(2):
        rows = slice(i * 256, (i + 1) * 256)
        grad = nt(dq_ref[rows, :OWN], cq_ref[...]) + nt(dq_ref[rows, OWN:], cqo_ref[...])
        back, gain = rms_back(h1_ref[rows, :], gain2_ref[...], grad)
        gains_ref[1:2, :] += gain
        grad = gh2_ref[rows, :] + back
        gh1_ref[rows, :] = grad
        low = grad.astype(bf16)
        gb1_ref[rows, :] = low
        alive = live_ref[rows, 0:1]
        gm1_ref[rows, :] = (nt(low, so_ref[...]) * alive).astype(bf16)
        gm1o_ref[rows, :] = (nt(low, soo_ref[...]) * alive).astype(bf16)


def cross_weights_kernel(
    io, place_ref, mem_ref, dk_ref, dv_ref, n2_ref, dq_ref, mixed_ref, gb2_ref, keep_ref, gb1_ref, recv_ref,
    hold_ref, holdo_ref, send_ref,
    memt_ref, fold_ref,
):
    c = place_ref[1]
    io.ready(mem_ref, dk_ref, dv_ref, n2_ref, dq_ref, mixed_ref, gb2_ref, keep_ref, gb1_ref, recv_ref)
    memt_ref[...] = jnp.transpose(mem_ref[...].astype(f32)).astype(bf16)
    n2t = jnp.transpose(n2_ref[...].astype(f32)).astype(bf16)
    for side in range(2):
        lanes = slice(side * OWN, (side + 1) * OWN)
        mixed1 = keep_ref if side == 0 else recv_ref
        fold_ref[0] = tn(mixed_ref[:, lanes], gb2_ref[...]).astype(bf16)
        fold_ref[1] = tn(mixed1[...], gb1_ref[...]).astype(bf16)
        fold(fold_ref, 2, nn(n2t, dq_ref[:, lanes]))
        fold(fold_ref, 3, nn(memt_ref[...], dk_ref[:, lanes]))
        fold(fold_ref, 4, nn(memt_ref[...], dv_ref[:, lanes]))
        deal(c, fold_ref, hold_ref if side == 0 else holdo_ref, send_ref, side * 640)


def memory_back_kernel(
    io, place_ref, dk_ref, ck_ref, cko_ref, dv_ref, cv_ref, cvo_ref, gmem_ref, gmems_ref
):
    t = place_ref[0]
    io.ready(dk_ref, ck_ref, cko_ref, dv_ref, cv_ref, cvo_ref)
    for i in range(4):
        rows = slice(i * 256, (i + 1) * 256)
        grads = nt(dk_ref[rows, :OWN], ck_ref[...]) + nt(dk_ref[rows, OWN:], cko_ref[...])
        grads += nt(dv_ref[rows, :OWN], cv_ref[...]) + nt(dv_ref[rows, OWN:], cvo_ref[...])
        low = grads.astype(bf16)

        @pl.when(t == 0)
        def _():
            gmem_ref[rows, :] = low[:, :OWN]
            gmems_ref[rows, :] = low[:, OWN:]

        @pl.when(t != 0)
        def _():
            gmem_ref[rows, :] = low[:, OWN:]
            gmems_ref[rows, :] = low[:, :OWN]


def fold(fold_ref, k, weight):
    low = weight.astype(bf16)
    fold_ref[k, :, :OWN] = low[:256]
    fold_ref[k, :, OWN:] = low[256:]


def deal(c, fold_ref, hold_ref, send_ref, base):
    for k in range(fold_ref.shape[0]):
        rows = slice(k * BLK, (k + 1) * BLK)
        hold_ref[rows, :] = fold_ref[k, pl.ds(pl.multiple_of(c * BLK, BLK), BLK), :]
        rows = slice(base + k * BLK, base + (k + 1) * BLK)
        send_ref[rows, :] = fold_ref[k, pl.ds(pl.multiple_of((1 - c) * BLK, BLK), BLK), :]


def self_back_blocks(
    half, ends, live, start_ref, g_ref, mixed_ref, q_ref, k_ref, kt_ref, v_ref, bias_ref, lse_ref,
    dq_ref, dk_acc, dv_acc, near_acc, qs_ref, gs_ref, acc_ref,
):
    def step(i, carry):
        b = half * 4 + i
        alive, first, n = self_spans(b, ends, live)
        rows = pl.ds(pl.multiple_of(i * BLK, BLK), BLK)

        @pl.when(alive)
        def _():
            start2 = twice(start_ref[pl.ds(b, 1), :])
            inner = []
            for p in range(2):
                lanes = slice(p * BLK, (p + 1) * BLK)
                qs_ref[p] = stacked(q_ref[pl.ds(pl.multiple_of(b * BLK, BLK), BLK), lanes])
                gs_ref[p] = stacked(g_ref[rows, lanes])
                inner.append(inner_row(g_ref[rows, lanes], mixed_ref[rows, lanes]))
            acc_ref[...] = jnp.zeros(acc_ref.shape, f32)

            def chunk(j, m):
                kstart = pl.multiple_of((first + j) * BLK, BLK)
                span = pl.ds(kstart, m * BLK)
                distances = [jnp.minimum(n - 1 - j - k, 2) for k in range(m)]
                for p in range(2):
                    lanes = slice(p * BLK, (p + 1) * BLK)
                    scores = self_scores(distances, p, kstart, qs_ref, k_ref, bias_ref, start2)
                    probs = jnp.exp(scores - lse_ref[p, pl.ds(i, 1), :])
                    grad_scores = probs * (nt(v_ref[span, lanes], gs_ref[p]) - inner[p])
                    for k, d in enumerate(distances):
                        near_acc[2 * d + p] += grad_scores[k * BLK : (k + 1) * BLK]
                    low = grad_scores.astype(bf16)
                    dk_acc[span, lanes] += nn(low, qs_ref[p])
                    dv_acc[span, lanes] += nn(probs.astype(bf16), gs_ref[p])
                    acc_ref[p] += diagonal(nn(kt_ref[lanes, span], low))

            in_chunks(n, chunk)
            for p in range(2):
                dq_ref[rows, p * BLK : (p + 1) * BLK] = jnp.transpose(acc_ref[p]).astype(bf16)

        @pl.when(jnp.logical_not(alive))
        def _():
            dq_ref[rows, :] = jnp.zeros((BLK, OWN), bf16)

        return carry

    lax.fori_loop(0, 4, step, 0)


def self_back_own_kernel(
    io, place_ref, len_ref, cnt_ref,
    gm_ref, mixed_ref, q_ref, k_ref, kt_ref, v_ref, bias_ref, lse_ref,
    dq_ref, dk_acc, dv_acc, near_acc,
    start_ref, *work,
):
    ends = running_ends(len_ref)
    live = live_tokens(ends, cnt_ref[0])
    set_starts(ends, live, start_ref)
    for ref in (dk_acc, dv_acc, near_acc):
        ref[...] = jnp.zeros_like(ref)
    io.ready(gm_ref, mixed_ref, q_ref, k_ref, kt_ref, v_ref, bias_ref, lse_ref)
    self_back_blocks(
        place_ref[0], ends, live, start_ref, gm_ref, mixed_ref, q_ref, k_ref, kt_ref, v_ref, bias_ref, lse_ref,
        dq_ref, dk_acc, dv_acc, near_acc, *work,
    )


def self_back_kernel(
    io, place_ref, len_ref, cnt_ref,
    gmr_ref, mixed_ref, dqm_ref, dkm_ref, dvm_ref, nearm_ref, q_ref, k_ref, kt_ref, v_ref, bias_ref, lse_ref,
    n1_ref, x_ref, gh1_ref, gain1_ref, gains_ref, wq_ref, wk_ref, wv_ref,
    hold_ref, send_ref, gia_ref, gib_ref,
    start_ref, dqo_ref, dq_ref, dk_acc, dv_acc, near_acc, n1t_ref, fold_ref, sums_ref, small_ref, *work,
):
    t = place_ref[0]
    ends = running_ends(len_ref)
    live = live_tokens(ends, cnt_ref[0])
    set_starts(ends, live, start_ref)
    small_ref[...] = jnp.zeros_like(small_ref)
    for ref, so_far in ((dk_acc, dkm_ref), (dv_acc, dvm_ref), (near_acc, nearm_ref)):
        ref[...] = so_far[...]
    io.ready(mixed_ref, q_ref, k_ref, kt_ref, v_ref, bias_ref, lse_ref)
    self_back_blocks(
        1 - t, ends, live, start_ref, gmr_ref, mixed_ref, q_ref, k_ref, kt_ref, v_ref, bias_ref, lse_ref,
        dqo_ref, dk_acc, dv_acc, near_acc, *work,
    )
    dq_ref[pl.ds(pl.multiple_of(t * HALF, HALF), HALF), :] = dqm_ref[...]
    dq_ref[pl.ds(pl.multiple_of((1 - t) * HALF, HALF), HALF), :] = dqo_ref[...]

    io.ready(n1_ref)
    n1t_ref[...] = jnp.transpose(n1_ref[...].astype(f32)).astype(bf16)
    low_k, low_v = dk_acc[...].astype(bf16), dv_acc[...].astype(bf16)
    for k, grads in enumerate((dq_ref[...], low_k, low_v)):
        fold(fold_ref, k, nn(n1t_ref[...], grads))
    deal(place_ref[1], fold_ref, hold_ref, send_ref, 0)
    io.ready(x_ref, gh1_ref, gain1_ref, gains_ref, wq_ref, wk_ref, wv_ref)
    gain1 = jnp.zeros((1, WIDTH), f32)
    for i in range(4):
        rows = slice(i * 256, (i + 1) * 256)
        grads = nt(dq_ref[rows, :], wq_ref[...]) + nt(low_k[rows], wk_ref[...]) + nt(low_v[rows], wv_ref[...])
        back, gain = rms_back(x_ref[rows, :].astype(f32), gain1_ref[...], grads)
        gain1 += gain
        mine = (t == i // 2).astype(f32)
        back += mine * gh1_ref[(i % 2) * 256 : (i % 2 + 1) * 256, :]
        (gia_ref if i < 2 else gib_ref)[(i % 2) * 256 : (i % 2 + 1) * 256, :] = back.astype(bf16)
    io.done(gia_ref, gib_ref)
    key = lax.broadcasted_iota(jnp.int32, (BLK, BLK), 0)
    query = lax.broadcasted_iota(jnp.int32, (BLK, BLK), 1)
    gaps = [query - key, BLK + query - key]
    for level in range(NB):
        for p in range(2):
            row = jnp.zeros((1, 2 * BLK), f32)
            for d in range(2):
                inside = gaps[d] >= THRESHOLDS[level]
                if level + 1 < NB:
                    inside &= gaps[d] < THRESHOLDS[level + 1]
                picked = jnp.where(twice(inside.astype(f32)) > 0, near_acc[2 * d + p], 0.0)
                row += jnp.sum(picked, axis=0, keepdims=True)
            if level == NB - 1:
                row += jnp.sum(near_acc[4 + p], axis=0, keepdims=True)
            sums_ref[level : level + 1, p * 256 : (p + 1) * 256] = row
    for h in range(4):
        lanes = jnp.transpose(sums_ref[:, h * BLK : (h + 1) * BLK])
        small_ref[3 + h : 4 + h, :NB] = jnp.sum(lanes, axis=0, keepdims=True)
    for k, gain in enumerate((gain1, gains_ref[1:2, :], gains_ref[0:1, :])):
        small_ref[k : k + 1, :] = gain
    low = small_ref[...].astype(bf16)
    hold_ref[384:, :] = low
    send_ref[384:, :] = low


def join_kernel(io, place_ref, own_ref, got_ref, recv_ref, mine_ref, theirs_ref, hold_ref, send_ref):
    x = place_ref[2]
    io.ready(own_ref, got_ref, recv_ref, mine_ref, theirs_ref)
    for k in range(8):
        if k < 5:
            rows = slice(k * BLK, (k + 1) * BLK)
            total = own_ref[rows, :].astype(f32) + got_ref[rows, :].astype(f32) + recv_ref[rows, :].astype(f32)
        else:
            rows = slice((k - 5) * BLK, (k - 4) * BLK)
            total = mine_ref[rows, :].astype(f32) + theirs_ref[rows, :].astype(f32)
        low = total.astype(bf16)
        rows = slice((k % 4) * BLK, (k % 4 + 1) * BLK)

        @pl.when(x == k // 4)
        def _():
            hold_ref[rows, :] = low

        @pl.when(x != k // 4)
        def _():
            send_ref[rows, :] = low

    low = (mine_ref[384:, :].astype(f32) + theirs_ref[384:, :].astype(f32)).astype(bf16)
    hold_ref[HALF:, :] = low
    send_ref[HALF:, :] = low


def feed_halve_kernel(io, place_ref, hold_ref, gota_ref, gotb_ref, gotc_ref, gotd_ref, keep_ref, send_ref):
    x = place_ref[2]
    for k, got_ref in enumerate((gota_ref, gotb_ref, gotc_ref, gotd_ref)):
        rows, to = slice(k * 256, (k + 1) * 256), slice((k % 2) * 256, (k % 2 + 1) * 256)
        low = (hold_ref[rows, :].astype(f32) + got_ref[...].astype(f32)).astype(bf16)

        @pl.when(x == k // 2)
        def _():
            keep_ref[to, :] = low

        @pl.when(x != k // 2)
        def _():
            send_ref[to, :] = low


def halve_kernel(slot, every, io, place_ref, hold_ref, got_ref, keep_ref, send_ref):
    bit, size = place_ref[slot], keep_ref.shape[0] - every
    io.ready(hold_ref, got_ref)
    for k in range(2):
        rows = slice(k * size, (k + 1) * size)
        low = (hold_ref[rows, :].astype(f32) + got_ref[rows, :].astype(f32)).astype(bf16)

        @pl.when(bit == k)
        def _():
            keep_ref[:size, :] = low

        @pl.when(bit != k)
        def _():
            send_ref[:size, :] = low

    if every:
        low = (hold_ref[2 * size :, :].astype(f32) + got_ref[2 * size :, :].astype(f32)).astype(bf16)
        keep_ref[size:, :] = low
        send_ref[size:, :] = low


def total_kernel(io, _, hold_ref, got_ref, out_ref, *small_refs):
    io.ready(hold_ref, got_ref)
    total = hold_ref[...].astype(f32) + got_ref[...].astype(f32)
    out_ref[...] = total[: out_ref.shape[0]].astype(bf16)
    for small_ref in small_refs:
        small_ref[...] = total[out_ref.shape[0] :]


def merge_kernel(slot, io, place_ref, own_ref, got_ref, out_ref):
    bit, size = place_ref[slot], own_ref.shape[0]
    io.ready(own_ref, got_ref)
    out_ref[pl.ds(pl.multiple_of(bit * size, size), size), :] = own_ref[...]
    out_ref[pl.ds(pl.multiple_of((1 - bit) * size, size), size), :] = got_ref[...]


def feed_unfold_kernel(io, place_ref, own_ref, pair_ref, core_ref, both_ref, fi_ref, fo_ref):
    c, x = place_ref[1], place_ref[2]
    io.ready(own_ref, pair_ref, core_ref, both_ref)
    for ref, core, bit in ((own_ref, c, x), (pair_ref, c, 1 - x), (core_ref, 1 - c, x), (both_ref, 1 - c, 1 - x)):
        at = pl.ds(pl.multiple_of(bit * WIDTH, WIDTH), WIDTH)

        @pl.when(core == 0)
        def _():
            fi_ref[:, at] = ref[...].astype(f32)

        @pl.when(core != 0)
        def _():
            fo_ref[at, :] = ref[...].astype(f32)


def unfold_kernel(
    io, place_ref, own_ref, pair_ref, core_ref, both_ref,
    co_ref, so_ref, cq_ref, ck_ref, cv_ref, wq_ref, wk_ref, wv_ref,
):
    c, x = place_ref[1], place_ref[2]
    outs = (co_ref, so_ref, cq_ref, ck_ref, cv_ref, wq_ref, wk_ref, wv_ref)

    def spread(ref, core, bit):
        low = pl.ds(pl.multiple_of(core * BLK, BLK), BLK)
        high = pl.ds(pl.multiple_of(256 + core * BLK, BLK), BLK)
        for k, out in enumerate(outs):
            rows = slice((k % 4) * BLK, (k % 4 + 1) * BLK)

            @pl.when(bit == k // 4)
            def _():
                if k < 2:
                    out[low, :] = ref[rows, :].astype(f32)
                else:
                    out[low, :] = ref[rows, :OWN].astype(f32)
                    out[high, :] = ref[rows, OWN:].astype(f32)

    for ref, core, bit in ((own_ref, c, x), (pair_ref, c, 1 - x), (core_ref, 1 - c, x), (both_ref, 1 - c, 1 - x)):
        io.ready(ref)
        spread(ref, core, bit)


def swap(value, axis="tensor", bit=0):
    return lax.ppermute(value, axis, [(i, i ^ (1 << bit)) for i in range(lax.axis_size(axis))])


def shards(
    inputs, memory, cotangent, dec_lengths, mem_lengths, counts,
    self_gain, self_query, self_key, self_value, self_out, rel_table,
    cross_gain, cross_query, cross_key, cross_value, cross_out,
    feed_gain, feed_in, feed_out,
):
    v = pltpu.VMEM
    i32 = jnp.int32
    t, c, x = (lax.axis_index(name).astype(i32) for name in ("tensor", "core", "pair"))
    ring = lax.axis_size("ring")
    at_ring = lax.axis_index("ring").astype(i32)
    bits = range(ring.bit_length() - 1)
    ring_bits = [lax.shift_right_logical(at_ring, k) & 1 for k in bits]
    place = jnp.stack([t, c, x, *ring_bits])
    place_oth = jnp.stack([1 - t, c, x, *ring_bits])

    def halve(hold, got, slot, every=0):
        shape = (((hold.shape[0] - every) // 2 + every, WIDTH), bf16, "near")
        return call(
            functools.partial(halve_kernel, slot, every), [shape, shape], [], (place, Near(hold), Near(got)), us=SHORT
        )

    def merge(own, got, slot):
        shape = ((2 * own.shape[0], WIDTH), bf16, "near")
        return call(functools.partial(merge_kernel, slot), [shape], [], (place, Near(own), Near(got)), us=SHORT)[0]

    def tie(*arrays):
        return lax.optimization_barrier(arrays)
    gain1, gain2, gain3 = (g.reshape(1, WIDTH) for g in (self_gain, cross_gain, feed_gain))
    table = rel_table.T

    tok = (LEN, WIDTH)
    half = (HALF, WIDTH)
    heads, heads_t, part = (LEN, OWN), (OWN, LEN), (HALF, OWN)
    narrow, wide = (OWN, WIDTH), (WIDTH, OWN)
    row_tile = v((LEN // BLK, BLK), i32)
    tiles = ((6, BLK, 2 * BLK), f32)

    def forward_work(n):
        rows = v((n, 8, 2 * BLK), f32)
        return [v((n, 2 * BLK, BLK), bf16), rows, rows, v((n, BLK, BLK), f32)]

    def backward_work(n):
        return [v((n, 2 * BLK, BLK), bf16), v((n, 2 * BLK, BLK), bf16), v((n, BLK, BLK), f32)]

    pack, x_near, gain1_near, wq, wk, wv = call(
        pack_kernel,
        [((PACKED, WIDTH), bf16, "near")],
        [pltpu.SemaphoreType.DMA((6,))],
        (place, *map(Raw, (self_out, cross_out, cross_query, cross_key, cross_value))),
        us=SHORT, fetch=(inputs, gain1, self_query, self_key, self_value),
    )
    pack = swap(pack)
    n1, q, q_far, k, k_far, val, vt, kt, bias, bias_far, send1, lse1_oth = call(
        first_kernel,
        [(tok, bf16, "far"), (heads, bf16, "both"), (heads, bf16, "both"), (heads, bf16, "far"),
         (heads_t, bf16, "near"), (heads_t, bf16, "far"), (*tiles, "both"), (part, bf16, "near"),
         ((2, 4, 2 * BLK), f32, "near")],
        [row_tile, *forward_work(2)],
        (place, dec_lengths, counts, table, *map(Near, (x_near, gain1_near, wq, wk, wv))),
        smem=4, us=6,
    )
    mixed1_recv = swap(send1)
    mixed1_keep, lse1, memory_near, ck, cv, lse1_oth, send_far = call(
        second_kernel,
        [(part, bf16, "near"), ((2, 4, 2 * BLK), f32, "near")],
        [row_tile, *forward_work(2)],
        (place, dec_lengths, counts, Near(q), Near(k), Near(vt), Near(bias)),
        smem=3, us=SHORT, fetch=(memory, cross_key, cross_value), forward=(lse1_oth, send1),
    )
    pack, mixed1_keep = lax.optimization_barrier((pack, mixed1_keep))
    pack_core = swap(pack, "core")
    mk, mv, mkt, mvt, so_oth, co_oth, cq_oth, ck_oth, cv_oth, x_half, so, gain2_near, cq_w, co, gain3_near, keep_far, lse1 = call(
        memory_kernel,
        [(tok, bf16, "near"), (tok, bf16, "near"), ((WIDTH, LEN), bf16, "near"), ((WIDTH, LEN), bf16, "near"),
         (narrow, bf16, "near"), (narrow, bf16, "near"), (wide, bf16, "near"), (wide, bf16, "near"), (wide, bf16, "near")],
        [],
        (place, *map(Near, (memory_near, ck, cv, pack, pack_core))),
        us=SHORT, fetch=(Half(inputs), self_out, gain2, cross_query, cross_out, gain3), forward=(mixed1_keep, lse1),
    )
    (h1, n2, cq, mixed2, lse2, h2, n3, fi, cot, fo,
     mk, mv, mkt, so_oth_far, co_oth_far, cq_oth_far, ck_oth, cv_oth, recv_far) = call(
        third_kernel,
        [(half, f32, "far"), (half, bf16, "far"), (half, bf16, "far"), (half, bf16, "far"),
         ((4, 4, 2 * BLK), f32, "far"), (half, f32, "near"), (half, bf16, "near")],
        [row_tile, row_tile, *forward_work(4)],
        (place, dec_lengths, mem_lengths, counts,
         *map(Near, (x_half, mixed1_keep, mixed1_recv, so, so_oth, gain2_near, cq_w, cq_oth, mk, mvt, co, co_oth, gain3_near))),
        smem=4, us=9,
        fetch=(feed_in, cotangent, feed_out),
        forward=(mk, mv, mkt, so_oth, co_oth, cq_oth, ck_oth, cv_oth, mixed1_recv),
    )
    n3_recv = swap(n3)

    hidden = feed_in.shape[1]
    units = (HALF, hidden)
    out_own, gn3_own, act, gp, h2_far, n3_far = call(
        feed_kernel,
        [(half, bf16, "far"), (half, bf16, "far"), (units, bf16, "far"), (units, bf16, "far")],
        [],
        (place, *map(Near, (n3, fi, cot, fo))),
        us=5, forward=(h2, n3),
    )
    h2 = h2_far
    n3_recv, act = lax.optimization_barrier((n3_recv, act))
    out_oth, gn3_oth, act_oth, gp_oth = call(
        feed_kernel,
        [(half, bf16, "near"), (half, bf16, "near"), (units, bf16, "near"), (units, bf16, "near")],
        [],
        (place_oth, *map(Near, (n3_recv, fi, cot, fo))),
        us=5,
    )
    gn3_recv = swap(gn3_oth)
    quarter = ((256, WIDTH), bf16, "near")
    feed_hold, *feed_send, out_a, out_b = call(
        feed_weights_kernel,
        [((2 * WIDTH, WIDTH), bf16, "near"), *[quarter] * 4, (half, bf16, "far"), (half, bf16, "far")],
        [v((WIDTH, LEN), bf16)],
        (place, h2, out_own, Near(out_oth), n3_far, gp, Near(n3_recv), Near(gp_oth), act, Near(cot), Near(act_oth)),
        us=5,
    )
    feed_hold, feed_send = call(
        feed_halve_kernel,
        [(half, bf16, "near")] * 2,
        [],
        (place, Near(feed_hold), *(Near(swap(part, "core")) for part in feed_send)),
        us=SHORT,
    )
    gn3_recv, feed_send = tie(gn3_recv, feed_send)
    feed_got = swap(feed_send, "pair")

    (gb2, dcq, dmk, dmv, gh1, gb1, gm1, gm1_oth, gains, memory_near, n2_near, mixed2_near, keep, recv) = call(
        cross_back_kernel,
        [(half, bf16, "near"), (half, bf16, "near"), (tok, bf16, "near"), (tok, bf16, "near"), (half, f32, "near"),
         (half, bf16, "near"), (part, bf16, "near"), (part, bf16, "near"), ((8, WIDTH), f32, "near")],
        [row_tile, row_tile, v((HALF, BLK), f32), v(half, bf16), v(tok, f32), v(tok, f32), v(half, f32), *backward_work(4)],
        (place, dec_lengths, mem_lengths, counts, gn3_own, Near(gn3_recv), h2, gain3, Half(cotangent),
         cross_out, co_oth_far, cq, mk, mkt, mv, lse2, mixed2, cross_query, cq_oth_far, h1, gain2, self_out, so_oth_far),
        smem=4, us=12, fetch=(memory, n2, mixed2, keep_far, recv_far),
    )
    out_a_recv = swap(out_a)
    feed_hold, feed_send = halve(feed_hold, feed_got, 3)
    gb2, feed_send, out_a_recv = tie(gb2, feed_send, out_a_recv)
    feed_got = swap(feed_send, "ring")
    gm1_recv = swap(gm1_oth)
    (cross_hold, cross_hold_oth, cross_send, q, k, kt_near, v_near, bias, lse1_near, lse1_oth_near, sent,
     dmk, dmv) = call(
        cross_weights_kernel,
        [((640, WIDTH), bf16, "near"), ((640, WIDTH), bf16, "near"), ((1280, WIDTH), bf16, "near")],
        [v((WIDTH, LEN), bf16), v((5, 256, WIDTH), bf16)],
        (place, *map(Near, (memory_near, dmk, dmv, n2_near, dcq, mixed2_near, gb2, keep, gb1, recv))),
        us=3, fetch=(q_far, k_far, kt, val, bias_far, lse1, lse1_oth, send_far), forward=(dmk, dmv),
    )
    cross_got = swap(cross_send, "core")
    cross_oth = (cross_hold_oth.astype(f32) + cross_got[640:].astype(f32)).astype(bf16)
    gm1, cross_oth = tie(gm1, cross_oth)
    cross_recv = swap(cross_oth)
    acc = ((LEN, OWN), f32)
    dq1, dk1, dv1, near1, n1_near, x_near, gain1_near, wq, wk, wv = call(
        self_back_own_kernel,
        [(part, bf16, "near"), (*acc, "near"), (*acc, "near"), (*tiles, "near")],
        [row_tile, *backward_work(2)],
        (place, dec_lengths, counts, *map(Near, (gm1, keep, q, k, kt_near, v_near, bias, lse1_near))),
        smem=3, us=3, fetch=(n1, inputs, gain1, self_query, self_key, self_value),
    )
    for bit in bits[1:]:
        feed_got, dq1 = tie(feed_got, dq1)
        feed_hold, feed_send = halve(feed_hold, feed_got, 3 + bit)
        gm1_recv, feed_send = tie(gm1_recv, feed_send)
        feed_got = swap(feed_send, "ring", bit)
    self_hold, self_send, gi_a, gi_b = call(
        self_back_kernel,
        [((384 + SMALL, WIDTH), bf16, "near"), ((384 + SMALL, WIDTH), bf16, "near"),
         (half, bf16, "far"), (half, bf16, "far")],
        [row_tile, v(part, bf16), v(heads, bf16), v(*acc), v(*acc), v(*tiles),
         v((WIDTH, LEN), bf16), v((3, 256, WIDTH), bf16), v((NB, WIDTH), f32), v((SMALL, WIDTH), f32), *backward_work(2)],
        (place, dec_lengths, counts,
         *map(Near, (gm1_recv, sent, dq1, dk1, dv1, near1, q, k, kt_near, v_near, bias, lse1_oth_near,
                     n1_near, x_near, gh1, gain1_near, gains, wq, wk, wv))),
        smem=3, us=1.5,
    )
    self_got = swap(self_send, "core")
    (feed_own,) = call(
        total_kernel, [((feed_hold.shape[0], WIDTH), bf16, "near")], [], (place, Near(feed_hold), Near(feed_got)), us=SHORT
    )
    joined = ((HALF + SMALL, WIDTH), bf16, "near")
    hold, send = call(
        join_kernel,
        [joined, joined],
        [],
        (place, *map(Near, (cross_hold, cross_got, cross_recv, self_hold, self_got))),
        us=SHORT,
    )
    got, gi_a_recv = swap(send, "pair"), swap(gi_a)
    got, feed_own, gi_a_recv = tie(got, feed_own, gi_a_recv)
    hold, send = halve(hold, got, 3, SMALL)
    for k in reversed(bits[1:]):
        feed_own = merge(feed_own, swap(feed_own, "ring", k), 3 + k)
    send, dmk = tie(send, dmk)
    gmem, gmem_send = call(
        memory_back_kernel,
        [(heads, bf16, "far"), (heads, bf16, "near")],
        [],
        (place, dmk, cross_key, ck_oth, dmv, cross_value, cv_oth),
        us=SHORT,
    )
    gi_b_recv, out_b_recv, gmem_recv = swap(gi_b), swap(out_b), swap(gmem_send)
    for k in bits[1:]:
        got = swap(send, "ring", k - 1)
        if k == 1:
            got, gmem_send, feed_own, gi_b_recv = tie(got, gmem_send, feed_own, gi_b_recv)
        hold, send = halve(hold, got, 3 + k, SMALL)
    feed_own = merge(feed_own, swap(feed_own, "ring"), 3)
    got = swap(send, "ring", bits[-1])
    got, out_b_recv, feed_own = tie(got, out_b_recv, feed_own)
    feed_pair, feed_core = swap(feed_own, "pair"), swap(feed_own, "core")
    own, small = call(
        total_kernel,
        [((hold.shape[0] - SMALL, WIDTH), bf16, "near"), ((SMALL, WIDTH), f32, "near")],
        [],
        (place, Near(hold), Near(got)),
        us=SHORT,
    )
    for k in reversed(bits):
        got = swap(own, "ring", k)
        if k == 0:
            got, feed_pair = tie(got, feed_pair)
        own = merge(own, got, 3 + k)
    own, gmem_recv = tie(own, gmem_recv)
    pair, core_own = swap(own, "pair"), swap(own, "core")
    gain_grads = small[:8] + swap(small[:8])

    def both(part, other):
        return (part.astype(f32) + other.astype(f32)).astype(bf16)

    output = jnp.concatenate([both(out_a, out_a_recv), both(out_b, out_b_recv)])
    grad_inputs = jnp.concatenate([both(gi_a, gi_a_recv), both(gi_b, gi_b_recv)])
    grad_memory = both(gmem, gmem_recv)
    wide_hidden, tall_hidden = ((WIDTH, hidden), f32, "far"), ((hidden, WIDTH), f32, "far")
    feed_in_grad, feed_out_grad = call(
        feed_unfold_kernel,
        [wide_hidden, tall_hidden],
        [],
        (place, *map(Near, (feed_own, feed_pair, feed_core, swap(feed_pair, "core")))),
        us=SHORT,
    )
    pair, output, grad_inputs, grad_memory, feed_in_grad, feed_out_grad = lax.optimization_barrier(
        (pair, output, grad_inputs, grad_memory, feed_in_grad, feed_out_grad)
    )
    narrows, wides = (narrow, f32, "far"), (wide, f32, "far")
    co_grad, so_grad, cq_grad, ck_grad, cv_grad, wq_grad, wk_grad, wv_grad = call(
        unfold_kernel,
        [narrows] * 2 + [wides] * 6,
        [],
        (place, *map(Near, (own, pair, core_own, swap(pair, "core")))),
    )
    return (
        output,
        grad_inputs,
        grad_memory,
        gain_grads[0],
        wq_grad,
        wk_grad,
        wv_grad,
        so_grad,
        small[3:7, :NB].T,
        gain_grads[1],
        cq_grad,
        ck_grad,
        cv_grad,
        co_grad,
        gain_grads[2],
        feed_in_grad,
        feed_out_grad,
    )


def solution(mesh):
    devices = mesh.devices
    rows, tensor = devices.shape
    mesh = Mesh(devices.reshape(rows // 4, 2, 2, tensor), ("ring", "pair", "core", "tensor"))
    dp = ("ring", "pair", "core")
    split = P(dp, None)
    columns, rows = P(None, "tensor"), P("tensor", None)
    return jax.shard_map(
        shards,
        mesh=mesh,
        in_specs=(
            split, split, split, split, split, P(dp),
            P(), columns, columns, columns, rows, columns,
            P(), columns, columns, columns, rows,
            P(), columns, rows,
        ),
        out_specs=(
            split, split, P(dp, "tensor"),
            P(), columns, columns, columns, rows, columns,
            P(), columns, columns, columns, rows,
            P(), columns, rows,
        ),
        check_vma=False,
    )
```

```python
import functools
import math

import jax
import jax.numpy as jnp
from jax import lax
from jax.experimental import pallas as pl
from jax.experimental.pallas import tpu as pltpu
from jax.sharding import Mesh
from jax.sharding import PartitionSpec as P

NB = 32
MAXDIST = 128
SEGS = 16
LEN = 1024
HALF = 512
WIDTH = 512
OWN = 256
BLK = 128
BIG = 1 << 30
MASKED = -1e30
EPS = 1e-06
f32 = jnp.float32
bf16 = jnp.bfloat16
ROOM = 11 * 1024 * 1024
SHORT = 0.05


def thresholds():
    exact = NB // 2
    edges = [
        math.ceil(exact * (MAXDIST / exact) ** (level / (NB - exact)))
        for level in range(1, NB - exact)
    ]
    return list(range(exact + 1)) + edges


THRESHOLDS = thresholds()


def nn(a, b):
    return jnp.dot(a, b, preferred_element_type=f32)


def nt(a, b):
    return lax.dot_general(a, b, (((1,), (1,)), ((), ())), preferred_element_type=f32)


def tn(a, b):
    return lax.dot_general(a, b, (((0,), (0,)), ((), ())), preferred_element_type=f32)


class Half:
    def __init__(self, array):
        self.array = array


class Near:
    def __init__(self, array):
        self.array = array


class Raw:
    def __init__(self, array):
        self.array = array


PACKED = 640
SMALL = 16


def packed_parts(core):
    def at(start, size):
        return pl.ds(pl.multiple_of(start, BLK), size)

    left, right, all_lanes = slice(0, OWN), slice(OWN, WIDTH), slice(0, WIDTH)
    return (
        [(at(core * BLK, BLK), (slice(0, 128), all_lanes))],
        [(at(core * BLK, BLK), (slice(128, 256), all_lanes))],
        [(at(core * 256, 256), (slice(256, 512), left))],
        [(at(core * 256, 256), (slice(256, 512), right))],
        [(at(core * 256, BLK), (slice(512, 640), left)), (at(core * 256 + BLK, BLK), (slice(512, 640), right))],
    )


def pack_kernel(io, place_ref, *refs):
    *weights, pack_ref, sems = refs
    copies = []
    for ref, parts in zip(weights, packed_parts(place_ref[1]), strict=True):
        for rows, where in parts:
            copy = pltpu.make_async_copy(ref.at[rows, :], pack_ref.at[where], sems.at[len(copies)])
            copy.start()
            copies.append(copy)
    for copy in copies:
        copy.wait()


class Copies:
    def __init__(self, sems):
        self.sems, self.used, self.waits, self.out = sems, 0, {}, {}

    def start(self, source, target):
        copy = pltpu.make_async_copy(source, target, self.sems.at[self.used])
        self.used += 1
        copy.start()
        return copy

    def ready(self, *refs):
        for ref in refs:
            for copy in self.waits.pop(id(ref), ()):
                copy.wait()

    def done(self, *refs):
        for ref in refs:
            target, copy = self.out.get(id(ref), (None, True))
            if copy is None:
                self.out[id(ref)] = (target, self.start(ref, target))


def size_of(shape, dtype):
    return math.prod(shape) * jnp.dtype(dtype).itemsize


def call(body, outs, scratch, args, smem=1, us=3, fetch=(), forward=(), late=0):
    tables, operands = args[:smem], args[smem:]
    arrays, in_specs, fetched = [], [], []
    hbm, vmem = pl.BlockSpec(memory_space=pltpu.HBM), pl.BlockSpec(memory_space=pltpu.VMEM)

    def shape_of(operand):
        if isinstance(operand, Half):
            return (HALF, *operand.array.shape[1:]), operand.array.dtype
        return operand.shape, operand.dtype

    for operand in (*operands, *fetch, *map(Near, forward)):
        array = operand.array if isinstance(operand, (Near, Raw, Half)) else operand
        near = isinstance(operand, Near)
        arrays.append(array if near else pltpu.with_memory_space_constraint(array, pltpu.HBM))
        in_specs.append(vmem if near else hbm)
    fetched = [shape_of(o) for o in operands if not isinstance(o, (Near, Raw))]
    out_shapes, out_specs, sent = [], [], []
    extra = [(*shape_of(o), "near") for o in fetch] + [(o.shape, o.dtype, "far") for o in forward]
    for k, (shape, dtype, kind) in enumerate([*outs, *extra]):
        if kind != "far":
            out_shapes.append(jax.ShapeDtypeStruct(shape, dtype))
            out_specs.append(vmem)
        if kind != "near":
            out_shapes.append(pltpu.HBM(shape, dtype))
            out_specs.append(hbm)
        if kind == "far" and k < len(outs):
            sent.append((shape, dtype))
    n_copies = len(fetched) + sum(kind != "near" for _, _, kind in outs) + len(extra)

    def kernel(*refs):
        refs = list(refs)

        def take(n):
            taken = refs[:n]
            del refs[:n]
            return taken

        scalars, sources = take(smem), take(len(operands))
        extra_sources = take(len(extra))
        targets = take(len(out_shapes) - len(extra))
        extra_targets = take(len(extra))
        inner, outer = take(len(fetched)), take(len(sent))
        io = Copies(take(1)[0] if n_copies else None)
        inputs, outputs, wanted = [], [], []

        def source_of(operand, source):
            if isinstance(operand, Half):
                return source.at[pl.ds(pl.multiple_of(scalars[0][0] * HALF, HALF), HALF), :]
            return source

        for operand, source in zip(operands, sources, strict=True):
            if isinstance(operand, (Near, Raw)):
                inputs.append(source)
                continue
            ref = inner.pop(0)
            inputs.append(ref)
            wanted.append((ref, source_of(operand, source)))
        for ref, source in wanted[late:] + wanted[:late]:
            io.waits[id(ref)] = [io.start(source, ref)]
        moved = [
            io.start(source_of(operand, source), target)
            for operand, source, target in zip((*fetch, *forward), extra_sources, extra_targets, strict=True)
        ]
        for _, _, kind in outs:
            ref = outer.pop(0) if kind == "far" else targets.pop(0)
            outputs.append(ref)
            if kind != "near":
                io.out[id(ref)] = (targets.pop(0), None)
        body(io, *scalars, *inputs, *outputs, *refs)
        io.ready(*inputs)
        io.done(*outputs)
        for copy in (*(copy for _, copy in io.out.values()), *moved):
            copy.wait()

    own = [pltpu.VMEM(s, d) for s, d in fetched + sent]
    used = sum(size_of(s, d) for s, d in fetched + sent) + sum(
        size_of(s.shape, s.dtype) for s in scratch if s.memory_space == pltpu.VMEM
    )
    return pl.pallas_call(
        kernel,
        out_shape=tuple(out_shapes),
        in_specs=[pl.BlockSpec(memory_space=pltpu.SMEM)] * smem + in_specs,
        out_specs=tuple(out_specs),
        scratch_shapes=[*own, *([pltpu.SemaphoreType.DMA((n_copies,))] if n_copies else []), *scratch],
        compiler_params=pltpu.CompilerParams(vmem_limit_bytes=used + ROOM),
        cost_estimate=pl.CostEstimate(flops=int(us * 3.3e9), bytes_accessed=int(us * 1e7), transcendentals=0),
    )(*tables, *arrays)


def running_ends(len_ref):
    ends, total = [], 0
    for k in range(SEGS):
        total = total + len_ref[0, k]
        ends.append(total)
    return ends


def live_tokens(ends, count):
    total = 0
    for k in range(SEGS):
        total = jnp.where(k < count, ends[k], total)
    return total


def lookup(pos, ends, values, first):
    found = first
    for k in range(SEGS - 1):
        found = jnp.where(pos >= ends[k], values[k], found)
    return found


def token_positions():
    shape = (LEN // BLK, BLK)
    return lax.broadcasted_iota(jnp.int32, shape, 0) * BLK + lax.broadcasted_iota(
        jnp.int32, shape, 1
    )


def twice(row):
    return jnp.concatenate([row, row], axis=1)


def stacked(pair):
    lane = lax.broadcasted_iota(jnp.int32, pair.shape, 1)
    zero = jnp.zeros_like(pair)
    return jnp.concatenate(
        [jnp.where(lane < 64, pair, zero), jnp.where(lane < 64, zero, pair)], axis=0
    )


def diagonal(product):
    return jnp.concatenate([product[:64, :BLK], product[64:, BLK:]], axis=0)


def own_rows(row):
    return jnp.concatenate(
        [jnp.broadcast_to(row[:, :BLK], (64, BLK)), jnp.broadcast_to(row[:, BLK:], (64, BLK))], axis=0
    )


def in_chunks(n, body):
    def four(j, carry):
        body(4 * j, 4)
        return carry

    lax.fori_loop(0, lax.shift_right_logical(n, 2), four, 0)
    for rest in (3, 2, 1):
        pl.when((n & 3) == rest)(functools.partial(body, n & ~3, rest))


def reset(m_ref, l_ref, acc_ref):
    m_ref[...] = jnp.full(m_ref.shape, MASKED, f32)
    l_ref[...] = jnp.zeros(l_ref.shape, f32)
    acc_ref[...] = jnp.zeros(acc_ref.shape, f32)


def soften(p, scores, values_t, m_ref, l_ref, acc_ref):
    before = m_ref[p, 0:1, :]
    peak = jnp.maximum(before, jnp.max(scores, axis=0, keepdims=True))
    shrink = jnp.exp(before - peak)
    raised = jnp.exp(scores - peak)
    m_ref[p, 0:1, :] = peak
    l_ref[p, 0:1, :] = l_ref[p, 0:1, :] * shrink + jnp.sum(raised, axis=0, keepdims=True)
    acc_ref[p] = acc_ref[p] * own_rows(shrink) + diagonal(nn(values_t, raised.astype(bf16)))


def settle(p, alive, m_ref, l_ref, acc_ref):
    total = l_ref[p, 0:1, :]
    mixed = jnp.transpose(acc_ref[p] * own_rows(alive / total))
    return mixed.astype(bf16), m_ref[p, 0:1, :] + jnp.log(total)


def inner_row(grads, mixed):
    product = jnp.transpose(grads.astype(f32) * mixed.astype(f32))
    return jnp.concatenate(
        [jnp.sum(product[:64], axis=0, keepdims=True), jnp.sum(product[64:], axis=0, keepdims=True)], axis=1
    )


def rms_scale(value):
    return lax.rsqrt(jnp.mean(value * value, axis=-1, keepdims=True) + EPS)


def rms_back(value, gain, grad):
    scale = rms_scale(value)
    weighted = grad * gain
    inner = jnp.mean(weighted * value, axis=-1, keepdims=True)
    unit = value * scale
    return (
        scale * weighted - unit * (scale * scale * inner),
        jnp.sum(grad * unit, axis=0, keepdims=True),
    )


def fill_bias(table_ref, bias_ref):
    key = lax.broadcasted_iota(jnp.int32, (BLK, BLK), 0)
    query = lax.broadcasted_iota(jnp.int32, (BLK, BLK), 1)
    for d in range(2):
        gap = d * BLK + query - key
        tiles = [jnp.full((BLK, BLK), table_ref[h, 0], f32) for h in range(4)]
        for level in range(1, NB):
            reached = gap >= THRESHOLDS[level]
            tiles = [jnp.where(reached, table_ref[h, level], tiles[h]) for h in range(4)]
        if d == 0:
            tiles = [jnp.where(gap >= 0, tile, MASKED) for tile in tiles]
        for h in range(4):
            bias_ref[d * 2 + h // 2, :, (h % 2) * BLK : (h % 2 + 1) * BLK] = tiles[h]
    for h in range(4):
        far = jnp.full((BLK, BLK), table_ref[h, NB - 1], f32)
        bias_ref[4 + h // 2, :, (h % 2) * BLK : (h % 2 + 1) * BLK] = far


def self_scores(distances, p, kstart, qs_ref, k_ref, bias_ref, start2):
    m = len(distances)
    keys = k_ref[pl.ds(kstart, m * BLK), p * BLK : (p + 1) * BLK]
    scores = nt(keys, qs_ref[p])
    parts = [scores[k * BLK : (k + 1) * BLK] + bias_ref[2 * d + p] for k, d in enumerate(distances)]
    index = kstart + lax.broadcasted_iota(jnp.int32, (m * BLK, 2 * BLK), 0)
    return jnp.where(index >= start2, jnp.concatenate(parts, axis=0) if m > 1 else parts[0], MASKED)


def self_spans(b, ends, live):
    pos = b * BLK
    first = lax.shift_right_logical(lookup(pos, ends, ends, 0), 7)
    return pos < live, first, b - first + 1


def self_forward(half, ends, live, q_ref, k_ref, vt_ref, bias_ref, start_ref, o_ref, lse_ref, qs_ref, m_ref, l_ref, acc_ref):
    def step(i, carry):
        b = half * 4 + i
        alive, first, n = self_spans(b, ends, live)
        rows = pl.ds(pl.multiple_of(i * BLK, BLK), BLK)

        @pl.when(alive)
        def _():
            start2 = twice(start_ref[pl.ds(b, 1), :])
            for p in range(2):
                lanes = slice(p * BLK, (p + 1) * BLK)
                qs_ref[p] = stacked(q_ref[pl.ds(pl.multiple_of(b * BLK, BLK), BLK), lanes])
            reset(m_ref, l_ref, acc_ref)

            def chunk(j, m):
                kstart = pl.multiple_of((first + j) * BLK, BLK)
                distances = [jnp.minimum(n - 1 - j - k, 2) for k in range(m)]
                for p in range(2):
                    scores = self_scores(distances, p, kstart, qs_ref, k_ref, bias_ref, start2)
                    values_t = vt_ref[p * BLK : (p + 1) * BLK, pl.ds(kstart, m * BLK)]
                    soften(p, scores, values_t, m_ref, l_ref, acc_ref)

            in_chunks(n, chunk)
            for p in range(2):
                mixed, lse = settle(p, (start2 < BIG).astype(f32), m_ref, l_ref, acc_ref)
                o_ref[rows, p * BLK : (p + 1) * BLK] = mixed
                lse_ref[p, pl.ds(i, 1), :] = lse

        @pl.when(jnp.logical_not(alive))
        def _():
            o_ref[rows, :] = jnp.zeros((BLK, OWN), bf16)
            for p in range(2):
                lse_ref[p, pl.ds(i, 1), :] = jnp.zeros((1, 2 * BLK), f32)

        return carry

    lax.fori_loop(0, 4, step, 0)


def set_starts(ends, live, start_ref):
    pos = token_positions()
    start_ref[...] = jnp.where(pos < live, lookup(pos, ends, ends, 0), BIG)


def first_kernel(
    io, t_ref, len_ref, cnt_ref, table_ref,
    x_ref, gain_ref, wq_ref, wk_ref, wv_ref,
    n1_ref, q_ref, k_ref, v_ref, vt_ref, kt_ref, bias_ref, o_ref, lse_ref,
    start_ref, *work,
):
    ends = running_ends(len_ref)
    live = live_tokens(ends, cnt_ref[0])
    set_starts(ends, live, start_ref)
    fill_bias(table_ref, bias_ref)
    io.done(bias_ref)
    io.ready(x_ref, gain_ref, wq_ref, wk_ref, wv_ref)

    def project(i, carry):
        rows = pl.ds(pl.multiple_of(i * 256, 256), 256)
        value = x_ref[rows, :].astype(f32)
        low = (value * rms_scale(value) * gain_ref[...]).astype(bf16)
        n1_ref[rows, :] = low
        q_ref[rows, :] = nn(low, wq_ref[...]).astype(bf16)
        keys = nn(low, wk_ref[...])
        k_ref[rows, :] = keys.astype(bf16)
        kt_ref[:, rows] = jnp.transpose(keys).astype(bf16)
        values = nn(low, wv_ref[...])
        v_ref[rows, :] = values.astype(bf16)
        vt_ref[:, rows] = jnp.transpose(values).astype(bf16)
        return carry

    lax.fori_loop(0, 4, project, 0)
    io.done(n1_ref, q_ref, k_ref, v_ref, vt_ref, kt_ref)
    self_forward(
        1 - t_ref[0], ends, live, q_ref, k_ref, vt_ref, bias_ref, start_ref, o_ref, lse_ref, *work
    )


def second_kernel(
    io, t_ref, len_ref, cnt_ref,
    q_ref, k_ref, vt_ref, bias_ref,
    o_ref, lse_ref,
    start_ref, *work,
):
    ends = running_ends(len_ref)
    live = live_tokens(ends, cnt_ref[0])
    set_starts(ends, live, start_ref)
    io.ready(q_ref, k_ref, vt_ref, bias_ref)
    self_forward(
        t_ref[0], ends, live, q_ref, k_ref, vt_ref, bias_ref, start_ref, o_ref, lse_ref, *work
    )


def memory_kernel(
    io, place_ref, mem_ref, ck_ref, cv_ref, pack_ref, packo_ref,
    mk_ref, mv_ref, mkt_ref, mvt_ref, so_out, co_out, cq_out, cko_ref, cvo_ref,
):
    for core, pack in ((place_ref[1], pack_ref), (1 - place_ref[1], packo_ref)):
        for ref, parts in zip((so_out, co_out, cq_out, cko_ref, cvo_ref), packed_parts(core), strict=True):
            for rows, where in parts:
                ref[rows, :] = pack[where]
    io.done(so_out, co_out, cq_out, cko_ref, cvo_ref)
    io.ready(mem_ref, ck_ref, cv_ref)

    def project(i, carry):
        rows = pl.ds(pl.multiple_of(i * 256, 256), 256)
        value = mem_ref[rows, :]
        for side, (wk, wv) in enumerate(((ck_ref, cv_ref), (cko_ref, cvo_ref))):
            lanes = slice(side * OWN, (side + 1) * OWN)
            keys = nn(value, wk[...])
            mk_ref[rows, lanes] = keys.astype(bf16)
            mkt_ref[lanes, rows] = jnp.transpose(keys).astype(bf16)
            values = nn(value, wv[...])
            mv_ref[rows, lanes] = values.astype(bf16)
            mvt_ref[lanes, rows] = jnp.transpose(values).astype(bf16)
        return carry

    lax.fori_loop(0, 4, project, 0)


def set_ranges(ends, mends, live, low_ref, high_ref):
    pos = token_positions()
    low_ref[...] = jnp.where(pos < live, lookup(pos, ends, mends, 0), BIG)
    high_ref[...] = lookup(pos, ends, mends[1:], mends[0])


def cross_blocks(half, ends, mends, live, block, dead):
    def step(i, carry):
        b = half * 4 + i
        pos = b * BLK
        alive = pos < live
        last = jnp.minimum(pos + BLK, live) - 1
        first = lax.shift_right_logical(lookup(pos, ends, mends, 0), 7)
        end = lax.shift_right_logical(lookup(last, ends, mends[1:], mends[0]) + BLK - 1, 7)
        pl.when(alive)(lambda: block(i, b, first, end - first))
        pl.when(jnp.logical_not(alive))(lambda: dead(i))
        return carry

    lax.fori_loop(0, 4, step, 0)


def cross_allowed(kstart, m, low2, high2):
    index = kstart + lax.broadcasted_iota(jnp.int32, (m * BLK, 2 * BLK), 0)
    return (index >= low2) & (index < high2)


def third_kernel(
    io, t_ref, len_ref, mlen_ref, cnt_ref,
    x_ref, keep_ref, recv_ref, so_ref, soo_ref, gain2_ref, cq_ref, cqo_ref,
    mk_ref, mvt_ref, co_ref, coo_ref, gain3_ref,
    h1_ref, n2_ref, q_ref, mixed_ref, lse_ref, h2_ref, n3_ref,
    low_ref, high_ref, qs_ref, m_ref, l_ref, acc_ref,
):
    t = t_ref[0]
    ends, mends = running_ends(len_ref), running_ends(mlen_ref)
    live = live_tokens(ends, cnt_ref[0])
    set_ranges(ends, mends, live, low_ref, high_ref)

    io.ready(x_ref, keep_ref, recv_ref, so_ref, soo_ref, gain2_ref, cq_ref, cqo_ref)

    def before(i, carry):
        rows = pl.ds(pl.multiple_of(i * 256, 256), 256)
        value = x_ref[rows, :].astype(f32)
        value = value + nn(keep_ref[rows, :], so_ref[...]) + nn(recv_ref[rows, :], soo_ref[...])
        h1_ref[rows, :] = value
        low = (value * rms_scale(value) * gain2_ref[...]).astype(bf16)
        n2_ref[rows, :] = low
        q_ref[rows, :OWN] = nn(low, cq_ref[...]).astype(bf16)
        q_ref[rows, OWN:] = nn(low, cqo_ref[...]).astype(bf16)
        return carry

    lax.fori_loop(0, 2, before, 0)
    io.done(h1_ref, n2_ref, q_ref)
    io.ready(mk_ref, mvt_ref)

    def block(i, b, first, n):
        low2, high2 = twice(low_ref[pl.ds(b, 1), :]), twice(high_ref[pl.ds(b, 1), :])
        rows = pl.ds(pl.multiple_of(i * BLK, BLK), BLK)
        for p in range(4):
            qs_ref[p] = stacked(q_ref[rows, p * BLK : (p + 1) * BLK])
        reset(m_ref, l_ref, acc_ref)

        def chunk(j, m):
            kstart = pl.multiple_of((first + j) * BLK, BLK)
            span = pl.ds(kstart, m * BLK)
            allowed = cross_allowed(kstart, m, low2, high2)
            for p in range(4):
                lanes = slice(p * BLK, (p + 1) * BLK)
                scores = jnp.where(allowed, nt(mk_ref[span, lanes], qs_ref[p]), MASKED)
                soften(p, scores, mvt_ref[lanes, span], m_ref, l_ref, acc_ref)

        in_chunks(n, chunk)
        for p in range(4):
            mixed, lse = settle(p, (low2 < BIG).astype(f32), m_ref, l_ref, acc_ref)
            mixed_ref[rows, p * BLK : (p + 1) * BLK] = mixed
            lse_ref[p, pl.ds(i, 1), :] = lse

    def dead(i):
        mixed_ref[pl.ds(pl.multiple_of(i * BLK, BLK), BLK), :] = jnp.zeros((BLK, WIDTH), bf16)
        for p in range(4):
            lse_ref[p, pl.ds(i, 1), :] = jnp.zeros((1, 2 * BLK), f32)

    cross_blocks(t, ends, mends, live, block, dead)

    io.done(mixed_ref, lse_ref)
    io.ready(co_ref, coo_ref, gain3_ref)

    def after(i, carry):
        rows = pl.ds(pl.multiple_of(i * 256, 256), 256)
        value = h1_ref[rows, :]
        value = value + nn(mixed_ref[rows, :OWN], co_ref[...]) + nn(mixed_ref[rows, OWN:], coo_ref[...])
        h2_ref[rows, :] = value
        n3_ref[rows, :] = (value * rms_scale(value) * gain3_ref[...]).astype(bf16)
        return carry

    lax.fori_loop(0, 2, after, 0)


def feed_kernel(
    io, place_ref, n3_ref, fi_ref, cot_ref, fo_ref,
    gn_ref, act_ref, gp_ref, *out_refs,
):
    tile = 256
    n_tiles = fi_ref.shape[1] // tile
    root = math.sqrt(2 / math.pi)
    base = place_ref[0] * HALF
    io.ready(n3_ref, fi_ref, cot_ref, fo_ref)

    def hidden(j, carry):
        lanes = pl.ds(pl.multiple_of(j * tile, tile), tile)
        for i in range(2):
            rows = slice(i * 256, (i + 1) * 256)
            pre = nn(n3_ref[rows, :], fi_ref[:, lanes])
            square = pre * pre
            bent = jnp.tanh(pre * (root + (root * 0.044715) * square))
            gate = 0.5 + 0.5 * bent
            slope = gate + pre * (0.5 - 0.5 * bent * bent) * (root + (root * 0.134145) * square)
            act_ref[rows, lanes] = (pre * gate).astype(bf16)
            grads = nt(cot_ref[pl.ds(pl.multiple_of(base + i * 256, 256), 256), :], fo_ref[lanes, :])
            gp_ref[rows, lanes] = (grads * slope).astype(bf16)
        return carry

    lax.fori_loop(0, n_tiles, hidden, 0)
    io.done(act_ref, gp_ref)

    def outward(i, carry):
        rows = pl.ds(pl.multiple_of(i * 256, 256), 256)
        for out_ref in out_refs:
            out_ref[rows, :] = nn(act_ref[rows, :], fo_ref[...]).astype(bf16)
        gn_ref[rows, :] = nt(gp_ref[rows, :], fi_ref[...]).astype(bf16)
        return carry

    lax.fori_loop(0, 2, outward, 0)


def feed_weights_kernel(
    io, place_ref, h2_ref, own_ref, fo_ref, n3_ref, gp_ref, n3o_ref, gpo_ref, act_ref, cot_ref, acto_ref,
    hold_ref, senda_ref, sendb_ref, sendc_ref, sendd_ref, outa_ref, outb_ref,
    n3t_ref, both_ref,
):
    t, c = place_ref[0], place_ref[1]

    parts = (senda_ref, sendb_ref, sendc_ref, sendd_ref)
    mine = pl.ds(pl.multiple_of(t * HALF, HALF), HALF)
    theirs = pl.ds(pl.multiple_of((1 - t) * HALF, HALF), HALF)
    io.ready(n3_ref, gp_ref, n3o_ref, gpo_ref)
    n3t_ref[:, :HALF] = jnp.transpose(n3_ref[...])
    n3t_ref[:, HALF:] = jnp.transpose(n3o_ref[...])
    n_tiles = gp_ref.shape[1] // 256
    for j in range(n_tiles):
        lanes = slice(j * 256, (j + 1) * 256)
        grads = nn(n3t_ref[:, :HALF], gp_ref[:, lanes]) + nn(n3t_ref[:, HALF:], gpo_ref[:, lanes])
        both_ref[0, (j // 2) * WIDTH : (j // 2 + 1) * WIDTH, (j % 2) * 256 : (j % 2 + 1) * 256] = grads.astype(bf16)
    io.ready(act_ref, cot_ref, acto_ref)
    for j in range(n_tiles):
        lanes = slice(j * 256, (j + 1) * 256)
        grads = tn(act_ref[:, lanes], cot_ref[mine, :]) + tn(acto_ref[:, lanes], cot_ref[theirs, :])
        both_ref[1, lanes, :] = grads.astype(bf16)
    hold_ref[...] = both_ref[c]
    for k, ref in enumerate(parts):
        ref[...] = both_ref[1 - c, k * 256 : (k + 1) * 256, :]
    io.ready(h2_ref, own_ref)
    other = nn(acto_ref[...], fo_ref[...]).astype(bf16)
    own = (h2_ref[...] + own_ref[...].astype(f32)).astype(bf16)
    for k, out_ref in enumerate((outa_ref, outb_ref)):

        @pl.when(t == k)
        def _():
            out_ref[...] = own

        @pl.when(t != k)
        def _():
            out_ref[...] = other


def cross_back_kernel(
    io, t_ref, len_ref, mlen_ref, cnt_ref,
    gn_ref, gnr_ref, h2_ref, gain3_ref, cot_ref, co_ref, coo_ref,
    q_ref, mk_ref, mkt_ref, mv_ref, lse_ref, mixed_ref, cq_ref, cqo_ref, h1_ref, gain2_ref, so_ref, soo_ref,
    gb2_ref, dq_ref, dk_ref, dv_ref, gh1_ref, gb1_ref, gm1_ref, gm1o_ref, gains_ref,
    low_ref, high_ref, live_ref, gm_ref, dk_acc, dv_acc, gh2_ref, qs_ref, gs_ref, acc_ref,
):
    t = t_ref[0]
    ends, mends = running_ends(len_ref), running_ends(mlen_ref)
    live = live_tokens(ends, cnt_ref[0])
    set_ranges(ends, mends, live, low_ref, high_ref)
    alive_rows = t * HALF + lax.broadcasted_iota(jnp.int32, (HALF, BLK), 0)
    live_ref[...] = (alive_rows < live).astype(f32)
    dk_acc[...] = jnp.zeros_like(dk_acc)
    dv_acc[...] = jnp.zeros_like(dv_acc)
    gains_ref[...] = jnp.zeros_like(gains_ref)

    io.ready(gn_ref, gnr_ref, h2_ref, gain3_ref, cot_ref, co_ref, coo_ref)
    for i in range(2):
        rows = slice(i * 256, (i + 1) * 256)
        grad = gn_ref[rows, :].astype(f32) + gnr_ref[rows, :].astype(f32)
        back, gain = rms_back(h2_ref[rows, :], gain3_ref[...], grad)
        gains_ref[0:1, :] += gain
        grad = cot_ref[rows, :].astype(f32) + back
        gh2_ref[rows, :] = grad
        low = grad.astype(bf16)
        gb2_ref[rows, :] = low
        alive = live_ref[rows, 0:1]
        gm_ref[rows, :OWN] = (nt(low, co_ref[...]) * alive).astype(bf16)
        gm_ref[rows, OWN:] = (nt(low, coo_ref[...]) * alive).astype(bf16)
    io.done(gb2_ref)
    io.ready(q_ref, mk_ref, mkt_ref, mv_ref, lse_ref, mixed_ref)

    def block(i, b, first, n):
        low2, high2 = twice(low_ref[pl.ds(b, 1), :]), twice(high_ref[pl.ds(b, 1), :])
        rows = pl.ds(pl.multiple_of(i * BLK, BLK), BLK)
        inner = []
        for p in range(4):
            lanes = slice(p * BLK, (p + 1) * BLK)
            qs_ref[p] = stacked(q_ref[rows, lanes])
            gs_ref[p] = stacked(gm_ref[rows, lanes])
            inner.append(inner_row(gm_ref[rows, lanes], mixed_ref[rows, lanes]))
        acc_ref[...] = jnp.zeros(acc_ref.shape, f32)

        def chunk(j, m):
            kstart = pl.multiple_of((first + j) * BLK, BLK)
            span = pl.ds(kstart, m * BLK)
            allowed = cross_allowed(kstart, m, low2, high2)
            for p in range(4):
                lanes = slice(p * BLK, (p + 1) * BLK)
                scores = jnp.where(allowed, nt(mk_ref[span, lanes], qs_ref[p]), MASKED)
                probs = jnp.exp(scores - lse_ref[p, pl.ds(i, 1), :])
                low = (probs * (nt(mv_ref[span, lanes], gs_ref[p]) - inner[p])).astype(bf16)
                dk_acc[span, lanes] += nn(low, qs_ref[p])
                dv_acc[span, lanes] += nn(probs.astype(bf16), gs_ref[p])
                acc_ref[p] += diagonal(nn(mkt_ref[lanes, span], low))

        in_chunks(n, chunk)
        for p in range(4):
            dq_ref[rows, p * BLK : (p + 1) * BLK] = jnp.transpose(acc_ref[p]).astype(bf16)

    def dead(i):
        dq_ref[pl.ds(pl.multiple_of(i * BLK, BLK), BLK), :] = jnp.zeros((BLK, WIDTH), bf16)

    cross_blocks(t, ends, mends, live, block, dead)

    dk_ref[...] = dk_acc[...].astype(bf16)
    dv_ref[...] = dv_acc[...].astype(bf16)
    io.done(dq_ref, dk_ref, dv_ref)
    io.ready(cq_ref, cqo_ref, h1_ref, gain2_ref, so_ref, soo_ref)
    for i in range(2):
        rows = slice(i * 256, (i + 1) * 256)
        grad = nt(dq_ref[rows, :OWN], cq_ref[...]) + nt(dq_ref[rows, OWN:], cqo_ref[...])
        back, gain = rms_back(h1_ref[rows, :], gain2_ref[...], grad)
        gains_ref[1:2, :] += gain
        grad = gh2_ref[rows, :] + back
        gh1_ref[rows, :] = grad
        low = grad.astype(bf16)
        gb1_ref[rows, :] = low
        alive = live_ref[rows, 0:1]
        gm1_ref[rows, :] = (nt(low, so_ref[...]) * alive).astype(bf16)
        gm1o_ref[rows, :] = (nt(low, soo_ref[...]) * alive).astype(bf16)


def cross_weights_kernel(
    io, place_ref, mem_ref, dk_ref, dv_ref, n2_ref, dq_ref, mixed_ref, gb2_ref, keep_ref, gb1_ref, recv_ref,
    hold_ref, holdo_ref, send_ref,
    memt_ref, fold_ref,
):
    c = place_ref[1]
    io.ready(mem_ref, dk_ref, dv_ref, n2_ref, dq_ref, mixed_ref, gb2_ref, keep_ref, gb1_ref, recv_ref)
    memt_ref[...] = jnp.transpose(mem_ref[...])
    n2t = jnp.transpose(n2_ref[...])
    for side in range(2):
        lanes = slice(side * OWN, (side + 1) * OWN)
        mixed1 = keep_ref if side == 0 else recv_ref
        fold_ref[0] = tn(mixed_ref[:, lanes], gb2_ref[...]).astype(bf16)
        fold_ref[1] = tn(mixed1[...], gb1_ref[...]).astype(bf16)
        fold(fold_ref, 2, nn(n2t, dq_ref[:, lanes]))
        fold(fold_ref, 3, nn(memt_ref[...], dk_ref[:, lanes]))
        fold(fold_ref, 4, nn(memt_ref[...], dv_ref[:, lanes]))
        deal(c, fold_ref, hold_ref if side == 0 else holdo_ref, send_ref, side * 640)


def memory_back_kernel(
    io, place_ref, dk_ref, ck_ref, cko_ref, dv_ref, cv_ref, cvo_ref, gmem_ref, gmems_ref
):
    t = place_ref[0]
    io.ready(dk_ref, ck_ref, cko_ref, dv_ref, cv_ref, cvo_ref)
    for i in range(4):
        rows = slice(i * 256, (i + 1) * 256)
        grads = nt(dk_ref[rows, :OWN], ck_ref[...]) + nt(dk_ref[rows, OWN:], cko_ref[...])
        grads += nt(dv_ref[rows, :OWN], cv_ref[...]) + nt(dv_ref[rows, OWN:], cvo_ref[...])
        low = grads.astype(bf16)

        @pl.when(t == 0)
        def _():
            gmem_ref[rows, :] = low[:, :OWN]
            gmems_ref[rows, :] = low[:, OWN:]

        @pl.when(t != 0)
        def _():
            gmem_ref[rows, :] = low[:, OWN:]
            gmems_ref[rows, :] = low[:, :OWN]


def fold(fold_ref, k, weight):
    low = weight.astype(bf16)
    fold_ref[k, :, :OWN] = low[:256]
    fold_ref[k, :, OWN:] = low[256:]


def deal(c, fold_ref, hold_ref, send_ref, base):
    for k in range(fold_ref.shape[0]):
        rows = slice(k * BLK, (k + 1) * BLK)
        hold_ref[rows, :] = fold_ref[k, pl.ds(pl.multiple_of(c * BLK, BLK), BLK), :]
        rows = slice(base + k * BLK, base + (k + 1) * BLK)
        send_ref[rows, :] = fold_ref[k, pl.ds(pl.multiple_of((1 - c) * BLK, BLK), BLK), :]


def self_back_blocks(
    half, ends, live, start_ref, g_ref, mixed_ref, q_ref, k_ref, kt_ref, v_ref, bias_ref, lse_ref,
    dq_ref, dk_acc, dv_acc, near_acc, qs_ref, gs_ref, acc_ref,
):
    def step(i, carry):
        b = half * 4 + i
        alive, first, n = self_spans(b, ends, live)
        rows = pl.ds(pl.multiple_of(i * BLK, BLK), BLK)

        @pl.when(alive)
        def _():
            start2 = twice(start_ref[pl.ds(b, 1), :])
            inner = []
            for p in range(2):
                lanes = slice(p * BLK, (p + 1) * BLK)
                qs_ref[p] = stacked(q_ref[pl.ds(pl.multiple_of(b * BLK, BLK), BLK), lanes])
                gs_ref[p] = stacked(g_ref[rows, lanes])
                inner.append(inner_row(g_ref[rows, lanes], mixed_ref[rows, lanes]))
            acc_ref[...] = jnp.zeros(acc_ref.shape, f32)

            def chunk(j, m):
                kstart = pl.multiple_of((first + j) * BLK, BLK)
                span = pl.ds(kstart, m * BLK)
                distances = [jnp.minimum(n - 1 - j - k, 2) for k in range(m)]
                for p in range(2):
                    lanes = slice(p * BLK, (p + 1) * BLK)
                    scores = self_scores(distances, p, kstart, qs_ref, k_ref, bias_ref, start2)
                    probs = jnp.exp(scores - lse_ref[p, pl.ds(i, 1), :])
                    grad_scores = probs * (nt(v_ref[span, lanes], gs_ref[p]) - inner[p])
                    for k, d in enumerate(distances):
                        near_acc[2 * d + p] += grad_scores[k * BLK : (k + 1) * BLK]
                    low = grad_scores.astype(bf16)
                    dk_acc[span, lanes] += nn(low, qs_ref[p])
                    dv_acc[span, lanes] += nn(probs.astype(bf16), gs_ref[p])
                    acc_ref[p] += diagonal(nn(kt_ref[lanes, span], low))

            in_chunks(n, chunk)
            for p in range(2):
                dq_ref[rows, p * BLK : (p + 1) * BLK] = jnp.transpose(acc_ref[p]).astype(bf16)

        @pl.when(jnp.logical_not(alive))
        def _():
            dq_ref[rows, :] = jnp.zeros((BLK, OWN), bf16)

        return carry

    lax.fori_loop(0, 4, step, 0)


def self_back_own_kernel(
    io, place_ref, len_ref, cnt_ref,
    gm_ref, mixed_ref, q_ref, k_ref, kt_ref, v_ref, bias_ref, lse_ref,
    dq_ref, dk_acc, dv_acc, near_acc,
    start_ref, *work,
):
    ends = running_ends(len_ref)
    live = live_tokens(ends, cnt_ref[0])
    set_starts(ends, live, start_ref)
    for ref in (dk_acc, dv_acc, near_acc):
        ref[...] = jnp.zeros_like(ref)
    io.ready(gm_ref, mixed_ref, q_ref, k_ref, kt_ref, v_ref, bias_ref, lse_ref)
    self_back_blocks(
        place_ref[0], ends, live, start_ref, gm_ref, mixed_ref, q_ref, k_ref, kt_ref, v_ref, bias_ref, lse_ref,
        dq_ref, dk_acc, dv_acc, near_acc, *work,
    )


def self_back_kernel(
    io, place_ref, len_ref, cnt_ref,
    gmr_ref, mixed_ref, dqm_ref, dkm_ref, dvm_ref, nearm_ref, q_ref, k_ref, kt_ref, v_ref, bias_ref, lse_ref,
    n1_ref, x_ref, gh1_ref, gain1_ref, gains_ref, wq_ref, wk_ref, wv_ref,
    hold_ref, send_ref, gia_ref, gib_ref,
    start_ref, dqo_ref, dq_ref, dk_acc, dv_acc, near_acc, n1t_ref, fold_ref, sums_ref, small_ref, *work,
):
    t = place_ref[0]
    ends = running_ends(len_ref)
    live = live_tokens(ends, cnt_ref[0])
    set_starts(ends, live, start_ref)
    small_ref[...] = jnp.zeros_like(small_ref)
    for ref, so_far in ((dk_acc, dkm_ref), (dv_acc, dvm_ref), (near_acc, nearm_ref)):
        ref[...] = so_far[...]
    io.ready(mixed_ref, q_ref, k_ref, kt_ref, v_ref, bias_ref, lse_ref)
    self_back_blocks(
        1 - t, ends, live, start_ref, gmr_ref, mixed_ref, q_ref, k_ref, kt_ref, v_ref, bias_ref, lse_ref,
        dqo_ref, dk_acc, dv_acc, near_acc, *work,
    )
    dq_ref[pl.ds(pl.multiple_of(t * HALF, HALF), HALF), :] = dqm_ref[...]
    dq_ref[pl.ds(pl.multiple_of((1 - t) * HALF, HALF), HALF), :] = dqo_ref[...]

    io.ready(n1_ref)
    n1t_ref[...] = jnp.transpose(n1_ref[...])
    low_k, low_v = dk_acc[...].astype(bf16), dv_acc[...].astype(bf16)
    for k, grads in enumerate((dq_ref[...], low_k, low_v)):
        fold(fold_ref, k, nn(n1t_ref[...], grads))
    deal(place_ref[1], fold_ref, hold_ref, send_ref, 0)
    io.ready(x_ref, gh1_ref, gain1_ref, gains_ref, wq_ref, wk_ref, wv_ref)
    gain1 = jnp.zeros((1, WIDTH), f32)
    for i in range(4):
        rows = slice(i * 256, (i + 1) * 256)
        grads = nt(dq_ref[rows, :], wq_ref[...]) + nt(low_k[rows], wk_ref[...]) + nt(low_v[rows], wv_ref[...])
        back, gain = rms_back(x_ref[rows, :].astype(f32), gain1_ref[...], grads)
        gain1 += gain
        mine = (t == i // 2).astype(f32)
        back += mine * gh1_ref[(i % 2) * 256 : (i % 2 + 1) * 256, :]
        (gia_ref if i < 2 else gib_ref)[(i % 2) * 256 : (i % 2 + 1) * 256, :] = back.astype(bf16)
    io.done(gia_ref, gib_ref)
    key = lax.broadcasted_iota(jnp.int32, (BLK, BLK), 0)
    query = lax.broadcasted_iota(jnp.int32, (BLK, BLK), 1)
    gaps = [query - key, BLK + query - key]
    for level in range(NB):
        for p in range(2):
            row = jnp.zeros((1, 2 * BLK), f32)
            for d in range(2):
                inside = gaps[d] >= THRESHOLDS[level]
                if level + 1 < NB:
                    inside &= gaps[d] < THRESHOLDS[level + 1]
                picked = jnp.where(twice(inside.astype(f32)) > 0, near_acc[2 * d + p], 0.0)
                row += jnp.sum(picked, axis=0, keepdims=True)
            if level == NB - 1:
                row += jnp.sum(near_acc[4 + p], axis=0, keepdims=True)
            sums_ref[level : level + 1, p * 256 : (p + 1) * 256] = row
    for h in range(4):
        lanes = jnp.transpose(sums_ref[:, h * BLK : (h + 1) * BLK])
        small_ref[3 + h : 4 + h, :NB] = jnp.sum(lanes, axis=0, keepdims=True)
    for k, gain in enumerate((gain1, gains_ref[1:2, :], gains_ref[0:1, :])):
        small_ref[k : k + 1, :] = gain
    low = small_ref[...].astype(bf16)
    hold_ref[384:, :] = low
    send_ref[384:, :] = low


def join_kernel(io, place_ref, own_ref, got_ref, recv_ref, mine_ref, theirs_ref, hold_ref, send_ref):
    x = place_ref[2]
    io.ready(own_ref, got_ref, recv_ref, mine_ref, theirs_ref)
    for k in range(8):
        if k < 5:
            rows = slice(k * BLK, (k + 1) * BLK)
            total = own_ref[rows, :].astype(f32) + got_ref[rows, :].astype(f32) + recv_ref[rows, :].astype(f32)
        else:
            rows = slice((k - 5) * BLK, (k - 4) * BLK)
            total = mine_ref[rows, :].astype(f32) + theirs_ref[rows, :].astype(f32)
        low = total.astype(bf16)
        rows = slice((k % 4) * BLK, (k % 4 + 1) * BLK)

        @pl.when(x == k // 4)
        def _():
            hold_ref[rows, :] = low

        @pl.when(x != k // 4)
        def _():
            send_ref[rows, :] = low

    low = (mine_ref[384:, :].astype(f32) + theirs_ref[384:, :].astype(f32)).astype(bf16)
    hold_ref[HALF:, :] = low
    send_ref[HALF:, :] = low


def feed_halve_kernel(io, place_ref, hold_ref, gota_ref, gotb_ref, gotc_ref, gotd_ref, keep_ref, send_ref):
    x = place_ref[2]
    for k, got_ref in enumerate((gota_ref, gotb_ref, gotc_ref, gotd_ref)):
        rows, to = slice(k * 256, (k + 1) * 256), slice((k % 2) * 256, (k % 2 + 1) * 256)
        low = (hold_ref[rows, :].astype(f32) + got_ref[...].astype(f32)).astype(bf16)

        @pl.when(x == k // 2)
        def _():
            keep_ref[to, :] = low

        @pl.when(x != k // 2)
        def _():
            send_ref[to, :] = low


def halve_kernel(slot, every, io, place_ref, hold_ref, got_ref, keep_ref, send_ref):
    bit, size = place_ref[slot], keep_ref.shape[0] - every
    io.ready(hold_ref, got_ref)
    for k in range(2):
        rows = slice(k * size, (k + 1) * size)
        low = (hold_ref[rows, :].astype(f32) + got_ref[rows, :].astype(f32)).astype(bf16)

        @pl.when(bit == k)
        def _():
            keep_ref[:size, :] = low

        @pl.when(bit != k)
        def _():
            send_ref[:size, :] = low

    if every:
        low = (hold_ref[2 * size :, :].astype(f32) + got_ref[2 * size :, :].astype(f32)).astype(bf16)
        keep_ref[size:, :] = low
        send_ref[size:, :] = low


def total_kernel(io, _, hold_ref, got_ref, out_ref, *small_refs):
    io.ready(hold_ref, got_ref)
    total = hold_ref[...].astype(f32) + got_ref[...].astype(f32)
    out_ref[...] = total[: out_ref.shape[0]].astype(bf16)
    for small_ref in small_refs:
        small_ref[...] = total[out_ref.shape[0] :]


def merge_kernel(slot, io, place_ref, own_ref, got_ref, out_ref):
    bit, size = place_ref[slot], own_ref.shape[0]
    io.ready(own_ref, got_ref)
    out_ref[pl.ds(pl.multiple_of(bit * size, size), size), :] = own_ref[...]
    out_ref[pl.ds(pl.multiple_of((1 - bit) * size, size), size), :] = got_ref[...]


def feed_unfold_kernel(io, place_ref, own_ref, pair_ref, core_ref, both_ref, fi_ref, fo_ref):
    c, x = place_ref[1], place_ref[2]
    io.ready(own_ref, pair_ref, core_ref, both_ref)
    for ref, core, bit in ((own_ref, c, x), (pair_ref, c, 1 - x), (core_ref, 1 - c, x), (both_ref, 1 - c, 1 - x)):
        at = pl.ds(pl.multiple_of(bit * WIDTH, WIDTH), WIDTH)

        @pl.when(core == 0)
        def _():
            fi_ref[:, at] = ref[...].astype(f32)

        @pl.when(core != 0)
        def _():
            fo_ref[at, :] = ref[...].astype(f32)


def unfold_kernel(
    io, place_ref, own_ref, pair_ref, core_ref, both_ref,
    co_ref, so_ref, cq_ref, ck_ref, cv_ref, wq_ref, wk_ref, wv_ref,
):
    c, x = place_ref[1], place_ref[2]
    outs = (co_ref, so_ref, cq_ref, ck_ref, cv_ref, wq_ref, wk_ref, wv_ref)

    def spread(ref, core, bit):
        low = pl.ds(pl.multiple_of(core * BLK, BLK), BLK)
        high = pl.ds(pl.multiple_of(256 + core * BLK, BLK), BLK)
        for k, out in enumerate(outs):
            rows = slice((k % 4) * BLK, (k % 4 + 1) * BLK)

            @pl.when(bit == k // 4)
            def _():
                if k < 2:
                    out[low, :] = ref[rows, :].astype(f32)
                else:
                    out[low, :] = ref[rows, :OWN].astype(f32)
                    out[high, :] = ref[rows, OWN:].astype(f32)

    for ref, core, bit in ((own_ref, c, x), (pair_ref, c, 1 - x), (core_ref, 1 - c, x), (both_ref, 1 - c, 1 - x)):
        io.ready(ref)
        spread(ref, core, bit)


def swap(value, axis="tensor", bit=0):
    return lax.ppermute(value, axis, [(i, i ^ (1 << bit)) for i in range(lax.axis_size(axis))])


def shards(
    inputs, memory, cotangent, dec_lengths, mem_lengths, counts,
    self_gain, self_query, self_key, self_value, self_out, rel_table,
    cross_gain, cross_query, cross_key, cross_value, cross_out,
    feed_gain, feed_in, feed_out,
):
    v = pltpu.VMEM
    i32 = jnp.int32
    t, c, x = (lax.axis_index(name).astype(i32) for name in ("tensor", "core", "pair"))
    ring = lax.axis_size("ring")
    at_ring = lax.axis_index("ring").astype(i32)
    bits = range(ring.bit_length() - 1)
    ring_bits = [lax.shift_right_logical(at_ring, k) & 1 for k in bits]
    place = jnp.stack([t, c, x, *ring_bits])
    place_oth = jnp.stack([1 - t, c, x, *ring_bits])

    def halve(hold, got, slot, every=0):
        shape = (((hold.shape[0] - every) // 2 + every, WIDTH), bf16, "near")
        return call(
            functools.partial(halve_kernel, slot, every), [shape, shape], [], (place, Near(hold), Near(got)), us=SHORT
        )

    def merge(own, got, slot):
        shape = ((2 * own.shape[0], WIDTH), bf16, "near")
        return call(functools.partial(merge_kernel, slot), [shape], [], (place, Near(own), Near(got)), us=SHORT)[0]

    def tie(*arrays):
        return lax.optimization_barrier(arrays)
    gain1, gain2, gain3 = (g.reshape(1, WIDTH) for g in (self_gain, cross_gain, feed_gain))
    table = rel_table.T

    tok = (LEN, WIDTH)
    half = (HALF, WIDTH)
    heads, heads_t, part = (LEN, OWN), (OWN, LEN), (HALF, OWN)
    narrow, wide = (OWN, WIDTH), (WIDTH, OWN)
    row_tile = v((LEN // BLK, BLK), i32)
    tiles = ((6, BLK, 2 * BLK), f32)

    def forward_work(n):
        rows = v((n, 8, 2 * BLK), f32)
        return [v((n, 2 * BLK, BLK), bf16), rows, rows, v((n, BLK, BLK), f32)]

    def backward_work(n):
        return [v((n, 2 * BLK, BLK), bf16), v((n, 2 * BLK, BLK), bf16), v((n, BLK, BLK), f32)]

    pack, x_near, gain1_near, wq, wk, wv = call(
        pack_kernel,
        [((PACKED, WIDTH), bf16, "near")],
        [pltpu.SemaphoreType.DMA((6,))],
        (place, *map(Raw, (self_out, cross_out, cross_query, cross_key, cross_value))),
        us=SHORT, fetch=(inputs, gain1, self_query, self_key, self_value),
    )
    pack = swap(pack)
    n1, q, q_far, k, k_far, val, vt, kt, bias, bias_far, send1, lse1_oth = call(
        first_kernel,
        [(tok, bf16, "far"), (heads, bf16, "both"), (heads, bf16, "both"), (heads, bf16, "far"),
         (heads_t, bf16, "near"), (heads_t, bf16, "far"), (*tiles, "both"), (part, bf16, "near"),
         ((2, 4, 2 * BLK), f32, "near")],
        [row_tile, *forward_work(2)],
        (place, dec_lengths, counts, table, *map(Near, (x_near, gain1_near, wq, wk, wv))),
        smem=4, us=6,
    )
    mixed1_recv = swap(send1)
    mixed1_keep, lse1, memory_near, ck, cv, lse1_oth, send_far = call(
        second_kernel,
        [(part, bf16, "near"), ((2, 4, 2 * BLK), f32, "near")],
        [row_tile, *forward_work(2)],
        (place, dec_lengths, counts, Near(q), Near(k), Near(vt), Near(bias)),
        smem=3, us=SHORT, fetch=(memory, cross_key, cross_value), forward=(lse1_oth, send1),
    )
    pack, mixed1_keep = lax.optimization_barrier((pack, mixed1_keep))
    pack_core = swap(pack, "core")
    mk, mv, mkt, mvt, so_oth, co_oth, cq_oth, ck_oth, cv_oth, x_half, so, gain2_near, cq_w, co, gain3_near, keep_far, lse1 = call(
        memory_kernel,
        [(tok, bf16, "near"), (tok, bf16, "near"), ((WIDTH, LEN), bf16, "near"), ((WIDTH, LEN), bf16, "near"),
         (narrow, bf16, "near"), (narrow, bf16, "near"), (wide, bf16, "near"), (wide, bf16, "near"), (wide, bf16, "near")],
        [],
        (place, *map(Near, (memory_near, ck, cv, pack, pack_core))),
        us=SHORT, fetch=(Half(inputs), self_out, gain2, cross_query, cross_out, gain3), forward=(mixed1_keep, lse1),
    )
    (h1, n2, cq, mixed2, lse2, h2, n3, fi, cot, fo,
     mk, mv, mkt, so_oth_far, co_oth_far, cq_oth_far, ck_oth, cv_oth, recv_far) = call(
        third_kernel,
        [(half, f32, "far"), (half, bf16, "far"), (half, bf16, "far"), (half, bf16, "far"),
         ((4, 4, 2 * BLK), f32, "far"), (half, f32, "near"), (half, bf16, "near")],
        [row_tile, row_tile, *forward_work(4)],
        (place, dec_lengths, mem_lengths, counts,
         *map(Near, (x_half, mixed1_keep, mixed1_recv, so, so_oth, gain2_near, cq_w, cq_oth, mk, mvt, co, co_oth, gain3_near))),
        smem=4, us=9,
        fetch=(feed_in, cotangent, feed_out),
        forward=(mk, mv, mkt, so_oth, co_oth, cq_oth, ck_oth, cv_oth, mixed1_recv),
    )
    n3_recv = swap(n3)

    hidden = feed_in.shape[1]
    units = (HALF, hidden)
    gn3_own, act, gp, out_own, h2_far, n3_far = call(
        feed_kernel,
        [(half, bf16, "far"), (units, bf16, "far"), (units, bf16, "far"), (half, bf16, "far")],
        [],
        (place, *map(Near, (n3, fi, cot, fo))),
        us=5, forward=(h2, n3),
    )
    h2 = h2_far
    n3_recv, act = lax.optimization_barrier((n3_recv, act))
    gn3_oth, act_oth, gp_oth = call(
        feed_kernel,
        [(half, bf16, "near"), (units, bf16, "near"), (units, bf16, "near")],
        [],
        (place_oth, *map(Near, (n3_recv, fi, cot, fo))),
        us=5,
    )
    gn3_recv = swap(gn3_oth)
    quarter = ((256, WIDTH), bf16, "near")
    feed_hold, *feed_send, out_a, out_b = call(
        feed_weights_kernel,
        [((2 * WIDTH, WIDTH), bf16, "near"), *[quarter] * 4, (half, bf16, "far"), (half, bf16, "far")],
        [v((WIDTH, LEN), bf16), v((2, 2 * WIDTH, WIDTH), bf16)],
        (place, h2, out_own, Near(fo), n3_far, gp, Near(n3_recv), Near(gp_oth), act, Near(cot), Near(act_oth)),
        us=5, late=2,
    )
    feed_hold, feed_send = call(
        feed_halve_kernel,
        [(half, bf16, "near")] * 2,
        [],
        (place, Near(feed_hold), *(Near(swap(part, "core")) for part in feed_send)),
        us=SHORT,
    )
    gn3_recv, feed_send = tie(gn3_recv, feed_send)
    feed_got = swap(feed_send, "pair")

    (gb2, dcq, dmk, dmv, gh1, gb1, gm1, gm1_oth, gains, memory_near, n2_near, mixed2_near, keep, recv) = call(
        cross_back_kernel,
        [(half, bf16, "near"), (half, bf16, "near"), (tok, bf16, "near"), (tok, bf16, "near"), (half, f32, "near"),
         (half, bf16, "near"), (part, bf16, "near"), (part, bf16, "near"), ((8, WIDTH), f32, "near")],
        [row_tile, row_tile, v((HALF, BLK), f32), v(half, bf16), v(tok, f32), v(tok, f32), v(half, f32), *backward_work(4)],
        (place, dec_lengths, mem_lengths, counts, gn3_own, Near(gn3_recv), h2, gain3, Half(cotangent),
         cross_out, co_oth_far, cq, mk, mkt, mv, lse2, mixed2, cross_query, cq_oth_far, h1, gain2, self_out, so_oth_far),
        smem=4, us=12, fetch=(memory, n2, mixed2, keep_far, recv_far),
    )
    out_a_recv = swap(out_a)
    feed_hold, feed_send = halve(feed_hold, feed_got, 3)
    gb2, feed_send, out_a_recv = tie(gb2, feed_send, out_a_recv)
    feed_got = swap(feed_send, "ring")
    gm1_recv = swap(gm1_oth)
    (cross_hold, cross_hold_oth, cross_send, q, k, kt_near, v_near, bias, lse1_near, lse1_oth_near, sent,
     dmk, dmv) = call(
        cross_weights_kernel,
        [((640, WIDTH), bf16, "near"), ((640, WIDTH), bf16, "near"), ((1280, WIDTH), bf16, "near")],
        [v((WIDTH, LEN), bf16), v((5, 256, WIDTH), bf16)],
        (place, *map(Near, (memory_near, dmk, dmv, n2_near, dcq, mixed2_near, gb2, keep, gb1, recv))),
        us=3, fetch=(q_far, k_far, kt, val, bias_far, lse1, lse1_oth, send_far), forward=(dmk, dmv),
    )
    cross_got = swap(cross_send, "core")
    cross_oth = (cross_hold_oth.astype(f32) + cross_got[640:].astype(f32)).astype(bf16)
    gm1, cross_oth = tie(gm1, cross_oth)
    cross_recv = swap(cross_oth)
    acc = ((LEN, OWN), f32)
    dq1, dk1, dv1, near1, n1_near, x_near, gain1_near, wq, wk, wv = call(
        self_back_own_kernel,
        [(part, bf16, "near"), (*acc, "near"), (*acc, "near"), (*tiles, "near")],
        [row_tile, *backward_work(2)],
        (place, dec_lengths, counts, *map(Near, (gm1, keep, q, k, kt_near, v_near, bias, lse1_near))),
        smem=3, us=3, fetch=(n1, inputs, gain1, self_query, self_key, self_value),
    )
    for bit in bits[1:]:
        feed_got, dq1 = tie(feed_got, dq1)
        feed_hold, feed_send = halve(feed_hold, feed_got, 3 + bit)
        gm1_recv, feed_send = tie(gm1_recv, feed_send)
        feed_got = swap(feed_send, "ring", bit)
    self_hold, self_send, gi_a, gi_b = call(
        self_back_kernel,
        [((384 + SMALL, WIDTH), bf16, "near"), ((384 + SMALL, WIDTH), bf16, "near"),
         (half, bf16, "far"), (half, bf16, "far")],
        [row_tile, v(part, bf16), v(heads, bf16), v(*acc), v(*acc), v(*tiles),
         v((WIDTH, LEN), bf16), v((3, 256, WIDTH), bf16), v((NB, WIDTH), f32), v((SMALL, WIDTH), f32), *backward_work(2)],
        (place, dec_lengths, counts,
         *map(Near, (gm1_recv, sent, dq1, dk1, dv1, near1, q, k, kt_near, v_near, bias, lse1_oth_near,
                     n1_near, x_near, gh1, gain1_near, gains, wq, wk, wv))),
        smem=3, us=1.5,
    )
    self_got = swap(self_send, "core")
    (feed_own,) = call(
        total_kernel, [((feed_hold.shape[0], WIDTH), bf16, "near")], [], (place, Near(feed_hold), Near(feed_got)), us=SHORT
    )
    joined = ((HALF + SMALL, WIDTH), bf16, "near")
    hold, send = call(
        join_kernel,
        [joined, joined],
        [],
        (place, *map(Near, (cross_hold, cross_got, cross_recv, self_hold, self_got))),
        us=SHORT,
    )
    got, gi_a_recv = swap(send, "pair"), swap(gi_a)
    got, feed_own, gi_a_recv = tie(got, feed_own, gi_a_recv)
    hold, send = halve(hold, got, 3, SMALL)
    for k in reversed(bits[1:]):
        feed_own = merge(feed_own, swap(feed_own, "ring", k), 3 + k)
    send, dmk = tie(send, dmk)
    gmem, gmem_send = call(
        memory_back_kernel,
        [(heads, bf16, "far"), (heads, bf16, "near")],
        [],
        (place, dmk, cross_key, ck_oth, dmv, cross_value, cv_oth),
        us=SHORT,
    )
    gi_b_recv, out_b_recv, gmem_recv = swap(gi_b), swap(out_b), swap(gmem_send)
    for k in bits[1:]:
        got = swap(send, "ring", k - 1)
        if k == 1:
            got, gmem_send, feed_own, gi_b_recv = tie(got, gmem_send, feed_own, gi_b_recv)
        hold, send = halve(hold, got, 3 + k, SMALL)
    feed_own = merge(feed_own, swap(feed_own, "ring"), 3)
    got = swap(send, "ring", bits[-1])
    got, out_b_recv, feed_own = tie(got, out_b_recv, feed_own)
    feed_pair, feed_core = swap(feed_own, "pair"), swap(feed_own, "core")
    own, small = call(
        total_kernel,
        [((hold.shape[0] - SMALL, WIDTH), bf16, "near"), ((SMALL, WIDTH), f32, "near")],
        [],
        (place, Near(hold), Near(got)),
        us=SHORT,
    )
    for k in reversed(bits):
        got = swap(own, "ring", k)
        if k == 0:
            got, feed_pair = tie(got, feed_pair)
        own = merge(own, got, 3 + k)
    own, gmem_recv = tie(own, gmem_recv)
    pair, core_own = swap(own, "pair"), swap(own, "core")
    gain_grads = small[:8] + swap(small[:8])

    def both(part, other):
        return (part.astype(f32) + other.astype(f32)).astype(bf16)

    output = jnp.concatenate([both(out_a, out_a_recv), both(out_b, out_b_recv)])
    grad_inputs = jnp.concatenate([both(gi_a, gi_a_recv), both(gi_b, gi_b_recv)])
    grad_memory = both(gmem, gmem_recv)
    wide_hidden, tall_hidden = ((WIDTH, hidden), f32, "far"), ((hidden, WIDTH), f32, "far")
    feed_in_grad, feed_out_grad = call(
        feed_unfold_kernel,
        [wide_hidden, tall_hidden],
        [],
        (place, *map(Near, (feed_own, feed_pair, feed_core, swap(feed_pair, "core")))),
        us=SHORT,
    )
    pair, output, grad_inputs, grad_memory, feed_in_grad, feed_out_grad = lax.optimization_barrier(
        (pair, output, grad_inputs, grad_memory, feed_in_grad, feed_out_grad)
    )
    narrows, wides = (narrow, f32, "far"), (wide, f32, "far")
    co_grad, so_grad, cq_grad, ck_grad, cv_grad, wq_grad, wk_grad, wv_grad = call(
        unfold_kernel,
        [narrows] * 2 + [wides] * 6,
        [],
        (place, *map(Near, (own, pair, core_own, swap(pair, "core")))),
    )
    return (
        output,
        grad_inputs,
        grad_memory,
        gain_grads[0],
        wq_grad,
        wk_grad,
        wv_grad,
        so_grad,
        small[3:7, :NB].T,
        gain_grads[1],
        cq_grad,
        ck_grad,
        cv_grad,
        co_grad,
        gain_grads[2],
        feed_in_grad,
        feed_out_grad,
    )


def solution(mesh):
    devices = mesh.devices
    rows, tensor = devices.shape
    mesh = Mesh(devices.reshape(rows // 4, 2, 2, tensor), ("ring", "pair", "core", "tensor"))
    dp = ("ring", "pair", "core")
    split = P(dp, None)
    columns, rows = P(None, "tensor"), P("tensor", None)
    return jax.shard_map(
        shards,
        mesh=mesh,
        in_specs=(
            split, split, split, split, split, P(dp),
            P(), columns, columns, columns, rows, columns,
            P(), columns, columns, columns, rows,
            P(), columns, rows,
        ),
        out_specs=(
            split, split, P(dp, "tensor"),
            P(), columns, columns, columns, rows, columns,
            P(), columns, columns, columns, rows,
            P(), columns, rows,
        ),
        check_vma=False,
    )
```

```python
import functools
import math

import jax
import jax.numpy as jnp
from jax import lax
from jax.experimental import pallas as pl
from jax.experimental.pallas import tpu as pltpu
from jax.sharding import Mesh
from jax.sharding import PartitionSpec as P

NB = 32
MAXDIST = 128
SEGS = 16
LEN = 1024
HALF = 512
WIDTH = 512
OWN = 256
BLK = 128
BIG = 1 << 30
MASKED = -1e30
EPS = 1e-06
f32 = jnp.float32
bf16 = jnp.bfloat16
ROOM = 11 * 1024 * 1024
SHORT = 0.05


def thresholds():
    exact = NB // 2
    edges = [
        math.ceil(exact * (MAXDIST / exact) ** (level / (NB - exact)))
        for level in range(1, NB - exact)
    ]
    return list(range(exact + 1)) + edges


THRESHOLDS = thresholds()


def nn(a, b):
    return jnp.dot(a, b, preferred_element_type=f32)


def nt(a, b):
    return lax.dot_general(a, b, (((1,), (1,)), ((), ())), preferred_element_type=f32)


def tn(a, b):
    return lax.dot_general(a, b, (((0,), (0,)), ((), ())), preferred_element_type=f32)


class Half:
    def __init__(self, array):
        self.array = array


class Near:
    def __init__(self, array):
        self.array = array


class Raw:
    def __init__(self, array):
        self.array = array


PACKED = 640
SMALL = 16


def packed_parts(core):
    def at(start, size):
        return pl.ds(pl.multiple_of(start, BLK), size)

    left, right, all_lanes = slice(0, OWN), slice(OWN, WIDTH), slice(0, WIDTH)
    return (
        [(at(core * BLK, BLK), (slice(0, 128), all_lanes))],
        [(at(core * BLK, BLK), (slice(128, 256), all_lanes))],
        [(at(core * 256, 256), (slice(256, 512), left))],
        [(at(core * 256, 256), (slice(256, 512), right))],
        [(at(core * 256, BLK), (slice(512, 640), left)), (at(core * 256 + BLK, BLK), (slice(512, 640), right))],
    )


def pack_kernel(io, place_ref, *refs):
    *weights, pack_ref, sems = refs
    copies = []
    for ref, parts in zip(weights, packed_parts(place_ref[1]), strict=True):
        for rows, where in parts:
            copy = pltpu.make_async_copy(ref.at[rows, :], pack_ref.at[where], sems.at[len(copies)])
            copy.start()
            copies.append(copy)
    for copy in copies:
        copy.wait()


class Copies:
    def __init__(self, sems):
        self.sems, self.used, self.waits, self.out = sems, 0, {}, {}

    def start(self, source, target):
        copy = pltpu.make_async_copy(source, target, self.sems.at[self.used])
        self.used += 1
        copy.start()
        return copy

    def ready(self, *refs):
        for ref in refs:
            for copy in self.waits.pop(id(ref), ()):
                copy.wait()

    def done(self, *refs):
        for ref in refs:
            target, copy = self.out.get(id(ref), (None, True))
            if copy is None:
                self.out[id(ref)] = (target, self.start(ref, target))


def size_of(shape, dtype):
    return math.prod(shape) * jnp.dtype(dtype).itemsize


def call(body, outs, scratch, args, smem=1, us=3, fetch=(), forward=(), late=0):
    tables, operands = args[:smem], args[smem:]
    arrays, in_specs, fetched = [], [], []
    hbm, vmem = pl.BlockSpec(memory_space=pltpu.HBM), pl.BlockSpec(memory_space=pltpu.VMEM)

    def shape_of(operand):
        if isinstance(operand, Half):
            return (HALF, *operand.array.shape[1:]), operand.array.dtype
        return operand.shape, operand.dtype

    for operand in (*operands, *fetch, *map(Near, forward)):
        array = operand.array if isinstance(operand, (Near, Raw, Half)) else operand
        near = isinstance(operand, Near)
        arrays.append(array if near else pltpu.with_memory_space_constraint(array, pltpu.HBM))
        in_specs.append(vmem if near else hbm)
    fetched = [shape_of(o) for o in operands if not isinstance(o, (Near, Raw))]
    out_shapes, out_specs, sent = [], [], []
    extra = [(*shape_of(o), "near") for o in fetch] + [(o.shape, o.dtype, "far") for o in forward]
    for k, (shape, dtype, kind) in enumerate([*outs, *extra]):
        if kind != "far":
            out_shapes.append(jax.ShapeDtypeStruct(shape, dtype))
            out_specs.append(vmem)
        if kind != "near":
            out_shapes.append(pltpu.HBM(shape, dtype))
            out_specs.append(hbm)
        if kind == "far" and k < len(outs):
            sent.append((shape, dtype))
    n_copies = len(fetched) + sum(kind != "near" for _, _, kind in outs) + len(extra)

    def kernel(*refs):
        refs = list(refs)

        def take(n):
            taken = refs[:n]
            del refs[:n]
            return taken

        scalars, sources = take(smem), take(len(operands))
        extra_sources = take(len(extra))
        targets = take(len(out_shapes) - len(extra))
        extra_targets = take(len(extra))
        inner, outer = take(len(fetched)), take(len(sent))
        io = Copies(take(1)[0] if n_copies else None)
        inputs, outputs, wanted = [], [], []

        def source_of(operand, source):
            if isinstance(operand, Half):
                return source.at[pl.ds(pl.multiple_of(scalars[0][0] * HALF, HALF), HALF), :]
            return source

        for operand, source in zip(operands, sources, strict=True):
            if isinstance(operand, (Near, Raw)):
                inputs.append(source)
                continue
            ref = inner.pop(0)
            inputs.append(ref)
            wanted.append((ref, source_of(operand, source)))
        for ref, source in wanted[late:] + wanted[:late]:
            io.waits[id(ref)] = [io.start(source, ref)]
        moved = [
            io.start(source_of(operand, source), target)
            for operand, source, target in zip((*fetch, *forward), extra_sources, extra_targets, strict=True)
        ]
        for _, _, kind in outs:
            ref = outer.pop(0) if kind == "far" else targets.pop(0)
            outputs.append(ref)
            if kind != "near":
                io.out[id(ref)] = (targets.pop(0), None)
        body(io, *scalars, *inputs, *outputs, *refs)
        io.ready(*inputs)
        io.done(*outputs)
        for copy in (*(copy for _, copy in io.out.values()), *moved):
            copy.wait()

    own = [pltpu.VMEM(s, d) for s, d in fetched + sent]
    used = sum(size_of(s, d) for s, d in fetched + sent) + sum(
        size_of(s.shape, s.dtype) for s in scratch if s.memory_space == pltpu.VMEM
    )
    return pl.pallas_call(
        kernel,
        out_shape=tuple(out_shapes),
        in_specs=[pl.BlockSpec(memory_space=pltpu.SMEM)] * smem + in_specs,
        out_specs=tuple(out_specs),
        scratch_shapes=[*own, *([pltpu.SemaphoreType.DMA((n_copies,))] if n_copies else []), *scratch],
        compiler_params=pltpu.CompilerParams(vmem_limit_bytes=used + ROOM),
        cost_estimate=pl.CostEstimate(flops=int(us * 3.3e9), bytes_accessed=int(us * 1e7), transcendentals=0),
    )(*tables, *arrays)


def running_ends(len_ref):
    ends, total = [], 0
    for k in range(SEGS):
        total = total + len_ref[0, k]
        ends.append(total)
    return ends


def live_tokens(ends, count):
    total = 0
    for k in range(SEGS):
        total = jnp.where(k < count, ends[k], total)
    return total


def lookup(pos, ends, values, first):
    found = first
    for k in range(SEGS - 1):
        found = jnp.where(pos >= ends[k], values[k], found)
    return found


def token_positions():
    shape = (LEN // BLK, BLK)
    return lax.broadcasted_iota(jnp.int32, shape, 0) * BLK + lax.broadcasted_iota(
        jnp.int32, shape, 1
    )


def twice(row):
    return jnp.concatenate([row, row], axis=1)


def stacked(pair):
    lane = lax.broadcasted_iota(jnp.int32, pair.shape, 1)
    zero = jnp.zeros_like(pair)
    return jnp.concatenate(
        [jnp.where(lane < 64, pair, zero), jnp.where(lane < 64, zero, pair)], axis=0
    )


def diagonal(product):
    return jnp.concatenate([product[:64, :BLK], product[64:, BLK:]], axis=0)


def own_rows(row):
    return jnp.concatenate(
        [jnp.broadcast_to(row[:, :BLK], (64, BLK)), jnp.broadcast_to(row[:, BLK:], (64, BLK))], axis=0
    )


def in_chunks(n, body):
    def four(j, carry):
        body(4 * j, 4)
        return carry

    lax.fori_loop(0, lax.shift_right_logical(n, 2), four, 0)
    for rest in (3, 2, 1):
        pl.when((n & 3) == rest)(functools.partial(body, n & ~3, rest))


def reset(m_ref, l_ref, acc_ref):
    m_ref[...] = jnp.full(m_ref.shape, MASKED, f32)
    l_ref[...] = jnp.zeros(l_ref.shape, f32)
    acc_ref[...] = jnp.zeros(acc_ref.shape, f32)


def soften(p, scores, values_t, m_ref, l_ref, acc_ref):
    before = m_ref[p, 0:1, :]
    peak = jnp.maximum(before, jnp.max(scores, axis=0, keepdims=True))
    shrink = jnp.exp(before - peak)
    raised = jnp.exp(scores - peak)
    m_ref[p, 0:1, :] = peak
    l_ref[p, 0:1, :] = l_ref[p, 0:1, :] * shrink + jnp.sum(raised, axis=0, keepdims=True)
    acc_ref[p] = acc_ref[p] * own_rows(shrink) + diagonal(nn(values_t, raised.astype(bf16)))


def settle(p, alive, m_ref, l_ref, acc_ref):
    total = l_ref[p, 0:1, :]
    mixed = jnp.transpose(acc_ref[p] * own_rows(alive / total))
    return mixed.astype(bf16), m_ref[p, 0:1, :] + jnp.log(total)


def inner_row(grads, mixed):
    product = jnp.transpose(grads.astype(f32) * mixed.astype(f32))
    return jnp.concatenate(
        [jnp.sum(product[:64], axis=0, keepdims=True), jnp.sum(product[64:], axis=0, keepdims=True)], axis=1
    )


def rms_scale(value):
    return lax.rsqrt(jnp.mean(value * value, axis=-1, keepdims=True) + EPS)


def rms_back(value, gain, grad):
    scale = rms_scale(value)
    weighted = grad * gain
    inner = jnp.mean(weighted * value, axis=-1, keepdims=True)
    unit = value * scale
    return (
        scale * weighted - unit * (scale * scale * inner),
        jnp.sum(grad * unit, axis=0, keepdims=True),
    )


def fill_bias(table_ref, bias_ref):
    key = lax.broadcasted_iota(jnp.int32, (BLK, BLK), 0)
    query = lax.broadcasted_iota(jnp.int32, (BLK, BLK), 1)
    for d in range(2):
        gap = d * BLK + query - key
        tiles = [jnp.full((BLK, BLK), table_ref[h, 0], f32) for h in range(4)]
        for level in range(1, NB):
            reached = gap >= THRESHOLDS[level]
            tiles = [jnp.where(reached, table_ref[h, level], tiles[h]) for h in range(4)]
        if d == 0:
            tiles = [jnp.where(gap >= 0, tile, MASKED) for tile in tiles]
        for h in range(4):
            bias_ref[d * 2 + h // 2, :, (h % 2) * BLK : (h % 2 + 1) * BLK] = tiles[h]
    for h in range(4):
        far = jnp.full((BLK, BLK), table_ref[h, NB - 1], f32)
        bias_ref[4 + h // 2, :, (h % 2) * BLK : (h % 2 + 1) * BLK] = far


def self_scores(distances, p, kstart, qs_ref, k_ref, bias_ref, start2):
    m = len(distances)
    keys = k_ref[pl.ds(kstart, m * BLK), p * BLK : (p + 1) * BLK]
    scores = nt(keys, qs_ref[p])
    parts = [scores[k * BLK : (k + 1) * BLK] + bias_ref[2 * d + p] for k, d in enumerate(distances)]
    index = kstart + lax.broadcasted_iota(jnp.int32, (m * BLK, 2 * BLK), 0)
    return jnp.where(index >= start2, jnp.concatenate(parts, axis=0) if m > 1 else parts[0], MASKED)


def self_spans(b, ends, live):
    pos = b * BLK
    first = lax.shift_right_logical(lookup(pos, ends, ends, 0), 7)
    return pos < live, first, b - first + 1


def self_forward(half, ends, live, q_ref, k_ref, vt_ref, bias_ref, start_ref, o_ref, lse_ref, qs_ref, m_ref, l_ref, acc_ref):
    def step(i, carry):
        b = half * 4 + i
        alive, first, n = self_spans(b, ends, live)
        rows = pl.ds(pl.multiple_of(i * BLK, BLK), BLK)

        @pl.when(alive)
        def _():
            start2 = twice(start_ref[pl.ds(b, 1), :])
            for p in range(2):
                lanes = slice(p * BLK, (p + 1) * BLK)
                qs_ref[p] = stacked(q_ref[pl.ds(pl.multiple_of(b * BLK, BLK), BLK), lanes])
            reset(m_ref, l_ref, acc_ref)

            def chunk(j, m):
                kstart = pl.multiple_of((first + j) * BLK, BLK)
                distances = [jnp.minimum(n - 1 - j - k, 2) for k in range(m)]
                for p in range(2):
                    scores = self_scores(distances, p, kstart, qs_ref, k_ref, bias_ref, start2)
                    values_t = vt_ref[p * BLK : (p + 1) * BLK, pl.ds(kstart, m * BLK)]
                    soften(p, scores, values_t, m_ref, l_ref, acc_ref)

            in_chunks(n, chunk)
            for p in range(2):
                mixed, lse = settle(p, (start2 < BIG).astype(f32), m_ref, l_ref, acc_ref)
                o_ref[rows, p * BLK : (p + 1) * BLK] = mixed
                lse_ref[p, pl.ds(i, 1), :] = lse

        @pl.when(jnp.logical_not(alive))
        def _():
            o_ref[rows, :] = jnp.zeros((BLK, OWN), bf16)
            for p in range(2):
                lse_ref[p, pl.ds(i, 1), :] = jnp.zeros((1, 2 * BLK), f32)

        return carry

    lax.fori_loop(0, 4, step, 0)


def set_starts(ends, live, start_ref):
    pos = token_positions()
    start_ref[...] = jnp.where(pos < live, lookup(pos, ends, ends, 0), BIG)


def first_kernel(
    io, t_ref, len_ref, cnt_ref, table_ref,
    x_ref, gain_ref, wq_ref, wk_ref, wv_ref,
    n1_ref, q_ref, k_ref, v_ref, vt_ref, kt_ref, bias_ref, o_ref, lse_ref,
    start_ref, *work,
):
    ends = running_ends(len_ref)
    live = live_tokens(ends, cnt_ref[0])
    set_starts(ends, live, start_ref)
    fill_bias(table_ref, bias_ref)
    io.done(bias_ref)
    io.ready(x_ref, gain_ref, wq_ref, wk_ref, wv_ref)

    def project(i, carry):
        rows = pl.ds(pl.multiple_of(i * 256, 256), 256)
        value = x_ref[rows, :].astype(f32)
        low = (value * rms_scale(value) * gain_ref[...]).astype(bf16)
        n1_ref[rows, :] = low
        q_ref[rows, :] = nn(low, wq_ref[...]).astype(bf16)
        keys = nn(low, wk_ref[...])
        k_ref[rows, :] = keys.astype(bf16)
        kt_ref[:, rows] = jnp.transpose(keys).astype(bf16)
        values = nn(low, wv_ref[...])
        v_ref[rows, :] = values.astype(bf16)
        vt_ref[:, rows] = jnp.transpose(values).astype(bf16)
        return carry

    lax.fori_loop(0, 4, project, 0)
    io.done(n1_ref, q_ref, k_ref, v_ref, vt_ref, kt_ref)
    self_forward(
        1 - t_ref[0], ends, live, q_ref, k_ref, vt_ref, bias_ref, start_ref, o_ref, lse_ref, *work
    )


def second_kernel(
    io, t_ref, len_ref, cnt_ref,
    q_ref, k_ref, vt_ref, bias_ref,
    o_ref, lse_ref,
    start_ref, *work,
):
    ends = running_ends(len_ref)
    live = live_tokens(ends, cnt_ref[0])
    set_starts(ends, live, start_ref)
    io.ready(q_ref, k_ref, vt_ref, bias_ref)
    self_forward(
        t_ref[0], ends, live, q_ref, k_ref, vt_ref, bias_ref, start_ref, o_ref, lse_ref, *work
    )


def memory_kernel(
    io, place_ref, mem_ref, ck_ref, cv_ref, pack_ref, packo_ref,
    mk_ref, mv_ref, mkt_ref, mvt_ref, so_out, co_out, cq_out, cko_ref, cvo_ref,
):
    for core, pack in ((place_ref[1], pack_ref), (1 - place_ref[1], packo_ref)):
        for ref, parts in zip((so_out, co_out, cq_out, cko_ref, cvo_ref), packed_parts(core), strict=True):
            for rows, where in parts:
                ref[rows, :] = pack[where]
    io.done(so_out, co_out, cq_out, cko_ref, cvo_ref)
    io.ready(mem_ref, ck_ref, cv_ref)

    def project(i, carry):
        rows = pl.ds(pl.multiple_of(i * 256, 256), 256)
        value = mem_ref[rows, :]
        for side, (wk, wv) in enumerate(((ck_ref, cv_ref), (cko_ref, cvo_ref))):
            lanes = slice(side * OWN, (side + 1) * OWN)
            keys = nn(value, wk[...])
            mk_ref[rows, lanes] = keys.astype(bf16)
            mkt_ref[lanes, rows] = jnp.transpose(keys).astype(bf16)
            values = nn(value, wv[...])
            mv_ref[rows, lanes] = values.astype(bf16)
            mvt_ref[lanes, rows] = jnp.transpose(values).astype(bf16)
        return carry

    lax.fori_loop(0, 4, project, 0)


def set_ranges(ends, mends, live, low_ref, high_ref):
    pos = token_positions()
    low_ref[...] = jnp.where(pos < live, lookup(pos, ends, mends, 0), BIG)
    high_ref[...] = lookup(pos, ends, mends[1:], mends[0])


def cross_blocks(half, ends, mends, live, block, dead):
    def step(i, carry):
        b = half * 4 + i
        pos = b * BLK
        alive = pos < live
        last = jnp.minimum(pos + BLK, live) - 1
        first = lax.shift_right_logical(lookup(pos, ends, mends, 0), 7)
        end = lax.shift_right_logical(lookup(last, ends, mends[1:], mends[0]) + BLK - 1, 7)
        pl.when(alive)(lambda: block(i, b, first, end - first))
        pl.when(jnp.logical_not(alive))(lambda: dead(i))
        return carry

    lax.fori_loop(0, 4, step, 0)


def cross_allowed(kstart, m, low2, high2):
    index = kstart + lax.broadcasted_iota(jnp.int32, (m * BLK, 2 * BLK), 0)
    return (index >= low2) & (index < high2)


def third_kernel(
    io, t_ref, len_ref, mlen_ref, cnt_ref,
    x_ref, keep_ref, recv_ref, so_ref, soo_ref, gain2_ref, cq_ref, cqo_ref,
    mk_ref, mvt_ref, co_ref, coo_ref, gain3_ref,
    h1_ref, n2_ref, q_ref, mixed_ref, lse_ref, h2_ref, n3_ref,
    low_ref, high_ref, qs_ref, m_ref, l_ref, acc_ref,
):
    t = t_ref[0]
    ends, mends = running_ends(len_ref), running_ends(mlen_ref)
    live = live_tokens(ends, cnt_ref[0])
    set_ranges(ends, mends, live, low_ref, high_ref)

    io.ready(x_ref, keep_ref, recv_ref, so_ref, soo_ref, gain2_ref, cq_ref, cqo_ref)

    def before(i, carry):
        rows = pl.ds(pl.multiple_of(i * 256, 256), 256)
        value = x_ref[rows, :].astype(f32)
        value = value + nn(keep_ref[rows, :], so_ref[...]) + nn(recv_ref[rows, :], soo_ref[...])
        h1_ref[rows, :] = value
        low = (value * rms_scale(value) * gain2_ref[...]).astype(bf16)
        n2_ref[rows, :] = low
        q_ref[rows, :OWN] = nn(low, cq_ref[...]).astype(bf16)
        q_ref[rows, OWN:] = nn(low, cqo_ref[...]).astype(bf16)
        return carry

    lax.fori_loop(0, 2, before, 0)
    io.done(h1_ref, n2_ref, q_ref)
    io.ready(mk_ref, mvt_ref)

    def block(i, b, first, n):
        low2, high2 = twice(low_ref[pl.ds(b, 1), :]), twice(high_ref[pl.ds(b, 1), :])
        rows = pl.ds(pl.multiple_of(i * BLK, BLK), BLK)
        for p in range(4):
            qs_ref[p] = stacked(q_ref[rows, p * BLK : (p + 1) * BLK])
        reset(m_ref, l_ref, acc_ref)

        def chunk(j, m):
            kstart = pl.multiple_of((first + j) * BLK, BLK)
            span = pl.ds(kstart, m * BLK)
            allowed = cross_allowed(kstart, m, low2, high2)
            for p in range(4):
                lanes = slice(p * BLK, (p + 1) * BLK)
                scores = jnp.where(allowed, nt(mk_ref[span, lanes], qs_ref[p]), MASKED)
                soften(p, scores, mvt_ref[lanes, span], m_ref, l_ref, acc_ref)

        in_chunks(n, chunk)
        for p in range(4):
            mixed, lse = settle(p, (low2 < BIG).astype(f32), m_ref, l_ref, acc_ref)
            mixed_ref[rows, p * BLK : (p + 1) * BLK] = mixed
            lse_ref[p, pl.ds(i, 1), :] = lse

    def dead(i):
        mixed_ref[pl.ds(pl.multiple_of(i * BLK, BLK), BLK), :] = jnp.zeros((BLK, WIDTH), bf16)
        for p in range(4):
            lse_ref[p, pl.ds(i, 1), :] = jnp.zeros((1, 2 * BLK), f32)

    cross_blocks(t, ends, mends, live, block, dead)

    io.done(mixed_ref, lse_ref)
    io.ready(co_ref, coo_ref, gain3_ref)

    def after(i, carry):
        rows = pl.ds(pl.multiple_of(i * 256, 256), 256)
        value = h1_ref[rows, :]
        value = value + nn(mixed_ref[rows, :OWN], co_ref[...]) + nn(mixed_ref[rows, OWN:], coo_ref[...])
        h2_ref[rows, :] = value
        n3_ref[rows, :] = (value * rms_scale(value) * gain3_ref[...]).astype(bf16)
        return carry

    lax.fori_loop(0, 2, after, 0)


def feed_kernel(
    io, place_ref, n3_ref, fi_ref, cot_ref, fo_ref,
    gn_ref, act_ref, gp_ref, *out_refs,
):
    tile = 256
    n_tiles = fi_ref.shape[1] // tile
    root = math.sqrt(2 / math.pi)
    base = place_ref[0] * HALF
    io.ready(n3_ref, fi_ref, cot_ref, fo_ref)

    def hidden(j, carry):
        lanes = pl.ds(pl.multiple_of(j * tile, tile), tile)
        for i in range(2):
            rows = slice(i * 256, (i + 1) * 256)
            pre = nn(n3_ref[rows, :], fi_ref[:, lanes])
            square = pre * pre
            bent = jnp.tanh(pre * (root + (root * 0.044715) * square))
            gate = 0.5 + 0.5 * bent
            slope = gate + pre * (0.5 - 0.5 * bent * bent) * (root + (root * 0.134145) * square)
            act_ref[rows, lanes] = (pre * gate).astype(bf16)
            grads = nt(cot_ref[pl.ds(pl.multiple_of(base + i * 256, 256), 256), :], fo_ref[lanes, :])
            gp_ref[rows, lanes] = (grads * slope).astype(bf16)
        return carry

    lax.fori_loop(0, n_tiles, hidden, 0)
    io.done(act_ref, gp_ref)

    def outward(i, carry):
        rows = pl.ds(pl.multiple_of(i * 256, 256), 256)
        for out_ref in out_refs:
            out_ref[rows, :] = nn(act_ref[rows, :], fo_ref[...]).astype(bf16)
        gn_ref[rows, :] = nt(gp_ref[rows, :], fi_ref[...]).astype(bf16)
        return carry

    lax.fori_loop(0, 2, outward, 0)


def feed_weights_kernel(
    io, place_ref, h2_ref, own_ref, fo_ref, n3_ref, gp_ref, n3o_ref, gpo_ref, act_ref, cot_ref, acto_ref,
    hold_ref, senda_ref, sendb_ref, sendc_ref, sendd_ref, outa_ref, outb_ref,
    n3t_ref, both_ref,
):
    t, c = place_ref[0], place_ref[1]

    parts = (senda_ref, sendb_ref, sendc_ref, sendd_ref)
    mine = pl.ds(pl.multiple_of(t * HALF, HALF), HALF)
    theirs = pl.ds(pl.multiple_of((1 - t) * HALF, HALF), HALF)
    io.ready(n3_ref, gp_ref, n3o_ref, gpo_ref)
    n3t_ref[:, :HALF] = jnp.transpose(n3_ref[...])
    n3t_ref[:, HALF:] = jnp.transpose(n3o_ref[...])
    n_tiles = gp_ref.shape[1] // 256
    for j in range(n_tiles):
        lanes = slice(j * 256, (j + 1) * 256)
        grads = nn(n3t_ref[:, :HALF], gp_ref[:, lanes]) + nn(n3t_ref[:, HALF:], gpo_ref[:, lanes])
        both_ref[0, (j // 2) * WIDTH : (j // 2 + 1) * WIDTH, (j % 2) * 256 : (j % 2 + 1) * 256] = grads.astype(bf16)
    io.ready(act_ref, cot_ref, acto_ref)
    for j in range(n_tiles):
        lanes = slice(j * 256, (j + 1) * 256)
        grads = tn(act_ref[:, lanes], cot_ref[mine, :]) + tn(acto_ref[:, lanes], cot_ref[theirs, :])
        both_ref[1, lanes, :] = grads.astype(bf16)
    hold_ref[...] = both_ref[c]
    for k, ref in enumerate(parts):
        ref[...] = both_ref[1 - c, k * 256 : (k + 1) * 256, :]
    io.ready(h2_ref, own_ref)
    other = nn(acto_ref[...], fo_ref[...]).astype(bf16)
    own = (h2_ref[...] + own_ref[...].astype(f32)).astype(bf16)
    for k, out_ref in enumerate((outa_ref, outb_ref)):

        @pl.when(t == k)
        def _():
            out_ref[...] = own

        @pl.when(t != k)
        def _():
            out_ref[...] = other


def cross_back_kernel(
    io, t_ref, len_ref, mlen_ref, cnt_ref,
    gn_ref, gnr_ref, h2_ref, gain3_ref, cot_ref, co_ref, coo_ref,
    q_ref, mk_ref, mkt_ref, mv_ref, lse_ref, mixed_ref, cq_ref, cqo_ref, h1_ref, gain2_ref, so_ref, soo_ref,
    gb2_ref, dq_ref, dk_ref, dv_ref, gh1_ref, gb1_ref, gm1_ref, gm1o_ref, gains_ref,
    low_ref, high_ref, live_ref, gm_ref, dk_acc, dv_acc, gh2_ref, qs_ref, gs_ref, acc_ref,
):
    t = t_ref[0]
    ends, mends = running_ends(len_ref), running_ends(mlen_ref)
    live = live_tokens(ends, cnt_ref[0])
    set_ranges(ends, mends, live, low_ref, high_ref)
    alive_rows = t * HALF + lax.broadcasted_iota(jnp.int32, (HALF, BLK), 0)
    live_ref[...] = (alive_rows < live).astype(f32)
    dk_acc[...] = jnp.zeros_like(dk_acc)
    dv_acc[...] = jnp.zeros_like(dv_acc)
    gains_ref[...] = jnp.zeros_like(gains_ref)

    io.ready(gn_ref, gnr_ref, h2_ref, gain3_ref, cot_ref, co_ref, coo_ref)
    for i in range(2):
        rows = slice(i * 256, (i + 1) * 256)
        grad = gn_ref[rows, :].astype(f32) + gnr_ref[rows, :].astype(f32)
        back, gain = rms_back(h2_ref[rows, :], gain3_ref[...], grad)
        gains_ref[0:1, :] += gain
        grad = cot_ref[rows, :].astype(f32) + back
        gh2_ref[rows, :] = grad
        low = grad.astype(bf16)
        gb2_ref[rows, :] = low
        alive = live_ref[rows, 0:1]
        gm_ref[rows, :OWN] = (nt(low, co_ref[...]) * alive).astype(bf16)
        gm_ref[rows, OWN:] = (nt(low, coo_ref[...]) * alive).astype(bf16)
    io.done(gb2_ref)
    io.ready(q_ref, mk_ref, mkt_ref, mv_ref, lse_ref, mixed_ref)

    def block(i, b, first, n):
        low2, high2 = twice(low_ref[pl.ds(b, 1), :]), twice(high_ref[pl.ds(b, 1), :])
        rows = pl.ds(pl.multiple_of(i * BLK, BLK), BLK)
        inner = []
        for p in range(4):
            lanes = slice(p * BLK, (p + 1) * BLK)
            qs_ref[p] = stacked(q_ref[rows, lanes])
            gs_ref[p] = stacked(gm_ref[rows, lanes])
            inner.append(inner_row(gm_ref[rows, lanes], mixed_ref[rows, lanes]))
        acc_ref[...] = jnp.zeros(acc_ref.shape, f32)

        def chunk(j, m):
            kstart = pl.multiple_of((first + j) * BLK, BLK)
            span = pl.ds(kstart, m * BLK)
            allowed = cross_allowed(kstart, m, low2, high2)
            for p in range(4):
                lanes = slice(p * BLK, (p + 1) * BLK)
                scores = jnp.where(allowed, nt(mk_ref[span, lanes], qs_ref[p]), MASKED)
                probs = jnp.exp(scores - lse_ref[p, pl.ds(i, 1), :])
                low = (probs * (nt(mv_ref[span, lanes], gs_ref[p]) - inner[p])).astype(bf16)
                dk_acc[span, lanes] += nn(low, qs_ref[p])
                dv_acc[span, lanes] += nn(probs.astype(bf16), gs_ref[p])
                acc_ref[p] += diagonal(nn(mkt_ref[lanes, span], low))

        in_chunks(n, chunk)
        for p in range(4):
            dq_ref[rows, p * BLK : (p + 1) * BLK] = jnp.transpose(acc_ref[p]).astype(bf16)

    def dead(i):
        dq_ref[pl.ds(pl.multiple_of(i * BLK, BLK), BLK), :] = jnp.zeros((BLK, WIDTH), bf16)

    cross_blocks(t, ends, mends, live, block, dead)

    dk_ref[...] = dk_acc[...].astype(bf16)
    dv_ref[...] = dv_acc[...].astype(bf16)
    io.done(dq_ref, dk_ref, dv_ref)
    io.ready(cq_ref, cqo_ref, h1_ref, gain2_ref, so_ref, soo_ref)
    for i in range(2):
        rows = slice(i * 256, (i + 1) * 256)
        grad = nt(dq_ref[rows, :OWN], cq_ref[...]) + nt(dq_ref[rows, OWN:], cqo_ref[...])
        back, gain = rms_back(h1_ref[rows, :], gain2_ref[...], grad)
        gains_ref[1:2, :] += gain
        grad = gh2_ref[rows, :] + back
        gh1_ref[rows, :] = grad
        low = grad.astype(bf16)
        gb1_ref[rows, :] = low
        alive = live_ref[rows, 0:1]
        gm1_ref[rows, :] = (nt(low, so_ref[...]) * alive).astype(bf16)
        gm1o_ref[rows, :] = (nt(low, soo_ref[...]) * alive).astype(bf16)


def cross_weights_kernel(
    io, place_ref, mem_ref, dk_ref, dv_ref, n2_ref, dq_ref, mixed_ref, gb2_ref, keep_ref, gb1_ref, recv_ref,
    hold_ref, holdo_ref, send_ref,
    memt_ref, fold_ref,
):
    c = place_ref[1]
    io.ready(mem_ref, dk_ref, dv_ref, n2_ref, dq_ref, mixed_ref, gb2_ref, keep_ref, gb1_ref, recv_ref)
    memt_ref[...] = jnp.transpose(mem_ref[...])
    n2t = jnp.transpose(n2_ref[...])
    for side in range(2):
        lanes = slice(side * OWN, (side + 1) * OWN)
        mixed1 = keep_ref if side == 0 else recv_ref
        fold_ref[0] = tn(mixed_ref[:, lanes], gb2_ref[...]).astype(bf16)
        fold_ref[1] = tn(mixed1[...], gb1_ref[...]).astype(bf16)
        fold(fold_ref, 2, nn(n2t, dq_ref[:, lanes]))
        fold(fold_ref, 3, nn(memt_ref[...], dk_ref[:, lanes]))
        fold(fold_ref, 4, nn(memt_ref[...], dv_ref[:, lanes]))
        deal(c, fold_ref, hold_ref if side == 0 else holdo_ref, send_ref, side * 640)


def memory_back_kernel(
    io, place_ref, dk_ref, ck_ref, cko_ref, dv_ref, cv_ref, cvo_ref, gmem_ref, gmems_ref, both_ref
):
    t = place_ref[0]
    io.ready(dk_ref, ck_ref, cko_ref, dv_ref, cv_ref, cvo_ref)
    for i in range(4):
        rows = slice(i * 256, (i + 1) * 256)
        grads = nt(dk_ref[rows, :OWN], ck_ref[...]) + nt(dk_ref[rows, OWN:], cko_ref[...])
        grads += nt(dv_ref[rows, :OWN], cv_ref[...]) + nt(dv_ref[rows, OWN:], cvo_ref[...])
        low = grads.astype(bf16)
        both_ref[0, rows, :] = low[:, :OWN]
        both_ref[1, rows, :] = low[:, OWN:]
    gmem_ref[...] = both_ref[t]
    gmems_ref[...] = both_ref[1 - t]


def fold(fold_ref, k, weight):
    low = weight.astype(bf16)
    fold_ref[k, :, :OWN] = low[:256]
    fold_ref[k, :, OWN:] = low[256:]


def deal(c, fold_ref, hold_ref, send_ref, base):
    for k in range(fold_ref.shape[0]):
        rows = slice(k * BLK, (k + 1) * BLK)
        hold_ref[rows, :] = fold_ref[k, pl.ds(pl.multiple_of(c * BLK, BLK), BLK), :]
        rows = slice(base + k * BLK, base + (k + 1) * BLK)
        send_ref[rows, :] = fold_ref[k, pl.ds(pl.multiple_of((1 - c) * BLK, BLK), BLK), :]


def self_back_blocks(
    half, ends, live, start_ref, g_ref, mixed_ref, q_ref, k_ref, kt_ref, v_ref, bias_ref, lse_ref,
    dq_ref, dk_acc, dv_acc, near_acc, qs_ref, gs_ref, acc_ref,
):
    def step(i, carry):
        b = half * 4 + i
        alive, first, n = self_spans(b, ends, live)
        rows = pl.ds(pl.multiple_of(i * BLK, BLK), BLK)

        @pl.when(alive)
        def _():
            start2 = twice(start_ref[pl.ds(b, 1), :])
            inner = []
            for p in range(2):
                lanes = slice(p * BLK, (p + 1) * BLK)
                qs_ref[p] = stacked(q_ref[pl.ds(pl.multiple_of(b * BLK, BLK), BLK), lanes])
                gs_ref[p] = stacked(g_ref[rows, lanes])
                inner.append(inner_row(g_ref[rows, lanes], mixed_ref[rows, lanes]))
            acc_ref[...] = jnp.zeros(acc_ref.shape, f32)

            def chunk(j, m):
                kstart = pl.multiple_of((first + j) * BLK, BLK)
                span = pl.ds(kstart, m * BLK)
                distances = [jnp.minimum(n - 1 - j - k, 2) for k in range(m)]
                for p in range(2):
                    lanes = slice(p * BLK, (p + 1) * BLK)
                    scores = self_scores(distances, p, kstart, qs_ref, k_ref, bias_ref, start2)
                    probs = jnp.exp(scores - lse_ref[p, pl.ds(i, 1), :])
                    grad_scores = probs * (nt(v_ref[span, lanes], gs_ref[p]) - inner[p])
                    for k, d in enumerate(distances):
                        near_acc[2 * d + p] += grad_scores[k * BLK : (k + 1) * BLK]
                    low = grad_scores.astype(bf16)
                    dk_acc[span, lanes] += nn(low, qs_ref[p])
                    dv_acc[span, lanes] += nn(probs.astype(bf16), gs_ref[p])
                    acc_ref[p] += diagonal(nn(kt_ref[lanes, span], low))

            in_chunks(n, chunk)
            for p in range(2):
                dq_ref[rows, p * BLK : (p + 1) * BLK] = jnp.transpose(acc_ref[p]).astype(bf16)

        @pl.when(jnp.logical_not(alive))
        def _():
            dq_ref[rows, :] = jnp.zeros((BLK, OWN), bf16)

        return carry

    lax.fori_loop(0, 4, step, 0)


def self_back_own_kernel(
    io, place_ref, len_ref, cnt_ref,
    gm_ref, mixed_ref, q_ref, k_ref, kt_ref, v_ref, bias_ref, lse_ref,
    dq_ref, dk_acc, dv_acc, near_acc,
    start_ref, *work,
):
    ends = running_ends(len_ref)
    live = live_tokens(ends, cnt_ref[0])
    set_starts(ends, live, start_ref)
    for ref in (dk_acc, dv_acc, near_acc):
        ref[...] = jnp.zeros_like(ref)
    io.ready(gm_ref, mixed_ref, q_ref, k_ref, kt_ref, v_ref, bias_ref, lse_ref)
    self_back_blocks(
        place_ref[0], ends, live, start_ref, gm_ref, mixed_ref, q_ref, k_ref, kt_ref, v_ref, bias_ref, lse_ref,
        dq_ref, dk_acc, dv_acc, near_acc, *work,
    )


def self_back_kernel(
    io, place_ref, len_ref, cnt_ref,
    gmr_ref, mixed_ref, dqm_ref, dkm_ref, dvm_ref, nearm_ref, q_ref, k_ref, kt_ref, v_ref, bias_ref, lse_ref,
    n1_ref, x_ref, gh1_ref, gain1_ref, gains_ref, wq_ref, wk_ref, wv_ref,
    hold_ref, send_ref, gia_ref, gib_ref,
    start_ref, dqo_ref, dq_ref, dk_acc, dv_acc, near_acc, n1t_ref, fold_ref, sums_ref, small_ref, *work,
):
    t = place_ref[0]
    ends = running_ends(len_ref)
    live = live_tokens(ends, cnt_ref[0])
    set_starts(ends, live, start_ref)
    small_ref[...] = jnp.zeros_like(small_ref)
    for ref, so_far in ((dk_acc, dkm_ref), (dv_acc, dvm_ref), (near_acc, nearm_ref)):
        ref[...] = so_far[...]
    io.ready(mixed_ref, q_ref, k_ref, kt_ref, v_ref, bias_ref, lse_ref)
    self_back_blocks(
        1 - t, ends, live, start_ref, gmr_ref, mixed_ref, q_ref, k_ref, kt_ref, v_ref, bias_ref, lse_ref,
        dqo_ref, dk_acc, dv_acc, near_acc, *work,
    )
    dq_ref[pl.ds(pl.multiple_of(t * HALF, HALF), HALF), :] = dqm_ref[...]
    dq_ref[pl.ds(pl.multiple_of((1 - t) * HALF, HALF), HALF), :] = dqo_ref[...]

    io.ready(n1_ref)
    n1t_ref[...] = jnp.transpose(n1_ref[...])
    low_k, low_v = dk_acc[...].astype(bf16), dv_acc[...].astype(bf16)
    for k, grads in enumerate((dq_ref[...], low_k, low_v)):
        fold(fold_ref, k, nn(n1t_ref[...], grads))
    deal(place_ref[1], fold_ref, hold_ref, send_ref, 0)
    io.ready(x_ref, gh1_ref, gain1_ref, gains_ref, wq_ref, wk_ref, wv_ref)
    gain1 = jnp.zeros((1, WIDTH), f32)
    for i in range(4):
        rows = slice(i * 256, (i + 1) * 256)
        grads = nt(dq_ref[rows, :], wq_ref[...]) + nt(low_k[rows], wk_ref[...]) + nt(low_v[rows], wv_ref[...])
        back, gain = rms_back(x_ref[rows, :].astype(f32), gain1_ref[...], grads)
        gain1 += gain
        mine = (t == i // 2).astype(f32)
        back += mine * gh1_ref[(i % 2) * 256 : (i % 2 + 1) * 256, :]
        (gia_ref if i < 2 else gib_ref)[(i % 2) * 256 : (i % 2 + 1) * 256, :] = back.astype(bf16)
    io.done(gia_ref, gib_ref)
    key = lax.broadcasted_iota(jnp.int32, (BLK, BLK), 0)
    query = lax.broadcasted_iota(jnp.int32, (BLK, BLK), 1)
    gaps = [query - key, BLK + query - key]
    for level in range(NB):
        for p in range(2):
            row = jnp.zeros((1, 2 * BLK), f32)
            for d in range(2):
                inside = gaps[d] >= THRESHOLDS[level]
                if level + 1 < NB:
                    inside &= gaps[d] < THRESHOLDS[level + 1]
                picked = jnp.where(twice(inside.astype(f32)) > 0, near_acc[2 * d + p], 0.0)
                row += jnp.sum(picked, axis=0, keepdims=True)
            if level == NB - 1:
                row += jnp.sum(near_acc[4 + p], axis=0, keepdims=True)
            sums_ref[level : level + 1, p * 256 : (p + 1) * 256] = row
    for h in range(4):
        lanes = jnp.transpose(sums_ref[:, h * BLK : (h + 1) * BLK])
        small_ref[3 + h : 4 + h, :NB] = jnp.sum(lanes, axis=0, keepdims=True)
    for k, gain in enumerate((gain1, gains_ref[1:2, :], gains_ref[0:1, :])):
        small_ref[k : k + 1, :] = gain
    low = small_ref[...].astype(bf16)
    hold_ref[384:, :] = low
    send_ref[384:, :] = low


def join_kernel(io, place_ref, own_ref, got_ref, recv_ref, mine_ref, theirs_ref, hold_ref, send_ref):
    x = place_ref[2]
    io.ready(own_ref, got_ref, recv_ref, mine_ref, theirs_ref)
    for k in range(8):
        if k < 5:
            rows = slice(k * BLK, (k + 1) * BLK)
            total = own_ref[rows, :].astype(f32) + got_ref[rows, :].astype(f32) + recv_ref[rows, :].astype(f32)
        else:
            rows = slice((k - 5) * BLK, (k - 4) * BLK)
            total = mine_ref[rows, :].astype(f32) + theirs_ref[rows, :].astype(f32)
        low = total.astype(bf16)
        rows = slice((k % 4) * BLK, (k % 4 + 1) * BLK)

        @pl.when(x == k // 4)
        def _():
            hold_ref[rows, :] = low

        @pl.when(x != k // 4)
        def _():
            send_ref[rows, :] = low

    low = (mine_ref[384:, :].astype(f32) + theirs_ref[384:, :].astype(f32)).astype(bf16)
    hold_ref[HALF:, :] = low
    send_ref[HALF:, :] = low


def feed_halve_kernel(io, place_ref, hold_ref, gota_ref, gotb_ref, gotc_ref, gotd_ref, keep_ref, send_ref):
    x = place_ref[2]
    for k, got_ref in enumerate((gota_ref, gotb_ref, gotc_ref, gotd_ref)):
        rows, to = slice(k * 256, (k + 1) * 256), slice((k % 2) * 256, (k % 2 + 1) * 256)
        low = (hold_ref[rows, :].astype(f32) + got_ref[...].astype(f32)).astype(bf16)

        @pl.when(x == k // 2)
        def _():
            keep_ref[to, :] = low

        @pl.when(x != k // 2)
        def _():
            send_ref[to, :] = low


def halve_kernel(slot, every, io, place_ref, hold_ref, got_ref, keep_ref, send_ref):
    bit, size = place_ref[slot], keep_ref.shape[0] - every
    io.ready(hold_ref, got_ref)
    for k in range(2):
        rows = slice(k * size, (k + 1) * size)
        low = (hold_ref[rows, :].astype(f32) + got_ref[rows, :].astype(f32)).astype(bf16)

        @pl.when(bit == k)
        def _():
            keep_ref[:size, :] = low

        @pl.when(bit != k)
        def _():
            send_ref[:size, :] = low

    if every:
        low = (hold_ref[2 * size :, :].astype(f32) + got_ref[2 * size :, :].astype(f32)).astype(bf16)
        keep_ref[size:, :] = low
        send_ref[size:, :] = low


def total_kernel(io, _, hold_ref, got_ref, out_ref, *small_refs):
    io.ready(hold_ref, got_ref)
    total = hold_ref[...].astype(f32) + got_ref[...].astype(f32)
    out_ref[...] = total[: out_ref.shape[0]].astype(bf16)
    for small_ref in small_refs:
        small_ref[...] = total[out_ref.shape[0] :]


def merge_kernel(slot, io, place_ref, own_ref, got_ref, out_ref):
    bit, size = place_ref[slot], own_ref.shape[0]
    io.ready(own_ref, got_ref)
    out_ref[pl.ds(pl.multiple_of(bit * size, size), size), :] = own_ref[...]
    out_ref[pl.ds(pl.multiple_of((1 - bit) * size, size), size), :] = got_ref[...]


def feed_unfold_kernel(io, place_ref, own_ref, pair_ref, core_ref, both_ref, fi_ref, fo_ref):
    c, x = place_ref[1], place_ref[2]
    io.ready(own_ref, pair_ref, core_ref, both_ref)
    for ref, core, bit in ((own_ref, c, x), (pair_ref, c, 1 - x), (core_ref, 1 - c, x), (both_ref, 1 - c, 1 - x)):
        at = pl.ds(pl.multiple_of(bit * WIDTH, WIDTH), WIDTH)

        @pl.when(core == 0)
        def _():
            fi_ref[:, at] = ref[...].astype(f32)

        @pl.when(core != 0)
        def _():
            fo_ref[at, :] = ref[...].astype(f32)


def unfold_kernel(
    io, place_ref, own_ref, pair_ref, core_ref, both_ref,
    co_ref, so_ref, cq_ref, ck_ref, cv_ref, wq_ref, wk_ref, wv_ref,
):
    c, x = place_ref[1], place_ref[2]
    outs = (co_ref, so_ref, cq_ref, ck_ref, cv_ref, wq_ref, wk_ref, wv_ref)

    def spread(ref, core, bit):
        low = pl.ds(pl.multiple_of(core * BLK, BLK), BLK)
        high = pl.ds(pl.multiple_of(256 + core * BLK, BLK), BLK)
        for k, out in enumerate(outs):
            rows = slice((k % 4) * BLK, (k % 4 + 1) * BLK)

            @pl.when(bit == k // 4)
            def _():
                if k < 2:
                    out[low, :] = ref[rows, :].astype(f32)
                else:
                    out[low, :] = ref[rows, :OWN].astype(f32)
                    out[high, :] = ref[rows, OWN:].astype(f32)

    for ref, core, bit in ((own_ref, c, x), (pair_ref, c, 1 - x), (core_ref, 1 - c, x), (both_ref, 1 - c, 1 - x)):
        io.ready(ref)
        spread(ref, core, bit)


def swap(value, axis="tensor", bit=0):
    return lax.ppermute(value, axis, [(i, i ^ (1 << bit)) for i in range(lax.axis_size(axis))])


def shards(
    inputs, memory, cotangent, dec_lengths, mem_lengths, counts,
    self_gain, self_query, self_key, self_value, self_out, rel_table,
    cross_gain, cross_query, cross_key, cross_value, cross_out,
    feed_gain, feed_in, feed_out,
):
    v = pltpu.VMEM
    i32 = jnp.int32
    t, c, x = (lax.axis_index(name).astype(i32) for name in ("tensor", "core", "pair"))
    ring = lax.axis_size("ring")
    at_ring = lax.axis_index("ring").astype(i32)
    bits = range(ring.bit_length() - 1)
    ring_bits = [lax.shift_right_logical(at_ring, k) & 1 for k in bits]
    place = jnp.stack([t, c, x, *ring_bits])
    place_oth = jnp.stack([1 - t, c, x, *ring_bits])

    def halve(hold, got, slot, every=0):
        shape = (((hold.shape[0] - every) // 2 + every, WIDTH), bf16, "near")
        return call(
            functools.partial(halve_kernel, slot, every), [shape, shape], [], (place, Near(hold), Near(got)), us=SHORT
        )

    def merge(own, got, slot):
        shape = ((2 * own.shape[0], WIDTH), bf16, "near")
        return call(functools.partial(merge_kernel, slot), [shape], [], (place, Near(own), Near(got)), us=SHORT)[0]

    def tie(*arrays):
        return lax.optimization_barrier(arrays)
    gain1, gain2, gain3 = (g.reshape(1, WIDTH) for g in (self_gain, cross_gain, feed_gain))
    table = rel_table.T

    tok = (LEN, WIDTH)
    half = (HALF, WIDTH)
    heads, heads_t, part = (LEN, OWN), (OWN, LEN), (HALF, OWN)
    narrow, wide = (OWN, WIDTH), (WIDTH, OWN)
    row_tile = v((LEN // BLK, BLK), i32)
    tiles = ((6, BLK, 2 * BLK), f32)

    def forward_work(n):
        rows = v((n, 8, 2 * BLK), f32)
        return [v((n, 2 * BLK, BLK), bf16), rows, rows, v((n, BLK, BLK), f32)]

    def backward_work(n):
        return [v((n, 2 * BLK, BLK), bf16), v((n, 2 * BLK, BLK), bf16), v((n, BLK, BLK), f32)]

    pack, x_near, gain1_near, wq, wk, wv = call(
        pack_kernel,
        [((PACKED, WIDTH), bf16, "near")],
        [pltpu.SemaphoreType.DMA((6,))],
        (place, *map(Raw, (self_out, cross_out, cross_query, cross_key, cross_value))),
        us=SHORT, fetch=(inputs, gain1, self_query, self_key, self_value),
    )
    pack = swap(pack)
    n1, q, q_far, k, k_far, val, vt, kt, bias, bias_far, send1, lse1_oth = call(
        first_kernel,
        [(tok, bf16, "far"), (heads, bf16, "both"), (heads, bf16, "both"), (heads, bf16, "far"),
         (heads_t, bf16, "near"), (heads_t, bf16, "far"), (*tiles, "both"), (part, bf16, "near"),
         ((2, 4, 2 * BLK), f32, "near")],
        [row_tile, *forward_work(2)],
        (place, dec_lengths, counts, table, *map(Near, (x_near, gain1_near, wq, wk, wv))),
        smem=4, us=6,
    )
    mixed1_recv = swap(send1)
    mixed1_keep, lse1, memory_near, ck, cv, lse1_oth, send_far = call(
        second_kernel,
        [(part, bf16, "near"), ((2, 4, 2 * BLK), f32, "near")],
        [row_tile, *forward_work(2)],
        (place, dec_lengths, counts, Near(q), Near(k), Near(vt), Near(bias)),
        smem=3, us=SHORT, fetch=(memory, cross_key, cross_value), forward=(lse1_oth, send1),
    )
    pack, mixed1_keep = lax.optimization_barrier((pack, mixed1_keep))
    pack_core = swap(pack, "core")
    mk, mv, mkt, mvt, so_oth, co_oth, cq_oth, ck_oth, cv_oth, x_half, so, gain2_near, cq_w, co, gain3_near, keep_far, lse1 = call(
        memory_kernel,
        [(tok, bf16, "near"), (tok, bf16, "near"), ((WIDTH, LEN), bf16, "near"), ((WIDTH, LEN), bf16, "near"),
         (narrow, bf16, "near"), (narrow, bf16, "near"), (wide, bf16, "near"), (wide, bf16, "near"), (wide, bf16, "near")],
        [],
        (place, *map(Near, (memory_near, ck, cv, pack, pack_core))),
        us=SHORT, fetch=(Half(inputs), self_out, gain2, cross_query, cross_out, gain3), forward=(mixed1_keep, lse1),
    )
    (h1, n2, cq, mixed2, lse2, h2, n3, fi, cot, fo,
     mk, mv, mkt, so_oth_far, co_oth_far, cq_oth_far, ck_oth, cv_oth, recv_far) = call(
        third_kernel,
        [(half, f32, "far"), (half, bf16, "far"), (half, bf16, "far"), (half, bf16, "far"),
         ((4, 4, 2 * BLK), f32, "far"), (half, f32, "near"), (half, bf16, "near")],
        [row_tile, row_tile, *forward_work(4)],
        (place, dec_lengths, mem_lengths, counts,
         *map(Near, (x_half, mixed1_keep, mixed1_recv, so, so_oth, gain2_near, cq_w, cq_oth, mk, mvt, co, co_oth, gain3_near))),
        smem=4, us=9,
        fetch=(feed_in, cotangent, feed_out),
        forward=(mk, mv, mkt, so_oth, co_oth, cq_oth, ck_oth, cv_oth, mixed1_recv),
    )
    n3_recv = swap(n3)

    hidden = feed_in.shape[1]
    units = (HALF, hidden)
    gn3_own, act, gp, out_own, h2_far, n3_far = call(
        feed_kernel,
        [(half, bf16, "far"), (units, bf16, "far"), (units, bf16, "far"), (half, bf16, "far")],
        [],
        (place, *map(Near, (n3, fi, cot, fo))),
        us=5, forward=(h2, n3),
    )
    h2 = h2_far
    n3_recv, act = lax.optimization_barrier((n3_recv, act))
    gn3_oth, act_oth, gp_oth = call(
        feed_kernel,
        [(half, bf16, "near"), (units, bf16, "near"), (units, bf16, "near")],
        [],
        (place_oth, *map(Near, (n3_recv, fi, cot, fo))),
        us=5,
    )
    gn3_recv = swap(gn3_oth)
    quarter = ((256, WIDTH), bf16, "near")
    feed_hold, *feed_send, out_a, out_b = call(
        feed_weights_kernel,
        [((2 * WIDTH, WIDTH), bf16, "near"), *[quarter] * 4, (half, bf16, "far"), (half, bf16, "far")],
        [v((WIDTH, LEN), bf16), v((2, 2 * WIDTH, WIDTH), bf16)],
        (place, h2, out_own, Near(fo), n3_far, gp, Near(n3_recv), Near(gp_oth), act, Near(cot), Near(act_oth)),
        us=5, late=2,
    )
    feed_hold, feed_send = call(
        feed_halve_kernel,
        [(half, bf16, "near")] * 2,
        [],
        (place, Near(feed_hold), *(Near(swap(part, "core")) for part in feed_send)),
        us=SHORT,
    )
    gn3_recv, feed_send = tie(gn3_recv, feed_send)
    feed_got = swap(feed_send, "pair")

    (gb2, dcq, dmk, dmv, gh1, gb1, gm1, gm1_oth, gains, memory_near, n2_near, mixed2_near, keep, recv) = call(
        cross_back_kernel,
        [(half, bf16, "near"), (half, bf16, "near"), (tok, bf16, "near"), (tok, bf16, "near"), (half, f32, "near"),
         (half, bf16, "near"), (part, bf16, "near"), (part, bf16, "near"), ((8, WIDTH), f32, "near")],
        [row_tile, row_tile, v((HALF, BLK), f32), v(half, bf16), v(tok, f32), v(tok, f32), v(half, f32), *backward_work(4)],
        (place, dec_lengths, mem_lengths, counts, gn3_own, Near(gn3_recv), h2, gain3, Half(cotangent),
         cross_out, co_oth_far, cq, mk, mkt, mv, lse2, mixed2, cross_query, cq_oth_far, h1, gain2, self_out, so_oth_far),
        smem=4, us=12, fetch=(memory, n2, mixed2, keep_far, recv_far),
    )
    out_a_recv = swap(out_a)
    feed_hold, feed_send = halve(feed_hold, feed_got, 3)
    gb2, feed_send, out_a_recv = tie(gb2, feed_send, out_a_recv)
    feed_got = swap(feed_send, "ring")
    gm1_recv = swap(gm1_oth)
    (cross_hold, cross_hold_oth, cross_send, q, k, kt_near, v_near, bias, lse1_near, lse1_oth_near, sent,
     dmk, dmv) = call(
        cross_weights_kernel,
        [((640, WIDTH), bf16, "near"), ((640, WIDTH), bf16, "near"), ((1280, WIDTH), bf16, "near")],
        [v((WIDTH, LEN), bf16), v((5, 256, WIDTH), bf16)],
        (place, *map(Near, (memory_near, dmk, dmv, n2_near, dcq, mixed2_near, gb2, keep, gb1, recv))),
        us=3, fetch=(q_far, k_far, kt, val, bias_far, lse1, lse1_oth, send_far), forward=(dmk, dmv),
    )
    cross_got = swap(cross_send, "core")
    cross_oth = (cross_hold_oth.astype(f32) + cross_got[640:].astype(f32)).astype(bf16)
    gm1, cross_oth = tie(gm1, cross_oth)
    cross_recv = swap(cross_oth)
    acc = ((LEN, OWN), f32)
    dq1, dk1, dv1, near1, n1_near, x_near, gain1_near, wq, wk, wv = call(
        self_back_own_kernel,
        [(part, bf16, "near"), (*acc, "near"), (*acc, "near"), (*tiles, "near")],
        [row_tile, *backward_work(2)],
        (place, dec_lengths, counts, *map(Near, (gm1, keep, q, k, kt_near, v_near, bias, lse1_near))),
        smem=3, us=3, fetch=(n1, inputs, gain1, self_query, self_key, self_value),
    )
    for bit in bits[1:]:
        feed_got, dq1 = tie(feed_got, dq1)
        feed_hold, feed_send = halve(feed_hold, feed_got, 3 + bit)
        gm1_recv, feed_send = tie(gm1_recv, feed_send)
        feed_got = swap(feed_send, "ring", bit)
    self_hold, self_send, gi_a, gi_b = call(
        self_back_kernel,
        [((384 + SMALL, WIDTH), bf16, "near"), ((384 + SMALL, WIDTH), bf16, "near"),
         (half, bf16, "far"), (half, bf16, "far")],
        [row_tile, v(part, bf16), v(heads, bf16), v(*acc), v(*acc), v(*tiles),
         v((WIDTH, LEN), bf16), v((3, 256, WIDTH), bf16), v((NB, WIDTH), f32), v((SMALL, WIDTH), f32), *backward_work(2)],
        (place, dec_lengths, counts,
         *map(Near, (gm1_recv, sent, dq1, dk1, dv1, near1, q, k, kt_near, v_near, bias, lse1_oth_near,
                     n1_near, x_near, gh1, gain1_near, gains, wq, wk, wv))),
        smem=3, us=1.5,
    )
    self_got = swap(self_send, "core")
    (feed_own,) = call(
        total_kernel, [((feed_hold.shape[0], WIDTH), bf16, "near")], [], (place, Near(feed_hold), Near(feed_got)), us=SHORT
    )
    joined = ((HALF + SMALL, WIDTH), bf16, "near")
    hold, send = call(
        join_kernel,
        [joined, joined],
        [],
        (place, *map(Near, (cross_hold, cross_got, cross_recv, self_hold, self_got))),
        us=SHORT,
    )
    got, gi_a_recv = swap(send, "pair"), swap(gi_a)
    got, feed_own, gi_a_recv = tie(got, feed_own, gi_a_recv)
    hold, send = halve(hold, got, 3, SMALL)
    for k in reversed(bits[1:]):
        feed_own = merge(feed_own, swap(feed_own, "ring", k), 3 + k)
    send, dmk = tie(send, dmk)
    gmem, gmem_send = call(
        memory_back_kernel,
        [(heads, bf16, "far"), (heads, bf16, "near")],
        [v((2, *heads), bf16)],
        (place, dmk, cross_key, ck_oth, dmv, cross_value, cv_oth),
        us=SHORT,
    )
    gi_b_recv, out_b_recv, gmem_recv = swap(gi_b), swap(out_b), swap(gmem_send)
    for k in bits[1:]:
        got = swap(send, "ring", k - 1)
        if k == 1:
            got, gmem_send, feed_own, gi_b_recv = tie(got, gmem_send, feed_own, gi_b_recv)
        hold, send = halve(hold, got, 3 + k, SMALL)
    feed_own = merge(feed_own, swap(feed_own, "ring"), 3)
    got = swap(send, "ring", bits[-1])
    got, out_b_recv, feed_own = tie(got, out_b_recv, feed_own)
    feed_pair, feed_core = swap(feed_own, "pair"), swap(feed_own, "core")
    own, small = call(
        total_kernel,
        [((hold.shape[0] - SMALL, WIDTH), bf16, "near"), ((SMALL, WIDTH), f32, "near")],
        [],
        (place, Near(hold), Near(got)),
        us=SHORT,
    )
    for k in reversed(bits):
        got = swap(own, "ring", k)
        if k == 0:
            got, feed_pair = tie(got, feed_pair)
        own = merge(own, got, 3 + k)
    own, gmem_recv = tie(own, gmem_recv)
    pair, core_own = swap(own, "pair"), swap(own, "core")
    gain_grads = small[:8] + swap(small[:8])

    def both(part, other):
        return (part.astype(f32) + other.astype(f32)).astype(bf16)

    output = jnp.concatenate([both(out_a, out_a_recv), both(out_b, out_b_recv)])
    grad_inputs = jnp.concatenate([both(gi_a, gi_a_recv), both(gi_b, gi_b_recv)])
    grad_memory = both(gmem, gmem_recv)
    wide_hidden, tall_hidden = ((WIDTH, hidden), f32, "far"), ((hidden, WIDTH), f32, "far")
    feed_in_grad, feed_out_grad = call(
        feed_unfold_kernel,
        [wide_hidden, tall_hidden],
        [],
        (place, *map(Near, (feed_own, feed_pair, feed_core, swap(feed_pair, "core")))),
        us=SHORT,
    )
    pair, output, grad_inputs, grad_memory, feed_in_grad, feed_out_grad = lax.optimization_barrier(
        (pair, output, grad_inputs, grad_memory, feed_in_grad, feed_out_grad)
    )
    narrows, wides = (narrow, f32, "far"), (wide, f32, "far")
    co_grad, so_grad, cq_grad, ck_grad, cv_grad, wq_grad, wk_grad, wv_grad = call(
        unfold_kernel,
        [narrows] * 2 + [wides] * 6,
        [],
        (place, *map(Near, (own, pair, core_own, swap(pair, "core")))),
    )
    return (
        output,
        grad_inputs,
        grad_memory,
        gain_grads[0],
        wq_grad,
        wk_grad,
        wv_grad,
        so_grad,
        small[3:7, :NB].T,
        gain_grads[1],
        cq_grad,
        ck_grad,
        cv_grad,
        co_grad,
        gain_grads[2],
        feed_in_grad,
        feed_out_grad,
    )


def solution(mesh):
    devices = mesh.devices
    rows, tensor = devices.shape
    mesh = Mesh(devices.reshape(rows // 4, 2, 2, tensor), ("ring", "pair", "core", "tensor"))
    dp = ("ring", "pair", "core")
    split = P(dp, None)
    columns, rows = P(None, "tensor"), P("tensor", None)
    return jax.shard_map(
        shards,
        mesh=mesh,
        in_specs=(
            split, split, split, split, split, P(dp),
            P(), columns, columns, columns, rows, columns,
            P(), columns, columns, columns, rows,
            P(), columns, rows,
        ),
        out_specs=(
            split, split, P(dp, "tensor"),
            P(), columns, columns, columns, rows, columns,
            P(), columns, columns, columns, rows,
            P(), columns, rows,
        ),
        check_vma=False,
    )
```
